32 devices in a mesh: dp: 8 (over z, x), mode: 4 (over y, core).
Axes of the slice: x: 2, y: 2, z: 4, core: 2. Of those that a mesh axis runs over, the one named last changes fastest.
Arguments:
- inputs: bfloat16 [512, 96, 512], P(('dp', 'mode')), may hold values from -6 to 6
- observed: int32 [512, 96], P(('dp', 'mode')), may hold values 0 or 1
- out_grad: bfloat16 [512, 96, 512], P(('dp', 'mode')), may hold values from -6 to 6
- mode_index: int32 [48], replicated, may hold values from 1 to 48, as said below
- owner_list: int32 [256], replicated, may hold values from 0 to 255, each once
- dense_master: float32 [5120, 512], P(('dp', 'mode')), may hold values from -0.25 to 0.25
- dense_first: float32 [5120, 512], P(('dp', 'mode')), may hold values from -64 to 64
- dense_second: float32 [5120, 512], P(('dp', 'mode')), may hold values from 638.976 to 2555.904
- mixer_master: float32 [48, 512, 128], P('mode', 'dp'), may hold values from -0.625 to 0.625
- mixer_first: float32 [48, 512, 128], P('mode', 'dp'), may hold values from -20 to 20
- mixer_second: float32 [48, 512, 128], P('mode', 'dp'), may hold values from 51.2 to 204.8
- small_master: float32 [1044], replicated, may hold values from -3 to 3
- small_first: float32 [1044], replicated, may hold values from -64 to 64
- small_second: float32 [1044], replicated, may hold values from 638.976 to 2555.904
Outputs:
- output: bfloat16 [512, 96, 512], P(('dp', 'mode'))
- input_grad: float32 [512, 96, 512], P(('dp', 'mode'))
- dense_first_new: float32 [5120, 512], P(('dp', 'mode'))
- dense_second_new: float32 [5120, 512], P(('dp', 'mode'))
- dense_new: float32 [5120, 512], P(('dp', 'mode'))
- mixer_first_new: float32 [48, 512, 128], P('mode', 'dp')
- mixer_second_new: float32 [48, 512, 128], P('mode', 'dp')
- mixer_new: float32 [48, 512, 128], P('mode', 'dp')
- small_first_new: float32 [1044], replicated
- small_second_new: float32 [1044], replicated
- small_new: float32 [1044], replicated
- bias_out_grad: float32 [512], replicated
The draws below stay inside these ranges and needn't reach their ends.
Inputs may be any that keep to these rules, and one draw needn't show every extreme that they name: `mode_index`: distinct values. `owner_list`: a permutation of 0 to 255.
All inputs are finite; a program needn't handle non-finite values. No bound on the sum of `observed` on one device may be relied on, other than what follows from the above.
Results may differ from the reference program's by a relative error of at most 0.02.
Values may be sent and summed in bfloat16 or wider, within the bound.
A program may use at most 256 MiB of HBM per device.

```python
import math
import jax
import jax.numpy as jnp
from jax import lax

D = 512
HEADS = 8
FF = 2048
L = 96
MODES = 48
BLOCKS = 256
STEP = 10
WIN_DEV = 16
E = 64
WINDOWS = 512
TOKENS = 49152
ROWS = 5120
SMALL = 1044
N_MODE = 4


def draw_mode_index(key, part):
    key = jax.random.fold_in(key, 5)
    return (jax.random.permutation(key, MODES) + 1).astype(jnp.int32)


def set_ends(entries, key, smallest, top_value):
    longest = entries.shape.index(max(entries.shape))
    spots = []
    for shift in (0, 1):
        where = [jax.random.randint(jax.random.fold_in(key, axis), (), 0, length) for axis, length in enumerate(entries.shape)]
        where[longest] = (where[longest] + shift) % entries.shape[longest]
        spots.append(tuple(where))
    return entries.at[spots[0]].set(smallest).at[spots[1]].set(top_value)


def level_of(rng, shape, cuts, least, top_value):
    loudness = 1.0
    for axis_at, shards_of in cuts:
        draws = jax.random.uniform(jax.random.fold_in(jax.random.fold_in(rng, 6), axis_at), (shards_of,), jnp.float32, least / len(cuts), top_value / len(cuts))
        loudness = loudness * jnp.repeat(jnp.exp(draws), shape[axis_at] // shards_of).reshape((-1,) + (1,) * (len(shape) - 1 - axis_at))
    return loudness


def gaussian(rng, extent, scale, limit, cuts=(), kind=jnp.bfloat16):
    loudness = level_of(rng, extent, cuts, -0.22, 0.18) if cuts else 1.0
    values = jax.random.normal(rng, extent, jnp.float32) * scale * loudness
    return jnp.minimum(jnp.maximum(values, -limit), limit).astype(kind)


def setup_inputs(seed: int = 0) -> dict:
    arg_keys = jax.random.split(jax.random.key(seed), 15)
    return {
        "inputs": gaussian(arg_keys[0], (WINDOWS, L, D), 1.0, 6.0, ((0, 32),)),
        "observed": set_ends((jax.random.randint(arg_keys[1], (WINDOWS, L), 0, 4) < 3).astype(jnp.int32), jax.random.fold_in(arg_keys[1], 1), 0, 1),
        "out_grad": gaussian(arg_keys[2], (WINDOWS, L, D), 1.0, 6.0, ((0, 32),)),
        "mode_index": draw_mode_index(jax.random.fold_in(arg_keys[14], 71), 0),
        "owner_list": jax.random.permutation(arg_keys[4], BLOCKS).astype(jnp.int32),
        "dense_master": gaussian(arg_keys[5], (ROWS, D), D ** -0.5, 0.25, ((0, 32),), jnp.float32),
        "dense_first": gaussian(arg_keys[6], (ROWS, D), (0.055 * TOKENS ** 0.5), 64.0, ((0, 32),), jnp.float32),
        "dense_second": jnp.clip(jnp.exp(math.log(2555.904) - 1.3862944 * jax.random.uniform(arg_keys[7], (ROWS, D), jnp.float32) ** level_of(arg_keys[7], (ROWS, D), ((0, 32),), -0.2, 0.2)), 638.976, 2555.904),
        "mixer_master": gaussian(arg_keys[8], (MODES, D, 2 * E), 0.04, 0.625, ((0, 4), (1, 8)), jnp.float32),
        "mixer_first": gaussian(arg_keys[9], (MODES, D, 2 * E), (0.15 * WINDOWS ** 0.5), 20.0, ((0, 4), (1, 8)), jnp.float32),
        "mixer_second": jnp.clip(jnp.exp(math.log(204.8) - 1.3862944 * jax.random.uniform(arg_keys[10], (MODES, D, 2 * E), jnp.float32) ** level_of(arg_keys[10], (MODES, D, 2 * E), ((0, 4), (1, 8)), -0.2, 0.2)), 51.2, 204.8),
        "small_master": gaussian(arg_keys[11], (SMALL,), 0.5, 3.0, (), jnp.float32),
        "small_first": gaussian(arg_keys[12], (SMALL,), (0.055 * TOKENS ** 0.5), 64.0, (), jnp.float32),
        "small_second": jnp.clip(jnp.exp(jax.random.uniform(arg_keys[13], (SMALL,), jnp.float32, math.log(638.976), math.log(2555.904))), 638.976, 2555.904),
    }


@jax.custom_vjp
def low(v):
    return lax.optimization_barrier(v.astype(jnp.bfloat16)).astype(jnp.float32)

@jax.custom_vjp
def low_back(v):
    return v

def low_keep(v):
    return (low(v), None)

def low_pass(kept, grad):
    return (grad,)

def back_keep(v):
    return (v, None)

def back_low(kept, grad):
    return (low(grad),)
low.defvjp(low_keep, low_pass)
low_back.defvjp(back_keep, back_low)
HIGH = lax.Precision.HIGHEST
KERNEL_SIZES = (7, 12, 14, 24, 48)
BETA_ONE = 0.9
BETA_TWO = 0.95
ADAM_EPS = 1e-08
DECAY_RATE = 0.1
RATE_DENSE = 0.03
RATE_MIXER = 0.03
RATE_SMALL = 0.5

def average_tables(length):
    positions = jnp.arange(length, dtype=jnp.int32)
    tables = []
    for kernel in KERNEL_SIZES:
        offsets = jnp.arange(kernel, dtype=jnp.int32)
        clipped = jnp.clip(positions[:, None] - (kernel - 1) // 2 + offsets[None, :], 0, length - 1)
        counts = lax.optimization_barrier(jnp.sum((clipped[:, :, None] == positions[None, None, :]).astype(jnp.float32), axis=1))
        tables.append(counts / kernel)
    return jnp.stack(tables)

def fourier_tables(mode_index, length):
    positions = jnp.arange(length, dtype=jnp.int32)
    phases = mode_index.astype(jnp.int32)[:, None] * positions[None, :] % length
    angles = phases.astype(jnp.float32) * (2.0 * jnp.pi / length)
    forward = jnp.stack([jnp.cos(angles), -jnp.sin(angles)])
    slot_ids = jnp.arange(mode_index.shape[0], dtype=jnp.int32)
    back_phase = slot_ids[:, None] * positions[None, :] % length
    back_angle = back_phase.astype(jnp.float32) * (2.0 * jnp.pi / length)
    coefs = jnp.where(slot_ids == 0, 1.0, 2.0).astype(jnp.float32) / length
    inverse = jnp.stack([jnp.cos(back_angle) * coefs[:, None], -jnp.sin(back_angle) * coefs[:, None]])
    return (forward, jnp.transpose(inverse, (2, 0, 1)))

def decompose(series, params, tables):
    averages = jnp.einsum('ktu,bud->kbtd', tables, series, precision=HIGH)
    logits = params[:5, None, None, None] * series[None] + params[5:, None, None, None]
    shares = jax.nn.softmax(logits, axis=0)
    return series - lax.optimization_barrier(jnp.sum(shares * averages, axis=0))

def mix_modes(spectra, mixer_weights):
    head_size = mixer_weights.shape[2] // 2
    split_modes = spectra.reshape(spectra.shape[0], 2, spectra.shape[2], HEADS, head_size)
    kernel = mixer_weights.reshape(mixer_weights.shape[0], HEADS, head_size, 2 * head_size)
    products = jnp.einsum('bcmhi,mhio->bcmho', split_modes, kernel, precision=HIGH)
    real_part = products[:, 0, :, :, :head_size] - products[:, 1, :, :, head_size:]
    imag_part = products[:, 0, :, :, head_size:] + products[:, 1, :, :, :head_size]
    return jnp.stack([real_part, imag_part], axis=1).reshape(spectra.shape)

def encoder_layer(w_query, w_out, w_up, w_down, mixer_weights, small_weights, activations, forward, inverse, tables):
    model_width = activations.shape[-1]
    bias_query = small_weights[:model_width]
    bias_out = small_weights[model_width:2 * model_width]
    first_mix = small_weights[2 * model_width:2 * model_width + 10]
    second_mix = small_weights[2 * model_width + 10:2 * model_width + 20]
    acts_low = low(activations)
    query_full = low_back(jnp.einsum('btd,de->bte', acts_low, w_query, precision=HIGH)) + bias_query
    query_low = low(query_full)
    spectra = low(low_back(jnp.einsum('cmt,btd->bcmd', forward, query_low, precision=HIGH)))
    mixed_modes = low(low_back(mix_modes(spectra, mixer_weights)))
    signal = low(low_back(jnp.einsum('tcm,bcmd->btd', inverse, mixed_modes, precision=HIGH)))
    summed = activations + low_back(jnp.einsum('btd,de->bte', signal, w_out, precision=HIGH)) + bias_out
    first_out = decompose(summed, first_mix, tables)
    hidden = low_back(jnp.einsum('btd,fd->btf', low(first_out), w_up, precision=HIGH))
    active = low(jax.nn.gelu(hidden, approximate=False))
    branch = low_back(jnp.einsum('btf,fd->btd', active, w_down, precision=HIGH))
    return decompose(first_out + branch, second_mix, tables)

def adam_update(weight, gradient, moment, second, step_rate):
    moment_new = BETA_ONE * moment + (1.0 - BETA_ONE) * gradient
    second_new = BETA_TWO * second + (1.0 - BETA_TWO) * gradient * gradient
    scaled_m = moment_new / (1.0 - BETA_ONE ** STEP)
    scaled_v = second_new / (1.0 - BETA_TWO ** STEP)
    weight_new = weight - step_rate * (scaled_m / (jnp.sqrt(scaled_v) + ADAM_EPS) + DECAY_RATE * weight)
    return (moment_new, second_new, weight_new)

def reference(inputs, observed, out_grad, mode_index, owner_list, dense_master, dense_first, dense_second, mixer_master, mixer_first, mixer_second, small_master, small_first, small_second):
    restore = jnp.argsort(owner_list).astype(jnp.int32)
    weight_table = low(dense_master).reshape(BLOCKS, -1, D)[restore].reshape(ROWS, D)
    w_query = weight_table[:D]
    w_out = weight_table[D:2 * D]
    w_up = weight_table[2 * D:2 * D + FF]
    w_down = weight_table[2 * D + FF:]
    mixer_weights = low(mixer_master)
    forward, inverse = fourier_tables(mode_index, L)
    forward = low(forward)
    inverse = low(inverse)
    tables = average_tables(L)
    mask_values = observed.astype(jnp.float32)[:, :, None]
    activations = inputs.astype(jnp.float32) * mask_values
    group_size = WIN_DEV * N_MODE
    acts_blocks = activations.reshape(-1, group_size, L, D)
    grad_blocks = out_grad.astype(jnp.float32).reshape(-1, group_size, L, D)

    def block_step(totals, pieces):
        acts_piece, grad_piece = pieces

        def forward_pass(w_query_in, w_out_in, w_up_in, w_down_in, mixer_in, small_in, acts_in):
            return encoder_layer(w_query_in, w_out_in, w_up_in, w_down_in, mixer_in, small_in, acts_in, forward, inverse, tables)
        result, pullback = jax.vjp(forward_pass, w_query, w_out, w_up, w_down, mixer_weights, small_master, acts_piece)
        gradients = pullback(grad_piece)
        totals = tuple((total + gradient for total, gradient in zip(totals, gradients[:6])))
        return (totals, (result.astype(jnp.bfloat16), gradients[6]))
    start_totals = (jnp.zeros_like(w_query), jnp.zeros_like(w_out), jnp.zeros_like(w_up), jnp.zeros_like(w_down), jnp.zeros_like(mixer_weights), jnp.zeros_like(small_master))
    totals, (outputs_all, acts_grads) = lax.scan(block_step, start_totals, (acts_blocks, grad_blocks))
    output = outputs_all.reshape(WINDOWS, L, D)
    input_grad = acts_grads.reshape(WINDOWS, L, D) * mask_values
    g_query, g_out, g_up, g_down, g_mixer, g_small = totals
    dense_grad = jnp.concatenate([g_query, g_out, g_up, g_down], axis=0).reshape(BLOCKS, -1, D)[owner_list.astype(jnp.int32)].reshape(ROWS, D)
    dense_first_new, dense_second_new, dense_new = adam_update(dense_master, dense_grad, dense_first, dense_second, RATE_DENSE)
    mixer_first_new, mixer_second_new, mixer_new = adam_update(mixer_master, g_mixer, mixer_first, mixer_second, RATE_MIXER)
    small_first_new, small_second_new, small_new = adam_update(small_master, g_small, small_first, small_second, RATE_SMALL)
    bias_out_grad = g_small[D:2 * D]
    return (output, input_grad, dense_first_new, dense_second_new, dense_new, mixer_first_new, mixer_second_new, mixer_new, small_first_new, small_second_new, small_new, bias_out_grad)
```

```python
import functools
import math

import jax
import jax.numpy as jnp
import numpy as np
from jax import lax
from jax.experimental import pallas as pl
from jax.experimental.pallas import tpu as pltpu
from jax.sharding import PartitionSpec as P

STEP = 10
BETA_ONE = 0.9
BETA_TWO = 0.95
ADAM_EPS = 1e-08
DECAY_RATE = 0.1
RATE_DENSE = 0.03
RATE_MIXER = 0.03
RATE_SMALL = 0.5

KERNEL_SIZES = (7, 12, 14, 24, 48)
LOG2E = 1.4426950408889634
BF = jnp.bfloat16
F32 = jnp.float32
NT = (((1,), (1,)), ((), ()))
NN = (((1,), (0,)), ((), ()))
TN = (((0,), (0,)), ((), ()))


def dot(a, b, dims=NN):
    return lax.dot_general(a, b, dims, preferred_element_type=F32)


def average_counts(length):
    tables = []
    t = np.arange(length)
    for size in KERNEL_SIZES:
        u = np.clip(t[:, None] - (size - 1) // 2 + np.arange(size)[None, :], 0, length - 1)
        tables.append((u[:, :, None] == t[None, None, :]).sum(1))
    return np.stack(tables).astype(np.float32)


def gelu_parts(h):
    z = jnp.abs(h)
    e = jnp.exp2(h * h * (-0.5 * LOG2E))
    t = 1.0 / (1.0 + (0.3275911 * math.sqrt(0.5)) * z)
    poly = t * (0.5 * 0.254829592 + t * (-0.5 * 0.284496736 + t * (0.5 * 1.421413741 + t * (-0.5 * 1.453152027 + t * (0.5 * 1.061405429)))))
    tail = poly * e
    big = jnp.where(h < 0, tail, 1.0 - tail)
    return big, e * (1.0 / math.sqrt(2 * math.pi))


def middle_kernel(W, L, D, FF, steps,
                  mix_ref, acts_ref, sig_ref, og_ref, wq_ref, wup_ref, wdn_ref, bias_ref, invt_ref, cnt_ref, cntt_ref,
                  out_ref, gsum_ref, gmix_ref, gw_ref, gup_ref, gdn_ref, small_ref,
                  vs, base, avg1, c1, v1, active, dgelu, first, flow, gb, ghid, glow, avg2, stk, accs, accb):
    step = pl.program_id(0)
    T = W * L
    CH = 16
    CC = 256
    nc = D // CC
    nr = L // CH
    FT = 512

    @pl.when(step == 0)
    def _():
        vs[...] = jnp.zeros_like(vs)
        stk[...] = jnp.zeros_like(stk)
        accs[...] = jnp.zeros_like(accs)
        accb[...] = jnp.zeros_like(accb)
        gw_ref[...] = jnp.zeros_like(gw_ref)
        gup_ref[...] = jnp.zeros_like(gup_ref)
        gdn_ref[...] = jnp.zeros_like(gdn_ref)

    def fold(x):
        y = x[:, 0:128]
        for i in range(1, CC // 128):
            y = y + x[:, i * 128:(i + 1) * 128]
        return y[0:8] + y[8:16]

    def scaled_shares(v, base_at):
        logits = [mix_ref[base_at + k] * LOG2E * v + mix_ref[base_at + 5 + k] * LOG2E for k in range(5)]
        top = functools.reduce(jnp.maximum, logits)
        es = [jnp.exp2(l - top) for l in logits]
        r = 1.0 / functools.reduce(lambda a, b: a + b, es)
        return [e * (r * (1.0 / s)) for e, s in zip(es, KERNEL_SIZES)]

    def backward(v, g, cs, avs, mean, base_at):
        gv = g * v
        total = None
        for k in range(5):
            t = cs[k] * (KERNEL_SIZES[k] * mean - avs[k])
            total = mix_ref[base_at + k] * t if total is None else total + mix_ref[base_at + k] * t
            accs[base_at + k] += fold(gv * t)
            accs[base_at + 5 + k] += fold(g * t)
        return g, g * total

    def split(v, w, rows, cols):
        hi = v.astype(BF)
        vs[w, rows, cols] = hi
        return hi

    sig = sig_ref[...].reshape(T, D)
    base[...] = dot(sig, wq_ref[D:2 * D, :])

    def window_one(w, _):
        def rows_a(i, _):
            for c in range(nc):
                cols = slice(c * CC, (c + 1) * CC)
                rows = pl.ds(pl.multiple_of(w * L + i * CH, CH), CH)
                here = pl.ds(pl.multiple_of(i * CH, CH), CH)
                low_rows = pl.ds(pl.multiple_of(L + i * CH, CH), CH)
                v = base[rows, cols] + acts_ref[w, here, cols].astype(F32) + bias_ref[:, cols]
                v1[rows, cols] = v
                hi = v.astype(BF)
                vs[here, cols] = hi
                vs[low_rows, cols] = (v - hi.astype(F32)).astype(BF)
            return 0
        lax.fori_loop(0, nr, rows_a, 0)
        avg1[pl.ds(pl.multiple_of(w * 5 * L, 32), 5 * L), :] = dot(cnt_ref[...], vs[...])

        def rows_b(i, _):
            for c in range(nc):
                cols = slice(c * CC, (c + 1) * CC)
                rows = pl.ds(pl.multiple_of(w * L + i * CH, CH), CH)
                v = v1[rows, cols]
                cs = scaled_shares(v, 0)
                mean = None
                for k in range(5):
                    at = pl.ds(pl.multiple_of((w * 5 + k) * L + i * CH, CH), CH)
                    u = cs[k] * avg1[at, cols]
                    c1[at, cols] = cs[k]
                    mean = u if mean is None else mean + u
                f = v - mean
                first[rows, cols] = f
                flow[pl.ds(pl.multiple_of(step * T + w * L + i * CH, CH), CH), cols] = f.astype(BF)
            return 0
        lax.fori_loop(0, nr, rows_b, 0)
        return 0
    lax.fori_loop(0, W, window_one, 0)

    here_t = pl.ds(pl.multiple_of(step * T, CH), T)
    base[...] = first[...]

    def ffn(n, _):
        cols = pl.ds(pl.multiple_of(n * FT, FT), FT)
        h = dot(flow[here_t, :], wup_ref[cols, :], NT)
        big, small = gelu_parts(h)
        a = (h * big).astype(BF)
        active[here_t, cols] = a
        dgelu[:, cols] = (big + h * small).astype(BF)
        base[...] += dot(a, wdn_ref[cols, :])
        return 0
    lax.fori_loop(0, FF // FT, ffn, 0)

    def window_two(w, _):
        def rows_a(i, _):
            for c in range(nc):
                cols = slice(c * CC, (c + 1) * CC)
                rows = pl.ds(pl.multiple_of(w * L + i * CH, CH), CH)
                here = pl.ds(pl.multiple_of(i * CH, CH), CH)
                low_rows = pl.ds(pl.multiple_of(L + i * CH, CH), CH)
                v = base[rows, cols]
                hi = v.astype(BF)
                vs[here, cols] = hi
                vs[low_rows, cols] = (v - hi.astype(F32)).astype(BF)
            return 0
        lax.fori_loop(0, nr, rows_a, 0)
        avg2[...] = dot(cnt_ref[...], vs[...])

        def rows_b(i, _):
            for c in range(nc):
                cols = slice(c * CC, (c + 1) * CC)
                rows = pl.ds(pl.multiple_of(w * L + i * CH, CH), CH)
                here = pl.ds(pl.multiple_of(i * CH, CH), CH)
                v = base[rows, cols]
                cs = scaled_shares(v, 10)
                avs = [avg2[pl.ds(pl.multiple_of(k * L + i * CH, CH), CH), cols] for k in range(5)]
                mean = functools.reduce(lambda a, b: a + b, [c_ * a_ for c_, a_ in zip(cs, avs)])
                out_ref[w, here, cols] = (v - mean).astype(BF)
                g = og_ref[w, here, cols].astype(F32)
                for k in range(5):
                    stk[pl.ds(pl.multiple_of(k * L + i * CH, CH), CH), cols] = (cs[k] * g).astype(BF)
                g, extra = backward(v, g, cs, avs, mean, 10)
                base[rows, cols] = g + extra
            return 0
        lax.fori_loop(0, nr, rows_b, 0)
        rows = pl.ds(pl.multiple_of(w * L, L), L)
        gs = base[rows, :] - dot(cntt_ref[...], stk[...])
        base[rows, :] = gs
        gb[pl.ds(pl.multiple_of(step * T + w * L, 32), L), :] = gs.astype(BF)
        return 0
    lax.fori_loop(0, W, window_two, 0)

    def ffn_back(n, _):
        cols = pl.ds(pl.multiple_of(n * FT, FT), FT)
        ga = dot(gb[here_t, :], wdn_ref[cols, :], NT)
        gh = (ga * dgelu[:, cols].astype(F32)).astype(BF)
        ghid[here_t, cols] = gh
        base[...] += dot(gh, wup_ref[cols, :])
        return 0
    lax.fori_loop(0, FF // FT, ffn_back, 0)

    def window_three(w, _):
        def rows_b(i, _):
            for c in range(nc):
                cols = slice(c * CC, (c + 1) * CC)
                rows = pl.ds(pl.multiple_of(w * L + i * CH, CH), CH)
                v = v1[rows, cols]
                g = base[rows, cols]
                ats = [pl.ds(pl.multiple_of((w * 5 + k) * L + i * CH, CH), CH) for k in range(5)]
                cs = [c1[at, cols] for at in ats]
                avs = [avg1[at, cols] for at in ats]
                mean = v - first[rows, cols]
                for k in range(5):
                    stk[pl.ds(pl.multiple_of(k * L + i * CH, CH), CH), cols] = (cs[k] * g).astype(BF)
                g, extra = backward(v, g, cs, avs, mean, 0)
                base[rows, cols] = g + extra
                accb[:, cols] += extra[0:8] + extra[8:16]
            return 0
        lax.fori_loop(0, nr, rows_b, 0)
        rows = pl.ds(pl.multiple_of(w * L, L), L)
        gs = base[rows, :] - dot(cntt_ref[...], stk[...])
        gsum_ref[w] = gs
        glow[rows, :] = gs.astype(BF)
        return 0
    lax.fori_loop(0, W, window_three, 0)

    back = dot(glow[...], wq_ref[D:2 * D, :], NT).astype(BF)
    for w in range(W):
        gmix_ref[w] = dot(invt_ref[...], back[w * L:(w + 1) * L, :]).astype(BF)
    gw_ref[...] += dot(sig, glow[...], TN)

    @pl.when(step == steps - 1)
    def _():
        small_ref[0:8, :] = accb[...]
        for k in range(20):
            small_ref[8 + 8 * k:16 + 8 * k, 0:128] = accs[k]
            small_ref[8 + 8 * k:16 + 8 * k, 128:512] = jnp.zeros((8, 384), F32)

        def wgrad(n, _):
            cols = pl.ds(pl.multiple_of(n * FT, FT), FT)
            gup_ref[cols, :] = dot(ghid[:, cols], flow[...], TN)
            gdn_ref[cols, :] = dot(active[:, cols], gb[...], TN)
            return 0
        lax.fori_loop(0, FF // FT, wgrad, 0)


def middle(mix, acts, sig, og, wqo, wup, wdn, bias, inv, W=4):
    n, L, D = acts.shape
    FF = wup.shape[0]
    steps = n // W
    T = W * L
    A = average_counts(L)
    cnt = np.zeros((5 * L, 256), np.float32)
    cnt[:, :L] = A.reshape(5 * L, L)
    cnt[:, L:2 * L] = A.reshape(5 * L, L)
    cntt = np.zeros((L, 512), np.float32)
    cntt[:, :5 * L] = A.transpose(2, 0, 1).reshape(L, 5 * L)
    cnt = jnp.asarray(cnt, BF)
    cntt = jnp.asarray(cntt, BF)
    whole = lambda *s: pl.BlockSpec(s, lambda i: (0,) * len(s), pipeline_mode=pl.Buffered(1))
    piece = lambda *s: pl.BlockSpec(s, lambda i: (i,) + (0,) * (len(s) - 1))
    return pl.pallas_call(
        functools.partial(middle_kernel, W, L, D, FF, steps),
        grid=(steps,),
        out_shape=(
            jax.ShapeDtypeStruct((n, L, D), BF),
            jax.ShapeDtypeStruct((n, L, D), F32),
            jax.ShapeDtypeStruct((n, L, D), BF),
            jax.ShapeDtypeStruct((D, D), F32),
            jax.ShapeDtypeStruct((FF, D), F32),
            jax.ShapeDtypeStruct((FF, D), F32),
            jax.ShapeDtypeStruct((168, D), F32),
        ),
        in_specs=[
            pl.BlockSpec(memory_space=pltpu.SMEM),
            piece(W, L, D), piece(W, L, D), piece(W, L, D),
            whole(2 * D, D), whole(FF, D), whole(FF, D), whole(1, D), whole(L, L), whole(5 * L, 256), whole(L, 512),
        ],
        out_specs=(
            piece(W, L, D), piece(W, L, D), piece(W, L, D), whole(D, D), whole(FF, D), whole(FF, D), whole(168, D),
        ),
        scratch_shapes=[
            pltpu.VMEM((256, D), BF),
            pltpu.VMEM((T, D), F32),
            pltpu.VMEM((W * 5 * L, D), F32),
            pltpu.VMEM((W * 5 * L, D), F32),
            pltpu.VMEM((T, D), F32),
            pltpu.VMEM((n * L, FF), BF),
            pltpu.VMEM((T, FF), BF),
            pltpu.VMEM((T, D), F32),
            pltpu.VMEM((n * L, D), BF),
            pltpu.VMEM((n * L, D), BF),
            pltpu.VMEM((n * L, FF), BF),
            pltpu.VMEM((T, D), BF),
            pltpu.VMEM((5 * L, D), F32),
            pltpu.VMEM((512, D), BF),
            pltpu.VMEM((20, 8, 128), F32),
            pltpu.VMEM((8, D), F32),
        ],
        compiler_params=pltpu.CompilerParams(vmem_limit_bytes=60 * 1024 * 1024),
        name="middle",
    )(mix, acts, sig, og, wqo, wup, wdn, bias, inv.T, cnt, cntt)


def sign_lanes(rows, left, right):
    lane = lax.broadcasted_iota(jnp.int32, (rows, 128), 1)
    return jnp.where(lane < 64, left, right).astype(F32)


def interleave(real, imag, v):
    re, im = real[:, v * 128:(v + 1) * 128], imag[:, v * 128:(v + 1) * 128]
    low = lax.broadcasted_iota(jnp.int32, re.shape, 1) < 64
    return jnp.where(low, re, pltpu.roll(im, 64, 1)), jnp.where(low, pltpu.roll(re, 64, 1), im)


def gather_rows(tiles, w, slots, n):
    reals, imags = [], []
    for v in range(4):
        first = tiles[2 * v, pl.ds(w, slots, stride=n), :]
        second = tiles[2 * v + 1, pl.ds(w, slots, stride=n), :]
        low = lax.broadcasted_iota(jnp.int32, first.shape, 1) < 64
        reals.append(jnp.where(low, first, pltpu.roll(second, 64, 1)).astype(BF))
        imags.append(jnp.where(low, pltpu.roll(first, 64, 1), second).astype(BF))
    return jnp.concatenate([jnp.concatenate(reals, 1), jnp.concatenate(imags, 1)], 0)


def spread_rows(tiles, w, slots, n, spectrum):
    for v in range(4):
        one, two = interleave(spectrum[:slots], spectrum[slots:], v)
        tiles[2 * v, pl.ds(w, slots, stride=n), :] = one
        tiles[2 * v + 1, pl.ds(w, slots, stride=n), :] = two


def head_matrix(weights, h, pieces, mode, rows):
    top = jnp.concatenate([weights[h * pieces + q, mode, rows, :] for q in range(pieces)], 0)
    wide = top.astype(F32)
    low = pltpu.roll(wide, 64, 1) * sign_lanes(wide.shape[0], -1.0, 1.0)
    return jnp.concatenate([top, low.astype(BF)], 0)


def front_kernel(n, L, D, slots, in_ref, obs_ref, wq_ref, bias_ref, basis_ref, inv_ref, eye_ref, weights,
                 acts_ref, z_ref, sig_ref, query, tiles, outs):
    ndp, nmode = weights.shape[:2]
    per = slots // nmode
    heads = 8
    pieces = ndp // heads
    depth = 64 // pieces

    def mask(w, _):
        row = obs_ref[pl.ds(w, 1), :].astype(F32)
        rows = pl.ds(pl.multiple_of(w * L, 32), L)
        acts_ref[rows, :] = dot((eye_ref[...] * row).astype(BF), in_ref[rows, :]).astype(BF)
        return 0
    lax.fori_loop(0, n, mask, 0)
    T = 384

    def project(i, _):
        rows = pl.ds(pl.multiple_of(i * T, T), T)
        query[rows, :] = (dot(acts_ref[rows, :], wq_ref[...]) + bias_ref[...]).astype(BF)
        return 0
    lax.fori_loop(0, n * L // T, project, 0)

    def spectra(w, _):
        rows = pl.ds(pl.multiple_of(w * L, 32), L)
        spread_rows(tiles, w, slots, n, dot(basis_ref[...], query[rows, :]))
        return 0
    lax.fori_loop(0, n, spectra, 0)

    for mode in range(nmode):
        def slot(jl, _):
            at = pl.ds(pl.multiple_of((mode * per + jl) * n, n), n)
            rows = pl.ds(pl.multiple_of(jl * depth, depth), depth)
            for h in range(heads):
                x = tiles[h, at, :].astype(BF)
                z_ref[h, at, :] = x
                outs[h, at, :] = dot(x, head_matrix(weights, h, pieces, mode, rows))
            return 0
        lax.fori_loop(0, per, slot, 0)

    def signal(w, _):
        rows = pl.ds(pl.multiple_of(w * L, 32), L)
        sig_ref[rows, :] = dot(inv_ref[...], gather_rows(outs, w, slots, n)).astype(BF)
        return 0
    lax.fori_loop(0, n, signal, 0)


def front(inputs, observed, wqo, bias, basis, inv, weights):
    n, L, D = inputs.shape
    slots = basis.shape[0] // 2
    vm = pl.BlockSpec(memory_space=pltpu.VMEM)
    whole = lambda *s: pl.BlockSpec(s, lambda i: (0,) * len(s), pipeline_mode=pl.Buffered(1))
    return pl.pallas_call(
        functools.partial(front_kernel, n, L, D, slots),
        grid=(1,),
        out_shape=(
            jax.ShapeDtypeStruct((n * L, D), BF),
            jax.ShapeDtypeStruct((8, slots * n, 128), BF),
            jax.ShapeDtypeStruct((n * L, D), BF),
        ),
        in_specs=[whole(n * L, D), whole(n, L), whole(D, D), whole(1, D), whole(2 * slots, L), whole(L, 2 * slots), whole(L, L),
                  whole(*weights.shape)],
        out_specs=(whole(n * L, D), whole(8, slots * n, 128), whole(n * L, D)),
        scratch_shapes=[
            pltpu.VMEM((n * L, D), BF),
            pltpu.VMEM((8, slots * n, 128), F32),
            pltpu.VMEM((8, slots * n, 128), F32),
        ],
        compiler_params=pltpu.CompilerParams(vmem_limit_bytes=60 * 1024 * 1024),
        name="front",
    )(inputs.reshape(n * L, D), observed, wqo, bias, basis, inv, jnp.eye(L, dtype=F32), weights)


def back_kernel(n, L, D, slots, gmix_ref, z_ref, acts_ref, gsum_ref, obs_ref, wq_ref, basist_ref, eye_ref, weights,
                gin_ref, gq_ref, gbias_ref, gmixer_ref, tiles, outs, glow):
    ndp, nmode = weights.shape[:2]
    per = slots // nmode
    heads = 8
    pieces = ndp // heads
    depth = 64 // pieces

    def spectra(w, _):
        rows = pl.ds(pl.multiple_of(w * L, 32), L)
        spread_rows(tiles, w, slots, n, gmix_ref[rows, :].astype(F32))
        return 0
    lax.fori_loop(0, n, spectra, 0)

    for mode in range(nmode):
        def slot(jl, _):
            at = pl.ds(pl.multiple_of((mode * per + jl) * n, n), n)
            rows = pl.ds(pl.multiple_of(jl * depth, depth), depth)
            for h in range(heads):
                y = tiles[h, at, :].astype(BF)
                outs[h, at, :] = dot(y, head_matrix(weights, h, pieces, mode, rows), NT)
                g = dot(z_ref[h, at, :], y, TN)
                g = (g[:64] + pltpu.roll(g[64:], 64, 1) * sign_lanes(64, 1.0, -1.0)).astype(BF)
                for q in range(pieces):
                    gmixer_ref[h * pieces + q, mode, rows, :] = g[q * depth:(q + 1) * depth]
            return 0
        lax.fori_loop(0, per, slot, 0)
    gbias_ref[...] = jnp.zeros_like(gbias_ref)

    def query(w, _):
        rows = pl.ds(pl.multiple_of(w * L, 32), L)
        g = dot(basist_ref[...], gather_rows(outs, w, slots, n))
        glow[rows, :] = g.astype(BF)
        gbias_ref[...] += functools.reduce(lambda a, b: a + b, [g[i * 8:(i + 1) * 8] for i in range(L // 8)])
        return 0
    lax.fori_loop(0, n, query, 0)
    gq_ref[...] = dot(acts_ref[...], glow[...], TN)

    def input_grad(w, _):
        rows = pl.ds(pl.multiple_of(w * L, 32), L)
        row = obs_ref[pl.ds(w, 1), :].astype(F32)
        mask = dot((eye_ref[...] * row).astype(BF), jnp.ones((L, 128), BF))
        g = gsum_ref[rows, :] + dot(glow[rows, :], wq_ref[...], NT)
        for c in range(D // 128):
            gin_ref[rows, c * 128:(c + 1) * 128] = g[:, c * 128:(c + 1) * 128] * mask
        return 0
    lax.fori_loop(0, n, input_grad, 0)


def back(gmix, z, acts, gsum, observed, wqo, basist, weights):
    n, L = observed.shape
    D = acts.shape[1]
    slots = basist.shape[1] // 2
    whole = lambda *s: pl.BlockSpec(s, lambda i: (0,) * len(s), pipeline_mode=pl.Buffered(1))
    return pl.pallas_call(
        functools.partial(back_kernel, n, L, D, slots),
        grid=(1,),
        out_shape=(
            jax.ShapeDtypeStruct((n * L, D), F32),
            jax.ShapeDtypeStruct((D, D), F32),
            jax.ShapeDtypeStruct((8, D), F32),
            jax.ShapeDtypeStruct(weights.shape, BF),
        ),
        in_specs=[whole(n * L, D), whole(8, slots * n, 128), whole(n * L, D), whole(n * L, D), whole(n, L), whole(D, D),
                  whole(L, 2 * slots), whole(L, L), whole(*weights.shape)],
        out_specs=(whole(n * L, D), whole(D, D), whole(8, D), whole(*weights.shape)),
        scratch_shapes=[
            pltpu.VMEM((8, slots * n, 128), F32),
            pltpu.VMEM((8, slots * n, 128), F32),
            pltpu.VMEM((n * L, D), BF),
        ],
        compiler_params=pltpu.CompilerParams(vmem_limit_bytes=60 * 1024 * 1024),
        name="back",
    )(gmix, z, acts, gsum, observed, wqo, basist, jnp.eye(L, dtype=F32), weights)


def table_kernel(blocks, owner, in_ref, wqo_ref, wup_ref, wdn_ref, src, dst):
    rows = in_ref.shape[0]
    size = rows // blocks
    step = 256

    def widen(i, _):
        at = pl.ds(pl.multiple_of(i * step, step), step)
        src[at, :] = in_ref[at, :].astype(F32)
        return 0
    lax.fori_loop(0, rows // step, widen, 0)

    def move(j, _):
        dst[pl.ds(owner[j] * size, size), :] = src[pl.ds(j * size, size), :]
        return 0
    lax.fori_loop(0, blocks, move, 0, unroll=4)
    start = 0
    for ref in (wqo_ref, wup_ref, wdn_ref):
        def narrow(i, _):
            to = pl.ds(pl.multiple_of(i * step, step), step)
            at = pl.ds(pl.multiple_of(start + i * step, step), step)
            ref[to, :] = dst[at, :].astype(BF)
            return 0
        lax.fori_loop(0, ref.shape[0] // step, narrow, 0)
        start += ref.shape[0]


def to_table(gathered, owner_list, ff):
    rows, D = gathered.shape
    blocks = owner_list.shape[0]
    cols = lambda r: pl.BlockSpec((r, 128), lambda i, o: (0, i))
    return pl.pallas_call(
        functools.partial(table_kernel, blocks),
        grid_spec=pltpu.PrefetchScalarGridSpec(
            num_scalar_prefetch=1,
            grid=(D // 128,),
            in_specs=[cols(rows)],
            out_specs=(cols(2 * D), cols(ff), cols(ff)),
            scratch_shapes=[pltpu.VMEM((rows + 8, 128), F32), pltpu.VMEM((rows + 8, 128), F32)],
        ),
        out_shape=(
            jax.ShapeDtypeStruct((2 * D, D), BF),
            jax.ShapeDtypeStruct((ff, D), BF),
            jax.ShapeDtypeStruct((ff, D), BF),
        ),
        compiler_params=pltpu.CompilerParams(vmem_limit_bytes=40 * 1024 * 1024),
        name="to_table",
    )(owner_list, gathered)


def owners_kernel(blocks, owner, *refs):
    parts, out_ref, src, dst = refs[:4], refs[4], refs[5], refs[6]
    rows = out_ref.shape[0]
    size = rows // blocks
    step = 256
    start = 0
    for ref in parts:
        def take(i, _):
            to = pl.ds(pl.multiple_of(start + i * step, step), step)
            at = pl.ds(pl.multiple_of(i * step, step), step)
            src[to, :] = ref[at, :]
            return 0
        lax.fori_loop(0, ref.shape[0] // step, take, 0)
        start += ref.shape[0]

    def move(j, _):
        dst[pl.ds(j * size, size), :] = src[pl.ds(owner[j] * size, size), :]
        return 0
    lax.fori_loop(0, blocks, move, 0, unroll=4)

    def narrow(i, _):
        at = pl.ds(pl.multiple_of(i * step, step), step)
        out_ref[at, :] = dst[at, :].astype(BF)
        return 0
    lax.fori_loop(0, rows // step, narrow, 0)


def to_owners(parts, owner_list):
    D = parts[0].shape[1]
    rows = sum(p.shape[0] for p in parts)
    blocks = owner_list.shape[0]
    cols = lambda r: pl.BlockSpec((r, 128), lambda i, o: (0, i))
    return pl.pallas_call(
        functools.partial(owners_kernel, blocks),
        grid_spec=pltpu.PrefetchScalarGridSpec(
            num_scalar_prefetch=1,
            grid=(D // 128,),
            in_specs=[cols(p.shape[0]) for p in parts],
            out_specs=cols(rows),
            scratch_shapes=[pltpu.VMEM((rows + 8, 128), F32), pltpu.VMEM((rows + 8, 128), F32)],
        ),
        out_shape=jax.ShapeDtypeStruct((rows, D), BF),
        compiler_params=pltpu.CompilerParams(vmem_limit_bytes=40 * 1024 * 1024),
        name="to_owners",
    )(owner_list, *parts)


MESH = pl.DeviceIdType.MESH


def places():
    ndp, nmode = lax.axis_size("dp"), lax.axis_size("mode")
    sizes = {"a": ndp // 2, "b": 2, "y": nmode // 2, "c": 2}
    dp, mode = lax.axis_index("dp"), lax.axis_index("mode")
    here = {"a": dp // 2, "b": lax.rem(dp, 2), "y": mode // 2, "c": lax.rem(mode, 2)}
    return sizes, here


def number(sizes, at):
    return ((at["a"] * sizes["b"] + at["b"]) * sizes["y"] + at["y"]) * 2 + at["c"]


def device(sizes, at):
    return {"dp": at["a"] * sizes["b"] + at["b"], "mode": at["y"] * 2 + at["c"]}


def move(sizes, at, axis, d):
    return {**at, axis: lax.rem(at[axis] + d, sizes[axis])}


def greet():
    ndp, nmode = lax.axis_size("dp"), lax.axis_size("mode")
    dp, mode = lax.axis_index("dp"), lax.axis_index("mode")
    barrier = pltpu.get_barrier_semaphore()
    for d in range(1, nmode):
        pl.semaphore_signal(barrier, 1, device_id={"dp": dp, "mode": lax.rem(mode + d, nmode)}, device_id_type=MESH)
    for d in range(1, ndp):
        pl.semaphore_signal(barrier, 1, device_id={"dp": lax.rem(dp + d, ndp), "mode": mode}, device_id_type=MESH)
    pl.semaphore_wait(barrier, ndp + nmode - 2)


def staggered(count, *stages):
    k = len(stages)
    if count < k:
        for stage in stages:
            for t in range(count):
                stage(t)
        return
    for t in range(k - 1):
        for s in range(t + 1):
            stages[s](t - s)

    def body(t, _):
        for s in range(k):
            stages[s](t - s)
        return 0
    lax.fori_loop(k - 1, count, body, 0)
    for t in range(count, count + k - 1):
        for s in range(t - count + 1, k):
            stages[s](t - s)


def gather_kernel(*refs):
    kinds = 2
    ins, outs = refs[:kinds], refs[kinds:2 * kinds]
    recv, send, local = refs[2 * kinds:]
    sizes, here = places()
    greet()

    def copy(kind, at, to, stage, own=False):
        n = number(sizes, at)
        return pltpu.make_async_remote_copy(
            src_ref=ins[kind] if own else outs[kind].at[n], dst_ref=outs[kind].at[n],
            send_sem=send.at[kind, stage], recv_sem=recv.at[kind, n],
            device_id=device(sizes, to), device_id_type=MESH)

    def arrived(kind, at):
        copy(kind, at, here, 0).wait_recv()

    def drain(kind, stage, count):
        ref = outs[kind].at[pl.ds(0, count)]
        pltpu.make_async_copy(ref, ref, send.at[kind, stage]).wait()

    mine = [pltpu.make_async_copy(ins[k], outs[k].at[number(sizes, here)], local.at[k]) for k in range(kinds)]
    for c in mine:
        c.start()

    def run(u, v):
        na, nu, nv = sizes["a"], sizes[u], sizes[v]

        def onward(kind, at, axes, own=False):
            for axis, stage in axes:
                for d in range(1, sizes[axis]):
                    copy(kind, at, move(sizes, here, axis, d), stage, own).start()

        for kind in range(kinds):
            onward(kind, here, (("a", 0), (u, 1), (v, 2), ("c", 3)), True)

        def line(t):
            at = move(sizes, here, "a", t + 1)
            for kind in range(kinds):
                arrived(kind, at)
                onward(kind, at, ((u, 1), (v, 2), ("c", 3)))

        def second(t):
            for d in range(1, nu):
                at = move(sizes, move(sizes, here, "a", t), u, d)
                for kind in range(kinds):
                    arrived(kind, at)
                    onward(kind, at, ((v, 2), ("c", 3)))

        def third(t):
            for e in range(nu):
                for d in range(1, nv):
                    at = move(sizes, move(sizes, move(sizes, here, "a", t), u, e), v, d)
                    for kind in range(kinds):
                        arrived(kind, at)
                        onward(kind, at, (("c", 3),))

        second(0)
        staggered(na - 1, line, lambda t: second(t + 1), third)
        third(na - 1)
        for kind in range(kinds):
            drain(kind, 0, na - 1)
            drain(kind, 1, na * (nu - 1))
            drain(kind, 2, na * nu * (nv - 1))

    pl.when(here["c"] == 0)(lambda: run("b", "y"))
    pl.when(here["c"] == 1)(lambda: run("y", "b"))
    group = sizes["a"] * sizes["b"] * sizes["y"]
    other = move(sizes, here, "c", 1)

    def partner(i, _):
        for kind in range(kinds):
            copy(kind, {"a": i // (sizes["b"] * sizes["y"]), "b": lax.rem(i // sizes["y"], sizes["b"]),
                        "y": lax.rem(i, sizes["y"]), "c": other["c"]}, here, 0).wait_recv()
        return 0
    lax.fori_loop(0, group, partner, 0)
    for kind in range(kinds):
        drain(kind, 3, group)
    for c in mine:
        c.wait()


def gather(dense, mixer):
    nd = lax.axis_size("dp") * lax.axis_size("mode")
    anywhere = pl.BlockSpec(memory_space=pl.ANY)
    return pl.pallas_call(
        gather_kernel,
        out_shape=tuple(jax.ShapeDtypeStruct((nd,) + x.shape, x.dtype) for x in (dense, mixer)),
        in_specs=[anywhere] * 2,
        out_specs=(anywhere,) * 2,
        scratch_shapes=[pltpu.SemaphoreType.DMA((2, nd)), pltpu.SemaphoreType.DMA((2, 4)), pltpu.SemaphoreType.DMA((2,))],
        compiler_params=pltpu.CompilerParams(collective_id=0, has_side_effects=True),
        name="gather",
    )(dense, mixer)


def reduce_kernel(*refs):
    kinds = 2
    ins, small_in = refs[:2], refs[2]
    outs, small_out = refs[3:5], refs[5]
    acc, from_c, from_v, from_u, from_a = (refs[6 + 2 * i:8 + 2 * i] for i in range(5))
    small_one, small_two, local, recv_c, recv_v, recv_u, recv_a, send, small_send, small_recv = refs[16:]
    sizes, here = places()
    ndp, nmode = lax.axis_size("dp"), lax.axis_size("mode")
    dp, mode = lax.axis_index("dp"), lax.axis_index("mode")
    na, nb, ny = sizes["a"], sizes["b"], sizes["y"]
    group = na * nb * ny
    other = move(sizes, here, "c", 1)
    greet()

    def spot(at):
        return (at["a"] * nb + at["b"]) * ny + at["y"]

    loads = [pltpu.make_async_copy(ins[k].at[:, here["c"]], acc[k], local.at[k]) for k in range(kinds)]
    for load in loads:
        load.start()

    def to_partner(kind, at):
        n = spot(at)
        return pltpu.make_async_remote_copy(
            src_ref=ins[kind].at[n, other["c"]], dst_ref=from_c[kind].at[n],
            send_sem=send.at[kind, 0], recv_sem=recv_c.at[kind, n], device_id=device(sizes, other), device_id_type=MESH)

    small_one[mode] = small_in[...]

    def small_copy(buffer, axis, index, count, d, base):
        return pltpu.make_async_remote_copy(
            src_ref=buffer.at[index], dst_ref=buffer.at[index], send_sem=small_send.at[base + d - 1], recv_sem=small_recv.at[base + d - 1],
            device_id={**{"dp": dp, "mode": mode}, axis: lax.rem(index + d, count)}, device_id_type=MESH)
    ones = [small_copy(small_one, "mode", mode, nmode, d, 0) for d in range(1, nmode)]
    twos = [small_copy(small_two, "dp", dp, ndp, d, nmode - 1) for d in range(1, ndp)]
    for c in ones:
        c.start()

    def run(u, v):
        nu, nv = sizes[u], sizes[v]

        def owner(t, e, d):
            return move(sizes, move(sizes, move(sizes, here, "a", t + 1), u, e), v, d)

        for t in range(na):
            for d in list(range(1, nv)) + [0]:
                for e in list(range(1, nu)) + [0]:
                    for kind in range(kinds):
                        to_partner(kind, owner(t, e, d)).start()
        for load in loads:
            load.wait()

        def add(kind, n, terms):
            rows = acc[kind].shape[1]
            step = 16 if rows % 16 == 0 else rows

            def chunk(i, _):
                at = pl.ds(pl.multiple_of(i * step, step), step) if step != rows else slice(None)
                total = acc[kind][n, at, :].astype(F32)
                for ref, k in terms:
                    total = total + ref[k, at, :].astype(F32)
                acc[kind][n, at, :] = total.astype(BF)
                return 0
            lax.fori_loop(0, rows // step, chunk, 0)

        def slot_v(t, e, d):
            return (t * nu + e) * (nv - 1) + d - 1

        def copy_v(kind, t, e, d):
            at = owner(t, e, d)
            s = slot_v(t, e, d)
            return pltpu.make_async_remote_copy(
                src_ref=acc[kind].at[spot(at)], dst_ref=from_v[kind].at[s], send_sem=send.at[kind, 1], recv_sem=recv_v.at[kind, s],
                device_id=device(sizes, move(sizes, here, v, d)), device_id_type=MESH)

        def copy_u(kind, t, e):
            at = owner(t, e, 0)
            s = t * (nu - 1) + e - 1
            return pltpu.make_async_remote_copy(
                src_ref=acc[kind].at[spot(at)], dst_ref=from_u[kind].at[s], send_sem=send.at[kind, 2], recv_sem=recv_u.at[kind, s],
                device_id=device(sizes, move(sizes, here, u, e)), device_id_type=MESH)

        def copy_a(kind, t):
            at = owner(t, 0, 0)
            return pltpu.make_async_remote_copy(
                src_ref=acc[kind].at[spot(at)], dst_ref=from_a[kind].at[t], send_sem=send.at[kind, 3], recv_sem=recv_a.at[kind, t],
                device_id=device(sizes, at), device_id_type=MESH)

        def first(t):
            for d in range(1, nv):
                for e in list(range(1, nu)) + [0]:
                    at = owner(t, e, d)
                    for kind in range(kinds):
                        to_partner(kind, at).wait_recv()
                        add(kind, spot(at), [(from_c[kind], spot(at))])
                        copy_v(kind, t, e, d).start()

        def gathered(kind, t, e):
            at = owner(t, e, 0)
            to_partner(kind, at).wait_recv()
            terms = [(from_c[kind], spot(at))]
            for d in range(1, nv):
                copy_v(kind, t, e, d).wait_recv()
                terms.append((from_v[kind], slot_v(t, e, d)))
            return at, terms

        def second(t):
            for e in range(1, nu):
                for kind in range(kinds):
                    at, terms = gathered(kind, t, e)
                    add(kind, spot(at), terms)
                    copy_u(kind, t, e).start()

        def terms_of(kind, t):
            at, terms = gathered(kind, t, 0)
            for e in range(1, nu):
                copy_u(kind, t, e).wait_recv()
                terms.append((from_u[kind], t * (nu - 1) + e - 1))
            return at, terms

        def third(t):
            for kind in range(kinds):
                at, terms = terms_of(kind, t)
                add(kind, spot(at), terms)
                copy_a(kind, t).start()

        staggered(na - 1, first, second, third)
        first(na - 1)
        second(na - 1)
        for kind in range(kinds):
            at, terms = terms_of(kind, na - 1)
            for t in range(na - 1):
                copy_a(kind, t).wait_recv()
                terms.append((from_a[kind], t))
            n = spot(at)
            rows = acc[kind].shape[1]
            step = 16 if rows % 16 == 0 else rows

            def chunk(i, _):
                rows_at = pl.ds(pl.multiple_of(i * step, step), step) if step != rows else slice(None)
                total = acc[kind][n, rows_at, :].astype(F32)
                for ref, k in terms:
                    total = total + ref[k, rows_at, :].astype(F32)
                outs[kind][rows_at, :] = total
                return 0
            lax.fori_loop(0, rows // step, chunk, 0)

        def drain(kind, stage, count):
            ref = from_c[kind].at[pl.ds(0, count)]
            pltpu.make_async_copy(ref, ref, send.at[kind, stage]).wait()
        for kind in range(kinds):
            drain(kind, 0, group)
            drain(kind, 1, na * nu * (nv - 1))
            drain(kind, 2, na * (nu - 1))
            drain(kind, 3, na - 1)

    pl.when(here["c"] == 0)(lambda: run("b", "y"))
    pl.when(here["c"] == 1)(lambda: run("y", "b"))

    for c in ones:
        c.wait()
    small_two[dp] = functools.reduce(lambda p, q: p + q, [small_one[i] for i in range(nmode)])
    for c in twos:
        c.start()
    for c in twos:
        c.wait()
    small_out[...] = functools.reduce(lambda p, q: p + q, [small_two[i] for i in range(ndp)])


def reduce_scatter(dense, mixer, small):
    ndp, nmode = lax.axis_size("dp"), lax.axis_size("mode")
    nd = ndp * nmode
    group = nd // 2
    na, ny = ndp // 2, nmode // 2
    anywhere = pl.BlockSpec(memory_space=pl.ANY)
    vmem = pl.BlockSpec(memory_space=pltpu.VMEM)
    shapes = [x.shape[1:] for x in (dense, mixer)]
    count_v = max(na * 2 * (ny - 1), na * ny)
    count_u = na * max(ny - 1, 1)
    buffers = [pltpu.VMEM((count,) + s, BF) for count in (group, group, count_v, count_u, na - 1) for s in shapes]
    sem = lambda *s: pltpu.SemaphoreType.DMA(s)
    return pl.pallas_call(
        reduce_kernel,
        out_shape=tuple(jax.ShapeDtypeStruct(s, F32) for s in shapes) + (jax.ShapeDtypeStruct(small.shape, F32),),
        in_specs=[anywhere, anywhere, vmem],
        out_specs=(vmem,) * 3,
        scratch_shapes=buffers + [
            pltpu.VMEM((nmode,) + small.shape, F32), pltpu.VMEM((ndp,) + small.shape, F32),
            sem(2), sem(2, group), sem(2, count_v), sem(2, count_u), sem(2, na - 1), sem(2, 4),
            sem(ndp + nmode - 2), sem(ndp + nmode - 2),
        ],
        compiler_params=pltpu.CompilerParams(collective_id=1, has_side_effects=True, vmem_limit_bytes=60 * 1024 * 1024),
        name="reduce_scatter",
    )(dense.reshape((group, 2) + shapes[0]), mixer.reshape((group, 2) + shapes[1]), small)


def fourier_tables(mode_index, length):
    positions = jnp.arange(length, dtype=jnp.int32)
    phases = mode_index[:, None] * positions[None, :] % length
    angles = phases.astype(jnp.float32) * (2.0 * jnp.pi / length)
    forward = jnp.stack([jnp.cos(angles), -jnp.sin(angles)])
    slot_ids = jnp.arange(mode_index.shape[0], dtype=jnp.int32)
    back_phase = slot_ids[:, None] * positions[None, :] % length
    back_angle = back_phase.astype(jnp.float32) * (2.0 * jnp.pi / length)
    coefs = jnp.where(slot_ids == 0, 1.0, 2.0).astype(jnp.float32) / length
    inverse = jnp.stack(
        [jnp.cos(back_angle) * coefs[:, None], -jnp.sin(back_angle) * coefs[:, None]]
    )
    return (forward, jnp.transpose(inverse, (2, 0, 1)))


def adam_update(weight, gradient, moment, second, step_rate):
    moment_new = BETA_ONE * moment + (1.0 - BETA_ONE) * gradient
    second_new = BETA_TWO * second + (1.0 - BETA_TWO) * gradient * gradient
    scaled_m = moment_new / (1.0 - BETA_ONE**STEP)
    scaled_v = second_new / (1.0 - BETA_TWO**STEP)
    weight_new = weight - step_rate * (
        scaled_m / (jnp.sqrt(scaled_v) + ADAM_EPS) + DECAY_RATE * weight
    )
    return (moment_new, second_new, weight_new)


def shards(
    inputs,
    observed,
    out_grad,
    mode_index,
    owner_list,
    dense_master,
    dense_first,
    dense_second,
    mixer_master,
    mixer_first,
    mixer_second,
    small_master,
    small_first,
    small_second,
):
    ndp, nmode = lax.axis_size("dp"), lax.axis_size("mode")
    length, width = inputs.shape[1:]
    slots = mode_index.shape[0]
    hidden = (dense_master.shape[0] * ndp * nmode - 2 * width) // 2
    dense_all, mixer_all = gather(dense_master.astype(BF), mixer_master.astype(BF).reshape(-1, mixer_master.shape[2]))
    weights = mixer_all.reshape((ndp, nmode) + mixer_all.shape[1:])
    forward, inverse = fourier_tables(mode_index, length)
    basis = forward.astype(BF).reshape(2 * slots, length)
    inv = inverse.astype(BF).reshape(length, 2 * slots)
    wqo, wup, wdn = to_table(dense_all.reshape(-1, width), owner_list, hidden)
    acts, spectra, sig = front(inputs, observed, wqo, small_master[None, :width], basis, inv, weights)
    output, grad_summed, grad_mixed, g_out, g_up, g_down, sums = middle(
        small_master[2 * width :], acts.reshape(inputs.shape), sig.reshape(inputs.shape), out_grad, wqo, wup, wdn,
        small_master[None, width : 2 * width], inv,
    )
    input_grad, g_query, sum_query, g_mixer = back(
        grad_mixed.reshape(-1, width), spectra, acts, grad_summed.reshape(-1, width), observed, wqo, basis.T, weights
    )
    small_grad = jnp.concatenate(
        [
            jnp.sum(sum_query, axis=0).reshape(-1, 128),
            jnp.sum(sums[:8], axis=0).reshape(-1, 128),
            jnp.sum(sums[8:, :128].reshape(20, 8, 128), axis=1),
            jnp.zeros((4, 128), F32),
        ]
    )
    dense_grad = to_owners((g_query, g_out, g_up, g_down), owner_list)
    dense_mine, mixer_mine, small_all = reduce_scatter(
        dense_grad.reshape((ndp * nmode,) + dense_master.shape), g_mixer.reshape((ndp * nmode,) + g_mixer.shape[2:]), small_grad
    )
    small_total = jnp.concatenate([small_all[:8].reshape(-1), jnp.sum(small_all[8:28], axis=1)])
    dense_first_new, dense_second_new, dense_new = adam_update(
        dense_master, dense_mine, dense_first, dense_second, RATE_DENSE
    )
    mixer_first_new, mixer_second_new, mixer_new = adam_update(
        mixer_master, mixer_mine.reshape(mixer_master.shape), mixer_first, mixer_second, RATE_MIXER
    )
    small_first_new, small_second_new, small_new = adam_update(
        small_master, small_total, small_first, small_second, RATE_SMALL
    )
    return (
        output,
        input_grad.reshape(inputs.shape),
        dense_first_new,
        dense_second_new,
        dense_new,
        mixer_first_new,
        mixer_second_new,
        mixer_new,
        small_first_new,
        small_second_new,
        small_new,
        small_total[width : 2 * width],
    )


def solution(mesh):
    placed = (
        P(("dp", "mode"), None, None),
        P(("dp", "mode"), None),
        P(("dp", "mode"), None, None),
        P(),
        P(),
        P(("dp", "mode"), None),
        P(("dp", "mode"), None),
        P(("dp", "mode"), None),
        P("mode", "dp", None),
        P("mode", "dp", None),
        P("mode", "dp", None),
        P(),
        P(),
        P(),
    )
    return jax.shard_map(
        shards,
        mesh=mesh,
        in_specs=placed,
        out_specs=(
            P(("dp", "mode"), None, None),
            P(("dp", "mode"), None, None),
            P(("dp", "mode"), None),
            P(("dp", "mode"), None),
            P(("dp", "mode"), None),
            P("mode", "dp", None),
            P("mode", "dp", None),
            P("mode", "dp", None),
            P(),
            P(),
            P(),
            P(),
        ),
        check_vma=False,
    )
```

```python
import functools
import math

import jax
import jax.numpy as jnp
import numpy as np
from jax import lax
from jax.experimental import pallas as pl
from jax.experimental.pallas import tpu as pltpu
from jax.sharding import PartitionSpec as P

STEP = 10
BETA_ONE = 0.9
BETA_TWO = 0.95
ADAM_EPS = 1e-08
DECAY_RATE = 0.1
RATE_DENSE = 0.03
RATE_MIXER = 0.03
RATE_SMALL = 0.5

KERNEL_SIZES = (7, 12, 14, 24, 48)
LOG2E = 1.4426950408889634
BF = jnp.bfloat16
F32 = jnp.float32
NT = (((1,), (1,)), ((), ()))
NN = (((1,), (0,)), ((), ()))
TN = (((0,), (0,)), ((), ()))


def dot(a, b, dims=NN):
    return lax.dot_general(a, b, dims, preferred_element_type=F32)


def average_counts(length):
    tables = []
    t = np.arange(length)
    for size in KERNEL_SIZES:
        u = np.clip(t[:, None] - (size - 1) // 2 + np.arange(size)[None, :], 0, length - 1)
        tables.append((u[:, :, None] == t[None, None, :]).sum(1))
    return np.stack(tables).astype(np.float32)


def gelu_parts(h):
    z = jnp.abs(h)
    e = jnp.exp2(h * h * (-0.5 * LOG2E))
    t = 1.0 / (1.0 + (0.3275911 * math.sqrt(0.5)) * z)
    poly = t * (0.5 * 0.254829592 + t * (-0.5 * 0.284496736 + t * (0.5 * 1.421413741 + t * (-0.5 * 1.453152027 + t * (0.5 * 1.061405429)))))
    tail = poly * e
    big = jnp.where(h < 0, tail, 1.0 - tail)
    return big, e * (1.0 / math.sqrt(2 * math.pi))


def middle_kernel(W, L, D, FF, steps,
                  mix_ref, acts_ref, sig_ref, og_ref, wq_ref, wup_ref, wdn_ref, bias_ref, invt_ref, cnt_ref, cntt_ref,
                  out_ref, gsum_ref, gmix_ref, gw_ref, gup_ref, gdn_ref, small_ref,
                  vs, base, avg1, c1, v1, active, dgelu, first, flow, gb, ghid, glow, avg2, stk, accs, accb):
    step = pl.program_id(0)
    T = W * L
    CH = 16
    CC = 256
    nc = D // CC
    nr = L // CH
    FT = 512

    @pl.when(step == 0)
    def _():
        vs[...] = jnp.zeros_like(vs)
        stk[...] = jnp.zeros_like(stk)
        accs[...] = jnp.zeros_like(accs)
        accb[...] = jnp.zeros_like(accb)
        gw_ref[...] = jnp.zeros_like(gw_ref)
        gup_ref[...] = jnp.zeros_like(gup_ref)
        gdn_ref[...] = jnp.zeros_like(gdn_ref)

    def fold(x):
        y = x[:, 0:128]
        for i in range(1, CC // 128):
            y = y + x[:, i * 128:(i + 1) * 128]
        return y[0:8] + y[8:16]

    def scaled_shares(v, base_at):
        logits = [mix_ref[base_at + k] * LOG2E * v + mix_ref[base_at + 5 + k] * LOG2E for k in range(5)]
        top = functools.reduce(jnp.maximum, logits)
        es = [jnp.exp2(l - top) for l in logits]
        r = 1.0 / functools.reduce(lambda a, b: a + b, es)
        return [e * (r * (1.0 / s)) for e, s in zip(es, KERNEL_SIZES)]

    def backward(v, g, cs, avs, mean, base_at):
        gv = g * v
        total = None
        for k in range(5):
            t = cs[k] * (KERNEL_SIZES[k] * mean - avs[k])
            total = mix_ref[base_at + k] * t if total is None else total + mix_ref[base_at + k] * t
            accs[base_at + k] += fold(gv * t)
            accs[base_at + 5 + k] += fold(g * t)
        return g, g * total

    def split(v, w, rows, cols):
        hi = v.astype(BF)
        vs[w, rows, cols] = hi
        return hi

    sig = sig_ref[...].reshape(T, D)
    base[...] = dot(sig, wq_ref[D:2 * D, :])

    def window_one(w, _):
        def rows_a(i, _):
            for c in range(nc):
                cols = slice(c * CC, (c + 1) * CC)
                rows = pl.ds(pl.multiple_of(w * L + i * CH, CH), CH)
                here = pl.ds(pl.multiple_of(i * CH, CH), CH)
                low_rows = pl.ds(pl.multiple_of(L + i * CH, CH), CH)
                v = base[rows, cols] + acts_ref[w, here, cols].astype(F32) + bias_ref[:, cols]
                v1[rows, cols] = v
                hi = v.astype(BF)
                vs[here, cols] = hi
                vs[low_rows, cols] = (v - hi.astype(F32)).astype(BF)
            return 0
        lax.fori_loop(0, nr, rows_a, 0)
        avg1[pl.ds(pl.multiple_of(w * 5 * L, 32), 5 * L), :] = dot(cnt_ref[...], vs[...])

        def rows_b(i, _):
            for c in range(nc):
                cols = slice(c * CC, (c + 1) * CC)
                rows = pl.ds(pl.multiple_of(w * L + i * CH, CH), CH)
                v = v1[rows, cols]
                cs = scaled_shares(v, 0)
                mean = None
                for k in range(5):
                    at = pl.ds(pl.multiple_of((w * 5 + k) * L + i * CH, CH), CH)
                    u = cs[k] * avg1[at, cols]
                    c1[at, cols] = cs[k]
                    mean = u if mean is None else mean + u
                f = v - mean
                first[rows, cols] = f
                flow[pl.ds(pl.multiple_of(step * T + w * L + i * CH, CH), CH), cols] = f.astype(BF)
            return 0
        lax.fori_loop(0, nr, rows_b, 0)
        return 0
    lax.fori_loop(0, W, window_one, 0)

    here_t = pl.ds(pl.multiple_of(step * T, CH), T)
    base[...] = first[...]

    def ffn(n, _):
        cols = pl.ds(pl.multiple_of(n * FT, FT), FT)
        h = dot(flow[here_t, :], wup_ref[cols, :], NT)
        big, small = gelu_parts(h)
        a = (h * big).astype(BF)
        active[here_t, cols] = a
        dgelu[:, cols] = (big + h * small).astype(BF)
        base[...] += dot(a, wdn_ref[cols, :])
        return 0
    lax.fori_loop(0, FF // FT, ffn, 0)

    def window_two(w, _):
        def rows_a(i, _):
            for c in range(nc):
                cols = slice(c * CC, (c + 1) * CC)
                rows = pl.ds(pl.multiple_of(w * L + i * CH, CH), CH)
                here = pl.ds(pl.multiple_of(i * CH, CH), CH)
                low_rows = pl.ds(pl.multiple_of(L + i * CH, CH), CH)
                v = base[rows, cols]
                hi = v.astype(BF)
                vs[here, cols] = hi
                vs[low_rows, cols] = (v - hi.astype(F32)).astype(BF)
            return 0
        lax.fori_loop(0, nr, rows_a, 0)
        avg2[...] = dot(cnt_ref[...], vs[...])

        def rows_b(i, _):
            for c in range(nc):
                cols = slice(c * CC, (c + 1) * CC)
                rows = pl.ds(pl.multiple_of(w * L + i * CH, CH), CH)
                here = pl.ds(pl.multiple_of(i * CH, CH), CH)
                v = base[rows, cols]
                cs = scaled_shares(v, 10)
                avs = [avg2[pl.ds(pl.multiple_of(k * L + i * CH, CH), CH), cols] for k in range(5)]
                mean = functools.reduce(lambda a, b: a + b, [c_ * a_ for c_, a_ in zip(cs, avs)])
                out_ref[w, here, cols] = (v - mean).astype(BF)
                g = og_ref[w, here, cols].astype(F32)
                for k in range(5):
                    stk[pl.ds(pl.multiple_of(k * L + i * CH, CH), CH), cols] = (cs[k] * g).astype(BF)
                g, extra = backward(v, g, cs, avs, mean, 10)
                base[rows, cols] = g + extra
            return 0
        lax.fori_loop(0, nr, rows_b, 0)
        rows = pl.ds(pl.multiple_of(w * L, L), L)
        gs = base[rows, :] - dot(cntt_ref[...], stk[...])
        base[rows, :] = gs
        gb[pl.ds(pl.multiple_of(step * T + w * L, 32), L), :] = gs.astype(BF)
        return 0
    lax.fori_loop(0, W, window_two, 0)

    def ffn_back(n, _):
        cols = pl.ds(pl.multiple_of(n * FT, FT), FT)
        ga = dot(gb[here_t, :], wdn_ref[cols, :], NT)
        gh = (ga * dgelu[:, cols].astype(F32)).astype(BF)
        ghid[here_t, cols] = gh
        base[...] += dot(gh, wup_ref[cols, :])
        return 0
    lax.fori_loop(0, FF // FT, ffn_back, 0)

    def window_three(w, _):
        def rows_b(i, _):
            for c in range(nc):
                cols = slice(c * CC, (c + 1) * CC)
                rows = pl.ds(pl.multiple_of(w * L + i * CH, CH), CH)
                v = v1[rows, cols]
                g = base[rows, cols]
                ats = [pl.ds(pl.multiple_of((w * 5 + k) * L + i * CH, CH), CH) for k in range(5)]
                cs = [c1[at, cols] for at in ats]
                avs = [avg1[at, cols] for at in ats]
                mean = v - first[rows, cols]
                for k in range(5):
                    stk[pl.ds(pl.multiple_of(k * L + i * CH, CH), CH), cols] = (cs[k] * g).astype(BF)
                g, extra = backward(v, g, cs, avs, mean, 0)
                base[rows, cols] = g + extra
                accb[:, cols] += extra[0:8] + extra[8:16]
            return 0
        lax.fori_loop(0, nr, rows_b, 0)
        rows = pl.ds(pl.multiple_of(w * L, L), L)
        gs = base[rows, :] - dot(cntt_ref[...], stk[...])
        gsum_ref[w] = gs
        glow[rows, :] = gs.astype(BF)
        return 0
    lax.fori_loop(0, W, window_three, 0)

    back = dot(glow[...], wq_ref[D:2 * D, :], NT).astype(BF)
    for w in range(W):
        gmix_ref[w] = dot(invt_ref[...], back[w * L:(w + 1) * L, :]).astype(BF)
    gw_ref[...] += dot(sig, glow[...], TN)

    @pl.when(step == steps - 1)
    def _():
        small_ref[0:8, :] = accb[...]
        for k in range(20):
            small_ref[8 + 8 * k:16 + 8 * k, 0:128] = accs[k]
            small_ref[8 + 8 * k:16 + 8 * k, 128:512] = jnp.zeros((8, 384), F32)

        def wgrad(n, _):
            cols = pl.ds(pl.multiple_of(n * FT, FT), FT)
            gup_ref[cols, :] = dot(ghid[:, cols], flow[...], TN)
            gdn_ref[cols, :] = dot(active[:, cols], gb[...], TN)
            return 0
        lax.fori_loop(0, FF // FT, wgrad, 0)


def middle(mix, acts, sig, og, wqo, wup, wdn, bias, inv, W=4):
    n, L, D = acts.shape
    FF = wup.shape[0]
    steps = n // W
    T = W * L
    A = average_counts(L)
    cnt = np.zeros((5 * L, 256), np.float32)
    cnt[:, :L] = A.reshape(5 * L, L)
    cnt[:, L:2 * L] = A.reshape(5 * L, L)
    cntt = np.zeros((L, 512), np.float32)
    cntt[:, :5 * L] = A.transpose(2, 0, 1).reshape(L, 5 * L)
    cnt = jnp.asarray(cnt, BF)
    cntt = jnp.asarray(cntt, BF)
    whole = lambda *s: pl.BlockSpec(s, lambda i: (0,) * len(s), pipeline_mode=pl.Buffered(1))
    piece = lambda *s: pl.BlockSpec(s, lambda i: (i,) + (0,) * (len(s) - 1))
    return pl.pallas_call(
        functools.partial(middle_kernel, W, L, D, FF, steps),
        grid=(steps,),
        out_shape=(
            jax.ShapeDtypeStruct((n, L, D), BF),
            jax.ShapeDtypeStruct((n, L, D), F32),
            jax.ShapeDtypeStruct((n, L, D), BF),
            jax.ShapeDtypeStruct((D, D), F32),
            jax.ShapeDtypeStruct((FF, D), F32),
            jax.ShapeDtypeStruct((FF, D), F32),
            jax.ShapeDtypeStruct((168, D), F32),
        ),
        in_specs=[
            pl.BlockSpec(memory_space=pltpu.SMEM),
            piece(W, L, D), piece(W, L, D), piece(W, L, D),
            whole(2 * D, D), whole(FF, D), whole(FF, D), whole(1, D), whole(L, L), whole(5 * L, 256), whole(L, 512),
        ],
        out_specs=(
            piece(W, L, D), piece(W, L, D), piece(W, L, D), whole(D, D), whole(FF, D), whole(FF, D), whole(168, D),
        ),
        scratch_shapes=[
            pltpu.VMEM((256, D), BF),
            pltpu.VMEM((T, D), F32),
            pltpu.VMEM((W * 5 * L, D), F32),
            pltpu.VMEM((W * 5 * L, D), F32),
            pltpu.VMEM((T, D), F32),
            pltpu.VMEM((n * L, FF), BF),
            pltpu.VMEM((T, FF), BF),
            pltpu.VMEM((T, D), F32),
            pltpu.VMEM((n * L, D), BF),
            pltpu.VMEM((n * L, D), BF),
            pltpu.VMEM((n * L, FF), BF),
            pltpu.VMEM((T, D), BF),
            pltpu.VMEM((5 * L, D), F32),
            pltpu.VMEM((512, D), BF),
            pltpu.VMEM((20, 8, 128), F32),
            pltpu.VMEM((8, D), F32),
        ],
        compiler_params=pltpu.CompilerParams(vmem_limit_bytes=60 * 1024 * 1024),
        name="middle",
    )(mix, acts, sig, og, wqo, wup, wdn, bias, inv.T, cnt, cntt)


UNROLL = 4


def sign_lanes(rows, left, right):
    lane = lax.broadcasted_iota(jnp.int32, (rows, 128), 1)
    return jnp.where(lane < 64, left, right).astype(F32)


def interleave(real, imag, v):
    re, im = real[:, v * 128:(v + 1) * 128], imag[:, v * 128:(v + 1) * 128]
    low = lax.broadcasted_iota(jnp.int32, re.shape, 1) < 64
    return jnp.where(low, re, pltpu.roll(im, 64, 1)), jnp.where(low, pltpu.roll(re, 64, 1), im)


def gather_rows(tiles, w, slots, n):
    reals, imags = [], []
    for v in range(4):
        first = tiles[2 * v, pl.ds(w, slots, stride=n), :]
        second = tiles[2 * v + 1, pl.ds(w, slots, stride=n), :]
        low = lax.broadcasted_iota(jnp.int32, first.shape, 1) < 64
        reals.append(jnp.where(low, first, pltpu.roll(second, 64, 1)).astype(BF))
        imags.append(jnp.where(low, pltpu.roll(first, 64, 1), second).astype(BF))
    return jnp.concatenate([jnp.concatenate(reals, 1), jnp.concatenate(imags, 1)], 0)


def spread_rows(tiles, w, slots, n, spectrum):
    for v in range(4):
        one, two = interleave(spectrum[:slots], spectrum[slots:], v)
        tiles[2 * v, pl.ds(w, slots, stride=n), :] = one
        tiles[2 * v + 1, pl.ds(w, slots, stride=n), :] = two


def swap_halves(x):
    return pltpu.roll(x, 64, 1)


def head_weights(weights, h, pieces, mode, rows):
    return jnp.concatenate([weights[h * pieces + q, mode, rows, :] for q in range(pieces)], 0)


def front_kernel(n, L, D, slots, in_ref, obs_ref, wq_ref, bias_ref, basis_ref, inv_ref, eye_ref, weights,
                 acts_ref, z_ref, sig_ref, query, tiles, outs):
    ndp, nmode = weights.shape[:2]
    per = slots // nmode
    heads = 8
    pieces = ndp // heads
    depth = 64 // pieces

    def mask(w, _):
        row = obs_ref[pl.ds(w, 1), :].astype(F32)
        rows = pl.ds(pl.multiple_of(w * L, 32), L)
        acts_ref[rows, :] = dot((eye_ref[...] * row).astype(BF), in_ref[rows, :]).astype(BF)
        return 0
    lax.fori_loop(0, n, mask, 0)
    T = 384

    def project(i, _):
        rows = pl.ds(pl.multiple_of(i * T, T), T)
        query[rows, :] = (dot(acts_ref[rows, :], wq_ref[...]) + bias_ref[...]).astype(BF)
        return 0
    lax.fori_loop(0, n * L // T, project, 0)

    def spectra(w, _):
        rows = pl.ds(pl.multiple_of(w * L, 32), L)
        spread_rows(tiles, w, slots, n, dot(basis_ref[...], query[rows, :]))
        return 0
    lax.fori_loop(0, n, spectra, 0)

    for mode in range(nmode):
        def slot(jl, _):
            at = pl.ds(pl.multiple_of((mode * per + jl) * n, n), n)
            rows = pl.ds(pl.multiple_of(jl * depth, depth), depth)
            for h in range(heads):
                x = tiles[h, at, :]
                both = jnp.concatenate([x, swap_halves(x)], 0)[:, :64].astype(BF)
                z_ref[h, pl.ds(pl.multiple_of((mode * per + jl) * 2 * n, 2 * n), 2 * n), :] = both
                y = dot(both, head_weights(weights, h, pieces, mode, rows))
                outs[h, at, :] = y[:n] + swap_halves(y[n:]) * sign_lanes(n, -1.0, 1.0)
            return 0
        lax.fori_loop(0, per, slot, 0, unroll=UNROLL)

    def signal(w, _):
        rows = pl.ds(pl.multiple_of(w * L, 32), L)
        sig_ref[rows, :] = dot(inv_ref[...], gather_rows(outs, w, slots, n)).astype(BF)
        return 0
    lax.fori_loop(0, n, signal, 0)


def front(inputs, observed, wqo, bias, basis, inv, weights):
    n, L, D = inputs.shape
    slots = basis.shape[0] // 2
    vm = pl.BlockSpec(memory_space=pltpu.VMEM)
    whole = lambda *s: pl.BlockSpec(s, lambda i: (0,) * len(s), pipeline_mode=pl.Buffered(1))
    return pl.pallas_call(
        functools.partial(front_kernel, n, L, D, slots),
        grid=(1,),
        out_shape=(
            jax.ShapeDtypeStruct((n * L, D), BF),
            jax.ShapeDtypeStruct((8, 2 * slots * n, 64), BF),
            jax.ShapeDtypeStruct((n * L, D), BF),
        ),
        in_specs=[whole(n * L, D), whole(n, L), whole(D, D), whole(1, D), whole(2 * slots, L), whole(L, 2 * slots), whole(L, L),
                  whole(*weights.shape)],
        out_specs=(whole(n * L, D), whole(8, 2 * slots * n, 64), whole(n * L, D)),
        scratch_shapes=[
            pltpu.VMEM((n * L, D), BF),
            pltpu.VMEM((8, slots * n, 128), F32),
            pltpu.VMEM((8, slots * n, 128), F32),
        ],
        compiler_params=pltpu.CompilerParams(vmem_limit_bytes=60 * 1024 * 1024),
        name="front",
    )(inputs.reshape(n * L, D), observed, wqo, bias, basis, inv, jnp.eye(L, dtype=F32), weights)


def table_kernel(blocks, owner, in_ref, wqo_ref, wup_ref, wdn_ref, src, dst):
    rows = in_ref.shape[0]
    size = rows // blocks
    step = 256

    def widen(i, _):
        at = pl.ds(pl.multiple_of(i * step, step), step)
        src[at, :] = in_ref[at, :].astype(F32)
        return 0
    lax.fori_loop(0, rows // step, widen, 0)

    def move(j, _):
        dst[pl.ds(owner[j] * size, size), :] = src[pl.ds(j * size, size), :]
        return 0
    lax.fori_loop(0, blocks, move, 0, unroll=4)
    start = 0
    for ref in (wqo_ref, wup_ref, wdn_ref):
        def narrow(i, _):
            to = pl.ds(pl.multiple_of(i * step, step), step)
            at = pl.ds(pl.multiple_of(start + i * step, step), step)
            ref[to, :] = dst[at, :].astype(BF)
            return 0
        lax.fori_loop(0, ref.shape[0] // step, narrow, 0)
        start += ref.shape[0]


def to_table(gathered, owner_list, ff):
    rows, D = gathered.shape
    blocks = owner_list.shape[0]
    cols = lambda r: pl.BlockSpec((r, 128), lambda i, o: (0, i))
    return pl.pallas_call(
        functools.partial(table_kernel, blocks),
        grid_spec=pltpu.PrefetchScalarGridSpec(
            num_scalar_prefetch=1,
            grid=(D // 128,),
            in_specs=[cols(rows)],
            out_specs=(cols(2 * D), cols(ff), cols(ff)),
            scratch_shapes=[pltpu.VMEM((rows + 8, 128), F32), pltpu.VMEM((rows + 8, 128), F32)],
        ),
        out_shape=(
            jax.ShapeDtypeStruct((2 * D, D), BF),
            jax.ShapeDtypeStruct((ff, D), BF),
            jax.ShapeDtypeStruct((ff, D), BF),
        ),
        compiler_params=pltpu.CompilerParams(vmem_limit_bytes=40 * 1024 * 1024),
        name="to_table",
    )(owner_list, gathered)


MESH = pl.DeviceIdType.MESH


def places():
    ndp, nmode = lax.axis_size("dp"), lax.axis_size("mode")
    sizes = {"a": ndp // 2, "b": 2, "y": nmode // 2, "c": 2}
    dp, mode = lax.axis_index("dp"), lax.axis_index("mode")
    here = {"a": dp // 2, "b": lax.rem(dp, 2), "y": mode // 2, "c": lax.rem(mode, 2)}
    return sizes, here


def number(sizes, at):
    return ((at["a"] * sizes["b"] + at["b"]) * sizes["y"] + at["y"]) * 2 + at["c"]


def device(sizes, at):
    return {"dp": at["a"] * sizes["b"] + at["b"], "mode": at["y"] * 2 + at["c"]}


def move(sizes, at, axis, d):
    return {**at, axis: lax.rem(at[axis] + d, sizes[axis])}


def greet():
    ndp, nmode = lax.axis_size("dp"), lax.axis_size("mode")
    dp, mode = lax.axis_index("dp"), lax.axis_index("mode")
    barrier = pltpu.get_barrier_semaphore()
    for d in range(1, nmode):
        pl.semaphore_signal(barrier, 1, device_id={"dp": dp, "mode": lax.rem(mode + d, nmode)}, device_id_type=MESH)
    for d in range(1, ndp):
        pl.semaphore_signal(barrier, 1, device_id={"dp": lax.rem(dp + d, ndp), "mode": mode}, device_id_type=MESH)
    pl.semaphore_wait(barrier, ndp + nmode - 2)


def staggered(count, *stages):
    k = len(stages)
    if count < k:
        for stage in stages:
            for t in range(count):
                stage(t)
        return
    for t in range(k - 1):
        for s in range(t + 1):
            stages[s](t - s)

    def body(t, _):
        for s in range(k):
            stages[s](t - s)
        return 0
    lax.fori_loop(k - 1, count, body, 0)
    for t in range(count, count + k - 1):
        for s in range(t - count + 1, k):
            stages[s](t - s)


def gather_kernel(*refs):
    kinds = 2
    ins, outs = refs[:kinds], refs[kinds:2 * kinds]
    recv, send, local = refs[2 * kinds:]
    sizes, here = places()
    greet()

    def copy(kind, at, to, stage, own=False):
        n = number(sizes, at)
        return pltpu.make_async_remote_copy(
            src_ref=ins[kind] if own else outs[kind].at[n], dst_ref=outs[kind].at[n],
            send_sem=send.at[kind, stage], recv_sem=recv.at[kind, n],
            device_id=device(sizes, to), device_id_type=MESH)

    def arrived(kind, at):
        copy(kind, at, here, 0).wait_recv()

    def drain(kind, stage, count):
        ref = outs[kind].at[pl.ds(0, count)]
        pltpu.make_async_copy(ref, ref, send.at[kind, stage]).wait()

    mine = [pltpu.make_async_copy(ins[k], outs[k].at[number(sizes, here)], local.at[k]) for k in range(kinds)]
    for c in mine:
        c.start()

    def run(u, v):
        na, nu, nv = sizes["a"], sizes[u], sizes[v]

        def onward(kind, at, axes, own=False):
            for axis, stage in axes:
                for d in range(1, sizes[axis]):
                    copy(kind, at, move(sizes, here, axis, d), stage, own).start()

        for kind in range(kinds):
            onward(kind, here, (("a", 0), (u, 1), (v, 2), ("c", 3)), True)

        def line(t):
            at = move(sizes, here, "a", t + 1)
            for kind in range(kinds):
                arrived(kind, at)
                onward(kind, at, ((u, 1), (v, 2), ("c", 3)))

        def second(t):
            for d in range(1, nu):
                at = move(sizes, move(sizes, here, "a", t), u, d)
                for kind in range(kinds):
                    arrived(kind, at)
                    onward(kind, at, ((v, 2), ("c", 3)))

        def third(t):
            for e in range(nu):
                for d in range(1, nv):
                    at = move(sizes, move(sizes, move(sizes, here, "a", t), u, e), v, d)
                    for kind in range(kinds):
                        arrived(kind, at)
                        onward(kind, at, (("c", 3),))

        second(0)
        staggered(na - 1, line, lambda t: second(t + 1), third)
        third(na - 1)
        for kind in range(kinds):
            drain(kind, 0, na - 1)
            drain(kind, 1, na * (nu - 1))
            drain(kind, 2, na * nu * (nv - 1))

    pl.when(here["c"] == 0)(lambda: run("b", "y"))
    pl.when(here["c"] == 1)(lambda: run("y", "b"))
    group = sizes["a"] * sizes["b"] * sizes["y"]
    other = move(sizes, here, "c", 1)

    def partner(i, _):
        for kind in range(kinds):
            copy(kind, {"a": i // (sizes["b"] * sizes["y"]), "b": lax.rem(i // sizes["y"], sizes["b"]),
                        "y": lax.rem(i, sizes["y"]), "c": other["c"]}, here, 0).wait_recv()
        return 0
    lax.fori_loop(0, group, partner, 0)
    for kind in range(kinds):
        drain(kind, 3, group)
    for c in mine:
        c.wait()


def gather(dense, mixer):
    nd = lax.axis_size("dp") * lax.axis_size("mode")
    anywhere = pl.BlockSpec(memory_space=pl.ANY)
    return pl.pallas_call(
        gather_kernel,
        out_shape=tuple(jax.ShapeDtypeStruct((nd,) + x.shape, x.dtype) for x in (dense, mixer)),
        in_specs=[anywhere] * 2,
        out_specs=(anywhere,) * 2,
        scratch_shapes=[pltpu.SemaphoreType.DMA((2, nd)), pltpu.SemaphoreType.DMA((2, 4)), pltpu.SemaphoreType.DMA((2,))],
        compiler_params=pltpu.CompilerParams(collective_id=0, has_side_effects=True),
        name="gather",
    )(dense, mixer)


def roles():
    ndp, nmode = lax.axis_size("dp"), lax.axis_size("mode")
    half = nmode // 2
    dp, mode = lax.axis_index("dp"), lax.axis_index("mode")
    b, y, c = lax.rem(dp, half), mode // 2, lax.rem(mode, 2)
    here = {"a": dp // half, "u": jnp.where(c == 0, b, y), "v": jnp.where(c == 0, y, b), "c": c}
    return {"a": ndp // half, "u": half, "v": half, "c": 2}, here


def place_of(sizes, at):
    b = jnp.where(at["c"] == 0, at["u"], at["v"])
    y = jnp.where(at["c"] == 0, at["v"], at["u"])
    return at["a"] * sizes["u"] + b, y * 2 + at["c"]


def device_of(sizes, at):
    dp, mode = place_of(sizes, at)
    return {"dp": dp, "mode": mode}


def partner_of(at):
    return {"a": at["a"], "u": at["v"], "v": at["u"], "c": 1 - at["c"]}


def reducer(sizes, here, own, from_c, from_v, from_u, from_a, out, send, recv_c, recv_v, recv_u, recv_a):
    na, nu, nv = sizes["a"], sizes["u"], sizes["v"]
    rows = from_c.shape[1]
    step = next(s for s in (96, 32, rows) if rows % s == 0)

    def owner(t, e, d):
        return move(sizes, move(sizes, move(sizes, here, "a", t + 1), "u", e), "v", d)

    def spot(at):
        dp, mode = place_of(sizes, at)
        return dp * sizes["v"] + mode // 2

    def to_partner(at):
        n = spot(at)
        return pltpu.make_async_remote_copy(
            src_ref=own(at), dst_ref=from_c.at[n], send_sem=send.at[0], recv_sem=recv_c.at[n],
            device_id=device_of(sizes, partner_of(here)), device_id_type=MESH)

    def chunks(at, terms, store):
        mine = own(at)

        def chunk(i, _):
            part = pl.ds(pl.multiple_of(i * step, step), step) if step != rows else slice(None)
            total = mine[part, :].astype(F32)
            for ref, k in terms:
                total = total + ref[k, part, :].astype(F32)
            store(mine, part, total)
            return 0
        lax.fori_loop(0, rows // step, chunk, 0)

    def keep(mine, part, total):
        mine[part, :] = total.astype(BF)

    def finish(mine, part, total):
        out[part, :] = total

    def slot_v(t, e, d):
        return (t * nu + e) * (nv - 1) + d - 1

    def copy(at, buffer, s, stage, sems, to):
        return pltpu.make_async_remote_copy(
            src_ref=own(at), dst_ref=buffer.at[s], send_sem=send.at[stage], recv_sem=sems.at[s],
            device_id=device_of(sizes, to), device_id_type=MESH)

    def copy_v(t, e, d):
        s = slot_v(t, e, d)
        return copy(owner(t, e, d), from_v, s, 1, recv_v, move(sizes, here, "v", d))

    def copy_u(t, e):
        return copy(owner(t, e, 0), from_u, t * (nu - 1) + e - 1, 2, recv_u, move(sizes, here, "u", e))

    def copy_a(t):
        return copy(owner(t, 0, 0), from_a, t, 3, recv_a, owner(t, 0, 0))

    def heard(at):
        n = spot(at)
        pltpu.make_async_remote_copy(
            src_ref=own(at), dst_ref=from_c.at[n], send_sem=send.at[0], recv_sem=recv_c.at[n],
            device_id=device_of(sizes, partner_of(here)), device_id_type=MESH).wait_recv()
        return [(from_c, n)]

    def first(t):
        for d in range(1, nv):
            for e in range(nu):
                at = owner(t, e, d)
                chunks(at, heard(at), keep)
                copy_v(t, e, d).start()

    def after_v(t, e):
        terms = heard(owner(t, e, 0))
        for d in range(1, nv):
            copy_v(t, e, d).wait_recv()
            terms.append((from_v, slot_v(t, e, d)))
        return terms

    def second(t):
        for e in range(1, nu):
            chunks(owner(t, e, 0), after_v(t, e), keep)
            copy_u(t, e).start()

    def after_u(t):
        terms = after_v(t, 0)
        for e in range(1, nu):
            copy_u(t, e).wait_recv()
            terms.append((from_u, t * (nu - 1) + e - 1))
        return terms

    def third(t):
        chunks(owner(t, 0, 0), after_u(t), keep)
        copy_a(t).start()

    def last():
        terms = after_u(na - 1)
        for t in range(na - 1):
            copy_a(t).wait_recv()
            terms.append((from_a, t))
        chunks(here, terms, finish)

    def drain():
        for stage, count in ((0, from_c.shape[0]), (1, na * nu * (nv - 1)), (2, na * (nu - 1)), (3, na - 1)):
            ref = from_c.at[pl.ds(0, count)]
            pltpu.make_async_copy(ref, ref, send.at[stage]).wait()

    return to_partner, first, second, third, last, drain


def each(start, stop, *steps):
    def body(t, _):
        for s in steps:
            s(t)
        return 0
    lax.fori_loop(start, stop, body, 0)


def tail_kernel(n, L, D, slots, blocks, owner, gmix_h, z_h, acts_h, gsum_h, weights_h, gout_h, gup_h, gdn_h,
                obs_ref, wq_ref, basist_ref, eye_ref, sums_ref,
                dense_out, mixer_out, small_out, gin_h,
                gmix, z, acts, gsum, mix, src, tiles, glow, gbias, tmp, con,
                fc0, fc1, fv0, fv1, fu0, fu1, fa0, fa1, small_one, small_two,
                loads, send, recv_c, recv_v, recv_u, recv_a, small_send, small_recv):
    sizes, here = roles()
    ndp, nmode = lax.axis_size("dp"), lax.axis_size("mode")
    dp, mode = lax.axis_index("dp"), lax.axis_index("mode")
    na = sizes["a"]
    per = slots // nmode
    heads = 8
    pieces = ndp // heads
    depth = 64 // pieces
    rows = con.shape[1]
    size = con.shape[0] * rows // blocks

    def load(i, a, b):
        return pltpu.make_async_copy(a, b, loads.at[i])
    firsts = [load(0, gmix_h, gmix), load(1, z_h, z), load(2, weights_h, mix)]
    later = [load(3, acts_h, acts), load(4, gsum_h, gsum)]
    grads = []
    start = D
    for i, ref in enumerate((gout_h, gup_h, gdn_h)):
        for c in range(D // 128):
            grads.append(load(5 + i * 4 + c, ref.at[:, pl.ds(c * 128, 128)], src.at[c, pl.ds(start, ref.shape[0]), :]))
        start += ref.shape[0]
    for c in firsts + later + grads:
        c.start()
    greet()

    send_m, first_m, second_m, third_m, last_m, drain_m = reducer(
        sizes, here, lambda at: mix.at[place_of(sizes, at)], fc1, fv1, fu1, fa1, mixer_out,
        send.at[1], recv_c.at[1], recv_v.at[1], recv_u.at[1], recv_a.at[1])

    def con_at(at):
        p, m = place_of(sizes, at)
        return con.at[p * nmode + m]
    send_d, first_d, second_d, third_d, last_d, drain_d = reducer(
        sizes, here, con_at, fc0, fv0, fu0, fa0, dense_out,
        send.at[0], recv_c.at[0], recv_v.at[0], recv_u.at[0], recv_a.at[0])

    firsts[0].wait()

    def spectra(w):
        part = pl.ds(pl.multiple_of(w * L, 32), L)
        spread_rows(tiles, w, slots, n, gmix[part, :].astype(F32))
    each(0, n, spectra)
    firsts[1].wait()
    firsts[2].wait()

    def mix_mode(m):
        def slot(jl, _):
            at = pl.ds(pl.multiple_of((m * per + jl) * n, n), n)
            at2 = pl.ds(pl.multiple_of((m * per + jl) * 2 * n, 2 * n), 2 * n)
            part = pl.ds(pl.multiple_of(jl * depth, depth), depth)
            for h in range(heads):
                y = tiles[h, at, :]
                both = jnp.concatenate([y, swap_halves(y) * sign_lanes(n, 1.0, -1.0)], 0).astype(BF)
                x = dot(both, head_weights(mix, h, pieces, m, part), NT)
                tiles[h, at, :] = jnp.concatenate([x[:n], x[n:]], 1)
                g = dot(z[h, at2, :], both, TN).astype(BF)
                for q in range(pieces):
                    mix[h * pieces + q, m, part, :] = g[q * depth:(q + 1) * depth]
            return 0
        lax.fori_loop(0, per, slot, 0, unroll=2)

    mine_y = mode // 2

    def mode_at(i, core):
        return lax.rem(mine_y + 1 + i, nmode // 2) * 2 + core

    def other_modes(i):
        m = mode_at(i, 1 - here["c"])
        mix_mode(m)

        def hand(p):
            half = sizes["u"]
            b, y = lax.rem(p, half), m // 2
            core = 1 - here["c"]
            send_m({"a": p // half, "u": jnp.where(core == 0, b, y), "v": jnp.where(core == 0, y, b), "c": core}).start()
        each(0, ndp, hand)
    each(0, nmode // 2, other_modes)
    each(0, nmode // 2, lambda i: mix_mode(mode_at(i, here["c"])))
    each(0, na, first_m)

    gbias[...] = jnp.zeros_like(gbias)

    def query(w):
        part = pl.ds(pl.multiple_of(w * L, 32), L)
        g = dot(basist_ref[...], gather_rows(tiles, w, slots, n))
        glow[part, :] = g.astype(BF)
        gbias[...] += functools.reduce(lambda p, q: p + q, [g[i * 8:(i + 1) * 8] for i in range(L // 8)])
    each(0, n, query)

    for k, sums in ((0, gbias[...]), (4, sums_ref[0:8, :])):
        total = jnp.sum(sums, axis=0, keepdims=True)
        for c in range(D // 128):
            small_one[mode, k + c:k + c + 1, :] = total[:, c * 128:(c + 1) * 128]
    for k in range(20):
        small_one[mode, 8 + k:9 + k, :] = jnp.sum(sums_ref[8 + 8 * k:16 + 8 * k, 0:128], axis=0, keepdims=True)
    small_one[mode, 28:32, :] = jnp.zeros((4, 128), F32)

    def small_copy(buffer, axis, index, count, d, base):
        return pltpu.make_async_remote_copy(
            src_ref=buffer.at[index], dst_ref=buffer.at[index], send_sem=small_send.at[base + d - 1], recv_sem=small_recv.at[base + d - 1],
            device_id={**{"dp": dp, "mode": mode}, axis: lax.rem(index + d, count)}, device_id_type=MESH)
    ones = [small_copy(small_one, "mode", mode, nmode, d, 0) for d in range(1, nmode)]
    twos = [small_copy(small_two, "dp", dp, ndp, d, nmode - 1) for d in range(1, ndp)]
    for c in ones:
        c.start()

    for c in later:
        c.wait()
    g = dot(acts[...], glow[...], TN)
    for c in range(D // 128):
        src[c, 0:D, :] = g[:, c * 128:(c + 1) * 128]
    each(0, na // 2, second_m)
    for c in grads:
        c.wait()

    per_shard = rows // size
    join = 4 if per_shard % 4 == 0 else 1
    units = per_shard // join

    def pick(s):
        for k in range(units):
            for c in range(D // 128):
                for i in range(join):
                    row = owner[(s * units + k) * join + i] * size
                    tmp[c, i * size:(i + 1) * size, :] = src[c, pl.ds(row, size), :]
                part = slice(k * join * size, (k + 1) * join * size)
                con[s, part, c * 128:(c + 1) * 128] = tmp[c, 0:join * size, :].astype(BF)
    shards = con.shape[0]
    each(0, shards // 2, pick)
    each(na // 2, na, second_m)
    each(0, na // 2, third_m)
    each(shards // 2, shards, pick)

    def hand_line(t):
        other = partner_of(here)
        for d in list(range(1, sizes["v"])) + [0]:
            for e in range(sizes["u"]):
                send_d(move(sizes, move(sizes, move(sizes, other, "a", t + 1), "u", e), "v", d)).start()
    each(0, na, hand_line)
    each(na // 2, na - 1, third_m)

    def input_grad(w):
        part = pl.ds(pl.multiple_of(w * L, 32), L)
        row = obs_ref[pl.ds(w, 1), :].astype(F32)
        mask = dot((eye_ref[...] * row).astype(BF), jnp.ones((L, 128), BF))
        g = gsum[part, :] + dot(glow[part, :], wq_ref[...], NT)
        for c in range(D // 128):
            gsum[part, c * 128:(c + 1) * 128] = g[:, c * 128:(c + 1) * 128] * mask
    for c in ones:
        c.wait()
    small_two[dp] = functools.reduce(lambda p, q: p + q, [small_one[i] for i in range(nmode)])
    for c in twos:
        c.start()
    each(0, na, first_d)
    each(0, n, input_grad)
    result = load(17, gsum, gin_h)
    result.start()
    each(0, 1, second_d)
    each(1, na - 1, second_d, lambda t: third_d(t - 1))
    last_m()
    second_d(na - 1)
    third_d(na - 2)
    last_d()
    for c in twos:
        c.wait()
    small_out[...] = functools.reduce(lambda p, q: p + q, [small_two[i] for i in range(ndp)])
    drain_m()
    drain_d()
    result.wait()


def tail(gmix, z, acts, gsum, observed, wqo, basist, weights, gout, gup, gdn, sums, owner_list, shard_rows):
    n, L = observed.shape
    D = acts.shape[1]
    slots = basist.shape[1] // 2
    ndp, nmode, mixer_rows = weights.shape[:3]
    nd = ndp * nmode
    total = nd * shard_rows
    half = nmode // 2
    na = ndp // half
    group = nd // 2
    anywhere = pl.BlockSpec(memory_space=pl.ANY)
    vmem = pl.BlockSpec(memory_space=pltpu.VMEM)
    shapes = ((shard_rows, D), (mixer_rows, 128))
    counts = (group, na * half * (half - 1), na * (half - 1), na - 1)
    sem = lambda *s: pltpu.SemaphoreType.DMA(s)
    return pl.pallas_call(
        functools.partial(tail_kernel, n, L, D, slots, owner_list.shape[0]),
        out_shape=(
            jax.ShapeDtypeStruct(shapes[0], F32), jax.ShapeDtypeStruct(shapes[1], F32), jax.ShapeDtypeStruct((32, 128), F32),
            jax.ShapeDtypeStruct((n * L, D), F32),
        ),
        in_specs=[pl.BlockSpec(memory_space=pltpu.SMEM)] + [anywhere] * 8 + [
            vmem, pl.BlockSpec(memory_space=pltpu.VMEM), vmem, vmem, vmem],
        out_specs=(vmem, vmem, vmem, anywhere),
        scratch_shapes=[
            pltpu.VMEM((n * L, D), BF),
            pltpu.VMEM(z.shape, BF),
            pltpu.VMEM((n * L, D), BF),
            pltpu.VMEM((n * L, D), F32),
            pltpu.VMEM(weights.shape, BF),
            pltpu.VMEM((D // 128, total + 8, 128), F32),
            pltpu.VMEM((8, slots * n, 128), F32),
            pltpu.VMEM((n * L, D), BF),
            pltpu.VMEM((8, D), F32),
            pltpu.VMEM((D // 128, 80, 128), F32),
            pltpu.VMEM((nd, shard_rows, D), BF),
        ] + [pltpu.VMEM((count,) + s, BF) for count in counts for s in shapes] + [
            pltpu.VMEM((nmode, 32, 128), F32), pltpu.VMEM((ndp, 32, 128), F32),
            sem(18), sem(2, 4), sem(2, counts[0]), sem(2, counts[1]), sem(2, counts[2]), sem(2, counts[3]),
            sem(ndp + nmode - 2), sem(ndp + nmode - 2),
        ],
        compiler_params=pltpu.CompilerParams(collective_id=1, has_side_effects=True, vmem_limit_bytes=62 * 1024 * 1024),
        name="tail",
    )(owner_list, gmix, z, acts, gsum, weights, gout, gup, gdn, observed, wqo[:D], basist, jnp.eye(L, dtype=F32), sums)


def fourier_tables(mode_index, length):
    positions = jnp.arange(length, dtype=jnp.int32)
    phases = mode_index[:, None] * positions[None, :] % length
    angles = phases.astype(jnp.float32) * (2.0 * jnp.pi / length)
    forward = jnp.stack([jnp.cos(angles), -jnp.sin(angles)])
    slot_ids = jnp.arange(mode_index.shape[0], dtype=jnp.int32)
    back_phase = slot_ids[:, None] * positions[None, :] % length
    back_angle = back_phase.astype(jnp.float32) * (2.0 * jnp.pi / length)
    coefs = jnp.where(slot_ids == 0, 1.0, 2.0).astype(jnp.float32) / length
    inverse = jnp.stack(
        [jnp.cos(back_angle) * coefs[:, None], -jnp.sin(back_angle) * coefs[:, None]]
    )
    return (forward, jnp.transpose(inverse, (2, 0, 1)))


def adam_update(weight, gradient, moment, second, step_rate):
    moment_new = BETA_ONE * moment + (1.0 - BETA_ONE) * gradient
    second_new = BETA_TWO * second + (1.0 - BETA_TWO) * gradient * gradient
    scaled_m = moment_new / (1.0 - BETA_ONE**STEP)
    scaled_v = second_new / (1.0 - BETA_TWO**STEP)
    weight_new = weight - step_rate * (
        scaled_m / (jnp.sqrt(scaled_v) + ADAM_EPS) + DECAY_RATE * weight
    )
    return (moment_new, second_new, weight_new)


def shards(
    inputs,
    observed,
    out_grad,
    mode_index,
    owner_list,
    dense_master,
    dense_first,
    dense_second,
    mixer_master,
    mixer_first,
    mixer_second,
    small_master,
    small_first,
    small_second,
):
    ndp, nmode = lax.axis_size("dp"), lax.axis_size("mode")
    length, width = inputs.shape[1:]
    slots = mode_index.shape[0]
    hidden = (dense_master.shape[0] * ndp * nmode - 2 * width) // 2
    dense_all, mixer_all = gather(dense_master.astype(BF), mixer_master.astype(BF).reshape(-1, mixer_master.shape[2]))
    weights = mixer_all.reshape((ndp, nmode) + mixer_all.shape[1:])
    forward, inverse = fourier_tables(mode_index, length)
    basis = forward.astype(BF).reshape(2 * slots, length)
    inv = inverse.astype(BF).reshape(length, 2 * slots)
    wqo, wup, wdn = to_table(dense_all.reshape(-1, width), owner_list, hidden)
    acts, spectra, sig = front(inputs, observed, wqo, small_master[None, :width], basis, inv, weights)
    output, grad_summed, grad_mixed, g_out, g_up, g_down, sums = middle(
        small_master[2 * width :], acts.reshape(inputs.shape), sig.reshape(inputs.shape), out_grad, wqo, wup, wdn,
        small_master[None, width : 2 * width], inv,
    )
    dense_mine, mixer_mine, small_all, input_grad = tail(
        grad_mixed.reshape(-1, width), spectra, acts, grad_summed.reshape(-1, width), observed, wqo, basis.T, weights,
        g_out, g_up, g_down, sums, owner_list, dense_master.shape[0],
    )
    small_total = jnp.concatenate([small_all[:8].reshape(-1), jnp.sum(small_all[8:28], axis=1)])
    dense_first_new, dense_second_new, dense_new = adam_update(
        dense_master, dense_mine, dense_first, dense_second, RATE_DENSE
    )
    mixer_first_new, mixer_second_new, mixer_new = adam_update(
        mixer_master, mixer_mine.reshape(mixer_master.shape), mixer_first, mixer_second, RATE_MIXER
    )
    small_first_new, small_second_new, small_new = adam_update(
        small_master, small_total, small_first, small_second, RATE_SMALL
    )
    return (
        output,
        input_grad.reshape(inputs.shape),
        dense_first_new,
        dense_second_new,
        dense_new,
        mixer_first_new,
        mixer_second_new,
        mixer_new,
        small_first_new,
        small_second_new,
        small_new,
        small_total[width : 2 * width],
    )


def solution(mesh):
    placed = (
        P(("dp", "mode"), None, None),
        P(("dp", "mode"), None),
        P(("dp", "mode"), None, None),
        P(),
        P(),
        P(("dp", "mode"), None),
        P(("dp", "mode"), None),
        P(("dp", "mode"), None),
        P("mode", "dp", None),
        P("mode", "dp", None),
        P("mode", "dp", None),
        P(),
        P(),
        P(),
    )
    return jax.shard_map(
        shards,
        mesh=mesh,
        in_specs=placed,
        out_specs=(
            P(("dp", "mode"), None, None),
            P(("dp", "mode"), None, None),
            P(("dp", "mode"), None),
            P(("dp", "mode"), None),
            P(("dp", "mode"), None),
            P("mode", "dp", None),
            P("mode", "dp", None),
            P("mode", "dp", None),
            P(),
            P(),
            P(),
            P(),
        ),
        check_vma=False,
    )
```

```python
import functools
import math

import jax
import jax.numpy as jnp
import numpy as np
from jax import lax
from jax.experimental import pallas as pl
from jax.experimental.pallas import tpu as pltpu
from jax.sharding import PartitionSpec as P

STEP = 10
BETA_ONE = 0.9
BETA_TWO = 0.95
ADAM_EPS = 1e-08
DECAY_RATE = 0.1
RATE_DENSE = 0.03
RATE_MIXER = 0.03
RATE_SMALL = 0.5

KERNEL_SIZES = (7, 12, 14, 24, 48)
LOG2E = 1.4426950408889634
BF = jnp.bfloat16
F32 = jnp.float32
NT = (((1,), (1,)), ((), ()))
NN = (((1,), (0,)), ((), ()))
TN = (((0,), (0,)), ((), ()))


def dot(a, b, dims=NN):
    return lax.dot_general(a, b, dims, preferred_element_type=F32)


def average_counts(length):
    tables = []
    t = np.arange(length)
    for size in KERNEL_SIZES:
        u = np.clip(t[:, None] - (size - 1) // 2 + np.arange(size)[None, :], 0, length - 1)
        tables.append((u[:, :, None] == t[None, None, :]).sum(1))
    return np.stack(tables).astype(np.float32)


def gelu_parts(h):
    z = jnp.abs(h)
    e = jnp.exp2(h * h * (-0.5 * LOG2E))
    t = 1.0 / (1.0 + (0.3275911 * math.sqrt(0.5)) * z)
    poly = t * (0.5 * 0.254829592 + t * (-0.5 * 0.284496736 + t * (0.5 * 1.421413741 + t * (-0.5 * 1.453152027 + t * (0.5 * 1.061405429)))))
    tail = poly * e
    big = jnp.where(h < 0, tail, 1.0 - tail)
    return big, e * (1.0 / math.sqrt(2 * math.pi))


def middle_kernel(W, L, D, FF, steps,
                  mix_ref, acts_ref, sig_ref, og_ref, wq_ref, wup_ref, wdn_ref, bias_ref, invt_ref, cnt_ref, cntt_ref,
                  out_ref, gsum_ref, gmix_ref, gw_ref, gup_ref, gdn_ref, small_ref,
                  vs, base, avg1, c1, v1, active, dgelu, first, flow, gb, ghid, glow, avg2, stk, accs, accb):
    step = pl.program_id(0)
    T = W * L
    CH = 16
    CC = 256
    nc = D // CC
    nr = L // CH
    FT = 512

    @pl.when(step == 0)
    def _():
        vs[...] = jnp.zeros_like(vs)
        stk[...] = jnp.zeros_like(stk)
        accs[...] = jnp.zeros_like(accs)
        accb[...] = jnp.zeros_like(accb)
        gw_ref[...] = jnp.zeros_like(gw_ref)
        gup_ref[...] = jnp.zeros_like(gup_ref)
        gdn_ref[...] = jnp.zeros_like(gdn_ref)

    def fold(x):
        y = x[:, 0:128]
        for i in range(1, CC // 128):
            y = y + x[:, i * 128:(i + 1) * 128]
        return y[0:8] + y[8:16]

    def scaled_shares(v, base_at):
        logits = [mix_ref[base_at + k] * LOG2E * v + mix_ref[base_at + 5 + k] * LOG2E for k in range(5)]
        top = functools.reduce(jnp.maximum, logits)
        es = [jnp.exp2(l - top) for l in logits]
        r = 1.0 / functools.reduce(lambda a, b: a + b, es)
        return [e * (r * (1.0 / s)) for e, s in zip(es, KERNEL_SIZES)]

    def backward(v, g, cs, avs, mean, base_at):
        gv = g * v
        total = None
        for k in range(5):
            t = cs[k] * (KERNEL_SIZES[k] * mean - avs[k])
            total = mix_ref[base_at + k] * t if total is None else total + mix_ref[base_at + k] * t
            accs[base_at + k] += fold(gv * t)
            accs[base_at + 5 + k] += fold(g * t)
        return g, g * total

    def split(v, w, rows, cols):
        hi = v.astype(BF)
        vs[w, rows, cols] = hi
        return hi

    sig = sig_ref[...].reshape(T, D)
    base[...] = dot(sig, wq_ref[D:2 * D, :])

    def window_one(w, _):
        def rows_a(i, _):
            for c in range(nc):
                cols = slice(c * CC, (c + 1) * CC)
                rows = pl.ds(pl.multiple_of(w * L + i * CH, CH), CH)
                here = pl.ds(pl.multiple_of(i * CH, CH), CH)
                low_rows = pl.ds(pl.multiple_of(L + i * CH, CH), CH)
                v = base[rows, cols] + acts_ref[w, here, cols].astype(F32) + bias_ref[:, cols]
                v1[rows, cols] = v
                hi = v.astype(BF)
                vs[here, cols] = hi
                vs[low_rows, cols] = (v - hi.astype(F32)).astype(BF)
            return 0
        lax.fori_loop(0, nr, rows_a, 0)
        avg1[pl.ds(pl.multiple_of(w * 5 * L, 32), 5 * L), :] = dot(cnt_ref[...], vs[...])

        def rows_b(i, _):
            for c in range(nc):
                cols = slice(c * CC, (c + 1) * CC)
                rows = pl.ds(pl.multiple_of(w * L + i * CH, CH), CH)
                v = v1[rows, cols]
                cs = scaled_shares(v, 0)
                mean = None
                for k in range(5):
                    at = pl.ds(pl.multiple_of((w * 5 + k) * L + i * CH, CH), CH)
                    u = cs[k] * avg1[at, cols]
                    c1[at, cols] = cs[k]
                    mean = u if mean is None else mean + u
                f = v - mean
                first[rows, cols] = f
                flow[pl.ds(pl.multiple_of(step * T + w * L + i * CH, CH), CH), cols] = f.astype(BF)
            return 0
        lax.fori_loop(0, nr, rows_b, 0)
        return 0
    lax.fori_loop(0, W, window_one, 0)

    here_t = pl.ds(pl.multiple_of(step * T, CH), T)
    base[...] = first[...]

    def ffn(n, _):
        cols = pl.ds(pl.multiple_of(n * FT, FT), FT)
        h = dot(flow[here_t, :], wup_ref[cols, :], NT)
        big, small = gelu_parts(h)
        a = (h * big).astype(BF)
        active[here_t, cols] = a
        dgelu[:, cols] = (big + h * small).astype(BF)
        base[...] += dot(a, wdn_ref[cols, :])
        return 0
    lax.fori_loop(0, FF // FT, ffn, 0)

    def window_two(w, _):
        def rows_a(i, _):
            for c in range(nc):
                cols = slice(c * CC, (c + 1) * CC)
                rows = pl.ds(pl.multiple_of(w * L + i * CH, CH), CH)
                here = pl.ds(pl.multiple_of(i * CH, CH), CH)
                low_rows = pl.ds(pl.multiple_of(L + i * CH, CH), CH)
                v = base[rows, cols]
                hi = v.astype(BF)
                vs[here, cols] = hi
                vs[low_rows, cols] = (v - hi.astype(F32)).astype(BF)
            return 0
        lax.fori_loop(0, nr, rows_a, 0)
        avg2[...] = dot(cnt_ref[...], vs[...])

        def rows_b(i, _):
            for c in range(nc):
                cols = slice(c * CC, (c + 1) * CC)
                rows = pl.ds(pl.multiple_of(w * L + i * CH, CH), CH)
                here = pl.ds(pl.multiple_of(i * CH, CH), CH)
                v = base[rows, cols]
                cs = scaled_shares(v, 10)
                avs = [avg2[pl.ds(pl.multiple_of(k * L + i * CH, CH), CH), cols] for k in range(5)]
                mean = functools.reduce(lambda a, b: a + b, [c_ * a_ for c_, a_ in zip(cs, avs)])
                out_ref[w, here, cols] = (v - mean).astype(BF)
                g = og_ref[w, here, cols].astype(F32)
                for k in range(5):
                    stk[pl.ds(pl.multiple_of(k * L + i * CH, CH), CH), cols] = (cs[k] * g).astype(BF)
                g, extra = backward(v, g, cs, avs, mean, 10)
                base[rows, cols] = g + extra
            return 0
        lax.fori_loop(0, nr, rows_b, 0)
        rows = pl.ds(pl.multiple_of(w * L, L), L)
        gs = base[rows, :] - dot(cntt_ref[...], stk[...])
        base[rows, :] = gs
        gb[pl.ds(pl.multiple_of(step * T + w * L, 32), L), :] = gs.astype(BF)
        return 0
    lax.fori_loop(0, W, window_two, 0)

    def ffn_back(n, _):
        cols = pl.ds(pl.multiple_of(n * FT, FT), FT)
        ga = dot(gb[here_t, :], wdn_ref[cols, :], NT)
        gh = (ga * dgelu[:, cols].astype(F32)).astype(BF)
        ghid[here_t, cols] = gh
        base[...] += dot(gh, wup_ref[cols, :])
        return 0
    lax.fori_loop(0, FF // FT, ffn_back, 0)

    def window_three(w, _):
        def rows_b(i, _):
            for c in range(nc):
                cols = slice(c * CC, (c + 1) * CC)
                rows = pl.ds(pl.multiple_of(w * L + i * CH, CH), CH)
                v = v1[rows, cols]
                g = base[rows, cols]
                ats = [pl.ds(pl.multiple_of((w * 5 + k) * L + i * CH, CH), CH) for k in range(5)]
                cs = [c1[at, cols] for at in ats]
                avs = [avg1[at, cols] for at in ats]
                mean = v - first[rows, cols]
                for k in range(5):
                    stk[pl.ds(pl.multiple_of(k * L + i * CH, CH), CH), cols] = (cs[k] * g).astype(BF)
                g, extra = backward(v, g, cs, avs, mean, 0)
                base[rows, cols] = g + extra
                accb[:, cols] += extra[0:8] + extra[8:16]
            return 0
        lax.fori_loop(0, nr, rows_b, 0)
        rows = pl.ds(pl.multiple_of(w * L, L), L)
        gs = base[rows, :] - dot(cntt_ref[...], stk[...])
        gsum_ref[w] = gs
        glow[rows, :] = gs.astype(BF)
        return 0
    lax.fori_loop(0, W, window_three, 0)

    back = dot(glow[...], wq_ref[D:2 * D, :], NT).astype(BF)
    for w in range(W):
        gmix_ref[w] = dot(invt_ref[...], back[w * L:(w + 1) * L, :]).astype(BF)
    gw_ref[...] += dot(sig, glow[...], TN)

    @pl.when(step == steps - 1)
    def _():
        small_ref[0:8, :] = accb[...]
        for k in range(20):
            small_ref[8 + 8 * k:16 + 8 * k, 0:128] = accs[k]
            small_ref[8 + 8 * k:16 + 8 * k, 128:512] = jnp.zeros((8, 384), F32)

        def wgrad(n, _):
            cols = pl.ds(pl.multiple_of(n * FT, FT), FT)
            gup_ref[cols, :] = dot(ghid[:, cols], flow[...], TN)
            gdn_ref[cols, :] = dot(active[:, cols], gb[...], TN)
            return 0
        lax.fori_loop(0, FF // FT, wgrad, 0)


def middle(mix, acts, sig, og, wqo, wup, wdn, bias, inv, W=4):
    n, L, D = acts.shape
    FF = wup.shape[0]
    steps = n // W
    T = W * L
    A = average_counts(L)
    cnt = np.zeros((5 * L, 256), np.float32)
    cnt[:, :L] = A.reshape(5 * L, L)
    cnt[:, L:2 * L] = A.reshape(5 * L, L)
    cntt = np.zeros((L, 512), np.float32)
    cntt[:, :5 * L] = A.transpose(2, 0, 1).reshape(L, 5 * L)
    cnt = jnp.asarray(cnt, BF)
    cntt = jnp.asarray(cntt, BF)
    whole = lambda *s: pl.BlockSpec(s, lambda i: (0,) * len(s), pipeline_mode=pl.Buffered(1))
    piece = lambda *s: pl.BlockSpec(s, lambda i: (i,) + (0,) * (len(s) - 1))
    return pl.pallas_call(
        functools.partial(middle_kernel, W, L, D, FF, steps),
        grid=(steps,),
        out_shape=(
            jax.ShapeDtypeStruct((n, L, D), BF),
            jax.ShapeDtypeStruct((n, L, D), F32),
            jax.ShapeDtypeStruct((n, L, D), BF),
            jax.ShapeDtypeStruct((D, D), F32),
            jax.ShapeDtypeStruct((FF, D), F32),
            jax.ShapeDtypeStruct((FF, D), F32),
            jax.ShapeDtypeStruct((168, D), F32),
        ),
        in_specs=[
            pl.BlockSpec(memory_space=pltpu.SMEM),
            piece(W, L, D), piece(W, L, D), piece(W, L, D),
            whole(2 * D, D), whole(FF, D), whole(FF, D), whole(1, D), whole(L, L), whole(5 * L, 256), whole(L, 512),
        ],
        out_specs=(
            piece(W, L, D), piece(W, L, D), piece(W, L, D), whole(D, D), whole(FF, D), whole(FF, D), whole(168, D),
        ),
        scratch_shapes=[
            pltpu.VMEM((256, D), BF),
            pltpu.VMEM((T, D), F32),
            pltpu.VMEM((W * 5 * L, D), F32),
            pltpu.VMEM((W * 5 * L, D), F32),
            pltpu.VMEM((T, D), F32),
            pltpu.VMEM((n * L, FF), BF),
            pltpu.VMEM((T, FF), BF),
            pltpu.VMEM((T, D), F32),
            pltpu.VMEM((n * L, D), BF),
            pltpu.VMEM((n * L, D), BF),
            pltpu.VMEM((n * L, FF), BF),
            pltpu.VMEM((T, D), BF),
            pltpu.VMEM((5 * L, D), F32),
            pltpu.VMEM((512, D), BF),
            pltpu.VMEM((20, 8, 128), F32),
            pltpu.VMEM((8, D), F32),
        ],
        compiler_params=pltpu.CompilerParams(vmem_limit_bytes=60 * 1024 * 1024),
        name="middle",
    )(mix, acts, sig, og, wqo, wup, wdn, bias, inv.T, cnt, cntt)


def sign_lanes(rows, left, right):
    lane = lax.broadcasted_iota(jnp.int32, (rows, 128), 1)
    return jnp.where(lane < 64, left, right).astype(F32)


def interleave(real, imag, v):
    re, im = real[:, v * 128:(v + 1) * 128], imag[:, v * 128:(v + 1) * 128]
    low = lax.broadcasted_iota(jnp.int32, re.shape, 1) < 64
    return jnp.where(low, re, pltpu.roll(im, 64, 1)), jnp.where(low, pltpu.roll(re, 64, 1), im)


def gather_rows(tiles, w, slots, n):
    reals, imags = [], []
    for v in range(4):
        first = tiles[2 * v, pl.ds(w, slots, stride=n), :]
        second = tiles[2 * v + 1, pl.ds(w, slots, stride=n), :]
        low = lax.broadcasted_iota(jnp.int32, first.shape, 1) < 64
        reals.append(jnp.where(low, first, pltpu.roll(second, 64, 1)).astype(BF))
        imags.append(jnp.where(low, pltpu.roll(first, 64, 1), second).astype(BF))
    return jnp.concatenate([jnp.concatenate(reals, 1), jnp.concatenate(imags, 1)], 0)


def spread_rows(tiles, w, slots, n, spectrum):
    for v in range(4):
        one, two = interleave(spectrum[:slots], spectrum[slots:], v)
        tiles[2 * v, pl.ds(w, slots, stride=n), :] = one
        tiles[2 * v + 1, pl.ds(w, slots, stride=n), :] = two


def swap_halves(x):
    return pltpu.roll(x, 64, 1)


def head_weights(weights, h, pieces, mode, rows):
    return jnp.concatenate([weights[h * pieces + q, mode, rows, :] for q in range(pieces)], 0)


MESH = pl.DeviceIdType.MESH


def move(sizes, at, axis, d):
    return {**at, axis: lax.rem(at[axis] + d, sizes[axis])}


def greet():
    ndp, nmode = lax.axis_size("dp"), lax.axis_size("mode")
    dp, mode = lax.axis_index("dp"), lax.axis_index("mode")
    barrier = pltpu.get_barrier_semaphore()
    for d in range(1, nmode):
        pl.semaphore_signal(barrier, 1, device_id={"dp": dp, "mode": lax.rem(mode + d, nmode)}, device_id_type=MESH)
    for d in range(1, ndp):
        pl.semaphore_signal(barrier, 1, device_id={"dp": lax.rem(dp + d, ndp), "mode": mode}, device_id_type=MESH)
    pl.semaphore_wait(barrier, ndp + nmode - 2)


def staggered(count, *stages):
    k = len(stages)
    if count < k:
        for stage in stages:
            for t in range(count):
                stage(t)
        return
    for t in range(k - 1):
        for s in range(t + 1):
            stages[s](t - s)

    def body(t, _):
        for s in range(k):
            stages[s](t - s)
        return 0
    lax.fori_loop(k - 1, count, body, 0)
    for t in range(count, count + k - 1):
        for s in range(t - count + 1, k):
            stages[s](t - s)


def roles():
    ndp, nmode = lax.axis_size("dp"), lax.axis_size("mode")
    half = nmode // 2
    dp, mode = lax.axis_index("dp"), lax.axis_index("mode")
    b, y, c = lax.rem(dp, half), mode // 2, lax.rem(mode, 2)
    here = {"a": dp // half, "u": jnp.where(c == 0, b, y), "v": jnp.where(c == 0, y, b), "c": c}
    return {"a": ndp // half, "u": half, "v": half, "c": 2}, here


def place_of(sizes, at):
    b = jnp.where(at["c"] == 0, at["u"], at["v"])
    y = jnp.where(at["c"] == 0, at["v"], at["u"])
    return at["a"] * sizes["u"] + b, y * 2 + at["c"]


def device_of(sizes, at):
    dp, mode = place_of(sizes, at)
    return {"dp": dp, "mode": mode}


def partner_of(at):
    return {"a": at["a"], "u": at["v"], "v": at["u"], "c": 1 - at["c"]}


def reducer(sizes, here, own, from_c, from_v, from_u, from_a, out, send, recv_c, recv_v, recv_u, recv_a):
    na, nu, nv = sizes["a"], sizes["u"], sizes["v"]
    rows = from_c.shape[1]
    step = next(s for s in (96, 32, rows) if rows % s == 0)

    def owner(t, e, d):
        return move(sizes, move(sizes, move(sizes, here, "a", t + 1), "u", e), "v", d)

    def spot(at):
        dp, mode = place_of(sizes, at)
        return dp * sizes["v"] + mode // 2

    def to_partner(at):
        n = spot(at)
        return pltpu.make_async_remote_copy(
            src_ref=own(at), dst_ref=from_c.at[n], send_sem=send.at[0], recv_sem=recv_c.at[n],
            device_id=device_of(sizes, partner_of(here)), device_id_type=MESH)

    def chunks(at, terms, store):
        mine = own(at)

        def chunk(i, _):
            part = pl.ds(pl.multiple_of(i * step, step), step) if step != rows else slice(None)
            total = mine[part, :].astype(F32)
            for ref, k in terms:
                total = total + ref[k, part, :].astype(F32)
            store(mine, part, total)
            return 0
        lax.fori_loop(0, rows // step, chunk, 0)

    def keep(mine, part, total):
        mine[part, :] = total.astype(BF)

    def finish(mine, part, total):
        out[part, :] = total

    def slot_v(t, e, d):
        return (t * nu + e) * (nv - 1) + d - 1

    def copy(at, buffer, s, stage, sems, to):
        return pltpu.make_async_remote_copy(
            src_ref=own(at), dst_ref=buffer.at[s], send_sem=send.at[stage], recv_sem=sems.at[s],
            device_id=device_of(sizes, to), device_id_type=MESH)

    def copy_v(t, e, d):
        s = slot_v(t, e, d)
        return copy(owner(t, e, d), from_v, s, 1, recv_v, move(sizes, here, "v", d))

    def copy_u(t, e):
        return copy(owner(t, e, 0), from_u, t * (nu - 1) + e - 1, 2, recv_u, move(sizes, here, "u", e))

    def copy_a(t):
        return copy(owner(t, 0, 0), from_a, t, 3, recv_a, owner(t, 0, 0))

    def heard(at):
        n = spot(at)
        pltpu.make_async_remote_copy(
            src_ref=own(at), dst_ref=from_c.at[n], send_sem=send.at[0], recv_sem=recv_c.at[n],
            device_id=device_of(sizes, partner_of(here)), device_id_type=MESH).wait_recv()
        return [(from_c, n)]

    def first(t):
        for d in range(1, nv):
            for e in range(nu):
                at = owner(t, e, d)
                chunks(at, heard(at), keep)
                copy_v(t, e, d).start()

    def after_v(t, e):
        terms = heard(owner(t, e, 0))
        for d in range(1, nv):
            copy_v(t, e, d).wait_recv()
            terms.append((from_v, slot_v(t, e, d)))
        return terms

    def second(t):
        for e in range(1, nu):
            chunks(owner(t, e, 0), after_v(t, e), keep)
            copy_u(t, e).start()

    def after_u(t):
        terms = after_v(t, 0)
        for e in range(1, nu):
            copy_u(t, e).wait_recv()
            terms.append((from_u, t * (nu - 1) + e - 1))
        return terms

    def third(t):
        chunks(owner(t, 0, 0), after_u(t), keep)
        copy_a(t).start()

    def last():
        terms = after_u(na - 1)
        for t in range(na - 1):
            copy_a(t).wait_recv()
            terms.append((from_a, t))
        chunks(here, terms, finish)

    def drain():
        for stage, count in ((0, from_c.shape[0]), (1, na * nu * (nv - 1)), (2, na * (nu - 1)), (3, na - 1)):
            ref = from_c.at[pl.ds(0, count)]
            pltpu.make_async_copy(ref, ref, send.at[stage]).wait()

    return to_partner, first, second, third, last, drain


def each(start, stop, *steps):
    def body(t, _):
        for s in steps:
            s(t)
        return 0
    lax.fori_loop(start, stop, body, 0)


def tail_kernel(n, L, D, slots, blocks, owner, gmix_h, z_h, acts_h, gsum_h, weights_h, gout_h, gup_h, gdn_h,
                obs_ref, wq_ref, basist_ref, eye_ref, sums_ref,
                dense_out, mixer_out, small_out, gin_h,
                gmix, z, acts, gsum, mix, src, tiles, glow, gbias, tmp, con,
                fc0, fc1, fv0, fv1, fu0, fu1, fa0, fa1, small_one, small_two,
                loads, send, recv_c, recv_v, recv_u, recv_a, small_send, small_recv):
    sizes, here = roles()
    ndp, nmode = lax.axis_size("dp"), lax.axis_size("mode")
    dp, mode = lax.axis_index("dp"), lax.axis_index("mode")
    na = sizes["a"]
    per = slots // nmode
    heads = 8
    pieces = ndp // heads
    depth = 64 // pieces
    rows = con.shape[1]
    size = con.shape[0] * rows // blocks

    def load(i, a, b):
        return pltpu.make_async_copy(a, b, loads.at[i])
    firsts = [load(0, gmix_h, gmix), load(1, z_h, z), load(2, weights_h, mix)]
    later = [load(3, acts_h, acts), load(4, gsum_h, gsum)]
    grads = []
    start = D
    for i, ref in enumerate((gout_h, gup_h, gdn_h)):
        for c in range(D // 128):
            grads.append(load(5 + i * 4 + c, ref.at[:, pl.ds(c * 128, 128)], src.at[c, pl.ds(start, ref.shape[0]), :]))
        start += ref.shape[0]
    for c in firsts + later + grads:
        c.start()
    greet()

    send_m, first_m, second_m, third_m, last_m, drain_m = reducer(
        sizes, here, lambda at: mix.at[place_of(sizes, at)], fc1, fv1, fu1, fa1, mixer_out,
        send.at[1], recv_c.at[1], recv_v.at[1], recv_u.at[1], recv_a.at[1])

    def con_at(at):
        p, m = place_of(sizes, at)
        return con.at[p * nmode + m]
    send_d, first_d, second_d, third_d, last_d, drain_d = reducer(
        sizes, here, con_at, fc0, fv0, fu0, fa0, dense_out,
        send.at[0], recv_c.at[0], recv_v.at[0], recv_u.at[0], recv_a.at[0])

    firsts[0].wait()

    def spectra(w):
        part = pl.ds(pl.multiple_of(w * L, 32), L)
        spread_rows(tiles, w, slots, n, gmix[part, :].astype(F32))
    each(0, n, spectra)
    firsts[1].wait()
    firsts[2].wait()

    def mix_mode(m):
        def slot(jl, _):
            at = pl.ds(pl.multiple_of((m * per + jl) * n, n), n)
            at2 = pl.ds(pl.multiple_of((m * per + jl) * 2 * n, 2 * n), 2 * n)
            part = pl.ds(pl.multiple_of(jl * depth, depth), depth)
            for h in range(heads):
                y = tiles[h, at, :]
                both = jnp.concatenate([y, swap_halves(y) * sign_lanes(n, 1.0, -1.0)], 0).astype(BF)
                x = dot(both, head_weights(mix, h, pieces, m, part), NT)
                tiles[h, at, :] = jnp.concatenate([x[:n], x[n:]], 1)
                g = dot(z[h, at2, :], both, TN).astype(BF)
                for q in range(pieces):
                    mix[h * pieces + q, m, part, :] = g[q * depth:(q + 1) * depth]
            return 0
        lax.fori_loop(0, per, slot, 0, unroll=2)

    mine_y = mode // 2

    def mode_at(i, core):
        return lax.rem(mine_y + 1 + i, nmode // 2) * 2 + core

    def other_modes(i):
        m = mode_at(i, 1 - here["c"])
        mix_mode(m)

        def hand(p):
            half = sizes["u"]
            b, y = lax.rem(p, half), m // 2
            core = 1 - here["c"]
            send_m({"a": p // half, "u": jnp.where(core == 0, b, y), "v": jnp.where(core == 0, y, b), "c": core}).start()
        each(0, ndp, hand)
    each(0, nmode // 2, other_modes)
    each(0, nmode // 2, lambda i: mix_mode(mode_at(i, here["c"])))
    each(0, na, first_m)

    gbias[...] = jnp.zeros_like(gbias)

    def query(w):
        part = pl.ds(pl.multiple_of(w * L, 32), L)
        g = dot(basist_ref[...], gather_rows(tiles, w, slots, n))
        glow[part, :] = g.astype(BF)
        gbias[...] += functools.reduce(lambda p, q: p + q, [g[i * 8:(i + 1) * 8] for i in range(L // 8)])
    each(0, n, query)

    for k, sums in ((0, gbias[...]), (4, sums_ref[0:8, :])):
        total = jnp.sum(sums, axis=0, keepdims=True)
        for c in range(D // 128):
            small_one[mode, k + c:k + c + 1, :] = total[:, c * 128:(c + 1) * 128]
    for k in range(20):
        small_one[mode, 8 + k:9 + k, :] = jnp.sum(sums_ref[8 + 8 * k:16 + 8 * k, 0:128], axis=0, keepdims=True)
    small_one[mode, 28:32, :] = jnp.zeros((4, 128), F32)

    def small_copy(buffer, axis, index, count, d, base):
        return pltpu.make_async_remote_copy(
            src_ref=buffer.at[index], dst_ref=buffer.at[index], send_sem=small_send.at[base + d - 1], recv_sem=small_recv.at[base + d - 1],
            device_id={**{"dp": dp, "mode": mode}, axis: lax.rem(index + d, count)}, device_id_type=MESH)
    ones = [small_copy(small_one, "mode", mode, nmode, d, 0) for d in range(1, nmode)]
    twos = [small_copy(small_two, "dp", dp, ndp, d, nmode - 1) for d in range(1, ndp)]
    for c in ones:
        c.start()

    for c in later:
        c.wait()
    g = dot(acts[...], glow[...], TN)
    for c in range(D // 128):
        src[c, 0:D, :] = g[:, c * 128:(c + 1) * 128]
    each(0, na // 2, second_m)
    for c in grads:
        c.wait()

    per_shard = rows // size
    join = 4 if per_shard % 4 == 0 else 1
    units = per_shard // join

    def pick(s):
        for k in range(units):
            for c in range(D // 128):
                for i in range(join):
                    row = owner[(s * units + k) * join + i] * size
                    tmp[c, i * size:(i + 1) * size, :] = src[c, pl.ds(row, size), :]
                part = slice(k * join * size, (k + 1) * join * size)
                con[s, part, c * 128:(c + 1) * 128] = tmp[c, 0:join * size, :].astype(BF)
    shards = con.shape[0]
    each(0, shards // 2, pick)
    each(na // 2, na, second_m)
    each(0, na // 2, third_m)
    each(shards // 2, shards, pick)

    def hand_line(t):
        other = partner_of(here)
        for d in list(range(1, sizes["v"])) + [0]:
            for e in range(sizes["u"]):
                send_d(move(sizes, move(sizes, move(sizes, other, "a", t + 1), "u", e), "v", d)).start()
    each(0, na, hand_line)
    each(na // 2, na - 1, third_m)

    def input_grad(w):
        part = pl.ds(pl.multiple_of(w * L, 32), L)
        row = obs_ref[pl.ds(w, 1), :].astype(F32)
        mask = dot((eye_ref[...] * row).astype(BF), jnp.ones((L, 128), BF))
        g = gsum[part, :] + dot(glow[part, :], wq_ref[...], NT)
        for c in range(D // 128):
            gsum[part, c * 128:(c + 1) * 128] = g[:, c * 128:(c + 1) * 128] * mask
    for c in ones:
        c.wait()
    small_two[dp] = functools.reduce(lambda p, q: p + q, [small_one[i] for i in range(nmode)])
    for c in twos:
        c.start()
    each(0, na, first_d)
    each(0, n, input_grad)
    result = load(17, gsum, gin_h)
    result.start()
    each(0, 1, second_d)
    each(1, na - 1, second_d, lambda t: third_d(t - 1))
    last_m()
    second_d(na - 1)
    third_d(na - 2)
    last_d()
    for c in twos:
        c.wait()
    small_out[...] = functools.reduce(lambda p, q: p + q, [small_two[i] for i in range(ndp)])
    drain_m()
    drain_d()
    result.wait()


def tail(gmix, z, acts, gsum, observed, wqo, basist, weights, gout, gup, gdn, sums, owner_list, shard_rows):
    n, L = observed.shape
    D = acts.shape[1]
    slots = basist.shape[1] // 2
    ndp, nmode, mixer_rows = weights.shape[:3]
    nd = ndp * nmode
    total = nd * shard_rows
    half = nmode // 2
    na = ndp // half
    group = nd // 2
    anywhere = pl.BlockSpec(memory_space=pl.ANY)
    vmem = pl.BlockSpec(memory_space=pltpu.VMEM)
    shapes = ((shard_rows, D), (mixer_rows, 128))
    counts = (group, na * half * (half - 1), na * (half - 1), na - 1)
    sem = lambda *s: pltpu.SemaphoreType.DMA(s)
    return pl.pallas_call(
        functools.partial(tail_kernel, n, L, D, slots, owner_list.shape[0]),
        out_shape=(
            jax.ShapeDtypeStruct(shapes[0], F32), jax.ShapeDtypeStruct(shapes[1], F32), jax.ShapeDtypeStruct((32, 128), F32),
            jax.ShapeDtypeStruct((n * L, D), F32),
        ),
        in_specs=[pl.BlockSpec(memory_space=pltpu.SMEM)] + [anywhere] * 8 + [
            vmem, pl.BlockSpec(memory_space=pltpu.VMEM), vmem, vmem, vmem],
        out_specs=(vmem, vmem, vmem, anywhere),
        scratch_shapes=[
            pltpu.VMEM((n * L, D), BF),
            pltpu.VMEM(z.shape, BF),
            pltpu.VMEM((n * L, D), BF),
            pltpu.VMEM((n * L, D), F32),
            pltpu.VMEM(weights.shape, BF),
            pltpu.VMEM((D // 128, total + 8, 128), F32),
            pltpu.VMEM((8, slots * n, 128), F32),
            pltpu.VMEM((n * L, D), BF),
            pltpu.VMEM((8, D), F32),
            pltpu.VMEM((D // 128, 80, 128), F32),
            pltpu.VMEM((nd, shard_rows, D), BF),
        ] + [pltpu.VMEM((count,) + s, BF) for count in counts for s in shapes] + [
            pltpu.VMEM((nmode, 32, 128), F32), pltpu.VMEM((ndp, 32, 128), F32),
            sem(18), sem(2, 4), sem(2, counts[0]), sem(2, counts[1]), sem(2, counts[2]), sem(2, counts[3]),
            sem(ndp + nmode - 2), sem(ndp + nmode - 2),
        ],
        compiler_params=pltpu.CompilerParams(collective_id=1, has_side_effects=True, vmem_limit_bytes=62 * 1024 * 1024),
        name="tail",
    )(owner_list, gmix, z, acts, gsum, weights, gout, gup, gdn, observed, wqo[:D], basist, jnp.eye(L, dtype=F32), sums)


def gatherer(sizes, here, slot_of, whole_of, send, send_a, recv):
    na, nu, nv = sizes["a"], sizes["u"], sizes["v"]

    def spot(at):
        dp, mode = place_of(sizes, at)
        return dp * sizes["v"] * 2 + mode

    def copy(at, to, sem):
        ref = slot_of(at)
        return pltpu.make_async_remote_copy(
            src_ref=ref, dst_ref=ref, send_sem=sem, recv_sem=recv.at[spot(at)],
            device_id=device_of(sizes, to), device_id_type=MESH)

    def onward(at, axes):
        for axis, stage in axes:
            for d in range(1, sizes[axis]):
                copy(at, move(sizes, here, axis, d), send.at[stage]).start()
        copy(at, partner_of(here), send.at[2]).start()

    def hop(k, side):
        first, to = here["a"] - side * k, here["a"] + side
        there = (first >= 0) & (first < na) & (to >= 0) & (to < na)
        way = 0 if side == 1 else 1
        inside = lambda x: jnp.clip(x, 0, na - 1)
        return there, lambda: copy({**here, "a": inside(first)}, {**here, "a": inside(to)}, send_a.at[way, k])

    def hops(k, side):
        there, make = hop(k, side)
        pl.when(there)(lambda: make().start())

    def arrived(at):
        copy(at, here, send.at[0]).wait_recv()
        return at

    def lines(k, act):
        for side in ((1, -1) if k else (1,)):
            to = here["a"] - side * k
            pl.when((to >= 0) & (to < na))(lambda side=side, to=to: act({**here, "a": to}, side))

    def start():
        for side in (1, -1):
            hops(0, side)
        onward(here, (("u", 0), ("v", 1)))

    def line(k, then=lambda at: None):
        def act(at, side):
            arrived(at)
            hops(k, side)
            onward(at, (("u", 0), ("v", 1)))
            then(at)
        lines(k, act)

    def second(k, then=lambda at: None):
        def act(at, side):
            for d in range(1, nu):
                to = arrived(move(sizes, at, "u", d))
                onward(to, (("v", 1),))
                then(to)
        lines(k, act)

    def third(k, then=lambda at: None):
        def act(at, side):
            for e in range(nu):
                for d in range(1, nv):
                    to = arrived(move(sizes, move(sizes, at, "u", e), "v", d))
                    onward(to, ())
                    then(to)
        lines(k, act)

    def partner(t, then=lambda at: None):
        other = partner_of(here)
        for e in range(nu):
            for d in range(nv):
                then(arrived(move(sizes, move(sizes, move(sizes, other, "a", t), "u", e), "v", d)))

    def drain():
        for stage, count in ((0, na * (nu - 1)), (1, na * nu * (nv - 1)), (2, na * nu * nv)):
            ref = whole_of(count)
            pltpu.make_async_copy(ref, ref, send.at[stage]).wait()
        for k in range(na):
            for side in (1, -1):
                there, make = hop(k, side)
                pl.when(there)(lambda make=make: make().wait_send())

    return start, line, second, third, partner, drain


def head_kernel(n, L, D, slots, blocks, restore, in_h, dense_ref, mixer_ref, obs_ref, bias_ref, basis_ref, inv_ref, eye_ref,
                acts_h, z_h, sig_h, wqo_h, wup_h, wdn_h, weights_h,
                inputs, acts, query, tiles, z, sig, buf, src, table, mix, tmp,
                loads, send, send_a, recv):
    sizes, here = roles()
    ndp, nmode = lax.axis_size("dp"), lax.axis_size("mode")
    dp, mode = lax.axis_index("dp"), lax.axis_index("mode")
    na = sizes["a"]
    per = slots // nmode
    heads = 8
    pieces = ndp // heads
    depth = 64 // pieces
    rows = buf.shape[1]
    total = buf.shape[0] * rows
    size = total // blocks
    join = 4
    units = blocks // join

    def load(i, a, b):
        return pltpu.make_async_copy(a, b, loads.at[i])
    load_in = load(0, in_h, inputs)
    load_in.start()
    buf[dp * nmode + mode] = dense_ref[...].astype(BF)
    mix[dp, mode] = mixer_ref[...].astype(BF)
    greet()

    def buf_at(at):
        p, m = place_of(sizes, at)
        return buf.at[p * nmode + m]

    start_d, line_d, second_d, third_d, partner_d, drain_d = gatherer(
        sizes, here, buf_at, lambda count: buf.at[pl.ds(0, count)], send.at[0], send_a.at[0], recv.at[0])
    mix_at = lambda at: mix.at[place_of(sizes, at)]

    def mix_many(count):
        if count % nmode == 0:
            return mix.at[pl.ds(0, count // nmode)]
        return mix.at[pl.ds(0, count), 0] if count <= ndp else mix.at[pl.ds(0, count // 2), pl.ds(0, 2)]
    start_m, line_m, second_m, third_m, partner_m, drain_m = gatherer(
        sizes, here, mix_at, mix_many, send.at[1], send_a.at[1], recv.at[1])
    start_d()

    def widen(at):
        p, m = place_of(sizes, at)
        k = p * nmode + m
        for c in range(D // 128):
            src[c, pl.ds(k * rows, rows), :] = buf[k, :, c * 128:(c + 1) * 128].astype(F32)
    widen(here)
    load_in.wait()

    def mask(w):
        row = obs_ref[pl.ds(w, 1), :].astype(F32)
        part = pl.ds(pl.multiple_of(w * L, 32), L)
        acts[part, :] = dot((eye_ref[...] * row).astype(BF), inputs[part, :]).astype(BF)
    each(0, n, mask)
    outs = [load(1, acts, acts_h)]
    outs[0].start()
    for k in range(na + 2):
        if k < na - 1:
            line_d(k + 1, widen)
        if k < na:
            second_d(k, widen)
        if 1 <= k <= na:
            third_d(k - 1, widen)
        if k == 0:
            start_m()
        if 1 <= k < na:
            line_m(k)
        if 1 <= k <= na:
            second_m(k - 1)
        if 2 <= k <= na:
            third_m(k - 2)
    each(0, na, lambda t: partner_d(t, widen))

    def pick(p):
        for c in range(D // 128):
            for i in range(join):
                tmp[c, i * size:(i + 1) * size, :] = src[c, pl.ds(restore[p * join + i] * size, size), :]
            part = pl.ds(pl.multiple_of(p * join * size, 16), join * size)
            table[part, c * 128:(c + 1) * 128] = tmp[c].astype(BF)
    early = -(-D // (join * size))
    each(0, early, pick)
    T = 384

    def project(i):
        part = pl.ds(pl.multiple_of(i * T, T), T)
        query[part, :] = (dot(acts[part, :], table[0:D, :]) + bias_ref[...]).astype(BF)

    def spectra(w):
        part = pl.ds(pl.multiple_of(w * L, 32), L)
        spread_rows(tiles, w, slots, n, dot(basis_ref[...], query[part, :]))

    work = [lambda i=i: project(i) for i in range(n * L // T)]
    work += [lambda i=i: each(i * n // 4, (i + 1) * n // 4, spectra) for i in range(4)]
    cuts = [early + (units - early) * i // 4 for i in range(5)]
    work += [lambda i=i: each(cuts[i], cuts[i + 1], pick) for i in range(4)]
    for i, w in enumerate(work):
        w()
        if i == 1:
            third_m(na - 1)
    at = 0
    for i, ref in enumerate((wqo_h, wup_h, wdn_h)):
        outs.append(load(2 + i, table.at[pl.ds(at, ref.shape[0])], ref))
        outs[-1].start()
        at += ref.shape[0]
    each(0, na, partner_m)
    outs.append(load(5, mix, weights_h))
    outs[-1].start()

    def slot(j, _):
        m, jl = j // per, lax.rem(j, per)
        at = pl.ds(pl.multiple_of(j * n, n), n)
        part = pl.ds(pl.multiple_of(jl * depth, depth), depth)
        for h in range(heads):
            x = tiles[h, at, :]
            both = jnp.concatenate([x, swap_halves(x)], 0)[:, :64].astype(BF)
            z[h, pl.ds(pl.multiple_of(j * 2 * n, 2 * n), 2 * n), :] = both
            y = dot(both, head_weights(mix, h, pieces, m, part))
            tiles[h, at, :] = y[:n] + swap_halves(y[n:]) * sign_lanes(n, -1.0, 1.0)
        return 0
    lax.fori_loop(0, slots, slot, 0, unroll=4)
    outs.append(load(6, z, z_h))
    outs[-1].start()

    def signal(w):
        part = pl.ds(pl.multiple_of(w * L, 32), L)
        sig[part, :] = dot(inv_ref[...], gather_rows(tiles, w, slots, n)).astype(BF)
    each(0, n, signal)
    outs.append(load(7, sig, sig_h))
    outs[-1].start()
    drain_d()
    drain_m()
    for o in outs:
        o.wait()


def head(inputs, observed, dense, mixer, restore, bias, basis, inv, ff):
    n, L, D = inputs.shape
    slots = basis.shape[0] // 2
    ndp, nmode = lax.axis_size("dp"), lax.axis_size("mode")
    nd = ndp * nmode
    rows, mixer_rows = dense.shape[0], mixer.shape[0]
    anywhere = pl.BlockSpec(memory_space=pl.ANY)
    vmem = pl.BlockSpec(memory_space=pltpu.VMEM)
    sem = lambda *s: pltpu.SemaphoreType.DMA(s)
    tokens = n * L
    return pl.pallas_call(
        functools.partial(head_kernel, n, L, D, slots, restore.shape[0]),
        out_shape=(
            jax.ShapeDtypeStruct((tokens, D), BF),
            jax.ShapeDtypeStruct((8, 2 * slots * n, 64), BF),
            jax.ShapeDtypeStruct((tokens, D), BF),
            jax.ShapeDtypeStruct((2 * D, D), BF),
            jax.ShapeDtypeStruct((ff, D), BF),
            jax.ShapeDtypeStruct((ff, D), BF),
            jax.ShapeDtypeStruct((ndp, nmode, mixer_rows, 128), BF),
        ),
        in_specs=[pl.BlockSpec(memory_space=pltpu.SMEM), anywhere] + [vmem] * 7,
        out_specs=(anywhere,) * 7,
        scratch_shapes=[
            pltpu.VMEM((tokens, D), BF),
            pltpu.VMEM((tokens, D), BF),
            pltpu.VMEM((tokens, D), BF),
            pltpu.VMEM((8, slots * n, 128), F32),
            pltpu.VMEM((8, 2 * slots * n, 64), BF),
            pltpu.VMEM((tokens, D), BF),
            pltpu.VMEM((nd, rows, D), BF),
            pltpu.VMEM((D // 128, nd * rows + 8, 128), F32),
            pltpu.VMEM((nd * rows, D), BF),
            pltpu.VMEM((ndp, nmode, mixer_rows, 128), BF),
            pltpu.VMEM((D // 128, 4 * (nd * rows // restore.shape[0]), 128), F32),
            sem(8), sem(2, 3), sem(2, 2, ndp // (nmode // 2)), sem(2, nd),
        ],
        compiler_params=pltpu.CompilerParams(collective_id=0, has_side_effects=True, vmem_limit_bytes=62 * 1024 * 1024),
        name="head",
    )(restore, inputs.reshape(tokens, D), dense, mixer, observed, bias, basis, inv, jnp.eye(L, dtype=F32))


def fourier_tables(mode_index, length):
    positions = jnp.arange(length, dtype=jnp.int32)
    phases = mode_index[:, None] * positions[None, :] % length
    angles = phases.astype(jnp.float32) * (2.0 * jnp.pi / length)
    forward = jnp.stack([jnp.cos(angles), -jnp.sin(angles)])
    slot_ids = jnp.arange(mode_index.shape[0], dtype=jnp.int32)
    back_phase = slot_ids[:, None] * positions[None, :] % length
    back_angle = back_phase.astype(jnp.float32) * (2.0 * jnp.pi / length)
    coefs = jnp.where(slot_ids == 0, 1.0, 2.0).astype(jnp.float32) / length
    inverse = jnp.stack(
        [jnp.cos(back_angle) * coefs[:, None], -jnp.sin(back_angle) * coefs[:, None]]
    )
    return (forward, jnp.transpose(inverse, (2, 0, 1)))


def adam_update(weight, gradient, moment, second, step_rate):
    moment_new = BETA_ONE * moment + (1.0 - BETA_ONE) * gradient
    second_new = BETA_TWO * second + (1.0 - BETA_TWO) * gradient * gradient
    scaled_m = moment_new / (1.0 - BETA_ONE**STEP)
    scaled_v = second_new / (1.0 - BETA_TWO**STEP)
    weight_new = weight - step_rate * (
        scaled_m / (jnp.sqrt(scaled_v) + ADAM_EPS) + DECAY_RATE * weight
    )
    return (moment_new, second_new, weight_new)


def shards(
    inputs,
    observed,
    out_grad,
    mode_index,
    owner_list,
    dense_master,
    dense_first,
    dense_second,
    mixer_master,
    mixer_first,
    mixer_second,
    small_master,
    small_first,
    small_second,
):
    ndp, nmode = lax.axis_size("dp"), lax.axis_size("mode")
    length, width = inputs.shape[1:]
    slots = mode_index.shape[0]
    hidden = (dense_master.shape[0] * ndp * nmode - 2 * width) // 2
    forward, inverse = fourier_tables(mode_index, length)
    basis = forward.astype(BF).reshape(2 * slots, length)
    inv = inverse.astype(BF).reshape(length, 2 * slots)
    places = jnp.arange(owner_list.shape[0], dtype=jnp.int32)
    restore = jnp.sum(jnp.where(owner_list[None, :] == places[:, None], places[None, :], 0), axis=1)
    acts, spectra, sig, wqo, wup, wdn, weights = head(
        inputs, observed, dense_master, mixer_master.reshape(-1, mixer_master.shape[2]), restore, small_master[None, :width],
        basis, inv, hidden,
    )
    output, grad_summed, grad_mixed, g_out, g_up, g_down, sums = middle(
        small_master[2 * width :], acts.reshape(inputs.shape), sig.reshape(inputs.shape), out_grad, wqo, wup, wdn,
        small_master[None, width : 2 * width], inv,
    )
    dense_mine, mixer_mine, small_all, input_grad = tail(
        grad_mixed.reshape(-1, width), spectra, acts, grad_summed.reshape(-1, width), observed, wqo, basis.T, weights,
        g_out, g_up, g_down, sums, owner_list, dense_master.shape[0],
    )
    small_total = jnp.concatenate([small_all[:8].reshape(-1), jnp.sum(small_all[8:28], axis=1)])
    dense_first_new, dense_second_new, dense_new = adam_update(
        dense_master, dense_mine, dense_first, dense_second, RATE_DENSE
    )
    mixer_first_new, mixer_second_new, mixer_new = adam_update(
        mixer_master, mixer_mine.reshape(mixer_master.shape), mixer_first, mixer_second, RATE_MIXER
    )
    small_first_new, small_second_new, small_new = adam_update(
        small_master, small_total, small_first, small_second, RATE_SMALL
    )
    return (
        output,
        input_grad.reshape(inputs.shape),
        dense_first_new,
        dense_second_new,
        dense_new,
        mixer_first_new,
        mixer_second_new,
        mixer_new,
        small_first_new,
        small_second_new,
        small_new,
        small_total[width : 2 * width],
    )


def solution(mesh):
    placed = (
        P(("dp", "mode"), None, None),
        P(("dp", "mode"), None),
        P(("dp", "mode"), None, None),
        P(),
        P(),
        P(("dp", "mode"), None),
        P(("dp", "mode"), None),
        P(("dp", "mode"), None),
        P("mode", "dp", None),
        P("mode", "dp", None),
        P("mode", "dp", None),
        P(),
        P(),
        P(),
    )
    return jax.shard_map(
        shards,
        mesh=mesh,
        in_specs=placed,
        out_specs=(
            P(("dp", "mode"), None, None),
            P(("dp", "mode"), None, None),
            P(("dp", "mode"), None),
            P(("dp", "mode"), None),
            P(("dp", "mode"), None),
            P("mode", "dp", None),
            P("mode", "dp", None),
            P("mode", "dp", None),
            P(),
            P(),
            P(),
            P(),
        ),
        check_vma=False,
    )
```

```python
import functools
import math

import jax
import jax.numpy as jnp
import numpy as np
from jax import lax
from jax.experimental import pallas as pl
from jax.experimental.pallas import tpu as pltpu
from jax.sharding import PartitionSpec as P

STEP = 10
BETA_ONE = 0.9
BETA_TWO = 0.95
ADAM_EPS = 1e-08
DECAY_RATE = 0.1
RATE_DENSE = 0.03
RATE_MIXER = 0.03
RATE_SMALL = 0.5

KERNEL_SIZES = (7, 12, 14, 24, 48)
ODD = (7, 3, 7, 3, 3)
LOG2E = 1.4426950408889634
BF = jnp.bfloat16
F32 = jnp.float32
NT = (((1,), (1,)), ((), ()))
NN = (((1,), (0,)), ((), ()))
TN = (((0,), (0,)), ((), ()))


def dot(a, b, dims=NN):
    return lax.dot_general(a, b, dims, preferred_element_type=F32)


def average_counts(length):
    tables = []
    t = np.arange(length)
    for size in KERNEL_SIZES:
        u = np.clip(t[:, None] - (size - 1) // 2 + np.arange(size)[None, :], 0, length - 1)
        tables.append((u[:, :, None] == t[None, None, :]).sum(1) * (ODD[len(tables)] / size))
    return np.stack(tables).astype(np.float32)


def gelu_parts(h):
    z = jnp.abs(h)
    e = jnp.exp2(h * h * (-0.5 * LOG2E))
    t = 1.0 / (1.0 + (0.3275911 * math.sqrt(0.5)) * z)
    poly = t * (0.5 * 0.254829592 + t * (-0.5 * 0.284496736 + t * (0.5 * 1.421413741 + t * (-0.5 * 1.453152027 + t * (0.5 * 1.061405429)))))
    tail = poly * e
    big = jnp.where(h < 0, tail, 1.0 - tail)
    return big, e * (1.0 / math.sqrt(2 * math.pi))


def middle_kernel(W, L, D, FF, steps,
                  mix_ref, acts_ref, sig_ref, og_ref, wq_ref, wup_ref, wdn_ref, bias_ref, invt_ref, cnt_ref, cntt_ref,
                  out_ref, gsum_ref, gmix_ref, gw_ref, gup_ref, gdn_ref, small_ref,
                  vs, base, avg1, c1, v1, active, dgelu, first, flow, gb, ghid, glow, avg2, stk, accs, accb, hs, wg, wsem):
    step = pl.program_id(0)
    T = W * L
    CH = 16
    CC = 256
    nc = D // CC
    nr = L // CH
    FT = 512

    @pl.when(step == 0)
    def _():
        vs[...] = jnp.zeros_like(vs)
        stk[...] = jnp.zeros_like(stk)
        accs[...] = jnp.zeros_like(accs)
        accb[...] = jnp.zeros_like(accb)
        gw_ref[...] = jnp.zeros_like(gw_ref)

    def fold(x):
        y = x[:, 0:128]
        for i in range(1, CC // 128):
            y = y + x[:, i * 128:(i + 1) * 128]
        return y[0:8] + y[8:16]

    def scaled_shares(v, base_at):
        p = [mix_ref[2 * D + base_at + k] for k in range(10)]
        logits = [((p[k] - p[4]) * LOG2E) * v + (p[5 + k] - p[9]) * LOG2E for k in range(4)]
        top = jnp.maximum(functools.reduce(jnp.maximum, logits), 0.0)
        es = [jnp.exp2(l - top) for l in logits] + [jnp.exp2(-top)]
        r = 1.0 / functools.reduce(lambda a, b: a + b, es)
        scale = {7: r * (1.0 / 7.0), 3: r * (1.0 / 3.0)}
        return [e * scale[o] for e, o in zip(es, ODD)]

    def backward(v, g, cs, avs, mean, base_at, store):
        means = {7: 7.0 * mean, 3: 3.0 * mean}
        total = None
        for k in range(5):
            cg = cs[k] * g
            store(k, cg)
            if k < 4:
                t = cg * (means[ODD[k]] - avs[k])
                term = (mix_ref[2 * D + base_at + k] - mix_ref[2 * D + base_at + 4]) * t
                total = term if total is None else total + term
                accs[base_at + k] += fold(t * v)
                accs[base_at + 5 + k] += fold(t)
        return total

    sig = sig_ref[...].reshape(T, D)
    base[...] = dot(sig, wq_ref[D:2 * D, :])

    def cut(w, source):
        for i in range(nr):
            for c in range(nc):
                cols = slice(c * CC, (c + 1) * CC)
                v = source(w, i, cols)
                hi = v.astype(BF)
                vs[w % 2, i * CH:(i + 1) * CH, cols] = hi
                vs[w % 2, L + i * CH:L + (i + 1) * CH, cols] = (v - hi.astype(F32)).astype(BF)

    def summed(w, i, cols):
        rows = slice(w * L + i * CH, w * L + (i + 1) * CH)
        v = base[rows, cols] + acts_ref[w, i * CH:(i + 1) * CH, cols].astype(F32) + bias_ref[:, D + cols.start:D + cols.stop]
        v1[rows, cols] = v
        return v

    def averages_one(w):
        cut(w, summed)
        avg1[w * 5 * L:(w + 1) * 5 * L, :] = dot(cnt_ref[...], vs[w % 2])

    def decompose_one(w):
        for i in range(nr):
            for c in range(nc):
                cols = slice(c * CC, (c + 1) * CC)
                rows = slice(w * L + i * CH, w * L + (i + 1) * CH)
                v = v1[rows, cols]
                cs = scaled_shares(v, 0)
                mean = None
                for k in range(5):
                    at = slice((w * 5 + k) * L + i * CH, (w * 5 + k) * L + (i + 1) * CH)
                    u = cs[k] * avg1[at, cols]
                    c1[at, cols] = cs[k]
                    mean = u if mean is None else mean + u
                f = v - mean
                first[rows, cols] = f
                flow[pl.ds(pl.multiple_of(step * T + w * L + i * CH, CH), CH), cols] = f.astype(BF)

    averages_one(0)
    for w in range(W):
        if w + 1 < W:
            averages_one(w + 1)
        decompose_one(w)

    here_t = pl.ds(pl.multiple_of(step * T, CH), T)
    base[...] = first[...]

    def up(n):
        return dot(flow[here_t, :], wup_ref[n * FT:(n + 1) * FT, :], NT)

    tiles = FF // FT
    hs[0] = up(0)
    for n in range(tiles + 1):
        if n + 1 < tiles:
            hs[(n + 1) % 2] = up(n + 1)
        if n < tiles:
            h = hs[n % 2]
            big, small = gelu_parts(h)
            active[here_t, n * FT:(n + 1) * FT] = (h * big).astype(BF)
            dgelu[:, n * FT:(n + 1) * FT] = (big + h * small).astype(BF)
        if n:
            base[...] += dot(active[here_t, (n - 1) * FT:n * FT], wdn_ref[(n - 1) * FT:n * FT, :])

    def branch(w, i, cols):
        return base[w * L + i * CH:w * L + (i + 1) * CH, cols]

    def averages_two(w):
        cut(w, branch)
        avg2[w % 2] = dot(cnt_ref[...], vs[w % 2])

    def keep_at(w, i, cols):
        def keep(k, cg):
            stk[w % 2, k * L + i * CH:k * L + (i + 1) * CH, cols] = cg.astype(BF)
        return keep

    def decompose_two(w):
        for i in range(nr):
            for c in range(nc):
                cols = slice(c * CC, (c + 1) * CC)
                rows = slice(w * L + i * CH, w * L + (i + 1) * CH)
                here = slice(i * CH, (i + 1) * CH)
                v = base[rows, cols]
                cs = scaled_shares(v, 10)
                avs = [avg2[w % 2, k * L + i * CH:k * L + (i + 1) * CH, cols] for k in range(5)]
                mean = functools.reduce(lambda a, b: a + b, [c_ * a_ for c_, a_ in zip(cs, avs)])
                out_ref[w, here, cols] = (v - mean).astype(BF)
                g = og_ref[w, here, cols].astype(F32)
                base[rows, cols] = g + backward(v, g, cs, avs, mean, 10, keep_at(w, i, cols))

    def back_two(w):
        rows = slice(w * L, (w + 1) * L)
        gs = base[rows, :] - dot(cntt_ref[...], stk[w % 2])
        base[rows, :] = gs
        gb[pl.ds(pl.multiple_of(step * T + w * L, 32), L), :] = gs.astype(BF)

    averages_two(0)
    for w in range(W):
        if w + 1 < W:
            averages_two(w + 1)
        decompose_two(w)
        if w:
            back_two(w - 1)
    back_two(W - 1)

    def down(n):
        return dot(gb[here_t, :], wdn_ref[n * FT:(n + 1) * FT, :], NT)

    hs[0] = down(0)
    for n in range(tiles + 1):
        if n + 1 < tiles:
            hs[(n + 1) % 2] = down(n + 1)
        if n < tiles:
            ghid[here_t, n * FT:(n + 1) * FT] = (hs[n % 2] * dgelu[:, n * FT:(n + 1) * FT].astype(F32)).astype(BF)
        if n:
            base[...] += dot(ghid[here_t, (n - 1) * FT:n * FT], wup_ref[(n - 1) * FT:n * FT, :])

    def decompose_three(w):
        for i in range(nr):
            for c in range(nc):
                cols = slice(c * CC, (c + 1) * CC)
                rows = slice(w * L + i * CH, w * L + (i + 1) * CH)
                v = v1[rows, cols]
                g = base[rows, cols]
                ats = [slice((w * 5 + k) * L + i * CH, (w * 5 + k) * L + (i + 1) * CH) for k in range(5)]
                cs = [c1[at, cols] for at in ats]
                avs = [avg1[at, cols] for at in ats]
                mean = v - first[rows, cols]
                extra = backward(v, g, cs, avs, mean, 0, keep_at(w, i, cols))
                base[rows, cols] = g + extra
                accb[:, cols] += extra[0:8] + extra[8:16]

    def back_three(w):
        rows = slice(w * L, (w + 1) * L)
        gs = base[rows, :] - dot(cntt_ref[...], stk[w % 2])
        gsum_ref[w] = gs
        glow[rows, :] = gs.astype(BF)

    for w in range(W):
        decompose_three(w)
        if w:
            back_three(w - 1)
    back_three(W - 1)

    back = dot(glow[...], wq_ref[D:2 * D, :], NT).astype(BF)
    for w in range(W):
        gmix_ref[w] = dot(invt_ref[...], back[w * L:(w + 1) * L, :]).astype(BF)
    gw_ref[...] += dot(sig, glow[...], TN)

    @pl.when(step == steps - 1)
    def _():
        small_ref[0:8, :] = accb[...]
        for at in (4, 9, 14, 19):
            accs[at] = -(accs[at - 4] + accs[at - 3] + accs[at - 2] + accs[at - 1])
        for k in range(20):
            small_ref[8 + 8 * k:16 + 8 * k, 0:128] = accs[k]
            small_ref[8 + 8 * k:16 + 8 * k, 128:512] = jnp.zeros((8, 384), F32)

        copies = {}
        for n in range(tiles):
            part = slice(n * FT, (n + 1) * FT)
            for i, (left, right, ref) in enumerate(((ghid, flow, gup_ref), (active, gb, gdn_ref))):
                k = (n % 2) * 2 + i
                if n >= 2:
                    copies[n - 2, i].wait()
                wg[k] = dot(left[:, part], right[...], TN)
                copies[n, i] = pltpu.make_async_copy(wg.at[k], ref.at[pl.ds(n * FT, FT)], wsem.at[k])
                copies[n, i].start()
        for n in range(max(tiles - 2, 0), tiles):
            for i in range(2):
                copies[n, i].wait()


def middle(mix, acts, sig, og, wqo, wup, wdn, bias, invt, W=4):
    n, L, D = acts.shape
    FF = wup.shape[0]
    steps = n // W
    T = W * L
    A = average_counts(L)
    cnt = np.zeros((5 * L, 256), np.float32)
    cnt[:, :L] = A.reshape(5 * L, L)
    cnt[:, L:2 * L] = A.reshape(5 * L, L)
    cntt = np.zeros((L, 512), np.float32)
    cntt[:, :5 * L] = A.transpose(2, 0, 1).reshape(L, 5 * L)
    cnt, cntt = (np.asarray(x, BF) for x in (cnt, cntt))
    whole = lambda *s: pl.BlockSpec(s, lambda i: (0,) * len(s), pipeline_mode=pl.Buffered(1))
    anywhere = pl.BlockSpec(memory_space=pl.ANY)
    piece = lambda *s: pl.BlockSpec(s, lambda i: (i,) + (0,) * (len(s) - 1))
    return pl.pallas_call(
        functools.partial(middle_kernel, W, L, D, FF, steps),
        grid=(steps,),
        out_shape=(
            jax.ShapeDtypeStruct((n, L, D), BF),
            jax.ShapeDtypeStruct((n, L, D), F32),
            jax.ShapeDtypeStruct((n, L, D), BF),
            jax.ShapeDtypeStruct((D, D), F32),
            jax.ShapeDtypeStruct((FF, D), F32),
            jax.ShapeDtypeStruct((FF, D), F32),
            jax.ShapeDtypeStruct((168, D), F32),
        ),
        in_specs=[
            pl.BlockSpec(memory_space=pltpu.SMEM),
            piece(W, L, D), piece(W, L, D), piece(W, L, D),
            whole(2 * D, D), whole(FF, D), whole(FF, D), whole(1, bias.shape[1]), whole(L, L), whole(5 * L, 256), whole(L, 512),
        ],
        out_specs=(
            piece(W, L, D), piece(W, L, D), piece(W, L, D), whole(D, D), anywhere, anywhere, whole(168, D),
        ),
        scratch_shapes=[
            pltpu.VMEM((2, 256, D), BF),
            pltpu.VMEM((T, D), F32),
            pltpu.VMEM((W * 5 * L, D), F32),
            pltpu.VMEM((W * 5 * L, D), F32),
            pltpu.VMEM((T, D), F32),
            pltpu.VMEM((n * L, FF), BF),
            pltpu.VMEM((T, FF), BF),
            pltpu.VMEM((T, D), F32),
            pltpu.VMEM((n * L, D), BF),
            pltpu.VMEM((n * L, D), BF),
            pltpu.VMEM((n * L, FF), BF),
            pltpu.VMEM((T, D), BF),
            pltpu.VMEM((2, 5 * L, D), F32),
            pltpu.VMEM((2, 512, D), BF),
            pltpu.VMEM((20, 8, 128), F32),
            pltpu.VMEM((8, D), F32),
            pltpu.VMEM((2, T, 512), F32),
            pltpu.VMEM((4, 512, D), F32),
            pltpu.SemaphoreType.DMA((4,)),
        ],
        compiler_params=pltpu.CompilerParams(vmem_limit_bytes=60 * 1024 * 1024),
        name="middle",
    )(mix, acts, sig, og, wqo, wup, wdn, bias, invt, cnt, cntt)


def sign_lanes(rows, left, right):
    lane = lax.broadcasted_iota(jnp.int32, (rows, 128), 1)
    return jnp.where(lane < 64, left, right).astype(F32)


def interleave(real, imag, v):
    re, im = real[:, v * 128:(v + 1) * 128], imag[:, v * 128:(v + 1) * 128]
    low = lax.broadcasted_iota(jnp.int32, re.shape, 1) < 64
    return jnp.where(low, re, pltpu.roll(im, 64, 1)), jnp.where(low, pltpu.roll(re, 64, 1), im)


def gather_rows(tiles, w, slots, n):
    reals, imags = [], []
    for v in range(4):
        first = tiles[2 * v, pl.ds(w, slots, stride=n), :]
        second = tiles[2 * v + 1, pl.ds(w, slots, stride=n), :]
        low = lax.broadcasted_iota(jnp.int32, first.shape, 1) < 64
        reals.append(jnp.where(low, first, pltpu.roll(second, 64, 1)).astype(BF))
        imags.append(jnp.where(low, pltpu.roll(first, 64, 1), second).astype(BF))
    return jnp.concatenate([jnp.concatenate(reals, 1), jnp.concatenate(imags, 1)], 0)


def spread_rows(tiles, w, slots, n, spectrum):
    for v in range(4):
        one, two = interleave(spectrum[:slots], spectrum[slots:], v)
        tiles[2 * v, pl.ds(w, slots, stride=n), :] = one
        tiles[2 * v + 1, pl.ds(w, slots, stride=n), :] = two


def swap_halves(x):
    return pltpu.roll(x, 64, 1)


def head_weights(weights, h, pieces, mode, rows):
    return jnp.concatenate([weights[h * pieces + q, mode, rows, :] for q in range(pieces)], 0)


MESH = pl.DeviceIdType.MESH


def move(sizes, at, axis, d):
    return {**at, axis: lax.rem(at[axis] + d, sizes[axis])}


def greet():
    ndp, nmode = lax.axis_size("dp"), lax.axis_size("mode")
    dp, mode = lax.axis_index("dp"), lax.axis_index("mode")
    barrier = pltpu.get_barrier_semaphore()
    for d in range(1, nmode):
        pl.semaphore_signal(barrier, 1, device_id={"dp": dp, "mode": lax.rem(mode + d, nmode)}, device_id_type=MESH)
    for d in range(1, ndp):
        pl.semaphore_signal(barrier, 1, device_id={"dp": lax.rem(dp + d, ndp), "mode": mode}, device_id_type=MESH)
    pl.semaphore_wait(barrier, ndp + nmode - 2)


def staggered(count, *stages):
    k = len(stages)
    if count < k:
        for stage in stages:
            for t in range(count):
                stage(t)
        return
    for t in range(k - 1):
        for s in range(t + 1):
            stages[s](t - s)

    def body(t, _):
        for s in range(k):
            stages[s](t - s)
        return 0
    lax.fori_loop(k - 1, count, body, 0)
    for t in range(count, count + k - 1):
        for s in range(t - count + 1, k):
            stages[s](t - s)


def roles():
    ndp, nmode = lax.axis_size("dp"), lax.axis_size("mode")
    half = nmode // 2
    dp, mode = lax.axis_index("dp"), lax.axis_index("mode")
    b, y, c = lax.rem(dp, half), mode // 2, lax.rem(mode, 2)
    here = {"a": dp // half, "u": jnp.where(c == 0, b, y), "v": jnp.where(c == 0, y, b), "c": c}
    return {"a": ndp // half, "u": half, "v": half, "c": 2}, here


def place_of(sizes, at):
    b = jnp.where(at["c"] == 0, at["u"], at["v"])
    y = jnp.where(at["c"] == 0, at["v"], at["u"])
    return at["a"] * sizes["u"] + b, y * 2 + at["c"]


def device_of(sizes, at):
    dp, mode = place_of(sizes, at)
    return {"dp": dp, "mode": mode}


def partner_of(at):
    return {"a": at["a"], "u": at["v"], "v": at["u"], "c": 1 - at["c"]}


def reducer(sizes, here, own, from_c, from_v, from_u, from_a, out, send, recv_c, recv_v, recv_u, recv_a):
    na, nu, nv = sizes["a"], sizes["u"], sizes["v"]
    rows = from_c.shape[1]
    step = next(s for s in (96, 32, rows) if rows % s == 0)

    def owner(t, e, d):
        return move(sizes, move(sizes, move(sizes, here, "a", t + 1), "u", e), "v", d)

    def spot(at):
        dp, mode = place_of(sizes, at)
        return dp * sizes["v"] + mode // 2

    def to_partner(at):
        n = spot(at)
        return pltpu.make_async_remote_copy(
            src_ref=own(at), dst_ref=from_c.at[n], send_sem=send.at[0], recv_sem=recv_c.at[n],
            device_id=device_of(sizes, partner_of(here)), device_id_type=MESH)

    def chunks(at, terms, store):
        mine = own(at)

        def chunk(i, _):
            part = pl.ds(pl.multiple_of(i * step, step), step) if step != rows else slice(None)
            total = mine[part, :].astype(F32)
            for ref, k in terms:
                total = total + ref[k, part, :].astype(F32)
            store(mine, part, total)
            return 0
        lax.fori_loop(0, rows // step, chunk, 0)

    def keep(mine, part, total):
        mine[part, :] = total.astype(BF)

    def finish(mine, part, total):
        out[part, :] = total

    def slot_v(t, e, d):
        return (t * nu + e) * (nv - 1) + d - 1

    def copy(at, buffer, s, stage, sems, to):
        return pltpu.make_async_remote_copy(
            src_ref=own(at), dst_ref=buffer.at[s], send_sem=send.at[stage], recv_sem=sems.at[s],
            device_id=device_of(sizes, to), device_id_type=MESH)

    def copy_v(t, e, d):
        s = slot_v(t, e, d)
        return copy(owner(t, e, d), from_v, s, 1, recv_v, move(sizes, here, "v", d))

    def copy_u(t, e):
        return copy(owner(t, e, 0), from_u, t * (nu - 1) + e - 1, 2, recv_u, move(sizes, here, "u", e))

    def copy_a(t):
        return copy(owner(t, 0, 0), from_a, t, 3, recv_a, owner(t, 0, 0))

    def heard(at):
        n = spot(at)
        pltpu.make_async_remote_copy(
            src_ref=own(at), dst_ref=from_c.at[n], send_sem=send.at[0], recv_sem=recv_c.at[n],
            device_id=device_of(sizes, partner_of(here)), device_id_type=MESH).wait_recv()
        return [(from_c, n)]

    def first(t):
        for d in range(1, nv):
            for e in range(nu):
                at = owner(t, e, d)
                chunks(at, heard(at), keep)
                copy_v(t, e, d).start()

    def after_v(t, e):
        terms = heard(owner(t, e, 0))
        for d in range(1, nv):
            copy_v(t, e, d).wait_recv()
            terms.append((from_v, slot_v(t, e, d)))
        return terms

    def second(t):
        for e in range(1, nu):
            chunks(owner(t, e, 0), after_v(t, e), keep)
            copy_u(t, e).start()

    def after_u(t):
        terms = after_v(t, 0)
        for e in range(1, nu):
            copy_u(t, e).wait_recv()
            terms.append((from_u, t * (nu - 1) + e - 1))
        return terms

    def third(t):
        chunks(owner(t, 0, 0), after_u(t), keep)
        copy_a(t).start()

    def last():
        terms = after_u(na - 1)
        for t in range(na - 1):
            copy_a(t).wait_recv()
            terms.append((from_a, t))
        chunks(here, terms, finish)

    def drain():
        for stage, count in ((0, from_c.shape[0]), (1, na * nu * (nv - 1)), (2, na * (nu - 1)), (3, na - 1)):
            ref = from_c.at[pl.ds(0, count)]
            pltpu.make_async_copy(ref, ref, send.at[stage]).wait()

    return to_partner, first, second, third, last, drain


def each(start, stop, *steps):
    def body(t, _):
        for s in steps:
            s(t)
        return 0
    lax.fori_loop(start, stop, body, 0)


def tail_kernel(n, L, D, slots, blocks, owner, gmix_h, z_h, acts_h, gsum_h, weights_h, gout_h, gup_h, gdn_h,
                obs_ref, wqo_h, basis_ref, eye_ref, sums_ref,
                dense_out, mixer_out, small_out, gin_h,
                gmix, z, acts, gsum, mix, src, tiles, glow, gbias, tmp, con, basist, wq_ref,
                fc0, fc1, fv0, fv1, fu0, fu1, fa0, fa1, small_one, small_two,
                loads, send, recv_c, recv_v, recv_u, recv_a, small_send, small_recv):
    sizes, here = roles()
    ndp, nmode = lax.axis_size("dp"), lax.axis_size("mode")
    dp, mode = lax.axis_index("dp"), lax.axis_index("mode")
    na = sizes["a"]
    per = slots // nmode
    heads = 8
    pieces = ndp // heads
    depth = 64 // pieces
    rows = con.shape[1]
    size = con.shape[0] * rows // blocks

    def load(i, a, b):
        return pltpu.make_async_copy(a, b, loads.at[i])
    firsts = [load(0, gmix_h, gmix), load(1, z_h, z), load(2, weights_h, mix)]
    later = [load(3, acts_h, acts), load(4, gsum_h, gsum), load(18, wqo_h.at[pl.ds(0, D)], wq_ref)]
    grads = []
    start = D
    for i, ref in enumerate((gout_h, gup_h, gdn_h)):
        for c in range(D // 128):
            grads.append(load(5 + i * 4 + c, ref.at[:, pl.ds(c * 128, 128)], src.at[c, pl.ds(start, ref.shape[0]), :]))
        start += ref.shape[0]
    for c in firsts + later + grads:
        c.start()
    greet()

    send_m, first_m, second_m, third_m, last_m, drain_m = reducer(
        sizes, here, lambda at: mix.at[place_of(sizes, at)], fc1, fv1, fu1, fa1, mixer_out,
        send.at[1], recv_c.at[1], recv_v.at[1], recv_u.at[1], recv_a.at[1])

    def con_at(at):
        p, m = place_of(sizes, at)
        return con.at[p * nmode + m]
    send_d, first_d, second_d, third_d, last_d, drain_d = reducer(
        sizes, here, con_at, fc0, fv0, fu0, fa0, dense_out,
        send.at[0], recv_c.at[0], recv_v.at[0], recv_u.at[0], recv_a.at[0])

    basist[...] = basis_ref[...].astype(F32).T.astype(BF)
    firsts[0].wait()

    def spectra(w):
        part = pl.ds(pl.multiple_of(w * L, 32), L)
        spread_rows(tiles, w, slots, n, gmix[part, :].astype(F32))
    each(0, n, spectra)
    firsts[1].wait()
    firsts[2].wait()

    def mix_mode(m):
        def slot(jl, _):
            at = pl.ds(pl.multiple_of((m * per + jl) * n, n), n)
            at2 = pl.ds(pl.multiple_of((m * per + jl) * 2 * n, 2 * n), 2 * n)
            part = pl.ds(pl.multiple_of(jl * depth, depth), depth)
            for h in range(heads):
                y = tiles[h, at, :]
                both = jnp.concatenate([y, swap_halves(y) * sign_lanes(n, 1.0, -1.0)], 0).astype(BF)
                x = dot(both, head_weights(mix, h, pieces, m, part), NT)
                tiles[h, at, :] = jnp.concatenate([x[:n], x[n:]], 1)
                g = dot(z[h, at2, :], both, TN).astype(BF)
                for q in range(pieces):
                    mix[h * pieces + q, m, part, :] = g[q * depth:(q + 1) * depth]
            return 0
        lax.fori_loop(0, per, slot, 0, unroll=2)

    mine_y = mode // 2

    def mode_at(i, core):
        return lax.rem(mine_y + 1 + i, nmode // 2) * 2 + core

    def other_modes(i):
        m = mode_at(i, 1 - here["c"])
        mix_mode(m)

        def hand(p):
            half = sizes["u"]
            b, y = lax.rem(p, half), m // 2
            core = 1 - here["c"]
            send_m({"a": p // half, "u": jnp.where(core == 0, b, y), "v": jnp.where(core == 0, y, b), "c": core}).start()
        each(0, ndp, hand)
    each(0, nmode // 2, other_modes)
    each(0, nmode // 2, lambda i: mix_mode(mode_at(i, here["c"])))
    each(0, na, first_m)

    gbias[...] = jnp.zeros_like(gbias)

    def query(w):
        part = pl.ds(pl.multiple_of(w * L, 32), L)
        g = dot(basist[...], gather_rows(tiles, w, slots, n))
        glow[part, :] = g.astype(BF)
        gbias[...] += functools.reduce(lambda p, q: p + q, [g[i * 8:(i + 1) * 8] for i in range(L // 8)])
    each(0, n, query)

    for k, sums in ((0, gbias[...]), (4, sums_ref[0:8, :])):
        total = jnp.sum(sums, axis=0, keepdims=True)
        for c in range(D // 128):
            small_one[mode, k + c:k + c + 1, :] = total[:, c * 128:(c + 1) * 128]
    for k in range(20):
        small_one[mode, 8 + k:9 + k, :] = jnp.sum(sums_ref[8 + 8 * k:16 + 8 * k, 0:128], axis=0, keepdims=True)
    small_one[mode, 28:32, :] = jnp.zeros((4, 128), F32)

    def small_copy(buffer, axis, index, count, d, base):
        return pltpu.make_async_remote_copy(
            src_ref=buffer.at[index], dst_ref=buffer.at[index], send_sem=small_send.at[base + d - 1], recv_sem=small_recv.at[base + d - 1],
            device_id={**{"dp": dp, "mode": mode}, axis: lax.rem(index + d, count)}, device_id_type=MESH)
    ones = [small_copy(small_one, "mode", mode, nmode, d, 0) for d in range(1, nmode)]
    twos = [small_copy(small_two, "dp", dp, ndp, d, nmode - 1) for d in range(1, ndp)]
    for c in ones:
        c.start()

    for c in later:
        c.wait()
    g = dot(acts[...], glow[...], TN)
    for c in range(D // 128):
        src[c, 0:D, :] = g[:, c * 128:(c + 1) * 128]
    each(0, na // 2, second_m)
    for c in grads:
        c.wait()

    per_shard = rows // size
    join = 4 if per_shard % 4 == 0 else 1
    units = per_shard // join

    def pick(s):
        for k in range(units):
            for c in range(D // 128):
                for i in range(join):
                    row = owner[(s * units + k) * join + i] * size
                    tmp[c, i * size:(i + 1) * size, :] = src[c, pl.ds(row, size), :]
                part = slice(k * join * size, (k + 1) * join * size)
                con[s, part, c * 128:(c + 1) * 128] = tmp[c, 0:join * size, :].astype(BF)
    shards = con.shape[0]
    each(0, shards // 2, pick)
    each(na // 2, na, second_m)
    each(0, na // 2, third_m)
    each(shards // 2, shards, pick)

    def hand_line(t):
        other = partner_of(here)
        for d in list(range(1, sizes["v"])) + [0]:
            for e in range(sizes["u"]):
                send_d(move(sizes, move(sizes, move(sizes, other, "a", t + 1), "u", e), "v", d)).start()
    each(0, na, hand_line)
    each(na // 2, na - 1, third_m)

    def input_grad(w):
        part = pl.ds(pl.multiple_of(w * L, 32), L)
        row = obs_ref[pl.ds(w, 1), :].astype(F32)
        mask = dot((eye_ref[...] * row).astype(BF), jnp.ones((L, 128), BF))
        g = gsum[part, :] + dot(glow[part, :], wq_ref[...], NT)
        for c in range(D // 128):
            gsum[part, c * 128:(c + 1) * 128] = g[:, c * 128:(c + 1) * 128] * mask
    for c in ones:
        c.wait()
    small_two[dp] = functools.reduce(lambda p, q: p + q, [small_one[i] for i in range(nmode)])
    for c in twos:
        c.start()
    each(0, na, first_d)
    each(0, n, input_grad)
    result = load(17, gsum, gin_h)
    result.start()
    each(0, 1, second_d)
    each(1, na - 1, second_d, lambda t: third_d(t - 1))
    last_m()
    second_d(na - 1)
    third_d(na - 2)
    last_d()
    for c in twos:
        c.wait()
    small_out[...] = functools.reduce(lambda p, q: p + q, [small_two[i] for i in range(ndp)])
    drain_m()
    drain_d()
    result.wait()


def tail(gmix, z, acts, gsum, observed, wqo, basis, weights, gout, gup, gdn, sums, owner_list, shard_rows):
    n, L = observed.shape
    D = acts.shape[1]
    slots = basis.shape[0] // 2
    ndp, nmode, mixer_rows = weights.shape[:3]
    nd = ndp * nmode
    total = nd * shard_rows
    half = nmode // 2
    na = ndp // half
    group = nd // 2
    anywhere = pl.BlockSpec(memory_space=pl.ANY)
    vmem = pl.BlockSpec(memory_space=pltpu.VMEM)
    shapes = ((shard_rows, D), (mixer_rows, 128))
    counts = (group, na * half * (half - 1), na * (half - 1), na - 1)
    sem = lambda *s: pltpu.SemaphoreType.DMA(s)
    return pl.pallas_call(
        functools.partial(tail_kernel, n, L, D, slots, owner_list.shape[0]),
        out_shape=(
            jax.ShapeDtypeStruct(shapes[0], F32), jax.ShapeDtypeStruct(shapes[1], F32), jax.ShapeDtypeStruct((32, 128), F32),
            jax.ShapeDtypeStruct((n * L, D), F32),
        ),
        in_specs=[pl.BlockSpec(memory_space=pltpu.SMEM)] + [anywhere] * 8 + [
            vmem, anywhere, vmem, vmem, vmem],
        out_specs=(vmem, vmem, vmem, anywhere),
        scratch_shapes=[
            pltpu.VMEM((n * L, D), BF),
            pltpu.VMEM(z.shape, BF),
            pltpu.VMEM((n * L, D), BF),
            pltpu.VMEM((n * L, D), F32),
            pltpu.VMEM(weights.shape, BF),
            pltpu.VMEM((D // 128, total + 8, 128), F32),
            pltpu.VMEM((8, slots * n, 128), F32),
            pltpu.VMEM((n * L, D), BF),
            pltpu.VMEM((8, D), F32),
            pltpu.VMEM((D // 128, 80, 128), F32),
            pltpu.VMEM((nd, shard_rows, D), BF),
            pltpu.VMEM((L, 2 * slots), BF),
            pltpu.VMEM((D, D), BF),
        ] + [pltpu.VMEM((count,) + s, BF) for count in counts for s in shapes] + [
            pltpu.VMEM((nmode, 32, 128), F32), pltpu.VMEM((ndp, 32, 128), F32),
            sem(19), sem(2, 4), sem(2, counts[0]), sem(2, counts[1]), sem(2, counts[2]), sem(2, counts[3]),
            sem(ndp + nmode - 2), sem(ndp + nmode - 2),
        ],
        compiler_params=pltpu.CompilerParams(collective_id=1, has_side_effects=True, vmem_limit_bytes=62 * 1024 * 1024),
        name="tail",
    )(owner_list, gmix, z, acts, gsum, weights, gout, gup, gdn, observed, wqo, basis, np.eye(L, dtype=np.float32), sums)


def gatherer(sizes, here, slot_of, whole_of, send, send_a, recv):
    na, nu, nv = sizes["a"], sizes["u"], sizes["v"]

    def spot(at):
        dp, mode = place_of(sizes, at)
        return dp * sizes["v"] * 2 + mode

    def copy(at, to, sem):
        ref = slot_of(at)
        return pltpu.make_async_remote_copy(
            src_ref=ref, dst_ref=ref, send_sem=sem, recv_sem=recv.at[spot(at)],
            device_id=device_of(sizes, to), device_id_type=MESH)

    def onward(at, axes):
        for axis, stage in axes:
            for d in range(1, sizes[axis]):
                copy(at, move(sizes, here, axis, d), send.at[stage]).start()
        copy(at, partner_of(here), send.at[2]).start()

    def hop(k, side):
        first, to = here["a"] - side * k, here["a"] + side
        there = (first >= 0) & (first < na) & (to >= 0) & (to < na)
        way = 0 if side == 1 else 1
        inside = lambda x: jnp.clip(x, 0, na - 1)
        return there, lambda: copy({**here, "a": inside(first)}, {**here, "a": inside(to)}, send_a.at[way, k])

    def hops(k, side):
        there, make = hop(k, side)
        pl.when(there)(lambda: make().start())

    def arrived(at):
        copy(at, here, send.at[0]).wait_recv()
        return at

    def lines(k, act):
        for side in ((1, -1) if k else (1,)):
            to = here["a"] - side * k
            pl.when((to >= 0) & (to < na))(lambda side=side, to=to: act({**here, "a": to}, side))

    def start():
        for side in (1, -1):
            hops(0, side)
        onward(here, (("u", 0), ("v", 1)))

    def line(k, then=lambda at: None):
        def act(at, side):
            arrived(at)
            hops(k, side)
            onward(at, (("u", 0), ("v", 1)))
            then(at)
        lines(k, act)

    def second(k, then=lambda at: None):
        def act(at, side):
            for d in range(1, nu):
                to = arrived(move(sizes, at, "u", d))
                onward(to, (("v", 1),))
                then(to)
        lines(k, act)

    def third(k, then=lambda at: None):
        def act(at, side):
            for e in range(nu):
                for d in range(1, nv):
                    to = arrived(move(sizes, move(sizes, at, "u", e), "v", d))
                    onward(to, ())
                    then(to)
        lines(k, act)

    def partner(t, then=lambda at: None):
        other = partner_of(here)
        for e in range(nu):
            for d in range(nv):
                then(arrived(move(sizes, move(sizes, move(sizes, other, "a", t), "u", e), "v", d)))

    def drain():
        for stage, count in ((0, na * (nu - 1)), (1, na * nu * (nv - 1)), (2, na * nu * nv)):
            ref = whole_of(count)
            pltpu.make_async_copy(ref, ref, send.at[stage]).wait()
        for k in range(na):
            for side in (1, -1):
                there, make = hop(k, side)
                pl.when(there)(lambda make=make: make().wait_send())

    return start, line, second, third, partner, drain


def head_kernel(n, L, D, slots, blocks, restore, in_h, dense_ref, mixer_ref, obs_ref, bias_ref, basis_ref, inv_ref, eye_ref,
                acts_h, z_h, sig_h, wqo_h, wup_h, wdn_h, weights_h,
                inputs, acts, query, tiles, z, sig, buf, src, table, mix, tmp,
                loads, send, send_a, recv):
    sizes, here = roles()
    ndp, nmode = lax.axis_size("dp"), lax.axis_size("mode")
    dp, mode = lax.axis_index("dp"), lax.axis_index("mode")
    na = sizes["a"]
    per = slots // nmode
    heads = 8
    pieces = ndp // heads
    depth = 64 // pieces
    rows = buf.shape[1]
    total = buf.shape[0] * rows
    size = total // blocks
    join = 4
    units = blocks // join

    def load(i, a, b):
        return pltpu.make_async_copy(a, b, loads.at[i])
    load_in = load(0, in_h, inputs)
    load_in.start()
    buf[dp * nmode + mode] = dense_ref[...].astype(BF)
    mix[dp, mode] = mixer_ref[...].astype(BF)
    greet()

    def buf_at(at):
        p, m = place_of(sizes, at)
        return buf.at[p * nmode + m]

    start_d, line_d, second_d, third_d, partner_d, drain_d = gatherer(
        sizes, here, buf_at, lambda count: buf.at[pl.ds(0, count)], send.at[0], send_a.at[0], recv.at[0])
    mix_at = lambda at: mix.at[place_of(sizes, at)]

    def mix_many(count):
        if count % nmode == 0:
            return mix.at[pl.ds(0, count // nmode)]
        return mix.at[pl.ds(0, count), 0] if count <= ndp else mix.at[pl.ds(0, count // 2), pl.ds(0, 2)]
    start_m, line_m, second_m, third_m, partner_m, drain_m = gatherer(
        sizes, here, mix_at, mix_many, send.at[1], send_a.at[1], recv.at[1])
    start_d()

    def widen(at):
        p, m = place_of(sizes, at)
        k = p * nmode + m
        for c in range(D // 128):
            src[c, pl.ds(k * rows, rows), :] = buf[k, :, c * 128:(c + 1) * 128].astype(F32)
    widen(here)
    load_in.wait()

    def mask(w):
        row = obs_ref[pl.ds(w, 1), :].astype(F32)
        part = pl.ds(pl.multiple_of(w * L, 32), L)
        acts[part, :] = dot((eye_ref[...] * row).astype(BF), inputs[part, :]).astype(BF)
    each(0, n, mask)
    outs = [load(1, acts, acts_h)]
    outs[0].start()
    for k in range(na + 2):
        if k < na - 1:
            line_d(k + 1, widen)
        if k < na:
            second_d(k, widen)
        if 1 <= k <= na:
            third_d(k - 1, widen)
        if k == 0:
            start_m()
        if 1 <= k < na:
            line_m(k)
        if 1 <= k <= na:
            second_m(k - 1)
        if 2 <= k <= na:
            third_m(k - 2)
    each(0, na, lambda t: partner_d(t, widen))

    def pick(p):
        for c in range(D // 128):
            for i in range(join):
                tmp[c, i * size:(i + 1) * size, :] = src[c, pl.ds(restore[p * join + i] * size, size), :]
            part = pl.ds(pl.multiple_of(p * join * size, 16), join * size)
            table[part, c * 128:(c + 1) * 128] = tmp[c].astype(BF)
    early = -(-D // (join * size))
    each(0, early, pick)
    T = 384

    def project(i):
        part = pl.ds(pl.multiple_of(i * T, T), T)
        query[part, :] = (dot(acts[part, :], table[0:D, :]) + bias_ref[:, 0:D]).astype(BF)

    def spectra(w):
        part = pl.ds(pl.multiple_of(w * L, 32), L)
        spread_rows(tiles, w, slots, n, dot(basis_ref[...], query[part, :]))

    work = [lambda i=i: project(i) for i in range(n * L // T)]
    work += [lambda i=i: each(i * n // 4, (i + 1) * n // 4, spectra) for i in range(4)]
    cuts = [early + (units - early) * i // 4 for i in range(5)]
    work += [lambda i=i: each(cuts[i], cuts[i + 1], pick) for i in range(4)]
    for i, w in enumerate(work):
        w()
        if i == 1:
            third_m(na - 1)
    at = 0
    for i, ref in enumerate((wqo_h, wup_h, wdn_h)):
        outs.append(load(2 + i, table.at[pl.ds(at, ref.shape[0])], ref))
        outs[-1].start()
        at += ref.shape[0]
    each(0, na, partner_m)
    outs.append(load(5, mix, weights_h))
    outs[-1].start()

    def slot(j, _):
        m, jl = j // per, lax.rem(j, per)
        at = pl.ds(pl.multiple_of(j * n, n), n)
        part = pl.ds(pl.multiple_of(jl * depth, depth), depth)
        for h in range(heads):
            x = tiles[h, at, :]
            both = jnp.concatenate([x, swap_halves(x)], 0)[:, :64].astype(BF)
            z[h, pl.ds(pl.multiple_of(j * 2 * n, 2 * n), 2 * n), :] = both
            y = dot(both, head_weights(mix, h, pieces, m, part))
            tiles[h, at, :] = y[:n] + swap_halves(y[n:]) * sign_lanes(n, -1.0, 1.0)
        return 0
    lax.fori_loop(0, slots, slot, 0, unroll=4)
    outs.append(load(6, z, z_h))
    outs[-1].start()

    def signal(w):
        part = pl.ds(pl.multiple_of(w * L, 32), L)
        sig[part, :] = dot(inv_ref[...], gather_rows(tiles, w, slots, n)).astype(BF)
    each(0, n, signal)
    outs.append(load(7, sig, sig_h))
    outs[-1].start()
    drain_d()
    drain_m()
    for o in outs:
        o.wait()


def head(inputs, observed, dense, mixer, restore, bias, basis, inv, ff):
    n, L, D = inputs.shape
    slots = basis.shape[0] // 2
    ndp, nmode = lax.axis_size("dp"), lax.axis_size("mode")
    nd = ndp * nmode
    rows, mixer_rows = dense.shape[0], mixer.shape[0]
    anywhere = pl.BlockSpec(memory_space=pl.ANY)
    vmem = pl.BlockSpec(memory_space=pltpu.VMEM)
    sem = lambda *s: pltpu.SemaphoreType.DMA(s)
    tokens = n * L
    return pl.pallas_call(
        functools.partial(head_kernel, n, L, D, slots, restore.shape[0]),
        out_shape=(
            jax.ShapeDtypeStruct((tokens, D), BF),
            jax.ShapeDtypeStruct((8, 2 * slots * n, 64), BF),
            jax.ShapeDtypeStruct((tokens, D), BF),
            jax.ShapeDtypeStruct((2 * D, D), BF),
            jax.ShapeDtypeStruct((ff, D), BF),
            jax.ShapeDtypeStruct((ff, D), BF),
            jax.ShapeDtypeStruct((ndp, nmode, mixer_rows, 128), BF),
        ),
        in_specs=[pl.BlockSpec(memory_space=pltpu.SMEM), anywhere] + [vmem] * 7,
        out_specs=(anywhere,) * 7,
        scratch_shapes=[
            pltpu.VMEM((tokens, D), BF),
            pltpu.VMEM((tokens, D), BF),
            pltpu.VMEM((tokens, D), BF),
            pltpu.VMEM((8, slots * n, 128), F32),
            pltpu.VMEM((8, 2 * slots * n, 64), BF),
            pltpu.VMEM((tokens, D), BF),
            pltpu.VMEM((nd, rows, D), BF),
            pltpu.VMEM((D // 128, nd * rows + 8, 128), F32),
            pltpu.VMEM((nd * rows, D), BF),
            pltpu.VMEM((ndp, nmode, mixer_rows, 128), BF),
            pltpu.VMEM((D // 128, 4 * (nd * rows // restore.shape[0]), 128), F32),
            sem(8), sem(2, 3), sem(2, 2, ndp // (nmode // 2)), sem(2, nd),
        ],
        compiler_params=pltpu.CompilerParams(collective_id=0, has_side_effects=True, vmem_limit_bytes=62 * 1024 * 1024),
        name="head",
    )(restore, inputs.reshape(tokens, D), dense, mixer, observed, bias, basis, inv, np.eye(L, dtype=np.float32))


def adam_terms(weight, gradient, moment, second, step_rate):
    moment_new = BETA_ONE * moment + (1.0 - BETA_ONE) * gradient
    second_new = BETA_TWO * second + (1.0 - BETA_TWO) * gradient * gradient
    scaled_m = moment_new * (1.0 / (1.0 - BETA_ONE**STEP))
    scaled_v = second_new * (1.0 / (1.0 - BETA_TWO**STEP))
    weight_new = weight - step_rate * (scaled_m / (jnp.sqrt(scaled_v) + ADAM_EPS) + DECAY_RATE * weight)
    return moment_new, second_new, weight_new


def update_kernel(*refs):
    dense, mixer, passed = refs[:4], refs[4:8], refs[8]
    dense_out, mixer_out, passed_out, sem = refs[9:12], refs[12:15], refs[15], refs[16]
    copy = pltpu.make_async_copy(passed, passed_out, sem)
    copy.start()
    for ins, outs, rate in ((dense, dense_out, RATE_DENSE), (mixer, mixer_out, RATE_MIXER)):
        for ref, value in zip(outs, adam_terms(*(x[...] for x in ins), rate)):
            ref[...] = value
    copy.wait()


def update(dense, mixer, passed):
    vmem = pl.BlockSpec(memory_space=pltpu.VMEM)
    anywhere = pl.BlockSpec(memory_space=pl.ANY)
    like = lambda x: jax.ShapeDtypeStruct(x.shape, x.dtype)
    return pl.pallas_call(
        update_kernel,
        out_shape=(like(dense[0]),) * 3 + (like(mixer[0]),) * 3 + (like(passed),),
        in_specs=[vmem] * 8 + [anywhere],
        out_specs=(vmem,) * 6 + (anywhere,),
        scratch_shapes=[pltpu.SemaphoreType.DMA],
        compiler_params=pltpu.CompilerParams(vmem_limit_bytes=32 * 1024 * 1024),
        name="update",
    )(*dense, *mixer, passed)


def forward_table(mode_index, length):
    slots = mode_index.shape[0]
    row = jnp.arange(2 * slots, dtype=jnp.int32)
    mode = jnp.concatenate([mode_index, mode_index])
    turn = (mode[:, None] * jnp.arange(length, dtype=jnp.int32)[None, :] + (row >= slots)[:, None] * (length // 4)) % length
    return jnp.cos(turn.astype(F32) * (2.0 * math.pi / length)).astype(BF)


def inverse_table(slots, length):
    turn = np.arange(length)[:, None] * np.arange(slots)[None, :] % length
    angle = turn * (2.0 * np.pi / length)
    scale = np.where(np.arange(slots) == 0, 1.0, 2.0) / length
    return np.concatenate([np.cos(angle) * scale, -np.sin(angle) * scale], 1).astype(np.float32).astype(BF)


def shards(
    inputs,
    observed,
    out_grad,
    mode_index,
    owner_list,
    dense_master,
    dense_first,
    dense_second,
    mixer_master,
    mixer_first,
    mixer_second,
    small_master,
    small_first,
    small_second,
):
    ndp, nmode = lax.axis_size("dp"), lax.axis_size("mode")
    length, width = inputs.shape[1:]
    slots = mode_index.shape[0]
    hidden = (dense_master.shape[0] * ndp * nmode - 2 * width) // 2
    basis = forward_table(mode_index, length)
    inv = inverse_table(slots, length)
    small_row = small_master[None]
    places = jnp.arange(owner_list.shape[0], dtype=jnp.int32)
    restore = jnp.sum(jnp.where(owner_list[None, :] == places[:, None], places[None, :], 0), axis=1)
    acts, spectra, sig, wqo, wup, wdn, weights = head(
        inputs, observed, dense_master, mixer_master.reshape(-1, mixer_master.shape[2]), restore, small_row,
        basis, inv, hidden,
    )
    output, grad_summed, grad_mixed, g_out, g_up, g_down, sums = middle(
        small_master, acts.reshape(inputs.shape), sig.reshape(inputs.shape), out_grad, wqo, wup, wdn,
        small_row, np.ascontiguousarray(inv.T),
    )
    dense_mine, mixer_mine, small_all, input_grad = tail(
        grad_mixed.reshape(-1, width), spectra, acts, grad_summed.reshape(-1, width), observed, wqo, basis, weights,
        g_out, g_up, g_down, sums, owner_list, dense_master.shape[0],
    )
    small_total = jnp.concatenate([small_all[:8].reshape(-1), jnp.sum(small_all[8:28], axis=1)])
    flat = lambda x: x.reshape(-1, x.shape[-1])
    dense_first_new, dense_second_new, dense_new, mixer_first_new, mixer_second_new, mixer_new, input_grad = update(
        (dense_master, dense_mine, dense_first, dense_second),
        (flat(mixer_master), mixer_mine, flat(mixer_first), flat(mixer_second)),
        input_grad,
    )
    mixer_first_new, mixer_second_new, mixer_new = (
        x.reshape(mixer_master.shape) for x in (mixer_first_new, mixer_second_new, mixer_new)
    )
    small_first_new, small_second_new, small_new = adam_terms(
        small_master, small_total, small_first, small_second, RATE_SMALL
    )
    return (
        output,
        input_grad.reshape(inputs.shape),
        dense_first_new,
        dense_second_new,
        dense_new,
        mixer_first_new,
        mixer_second_new,
        mixer_new,
        small_first_new,
        small_second_new,
        small_new,
        small_total[width : 2 * width],
    )


def solution(mesh):
    placed = (
        P(("dp", "mode"), None, None),
        P(("dp", "mode"), None),
        P(("dp", "mode"), None, None),
        P(),
        P(),
        P(("dp", "mode"), None),
        P(("dp", "mode"), None),
        P(("dp", "mode"), None),
        P("mode", "dp", None),
        P("mode", "dp", None),
        P("mode", "dp", None),
        P(),
        P(),
        P(),
    )
    return jax.shard_map(
        shards,
        mesh=mesh,
        in_specs=placed,
        out_specs=(
            P(("dp", "mode"), None, None),
            P(("dp", "mode"), None, None),
            P(("dp", "mode"), None),
            P(("dp", "mode"), None),
            P(("dp", "mode"), None),
            P("mode", "dp", None),
            P("mode", "dp", None),
            P("mode", "dp", None),
            P(),
            P(),
            P(),
            P(),
        ),
        check_vma=False,
    )
```

```python
import functools
import math

import jax
import jax.numpy as jnp
import numpy as np
from jax import lax
from jax.experimental import pallas as pl
from jax.experimental.pallas import tpu as pltpu
from jax.sharding import PartitionSpec as P

STEP = 10
BETA_ONE = 0.9
BETA_TWO = 0.95
ADAM_EPS = 1e-08
DECAY_RATE = 0.1
RATE_DENSE = 0.03
RATE_MIXER = 0.03
RATE_SMALL = 0.5

KERNEL_SIZES = (7, 12, 14, 24, 48)
ODD = (7, 3, 7, 3, 3)
LOG2E = 1.4426950408889634
BF = jnp.bfloat16
F32 = jnp.float32
NT = (((1,), (1,)), ((), ()))
NN = (((1,), (0,)), ((), ()))
TN = (((0,), (0,)), ((), ()))


def dot(a, b, dims=NN):
    return lax.dot_general(a, b, dims, preferred_element_type=F32)


def average_counts(length):
    tables = []
    t = np.arange(length)
    for size in KERNEL_SIZES:
        u = np.clip(t[:, None] - (size - 1) // 2 + np.arange(size)[None, :], 0, length - 1)
        tables.append((u[:, :, None] == t[None, None, :]).sum(1) * (ODD[len(tables)] / size))
    return np.stack(tables).astype(np.float32)


def gelu_parts(h):
    z = jnp.abs(h)
    e = jnp.exp2(h * h * (-0.5 * LOG2E))
    t = 1.0 / (1.0 + (0.3275911 * math.sqrt(0.5)) * z)
    poly = t * (0.5 * 0.254829592 + t * (-0.5 * 0.284496736 + t * (0.5 * 1.421413741 + t * (-0.5 * 1.453152027 + t * (0.5 * 1.061405429)))))
    tail = poly * e
    big = jnp.where(h < 0, tail, 1.0 - tail)
    return big, e * (1.0 / math.sqrt(2 * math.pi))


def middle_kernel(W, L, D, FF, steps,
                  mix_ref, acts_ref, sig_ref, og_ref, wq_ref, wup_ref, wdn_ref, bias_ref, invt_ref, cnt_ref, cntt_ref,
                  out_ref, gsum_ref, gmix_ref, gw_ref, gup_ref, gdn_ref, small_ref,
                  vs, base, avg1, c1, v1, active, dgelu, first, flow, gb, ghid, glow, avg2, stk, accs, accb, hs, wg, wsem):
    step = pl.program_id(0)
    T = W * L
    CH = 16
    CC = 256
    nc = D // CC
    nr = L // CH
    FT = 512

    @pl.when(step == 0)
    def _():
        vs[...] = jnp.zeros_like(vs)
        stk[...] = jnp.zeros_like(stk)
        accs[...] = jnp.zeros_like(accs)
        accb[...] = jnp.zeros_like(accb)
        gw_ref[...] = jnp.zeros_like(gw_ref)

    def fold(x):
        y = x[:, 0:128]
        for i in range(1, CC // 128):
            y = y + x[:, i * 128:(i + 1) * 128]
        return y[0:8] + y[8:16]

    def scaled_shares(v, base_at):
        p = [mix_ref[2 * D + base_at + k] for k in range(10)]
        logits = [((p[k] - p[4]) * LOG2E) * v + (p[5 + k] - p[9]) * LOG2E for k in range(4)]
        top = jnp.maximum(functools.reduce(jnp.maximum, logits), 0.0)
        es = [jnp.exp2(l - top) for l in logits] + [jnp.exp2(-top)]
        r = 1.0 / functools.reduce(lambda a, b: a + b, es)
        scale = {7: r * (1.0 / 7.0), 3: r * (1.0 / 3.0)}
        return [e * scale[o] for e, o in zip(es, ODD)]

    def backward(v, g, cs, avs, mean, base_at, store):
        means = {7: 7.0 * mean, 3: 3.0 * mean}
        total = None
        for k in range(5):
            cg = cs[k] * g
            store(k, cg)
            if k < 4:
                t = cg * (means[ODD[k]] - avs[k])
                term = (mix_ref[2 * D + base_at + k] - mix_ref[2 * D + base_at + 4]) * t
                total = term if total is None else total + term
                accs[base_at + k] += fold(t * v)
                accs[base_at + 5 + k] += fold(t)
        return total

    sig = sig_ref[...].reshape(T, D)
    base[...] = dot(sig, wq_ref[D:2 * D, :])

    def cut(w, source):
        for i in range(nr):
            for c in range(nc):
                cols = slice(c * CC, (c + 1) * CC)
                v = source(w, i, cols)
                hi = v.astype(BF)
                vs[w % 2, i * CH:(i + 1) * CH, cols] = hi
                vs[w % 2, L + i * CH:L + (i + 1) * CH, cols] = (v - hi.astype(F32)).astype(BF)

    def summed(w, i, cols):
        rows = slice(w * L + i * CH, w * L + (i + 1) * CH)
        v = base[rows, cols] + acts_ref[w, i * CH:(i + 1) * CH, cols].astype(F32) + bias_ref[:, D + cols.start:D + cols.stop]
        v1[rows, cols] = v
        return v

    def averages_one(w):
        cut(w, summed)
        avg1[w * 5 * L:(w + 1) * 5 * L, :] = dot(cnt_ref[...], vs[w % 2])

    def decompose_one(w):
        for i in range(nr):
            for c in range(nc):
                cols = slice(c * CC, (c + 1) * CC)
                rows = slice(w * L + i * CH, w * L + (i + 1) * CH)
                v = v1[rows, cols]
                cs = scaled_shares(v, 0)
                mean = None
                for k in range(5):
                    at = slice((w * 5 + k) * L + i * CH, (w * 5 + k) * L + (i + 1) * CH)
                    u = cs[k] * avg1[at, cols]
                    c1[at, cols] = cs[k]
                    mean = u if mean is None else mean + u
                f = v - mean
                first[rows, cols] = f
                flow[pl.ds(pl.multiple_of(step * T + w * L + i * CH, CH), CH), cols] = f.astype(BF)

    averages_one(0)
    for w in range(W):
        if w + 1 < W:
            averages_one(w + 1)
        decompose_one(w)

    here_t = pl.ds(pl.multiple_of(step * T, CH), T)
    base[...] = first[...]

    def up(n):
        return dot(flow[here_t, :], wup_ref[n * FT:(n + 1) * FT, :], NT)

    tiles = FF // FT
    hs[0] = up(0)
    for n in range(tiles + 1):
        if n + 1 < tiles:
            hs[(n + 1) % 2] = up(n + 1)
        if n < tiles:
            h = hs[n % 2]
            big, small = gelu_parts(h)
            active[here_t, n * FT:(n + 1) * FT] = (h * big).astype(BF)
            dgelu[:, n * FT:(n + 1) * FT] = (big + h * small).astype(BF)
        if n:
            base[...] += dot(active[here_t, (n - 1) * FT:n * FT], wdn_ref[(n - 1) * FT:n * FT, :])

    def branch(w, i, cols):
        return base[w * L + i * CH:w * L + (i + 1) * CH, cols]

    def averages_two(w):
        cut(w, branch)
        avg2[w % 2] = dot(cnt_ref[...], vs[w % 2])

    def keep_at(w, i, cols):
        def keep(k, cg):
            stk[w % 2, k * L + i * CH:k * L + (i + 1) * CH, cols] = cg.astype(BF)
        return keep

    def decompose_two(w):
        for i in range(nr):
            for c in range(nc):
                cols = slice(c * CC, (c + 1) * CC)
                rows = slice(w * L + i * CH, w * L + (i + 1) * CH)
                here = slice(i * CH, (i + 1) * CH)
                v = base[rows, cols]
                cs = scaled_shares(v, 10)
                avs = [avg2[w % 2, k * L + i * CH:k * L + (i + 1) * CH, cols] for k in range(5)]
                mean = functools.reduce(lambda a, b: a + b, [c_ * a_ for c_, a_ in zip(cs, avs)])
                out_ref[w, here, cols] = (v - mean).astype(BF)
                g = og_ref[w, here, cols].astype(F32)
                base[rows, cols] = g + backward(v, g, cs, avs, mean, 10, keep_at(w, i, cols))

    def back_two(w):
        rows = slice(w * L, (w + 1) * L)
        gs = base[rows, :] - dot(cntt_ref[...], stk[w % 2])
        base[rows, :] = gs
        gb[pl.ds(pl.multiple_of(step * T + w * L, 32), L), :] = gs.astype(BF)

    averages_two(0)
    for w in range(W):
        if w + 1 < W:
            averages_two(w + 1)
        decompose_two(w)
        if w:
            back_two(w - 1)
    back_two(W - 1)

    def down(n):
        return dot(gb[here_t, :], wdn_ref[n * FT:(n + 1) * FT, :], NT)

    hs[0] = down(0)
    for n in range(tiles + 1):
        if n + 1 < tiles:
            hs[(n + 1) % 2] = down(n + 1)
        if n < tiles:
            ghid[here_t, n * FT:(n + 1) * FT] = (hs[n % 2] * dgelu[:, n * FT:(n + 1) * FT].astype(F32)).astype(BF)
        if n:
            base[...] += dot(ghid[here_t, (n - 1) * FT:n * FT], wup_ref[(n - 1) * FT:n * FT, :])

    def decompose_three(w):
        for i in range(nr):
            for c in range(nc):
                cols = slice(c * CC, (c + 1) * CC)
                rows = slice(w * L + i * CH, w * L + (i + 1) * CH)
                v = v1[rows, cols]
                g = base[rows, cols]
                ats = [slice((w * 5 + k) * L + i * CH, (w * 5 + k) * L + (i + 1) * CH) for k in range(5)]
                cs = [c1[at, cols] for at in ats]
                avs = [avg1[at, cols] for at in ats]
                mean = v - first[rows, cols]
                extra = backward(v, g, cs, avs, mean, 0, keep_at(w, i, cols))
                base[rows, cols] = g + extra
                accb[:, cols] += extra[0:8] + extra[8:16]

    def back_three(w):
        rows = slice(w * L, (w + 1) * L)
        gs = base[rows, :] - dot(cntt_ref[...], stk[w % 2])
        gsum_ref[w] = gs
        glow[rows, :] = gs.astype(BF)

    for w in range(W):
        decompose_three(w)
        if w:
            back_three(w - 1)
    back_three(W - 1)

    back = dot(glow[...], wq_ref[D:2 * D, :], NT).astype(BF)
    for w in range(W):
        gmix_ref[w] = dot(invt_ref[...], back[w * L:(w + 1) * L, :]).astype(BF)
    gw_ref[...] += dot(sig, glow[...], TN)

    @pl.when(step == steps - 1)
    def _():
        small_ref[0:8, :] = accb[...]
        for at in (4, 9, 14, 19):
            accs[at] = -(accs[at - 4] + accs[at - 3] + accs[at - 2] + accs[at - 1])
        for k in range(20):
            small_ref[8 + 8 * k:16 + 8 * k, 0:128] = accs[k]
            small_ref[8 + 8 * k:16 + 8 * k, 128:512] = jnp.zeros((8, 384), F32)

        copies = {}
        for n in range(tiles):
            part = slice(n * FT, (n + 1) * FT)
            for i, (left, right, ref) in enumerate(((ghid, flow, gup_ref), (active, gb, gdn_ref))):
                k = (n % 2) * 2 + i
                if n >= 2:
                    copies[n - 2, i].wait()
                wg[k] = dot(left[:, part], right[...], TN)
                copies[n, i] = pltpu.make_async_copy(wg.at[k], ref.at[pl.ds(n * FT, FT)], wsem.at[k])
                copies[n, i].start()
        for n in range(max(tiles - 2, 0), tiles):
            for i in range(2):
                copies[n, i].wait()


def middle(mix, acts, sig, og, wqo, wup, wdn, bias, invt, W=4):
    n, L, D = acts.shape
    FF = wup.shape[0]
    steps = n // W
    T = W * L
    A = average_counts(L)
    cnt = np.zeros((5 * L, 256), np.float32)
    cnt[:, :L] = A.reshape(5 * L, L)
    cnt[:, L:2 * L] = A.reshape(5 * L, L)
    cntt = np.zeros((L, 512), np.float32)
    cntt[:, :5 * L] = A.transpose(2, 0, 1).reshape(L, 5 * L)
    cnt, cntt = (np.asarray(x, BF) for x in (cnt, cntt))
    whole = lambda *s: pl.BlockSpec(s, lambda i: (0,) * len(s), pipeline_mode=pl.Buffered(1))
    anywhere = pl.BlockSpec(memory_space=pl.ANY)
    piece = lambda *s: pl.BlockSpec(s, lambda i: (i,) + (0,) * (len(s) - 1))
    return pl.pallas_call(
        functools.partial(middle_kernel, W, L, D, FF, steps),
        grid=(steps,),
        out_shape=(
            jax.ShapeDtypeStruct((n, L, D), BF),
            jax.ShapeDtypeStruct((n, L, D), F32),
            jax.ShapeDtypeStruct((n, L, D), BF),
            jax.ShapeDtypeStruct((D, D), F32),
            jax.ShapeDtypeStruct((FF, D), F32),
            jax.ShapeDtypeStruct((FF, D), F32),
            jax.ShapeDtypeStruct((168, D), F32),
        ),
        in_specs=[
            pl.BlockSpec(memory_space=pltpu.SMEM),
            piece(W, L, D), piece(W, L, D), piece(W, L, D),
            whole(2 * D, D), whole(FF, D), whole(FF, D), whole(1, bias.shape[1]), whole(L, L), whole(5 * L, 256), whole(L, 512),
        ],
        out_specs=(
            piece(W, L, D), piece(W, L, D), piece(W, L, D), whole(D, D), anywhere, anywhere, whole(168, D),
        ),
        scratch_shapes=[
            pltpu.VMEM((2, 256, D), BF),
            pltpu.VMEM((T, D), F32),
            pltpu.VMEM((W * 5 * L, D), F32),
            pltpu.VMEM((W * 5 * L, D), F32),
            pltpu.VMEM((T, D), F32),
            pltpu.VMEM((n * L, FF), BF),
            pltpu.VMEM((T, FF), BF),
            pltpu.VMEM((T, D), F32),
            pltpu.VMEM((n * L, D), BF),
            pltpu.VMEM((n * L, D), BF),
            pltpu.VMEM((n * L, FF), BF),
            pltpu.VMEM((T, D), BF),
            pltpu.VMEM((2, 5 * L, D), F32),
            pltpu.VMEM((2, 512, D), BF),
            pltpu.VMEM((20, 8, 128), F32),
            pltpu.VMEM((8, D), F32),
            pltpu.VMEM((2, T, 512), F32),
            pltpu.VMEM((4, 512, D), F32),
            pltpu.SemaphoreType.DMA((4,)),
        ],
        compiler_params=pltpu.CompilerParams(vmem_limit_bytes=60 * 1024 * 1024),
        name="middle",
    )(mix, acts, sig, og, wqo, wup, wdn, bias, invt, cnt, cntt)


def sign_lanes(rows, left, right):
    lane = lax.broadcasted_iota(jnp.int32, (rows, 128), 1)
    return jnp.where(lane < 64, left, right).astype(F32)


def interleave(real, imag, v):
    re, im = real[:, v * 128:(v + 1) * 128], imag[:, v * 128:(v + 1) * 128]
    low = lax.broadcasted_iota(jnp.int32, re.shape, 1) < 64
    return jnp.where(low, re, pltpu.roll(im, 64, 1)), jnp.where(low, pltpu.roll(re, 64, 1), im)


def gather_rows(tiles, w, slots, n):
    reals, imags = [], []
    for v in range(4):
        first = tiles[2 * v, pl.ds(w, slots, stride=n), :]
        second = tiles[2 * v + 1, pl.ds(w, slots, stride=n), :]
        low = lax.broadcasted_iota(jnp.int32, first.shape, 1) < 64
        reals.append(jnp.where(low, first, pltpu.roll(second, 64, 1)).astype(BF))
        imags.append(jnp.where(low, pltpu.roll(first, 64, 1), second).astype(BF))
    return jnp.concatenate([jnp.concatenate(reals, 1), jnp.concatenate(imags, 1)], 0)


def spread_rows(tiles, w, slots, n, spectrum):
    for v in range(4):
        one, two = interleave(spectrum[:slots], spectrum[slots:], v)
        tiles[2 * v, pl.ds(w, slots, stride=n), :] = one
        tiles[2 * v + 1, pl.ds(w, slots, stride=n), :] = two


def swap_halves(x):
    return pltpu.roll(x, 64, 1)


def head_weights(weights, h, pieces, mode, rows):
    return jnp.concatenate([weights[h * pieces + q, mode, rows, :] for q in range(pieces)], 0)


MESH = pl.DeviceIdType.MESH


def move(sizes, at, axis, d):
    return {**at, axis: lax.rem(at[axis] + d, sizes[axis])}


def greet():
    ndp, nmode = lax.axis_size("dp"), lax.axis_size("mode")
    dp, mode = lax.axis_index("dp"), lax.axis_index("mode")
    barrier = pltpu.get_barrier_semaphore()
    for d in range(1, nmode):
        pl.semaphore_signal(barrier, 1, device_id={"dp": dp, "mode": lax.rem(mode + d, nmode)}, device_id_type=MESH)
    for d in range(1, ndp):
        pl.semaphore_signal(barrier, 1, device_id={"dp": lax.rem(dp + d, ndp), "mode": mode}, device_id_type=MESH)
    pl.semaphore_wait(barrier, ndp + nmode - 2)


def staggered(count, *stages):
    k = len(stages)
    if count < k:
        for stage in stages:
            for t in range(count):
                stage(t)
        return
    for t in range(k - 1):
        for s in range(t + 1):
            stages[s](t - s)

    def body(t, _):
        for s in range(k):
            stages[s](t - s)
        return 0
    lax.fori_loop(k - 1, count, body, 0)
    for t in range(count, count + k - 1):
        for s in range(t - count + 1, k):
            stages[s](t - s)


JOIN = 12


def roles():
    ndp, nmode = lax.axis_size("dp"), lax.axis_size("mode")
    half = nmode // 2
    dp, mode = lax.axis_index("dp"), lax.axis_index("mode")
    b, y, c = lax.rem(dp, half), mode // 2, lax.rem(mode, 2)
    here = {"a": dp // half, "u": jnp.where(c == 0, b, y), "v": jnp.where(c == 0, y, b), "c": c}
    return {"a": ndp // half, "u": half, "v": half, "c": 2}, here


def place_of(sizes, at):
    b = jnp.where(at["c"] == 0, at["u"], at["v"])
    y = jnp.where(at["c"] == 0, at["v"], at["u"])
    return at["a"] * sizes["u"] + b, y * 2 + at["c"]


def device_of(sizes, at):
    dp, mode = place_of(sizes, at)
    return {"dp": dp, "mode": mode}


def partner_of(at):
    return {"a": at["a"], "u": at["v"], "v": at["u"], "c": 1 - at["c"]}


def reducer(sizes, here, own, from_c, from_v, from_u, from_a, out, send, recv_c, recv_v, recv_u, recv_a):
    na, nu, nv = sizes["a"], sizes["u"], sizes["v"]
    rows = from_c.shape[1]
    step = next(s for s in (96, 32, rows) if rows % s == 0)

    def owner(t, e, d):
        return move(sizes, move(sizes, move(sizes, here, "a", t + 1), "u", e), "v", d)

    def spot(at):
        dp, mode = place_of(sizes, at)
        return dp * sizes["v"] + mode // 2

    def to_partner(at):
        n = spot(at)
        return pltpu.make_async_remote_copy(
            src_ref=own(at), dst_ref=from_c.at[n], send_sem=send.at[0], recv_sem=recv_c.at[n],
            device_id=device_of(sizes, partner_of(here)), device_id_type=MESH)

    def chunks(at, terms, store):
        mine = own(at)

        def chunk(i, _):
            part = pl.ds(pl.multiple_of(i * step, step), step) if step != rows else slice(None)
            total = mine[part, :].astype(F32)
            for ref, k in terms:
                total = total + ref[k, part, :].astype(F32)
            store(mine, part, total)
            return 0
        lax.fori_loop(0, rows // step, chunk, 0)

    def keep(mine, part, total):
        mine[part, :] = total.astype(BF)

    def finish(mine, part, total):
        out[part, :] = total

    def slot_v(t, e, d):
        return (t * nu + e) * (nv - 1) + d - 1

    def copy(at, buffer, s, stage, sems, to):
        return pltpu.make_async_remote_copy(
            src_ref=own(at), dst_ref=buffer.at[s], send_sem=send.at[stage], recv_sem=sems.at[s],
            device_id=device_of(sizes, to), device_id_type=MESH)

    def copy_v(t, e, d):
        s = slot_v(t, e, d)
        return copy(owner(t, e, d), from_v, s, 1, recv_v, move(sizes, here, "v", d))

    def copy_u(t, e):
        return copy(owner(t, e, 0), from_u, t * (nu - 1) + e - 1, 2, recv_u, move(sizes, here, "u", e))

    def copy_a(t):
        return copy(owner(t, 0, 0), from_a, t, 3, recv_a, owner(t, 0, 0))

    def heard(at):
        n = spot(at)
        pltpu.make_async_remote_copy(
            src_ref=own(at), dst_ref=from_c.at[n], send_sem=send.at[0], recv_sem=recv_c.at[n],
            device_id=device_of(sizes, partner_of(here)), device_id_type=MESH).wait_recv()
        return [(from_c, n)]

    def first(t):
        for d in range(1, nv):
            for e in range(nu):
                at = owner(t, e, d)
                chunks(at, heard(at), keep)
                copy_v(t, e, d).start()

    def after_v(t, e):
        terms = heard(owner(t, e, 0))
        for d in range(1, nv):
            copy_v(t, e, d).wait_recv()
            terms.append((from_v, slot_v(t, e, d)))
        return terms

    def second(t):
        for e in range(1, nu):
            chunks(owner(t, e, 0), after_v(t, e), keep)
            copy_u(t, e).start()

    def after_u(t):
        terms = after_v(t, 0)
        for e in range(1, nu):
            copy_u(t, e).wait_recv()
            terms.append((from_u, t * (nu - 1) + e - 1))
        return terms

    def third(t):
        chunks(owner(t, 0, 0), after_u(t), keep)
        copy_a(t).start()

    def last():
        terms = after_u(na - 1)
        for t in range(na - 1):
            copy_a(t).wait_recv()
            terms.append((from_a, t))
        chunks(here, terms, finish)

    def drain():
        for stage, count in ((0, from_c.shape[0]), (1, na * nu * (nv - 1)), (2, na * (nu - 1)), (3, na - 1)):
            ref = from_c.at[pl.ds(0, count)]
            pltpu.make_async_copy(ref, ref, send.at[stage]).wait()

    return to_partner, first, second, third, last, drain


def each(start, stop, *steps):
    def body(t, _):
        for s in steps:
            s(t)
        return 0
    lax.fori_loop(start, stop, body, 0)


def tail_kernel(n, L, D, slots, blocks, owner, gmix_h, z_h, acts_h, gsum_h, weights_h, gout_h, gup_h, gdn_h,
                obs_ref, wqo_h, basis_ref, eye_ref, sums_ref,
                dense_out, mixer_out, small_out, gin_h,
                gmix, z, acts, gsum, mix, src, tiles, glow, gbias, tmp, con, basist, wq_ref,
                fc0, fc1, fv0, fv1, fu0, fu1, fa0, fa1, small_one, small_two,
                loads, send, recv_c, recv_v, recv_u, recv_a, small_send, small_recv):
    sizes, here = roles()
    ndp, nmode = lax.axis_size("dp"), lax.axis_size("mode")
    dp, mode = lax.axis_index("dp"), lax.axis_index("mode")
    na = sizes["a"]
    per = slots // nmode
    heads = 8
    pieces = ndp // heads
    depth = 64 // pieces
    rows = con.shape[1]
    size = con.shape[0] * rows // blocks

    def load(i, a, b):
        return pltpu.make_async_copy(a, b, loads.at[i])
    firsts = [load(0, gmix_h, gmix), load(1, z_h, z), load(2, weights_h, mix)]
    later = [load(3, acts_h, acts), load(4, gsum_h, gsum), load(18, wqo_h.at[pl.ds(0, D)], wq_ref)]
    grads = []
    start = D
    for i, ref in enumerate((gout_h, gup_h, gdn_h)):
        for c in range(D // 128):
            grads.append(load(5 + i * 4 + c, ref.at[:, pl.ds(c * 128, 128)], src.at[c, pl.ds(start, ref.shape[0]), :]))
        start += ref.shape[0]
    for c in firsts + later + grads:
        c.start()
    greet()

    send_m, first_m, second_m, third_m, last_m, drain_m = reducer(
        sizes, here, lambda at: mix.at[place_of(sizes, at)], fc1, fv1, fu1, fa1, mixer_out,
        send.at[1], recv_c.at[1], recv_v.at[1], recv_u.at[1], recv_a.at[1])

    def con_at(at):
        p, m = place_of(sizes, at)
        return con.at[p * nmode + m]
    send_d, first_d, second_d, third_d, last_d, drain_d = reducer(
        sizes, here, con_at, fc0, fv0, fu0, fa0, dense_out,
        send.at[0], recv_c.at[0], recv_v.at[0], recv_u.at[0], recv_a.at[0])

    basist[...] = basis_ref[...].astype(F32).T.astype(BF)
    firsts[0].wait()

    def spectra(w):
        part = pl.ds(pl.multiple_of(w * L, 32), L)
        spread_rows(tiles, w, slots, n, gmix[part, :].astype(F32))
    each(0, n, spectra)
    firsts[1].wait()
    firsts[2].wait()

    def mix_slots(places):
        taken = []
        for m, jl, h in places:
            y = tiles[h, pl.ds(pl.multiple_of((m * per + jl) * n, n), n), :]
            both = jnp.concatenate([y, swap_halves(y) * sign_lanes(n, 1.0, -1.0)], 0).astype(BF)
            part = pl.ds(pl.multiple_of(jl * depth, depth), depth)
            x = z[h, pl.ds(pl.multiple_of((m * per + jl) * 2 * n, 2 * n), 2 * n), :]
            taken.append((both, head_weights(mix, h, pieces, m, part), x))
        products = [(dot(both, w, NT), dot(x, both, TN).astype(BF)) for both, w, x in taken]
        for (m, jl, h), (x, g) in zip(places, products):
            part = pl.ds(pl.multiple_of(jl * depth, depth), depth)
            tiles[h, pl.ds(pl.multiple_of((m * per + jl) * n, n), n), :] = jnp.concatenate([x[:n], x[n:]], 1)
            for q in range(pieces):
                mix[h * pieces + q, m, part, :] = g[q * depth:(q + 1) * depth]

    if pieces == 1:
        def mix_shard(at):
            p, m = place_of(sizes, at)

            for at in range(0, per, JOIN):
                mix_slots([(m, jl, p) for jl in range(at, min(at + JOIN, per))])

        def feed(t, d):
            def pair(e):
                other = move(sizes, move(sizes, move(sizes, partner_of(here), "a", t + 1), "u", e), "v", d)
                mix_shard(other)
                send_m(other).start()
                mix_shard(move(sizes, move(sizes, move(sizes, here, "a", t + 1), "u", e), "v", d))
            each(0, sizes["u"], pair)
        for d in range(1, sizes["v"]):
            each(0, na, lambda t: feed(t, d))
        each(0, na, first_m)
        each(0, na, lambda t: feed(t, 0))
    else:
        def mix_mode(m):
            def slot(jl, _):
                mix_slots([(m, jl, h) for h in range(heads)])
                return 0
            lax.fori_loop(0, per, slot, 0, unroll=2)

        def mode_at(i, core):
            return lax.rem(mode // 2 + 1 + i, nmode // 2) * 2 + core

        def other_modes(i):
            m = mode_at(i, 1 - here["c"])
            mix_mode(m)

            def hand(p):
                half = sizes["u"]
                b, y = lax.rem(p, half), m // 2
                core = 1 - here["c"]
                send_m({"a": p // half, "u": jnp.where(core == 0, b, y), "v": jnp.where(core == 0, y, b), "c": core}).start()
            each(0, ndp, hand)
        each(0, nmode // 2, other_modes)
        each(0, nmode // 2, lambda i: mix_mode(mode_at(i, here["c"])))
        each(0, na, first_m)

    gbias[...] = jnp.zeros_like(gbias)

    def query(w):
        part = pl.ds(pl.multiple_of(w * L, 32), L)
        g = dot(basist[...], gather_rows(tiles, w, slots, n))
        glow[part, :] = g.astype(BF)
        gbias[...] += functools.reduce(lambda p, q: p + q, [g[i * 8:(i + 1) * 8] for i in range(L // 8)])
    each(0, n, query)

    for k, sums in ((0, gbias[...]), (4, sums_ref[0:8, :])):
        total = jnp.sum(sums, axis=0, keepdims=True)
        for c in range(D // 128):
            small_one[mode, k + c:k + c + 1, :] = total[:, c * 128:(c + 1) * 128]
    for k in range(20):
        small_one[mode, 8 + k:9 + k, :] = jnp.sum(sums_ref[8 + 8 * k:16 + 8 * k, 0:128], axis=0, keepdims=True)
    small_one[mode, 28:32, :] = jnp.zeros((4, 128), F32)

    def small_copy(buffer, axis, index, count, d, base):
        return pltpu.make_async_remote_copy(
            src_ref=buffer.at[index], dst_ref=buffer.at[index], send_sem=small_send.at[base + d - 1], recv_sem=small_recv.at[base + d - 1],
            device_id={**{"dp": dp, "mode": mode}, axis: lax.rem(index + d, count)}, device_id_type=MESH)
    ones = [small_copy(small_one, "mode", mode, nmode, d, 0) for d in range(1, nmode)]
    twos = [small_copy(small_two, "dp", dp, ndp, d, nmode - 1) for d in range(1, ndp)]
    for c in ones:
        c.start()

    for c in later:
        c.wait()
    g = dot(acts[...], glow[...], TN)
    for c in range(D // 128):
        src[c, 0:D, :] = g[:, c * 128:(c + 1) * 128]
    each(0, na // 2, second_m)
    for c in grads:
        c.wait()

    per_shard = rows // size
    join = 4 if per_shard % 4 == 0 else 1
    units = per_shard // join

    def pick(s):
        for k in range(units):
            for c in range(D // 128):
                for i in range(join):
                    row = owner[(s * units + k) * join + i] * size
                    tmp[c, i * size:(i + 1) * size, :] = src[c, pl.ds(row, size), :]
                part = slice(k * join * size, (k + 1) * join * size)
                con[s, part, c * 128:(c + 1) * 128] = tmp[c, 0:join * size, :].astype(BF)
    shards = con.shape[0]
    each(0, shards // 2, pick)
    each(na // 2, na, second_m)
    each(0, na // 2, third_m)
    each(shards // 2, shards, pick)

    def hand_line(t):
        other = partner_of(here)
        for d in list(range(1, sizes["v"])) + [0]:
            for e in range(sizes["u"]):
                send_d(move(sizes, move(sizes, move(sizes, other, "a", t + 1), "u", e), "v", d)).start()
    each(0, na, hand_line)
    each(na // 2, na - 1, third_m)

    def input_grad(w):
        part = pl.ds(pl.multiple_of(w * L, 32), L)
        row = obs_ref[pl.ds(w, 1), :].astype(F32)
        mask = dot((eye_ref[...] * row).astype(BF), jnp.ones((L, 128), BF))
        g = gsum[part, :] + dot(glow[part, :], wq_ref[...], NT)
        for c in range(D // 128):
            gsum[part, c * 128:(c + 1) * 128] = g[:, c * 128:(c + 1) * 128] * mask
    for c in ones:
        c.wait()
    small_two[dp] = functools.reduce(lambda p, q: p + q, [small_one[i] for i in range(nmode)])
    for c in twos:
        c.start()
    each(0, na, first_d)
    each(0, n, input_grad)
    result = load(17, gsum, gin_h)
    result.start()
    each(0, 1, second_d)
    each(1, na - 1, second_d, lambda t: third_d(t - 1))
    last_m()
    second_d(na - 1)
    third_d(na - 2)
    last_d()
    for c in twos:
        c.wait()
    small_out[...] = functools.reduce(lambda p, q: p + q, [small_two[i] for i in range(ndp)])
    drain_m()
    drain_d()
    result.wait()


def tail(gmix, z, acts, gsum, observed, wqo, basis, weights, gout, gup, gdn, sums, owner_list, shard_rows):
    n, L = observed.shape
    D = acts.shape[1]
    slots = basis.shape[0] // 2
    ndp, nmode, mixer_rows = weights.shape[:3]
    nd = ndp * nmode
    total = nd * shard_rows
    half = nmode // 2
    na = ndp // half
    group = nd // 2
    anywhere = pl.BlockSpec(memory_space=pl.ANY)
    vmem = pl.BlockSpec(memory_space=pltpu.VMEM)
    shapes = ((shard_rows, D), (mixer_rows, 128))
    counts = (group, na * half * (half - 1), na * (half - 1), na - 1)
    sem = lambda *s: pltpu.SemaphoreType.DMA(s)
    return pl.pallas_call(
        functools.partial(tail_kernel, n, L, D, slots, owner_list.shape[0]),
        out_shape=(
            jax.ShapeDtypeStruct(shapes[0], F32), jax.ShapeDtypeStruct(shapes[1], F32), jax.ShapeDtypeStruct((32, 128), F32),
            jax.ShapeDtypeStruct((n * L, D), F32),
        ),
        in_specs=[pl.BlockSpec(memory_space=pltpu.SMEM)] + [anywhere] * 8 + [
            vmem, anywhere, vmem, vmem, vmem],
        out_specs=(vmem, vmem, vmem, anywhere),
        scratch_shapes=[
            pltpu.VMEM((n * L, D), BF),
            pltpu.VMEM(z.shape, BF),
            pltpu.VMEM((n * L, D), BF),
            pltpu.VMEM((n * L, D), F32),
            pltpu.VMEM(weights.shape, BF),
            pltpu.VMEM((D // 128, total + 8, 128), F32),
            pltpu.VMEM((8, slots * n, 128), F32),
            pltpu.VMEM((n * L, D), BF),
            pltpu.VMEM((8, D), F32),
            pltpu.VMEM((D // 128, 80, 128), F32),
            pltpu.VMEM((nd, shard_rows, D), BF),
            pltpu.VMEM((L, 2 * slots), BF),
            pltpu.VMEM((D, D), BF),
        ] + [pltpu.VMEM((count,) + s, BF) for count in counts for s in shapes] + [
            pltpu.VMEM((nmode, 32, 128), F32), pltpu.VMEM((ndp, 32, 128), F32),
            sem(19), sem(2, 4), sem(2, counts[0]), sem(2, counts[1]), sem(2, counts[2]), sem(2, counts[3]),
            sem(ndp + nmode - 2), sem(ndp + nmode - 2),
        ],
        compiler_params=pltpu.CompilerParams(collective_id=1, has_side_effects=True, vmem_limit_bytes=62 * 1024 * 1024),
        name="tail",
    )(owner_list, gmix, z, acts, gsum, weights, gout, gup, gdn, observed, wqo, basis, np.eye(L, dtype=np.float32), sums)


def gatherer(sizes, here, slot_of, whole_of, send, send_a, recv):
    na, nu, nv = sizes["a"], sizes["u"], sizes["v"]

    def spot(at):
        dp, mode = place_of(sizes, at)
        return dp * sizes["v"] * 2 + mode

    def copy(at, to, sem):
        ref = slot_of(at)
        return pltpu.make_async_remote_copy(
            src_ref=ref, dst_ref=ref, send_sem=sem, recv_sem=recv.at[spot(at)],
            device_id=device_of(sizes, to), device_id_type=MESH)

    def onward(at, axes):
        for axis, stage in axes:
            for d in range(1, sizes[axis]):
                copy(at, move(sizes, here, axis, d), send.at[stage]).start()
        copy(at, partner_of(here), send.at[2]).start()

    def hop(k, side):
        first, to = here["a"] - side * k, here["a"] + side
        there = (first >= 0) & (first < na) & (to >= 0) & (to < na)
        way = 0 if side == 1 else 1
        inside = lambda x: jnp.clip(x, 0, na - 1)
        return there, lambda: copy({**here, "a": inside(first)}, {**here, "a": inside(to)}, send_a.at[way, k])

    def hops(k, side):
        there, make = hop(k, side)
        pl.when(there)(lambda: make().start())

    def arrived(at):
        copy(at, here, send.at[0]).wait_recv()
        return at

    def lines(k, act):
        for side in ((1, -1) if k else (1,)):
            to = here["a"] - side * k
            pl.when((to >= 0) & (to < na))(lambda side=side, to=to: act({**here, "a": to}, side))

    def start():
        for side in (1, -1):
            hops(0, side)
        onward(here, (("u", 0), ("v", 1)))

    def line(k, then=lambda at: None):
        def act(at, side):
            arrived(at)
            hops(k, side)
            onward(at, (("u", 0), ("v", 1)))
            then(at)
        lines(k, act)

    def second(k, then=lambda at: None):
        def act(at, side):
            for d in range(1, nu):
                to = arrived(move(sizes, at, "u", d))
                onward(to, (("v", 1),))
                then(to)
        lines(k, act)

    def third(k, then=lambda at: None):
        def act(at, side):
            for e in range(nu):
                for d in range(1, nv):
                    to = arrived(move(sizes, move(sizes, at, "u", e), "v", d))
                    onward(to, ())
                    then(to)
        lines(k, act)

    def partner(t, then=lambda at: None):
        other = partner_of(here)
        for e in range(nu):
            for d in range(nv):
                then(arrived(move(sizes, move(sizes, move(sizes, other, "a", t), "u", e), "v", d)))

    def drain():
        for stage, count in ((0, na * (nu - 1)), (1, na * nu * (nv - 1)), (2, na * nu * nv)):
            ref = whole_of(count)
            pltpu.make_async_copy(ref, ref, send.at[stage]).wait()
        for k in range(na):
            for side in (1, -1):
                there, make = hop(k, side)
                pl.when(there)(lambda make=make: make().wait_send())

    return start, line, second, third, partner, drain


def head_kernel(n, L, D, slots, blocks, restore, in_h, dense_ref, mixer_ref, obs_ref, bias_ref, basis_ref, inv_ref, eye_ref,
                acts_h, z_h, sig_h, wqo_h, wup_h, wdn_h, weights_h,
                inputs, acts, query, tiles, z, sig, buf, src, table, mix, tmp,
                loads, send, send_a, recv):
    sizes, here = roles()
    ndp, nmode = lax.axis_size("dp"), lax.axis_size("mode")
    dp, mode = lax.axis_index("dp"), lax.axis_index("mode")
    na = sizes["a"]
    per = slots // nmode
    heads = 8
    pieces = ndp // heads
    depth = 64 // pieces
    rows = buf.shape[1]
    total = buf.shape[0] * rows
    size = total // blocks
    join = 4
    units = blocks // join

    def load(i, a, b):
        return pltpu.make_async_copy(a, b, loads.at[i])
    load_in = load(0, in_h, inputs)
    load_in.start()
    buf[dp * nmode + mode] = dense_ref[...].astype(BF)
    mix[dp, mode] = mixer_ref[...].astype(BF)
    greet()

    def buf_at(at):
        p, m = place_of(sizes, at)
        return buf.at[p * nmode + m]

    start_d, line_d, second_d, third_d, partner_d, drain_d = gatherer(
        sizes, here, buf_at, lambda count: buf.at[pl.ds(0, count)], send.at[0], send_a.at[0], recv.at[0])
    mix_at = lambda at: mix.at[place_of(sizes, at)]

    def mix_many(count):
        if count % nmode == 0:
            return mix.at[pl.ds(0, count // nmode)]
        return mix.at[pl.ds(0, count), 0] if count <= ndp else mix.at[pl.ds(0, count // 2), pl.ds(0, 2)]
    start_m, line_m, second_m, third_m, partner_m, drain_m = gatherer(
        sizes, here, mix_at, mix_many, send.at[1], send_a.at[1], recv.at[1])
    start_d()

    def widen(at):
        p, m = place_of(sizes, at)
        k = p * nmode + m
        for c in range(D // 128):
            src[c, pl.ds(k * rows, rows), :] = buf[k, :, c * 128:(c + 1) * 128].astype(F32)
    widen(here)
    load_in.wait()

    def mask(w):
        row = obs_ref[pl.ds(w, 1), :].astype(F32)
        part = pl.ds(pl.multiple_of(w * L, 32), L)
        acts[part, :] = dot((eye_ref[...] * row).astype(BF), inputs[part, :]).astype(BF)
    each(0, n, mask)
    outs = [load(1, acts, acts_h)]
    outs[0].start()
    for k in range(na + 2):
        if k < na - 1:
            line_d(k + 1, widen)
        if k < na:
            second_d(k, widen)
        if 1 <= k <= na:
            third_d(k - 1, widen)
        if k == 0:
            start_m()
        if 1 <= k < na:
            line_m(k)
        if 1 <= k <= na:
            second_m(k - 1)
        if 2 <= k <= na:
            third_m(k - 2)
    each(0, na, lambda t: partner_d(t, widen))

    def pick(p):
        for c in range(D // 128):
            for i in range(join):
                tmp[c, i * size:(i + 1) * size, :] = src[c, pl.ds(restore[p * join + i] * size, size), :]
            part = pl.ds(pl.multiple_of(p * join * size, 16), join * size)
            table[part, c * 128:(c + 1) * 128] = tmp[c].astype(BF)
    early = -(-D // (join * size))
    each(0, early, pick)
    T = 384

    def project(i):
        part = pl.ds(pl.multiple_of(i * T, T), T)
        query[part, :] = (dot(acts[part, :], table[0:D, :]) + bias_ref[:, 0:D]).astype(BF)

    def spectra(w):
        part = pl.ds(pl.multiple_of(w * L, 32), L)
        spread_rows(tiles, w, slots, n, dot(basis_ref[...], query[part, :]))

    work = [lambda i=i: project(i) for i in range(n * L // T)]
    work += [lambda i=i: each(i * n // 4, (i + 1) * n // 4, spectra) for i in range(4)]
    cuts = [early + (units - early) * i // 4 for i in range(5)]
    work += [lambda i=i: each(cuts[i], cuts[i + 1], pick) for i in range(4)]
    for i, w in enumerate(work):
        w()
        if i == 1:
            third_m(na - 1)
    at = 0
    for i, ref in enumerate((wqo_h, wup_h, wdn_h)):
        outs.append(load(2 + i, table.at[pl.ds(at, ref.shape[0])], ref))
        outs[-1].start()
        at += ref.shape[0]
    each(0, na, partner_m)
    outs.append(load(5, mix, weights_h))
    outs[-1].start()

    def slot(j, _):
        m, jl = j // per, lax.rem(j, per)
        at = pl.ds(pl.multiple_of(j * n, n), n)
        part = pl.ds(pl.multiple_of(jl * depth, depth), depth)
        for h in range(heads):
            x = tiles[h, at, :]
            both = jnp.concatenate([x, swap_halves(x)], 0)[:, :64].astype(BF)
            z[h, pl.ds(pl.multiple_of(j * 2 * n, 2 * n), 2 * n), :] = both
            y = dot(both, head_weights(mix, h, pieces, m, part))
            tiles[h, at, :] = y[:n] + swap_halves(y[n:]) * sign_lanes(n, -1.0, 1.0)
        return 0
    lax.fori_loop(0, slots, slot, 0, unroll=4)
    outs.append(load(6, z, z_h))
    outs[-1].start()

    def signal(w):
        part = pl.ds(pl.multiple_of(w * L, 32), L)
        sig[part, :] = dot(inv_ref[...], gather_rows(tiles, w, slots, n)).astype(BF)
    each(0, n, signal)
    outs.append(load(7, sig, sig_h))
    outs[-1].start()
    drain_d()
    drain_m()
    for o in outs:
        o.wait()


def head(inputs, observed, dense, mixer, restore, bias, basis, inv, ff):
    n, L, D = inputs.shape
    slots = basis.shape[0] // 2
    ndp, nmode = lax.axis_size("dp"), lax.axis_size("mode")
    nd = ndp * nmode
    rows, mixer_rows = dense.shape[0], mixer.shape[0]
    anywhere = pl.BlockSpec(memory_space=pl.ANY)
    vmem = pl.BlockSpec(memory_space=pltpu.VMEM)
    sem = lambda *s: pltpu.SemaphoreType.DMA(s)
    tokens = n * L
    return pl.pallas_call(
        functools.partial(head_kernel, n, L, D, slots, restore.shape[0]),
        out_shape=(
            jax.ShapeDtypeStruct((tokens, D), BF),
            jax.ShapeDtypeStruct((8, 2 * slots * n, 64), BF),
            jax.ShapeDtypeStruct((tokens, D), BF),
            jax.ShapeDtypeStruct((2 * D, D), BF),
            jax.ShapeDtypeStruct((ff, D), BF),
            jax.ShapeDtypeStruct((ff, D), BF),
            jax.ShapeDtypeStruct((ndp, nmode, mixer_rows, 128), BF),
        ),
        in_specs=[pl.BlockSpec(memory_space=pltpu.SMEM), anywhere] + [vmem] * 7,
        out_specs=(anywhere,) * 7,
        scratch_shapes=[
            pltpu.VMEM((tokens, D), BF),
            pltpu.VMEM((tokens, D), BF),
            pltpu.VMEM((tokens, D), BF),
            pltpu.VMEM((8, slots * n, 128), F32),
            pltpu.VMEM((8, 2 * slots * n, 64), BF),
            pltpu.VMEM((tokens, D), BF),
            pltpu.VMEM((nd, rows, D), BF),
            pltpu.VMEM((D // 128, nd * rows + 8, 128), F32),
            pltpu.VMEM((nd * rows, D), BF),
            pltpu.VMEM((ndp, nmode, mixer_rows, 128), BF),
            pltpu.VMEM((D // 128, 4 * (nd * rows // restore.shape[0]), 128), F32),
            sem(8), sem(2, 3), sem(2, 2, ndp // (nmode // 2)), sem(2, nd),
        ],
        compiler_params=pltpu.CompilerParams(collective_id=0, has_side_effects=True, vmem_limit_bytes=62 * 1024 * 1024),
        name="head",
    )(restore, inputs.reshape(tokens, D), dense, mixer, observed, bias, basis, inv, np.eye(L, dtype=np.float32))


def adam_terms(weight, gradient, moment, second, step_rate):
    moment_new = BETA_ONE * moment + (1.0 - BETA_ONE) * gradient
    second_new = BETA_TWO * second + (1.0 - BETA_TWO) * gradient * gradient
    scaled_m = moment_new * (1.0 / (1.0 - BETA_ONE**STEP))
    scaled_v = second_new * (1.0 / (1.0 - BETA_TWO**STEP))
    weight_new = weight - step_rate * (scaled_m / (jnp.sqrt(scaled_v) + ADAM_EPS) + DECAY_RATE * weight)
    return moment_new, second_new, weight_new


def update_kernel(*refs):
    dense, mixer, passed = refs[:4], refs[4:8], refs[8]
    dense_out, mixer_out, passed_out, sem = refs[9:12], refs[12:15], refs[15], refs[16]
    copy = pltpu.make_async_copy(passed, passed_out, sem)
    copy.start()
    for ins, outs, rate in ((dense, dense_out, RATE_DENSE), (mixer, mixer_out, RATE_MIXER)):
        for ref, value in zip(outs, adam_terms(*(x[...] for x in ins), rate)):
            ref[...] = value
    copy.wait()


def update(dense, mixer, passed):
    vmem = pl.BlockSpec(memory_space=pltpu.VMEM)
    anywhere = pl.BlockSpec(memory_space=pl.ANY)
    like = lambda x: jax.ShapeDtypeStruct(x.shape, x.dtype)
    return pl.pallas_call(
        update_kernel,
        out_shape=(like(dense[0]),) * 3 + (like(mixer[0]),) * 3 + (like(passed),),
        in_specs=[vmem] * 8 + [anywhere],
        out_specs=(vmem,) * 6 + (anywhere,),
        scratch_shapes=[pltpu.SemaphoreType.DMA],
        compiler_params=pltpu.CompilerParams(vmem_limit_bytes=62 * 1024 * 1024),
        name="update",
    )(*dense, *mixer, passed)


def forward_table(mode_index, length):
    slots = mode_index.shape[0]
    row = jnp.arange(2 * slots, dtype=jnp.int32)
    mode = jnp.concatenate([mode_index, mode_index])
    turn = (mode[:, None] * jnp.arange(length, dtype=jnp.int32)[None, :] + (row >= slots)[:, None] * (length // 4)) % length
    return jnp.cos(turn.astype(F32) * (2.0 * math.pi / length)).astype(BF)


def inverse_table(slots, length):
    turn = np.arange(length)[:, None] * np.arange(slots)[None, :] % length
    angle = turn * (2.0 * np.pi / length)
    scale = np.where(np.arange(slots) == 0, 1.0, 2.0) / length
    return np.concatenate([np.cos(angle) * scale, -np.sin(angle) * scale], 1).astype(np.float32).astype(BF)


def shards(
    inputs,
    observed,
    out_grad,
    mode_index,
    owner_list,
    dense_master,
    dense_first,
    dense_second,
    mixer_master,
    mixer_first,
    mixer_second,
    small_master,
    small_first,
    small_second,
):
    ndp, nmode = lax.axis_size("dp"), lax.axis_size("mode")
    length, width = inputs.shape[1:]
    slots = mode_index.shape[0]
    hidden = (dense_master.shape[0] * ndp * nmode - 2 * width) // 2
    basis = forward_table(mode_index, length)
    inv = inverse_table(slots, length)
    small_row = small_master[None]
    places = jnp.arange(owner_list.shape[0], dtype=jnp.int32)
    restore = jnp.sum(jnp.where(owner_list[None, :] == places[:, None], places[None, :], 0), axis=1)
    acts, spectra, sig, wqo, wup, wdn, weights = head(
        inputs, observed, dense_master, mixer_master.reshape(-1, mixer_master.shape[2]), restore, small_row,
        basis, inv, hidden,
    )
    output, grad_summed, grad_mixed, g_out, g_up, g_down, sums = middle(
        small_master, acts.reshape(inputs.shape), sig.reshape(inputs.shape), out_grad, wqo, wup, wdn,
        small_row, np.ascontiguousarray(inv.T),
    )
    dense_mine, mixer_mine, small_all, input_grad = tail(
        grad_mixed.reshape(-1, width), spectra, acts, grad_summed.reshape(-1, width), observed, wqo, basis, weights,
        g_out, g_up, g_down, sums, owner_list, dense_master.shape[0],
    )
    small_total = jnp.concatenate([small_all[:8].reshape(-1), jnp.sum(small_all[8:28], axis=1)])
    flat = lambda x: x.reshape(-1, x.shape[-1])
    dense_first_new, dense_second_new, dense_new, mixer_first_new, mixer_second_new, mixer_new, input_grad = update(
        (dense_master, dense_mine, dense_first, dense_second),
        (flat(mixer_master), mixer_mine, flat(mixer_first), flat(mixer_second)),
        input_grad,
    )
    mixer_first_new, mixer_second_new, mixer_new = (
        x.reshape(mixer_master.shape) for x in (mixer_first_new, mixer_second_new, mixer_new)
    )
    small_first_new, small_second_new, small_new = adam_terms(
        small_master, small_total, small_first, small_second, RATE_SMALL
    )
    return (
        output,
        input_grad.reshape(inputs.shape),
        dense_first_new,
        dense_second_new,
        dense_new,
        mixer_first_new,
        mixer_second_new,
        mixer_new,
        small_first_new,
        small_second_new,
        small_new,
        small_total[width : 2 * width],
    )


def solution(mesh):
    placed = (
        P(("dp", "mode"), None, None),
        P(("dp", "mode"), None),
        P(("dp", "mode"), None, None),
        P(),
        P(),
        P(("dp", "mode"), None),
        P(("dp", "mode"), None),
        P(("dp", "mode"), None),
        P("mode", "dp", None),
        P("mode", "dp", None),
        P("mode", "dp", None),
        P(),
        P(),
        P(),
    )
    return jax.shard_map(
        shards,
        mesh=mesh,
        in_specs=placed,
        out_specs=(
            P(("dp", "mode"), None, None),
            P(("dp", "mode"), None, None),
            P(("dp", "mode"), None),
            P(("dp", "mode"), None),
            P(("dp", "mode"), None),
            P("mode", "dp", None),
            P("mode", "dp", None),
            P("mode", "dp", None),
            P(),
            P(),
            P(),
            P(),
        ),
        check_vma=False,
    )
```

```python
import functools
import math

import jax
import jax.numpy as jnp
import numpy as np
from jax import lax
from jax.experimental import pallas as pl
from jax.experimental.pallas import tpu as pltpu
from jax.sharding import PartitionSpec as P

STEP = 10
BETA_ONE = 0.9
BETA_TWO = 0.95
ADAM_EPS = 1e-08
DECAY_RATE = 0.1
RATE_DENSE = 0.03
RATE_MIXER = 0.03
RATE_SMALL = 0.5

KERNEL_SIZES = (7, 12, 14, 24, 48)
ODD = (7, 3, 7, 3, 3)
LOG2E = 1.4426950408889634
BF = jnp.bfloat16
F32 = jnp.float32
NT = (((1,), (1,)), ((), ()))
NN = (((1,), (0,)), ((), ()))
TN = (((0,), (0,)), ((), ()))


def dot(a, b, dims=NN):
    return lax.dot_general(a, b, dims, preferred_element_type=F32)


def average_counts(length):
    tables = []
    t = np.arange(length)
    for size in KERNEL_SIZES:
        u = np.clip(t[:, None] - (size - 1) // 2 + np.arange(size)[None, :], 0, length - 1)
        tables.append((u[:, :, None] == t[None, None, :]).sum(1) * (ODD[len(tables)] / size))
    return np.stack(tables).astype(np.float32)


def gelu_parts(h):
    z = jnp.abs(h)
    e = jnp.exp2(h * h * (-0.5 * LOG2E))
    t = 1.0 / (1.0 + (0.3275911 * math.sqrt(0.5)) * z)
    poly = t * (0.5 * 0.254829592 + t * (-0.5 * 0.284496736 + t * (0.5 * 1.421413741 + t * (-0.5 * 1.453152027 + t * (0.5 * 1.061405429)))))
    tail = poly * e
    big = jnp.where(h < 0, tail, 1.0 - tail)
    return big, e * (1.0 / math.sqrt(2 * math.pi))


def middle_kernel(W, L, D, FF, steps,
                  mix_ref, acts_ref, sig_ref, og_ref, wq_ref, wup_ref, wdn_ref, bias_ref, invt_ref, cnt_ref, cntt_ref,
                  out_ref, gsum_ref, gmix_ref, gw_ref, gup_ref, gdn_ref, small_ref,
                  vs, base, avg1, c1, v1, active, dgelu, first, flow, gb, ghid, glow, avg2, stk, accs, accb, hs, wg, wsem):
    step = pl.program_id(0)
    T = W * L
    CH = 16
    CC = 256
    nc = D // CC
    nr = L // CH
    FT = 512

    @pl.when(step == 0)
    def _():
        vs[...] = jnp.zeros_like(vs)
        stk[...] = jnp.zeros_like(stk)
        accs[...] = jnp.zeros_like(accs)
        accb[...] = jnp.zeros_like(accb)
        gw_ref[...] = jnp.zeros_like(gw_ref)

    def fold(x):
        y = x[:, 0:128]
        for i in range(1, CC // 128):
            y = y + x[:, i * 128:(i + 1) * 128]
        return y[0:8] + y[8:16]

    def scaled_shares(v, base_at):
        p = [mix_ref[2 * D + base_at + k] for k in range(10)]
        logits = [((p[k] - p[4]) * LOG2E) * v + (p[5 + k] - p[9]) * LOG2E for k in range(4)]
        top = jnp.maximum(functools.reduce(jnp.maximum, logits), 0.0)
        es = [jnp.exp2(l - top) for l in logits] + [jnp.exp2(-top)]
        r = 1.0 / functools.reduce(lambda a, b: a + b, es)
        scale = {7: r * (1.0 / 7.0), 3: r * (1.0 / 3.0)}
        return [e * scale[o] for e, o in zip(es, ODD)]

    def backward(v, g, cs, avs, mean, base_at, store):
        means = {7: 7.0 * mean, 3: 3.0 * mean}
        total = None
        for k in range(5):
            cg = cs[k] * g
            store(k, cg)
            if k < 4:
                t = cg * (means[ODD[k]] - avs[k])
                term = (mix_ref[2 * D + base_at + k] - mix_ref[2 * D + base_at + 4]) * t
                total = term if total is None else total + term
                accs[base_at + k] += fold(t * v)
                accs[base_at + 5 + k] += fold(t)
        return total

    bias = row_of(bias_ref, D, D)
    sig = sig_ref[...].reshape(T, D)
    base[...] = dot(sig, wq_ref[D:2 * D, :])

    def cut(w, source):
        for i in range(nr):
            for c in range(nc):
                cols = slice(c * CC, (c + 1) * CC)
                v = source(w, i, cols)
                hi = v.astype(BF)
                vs[w % 2, i * CH:(i + 1) * CH, cols] = hi
                vs[w % 2, L + i * CH:L + (i + 1) * CH, cols] = (v - hi.astype(F32)).astype(BF)

    def summed(w, i, cols):
        rows = slice(w * L + i * CH, w * L + (i + 1) * CH)
        v = base[rows, cols] + acts_ref[w, i * CH:(i + 1) * CH, cols].astype(F32) + bias[:, cols]
        v1[rows, cols] = v
        return v

    def averages_one(w):
        cut(w, summed)
        avg1[w * 5 * L:(w + 1) * 5 * L, :] = dot(cnt_ref[...], vs[w % 2])

    def decompose_one(w):
        for i in range(nr):
            for c in range(nc):
                cols = slice(c * CC, (c + 1) * CC)
                rows = slice(w * L + i * CH, w * L + (i + 1) * CH)
                v = v1[rows, cols]
                cs = scaled_shares(v, 0)
                mean = None
                for k in range(5):
                    at = slice((w * 5 + k) * L + i * CH, (w * 5 + k) * L + (i + 1) * CH)
                    u = cs[k] * avg1[at, cols]
                    c1[at, cols] = cs[k]
                    mean = u if mean is None else mean + u
                f = v - mean
                first[rows, cols] = f
                flow[pl.ds(pl.multiple_of(step * T + w * L + i * CH, CH), CH), cols] = f.astype(BF)

    averages_one(0)
    for w in range(W):
        if w + 1 < W:
            averages_one(w + 1)
        decompose_one(w)

    here_t = pl.ds(pl.multiple_of(step * T, CH), T)
    base[...] = first[...]

    def up(n):
        return dot(flow[here_t, :], wup_ref[n * FT:(n + 1) * FT, :], NT)

    tiles = FF // FT
    hs[0] = up(0)
    for n in range(tiles + 1):
        if n + 1 < tiles:
            hs[(n + 1) % 2] = up(n + 1)
        if n < tiles:
            h = hs[n % 2]
            big, small = gelu_parts(h)
            active[here_t, n * FT:(n + 1) * FT] = (h * big).astype(BF)
            dgelu[:, n * FT:(n + 1) * FT] = (big + h * small).astype(BF)
        if n:
            base[...] += dot(active[here_t, (n - 1) * FT:n * FT], wdn_ref[(n - 1) * FT:n * FT, :])

    def branch(w, i, cols):
        return base[w * L + i * CH:w * L + (i + 1) * CH, cols]

    def averages_two(w):
        cut(w, branch)
        avg2[w % 2] = dot(cnt_ref[...], vs[w % 2])

    def keep_at(w, i, cols):
        def keep(k, cg):
            stk[w % 2, k * L + i * CH:k * L + (i + 1) * CH, cols] = cg.astype(BF)
        return keep

    def decompose_two(w):
        for i in range(nr):
            for c in range(nc):
                cols = slice(c * CC, (c + 1) * CC)
                rows = slice(w * L + i * CH, w * L + (i + 1) * CH)
                here = slice(i * CH, (i + 1) * CH)
                v = base[rows, cols]
                cs = scaled_shares(v, 10)
                avs = [avg2[w % 2, k * L + i * CH:k * L + (i + 1) * CH, cols] for k in range(5)]
                mean = functools.reduce(lambda a, b: a + b, [c_ * a_ for c_, a_ in zip(cs, avs)])
                out_ref[w, here, cols] = (v - mean).astype(BF)
                g = og_ref[w, here, cols].astype(F32)
                base[rows, cols] = g + backward(v, g, cs, avs, mean, 10, keep_at(w, i, cols))

    def back_two(w):
        rows = slice(w * L, (w + 1) * L)
        gs = base[rows, :] - dot(cntt_ref[...], stk[w % 2])
        base[rows, :] = gs
        gb[pl.ds(pl.multiple_of(step * T + w * L, 32), L), :] = gs.astype(BF)

    averages_two(0)
    for w in range(W):
        if w + 1 < W:
            averages_two(w + 1)
        decompose_two(w)
        if w:
            back_two(w - 1)
    back_two(W - 1)

    def down(n):
        return dot(gb[here_t, :], wdn_ref[n * FT:(n + 1) * FT, :], NT)

    hs[0] = down(0)
    for n in range(tiles + 1):
        if n + 1 < tiles:
            hs[(n + 1) % 2] = down(n + 1)
        if n < tiles:
            ghid[here_t, n * FT:(n + 1) * FT] = (hs[n % 2] * dgelu[:, n * FT:(n + 1) * FT].astype(F32)).astype(BF)
        if n:
            base[...] += dot(ghid[here_t, (n - 1) * FT:n * FT], wup_ref[(n - 1) * FT:n * FT, :])

    def decompose_three(w):
        for i in range(nr):
            for c in range(nc):
                cols = slice(c * CC, (c + 1) * CC)
                rows = slice(w * L + i * CH, w * L + (i + 1) * CH)
                v = v1[rows, cols]
                g = base[rows, cols]
                ats = [slice((w * 5 + k) * L + i * CH, (w * 5 + k) * L + (i + 1) * CH) for k in range(5)]
                cs = [c1[at, cols] for at in ats]
                avs = [avg1[at, cols] for at in ats]
                mean = v - first[rows, cols]
                extra = backward(v, g, cs, avs, mean, 0, keep_at(w, i, cols))
                base[rows, cols] = g + extra
                accb[:, cols] += extra[0:8] + extra[8:16]

    def back_three(w):
        rows = slice(w * L, (w + 1) * L)
        gs = base[rows, :] - dot(cntt_ref[...], stk[w % 2])
        gsum_ref[w] = gs
        glow[rows, :] = gs.astype(BF)

    for w in range(W):
        decompose_three(w)
        if w:
            back_three(w - 1)
    back_three(W - 1)

    back = dot(glow[...], wq_ref[D:2 * D, :], NT).astype(BF)
    for w in range(W):
        gmix_ref[w] = dot(invt_ref[...], back[w * L:(w + 1) * L, :]).astype(BF)
    gw_ref[...] += dot(sig, glow[...], TN)

    @pl.when(step == steps - 1)
    def _():
        small_ref[0:8, :] = accb[...]
        for at in (4, 9, 14, 19):
            accs[at] = -(accs[at - 4] + accs[at - 3] + accs[at - 2] + accs[at - 1])
        for k in range(20):
            small_ref[8 + 8 * k:16 + 8 * k, 0:128] = accs[k]
            small_ref[8 + 8 * k:16 + 8 * k, 128:512] = jnp.zeros((8, 384), F32)

        copies = {}
        for n in range(tiles):
            part = slice(n * FT, (n + 1) * FT)
            for i, (left, right, ref) in enumerate(((ghid, flow, gup_ref), (active, gb, gdn_ref))):
                k = (n % 2) * 2 + i
                if n >= 2:
                    copies[n - 2, i].wait()
                wg[k] = dot(left[:, part], right[...], TN)
                copies[n, i] = pltpu.make_async_copy(wg.at[k], ref.at[pl.ds(n * FT, FT)], wsem.at[k])
                copies[n, i].start()
        for n in range(max(tiles - 2, 0), tiles):
            for i in range(2):
                copies[n, i].wait()


def middle(mix, acts, sig, og, wqo, wup, wdn, bias, invt, W=4):
    n, L, D = acts.shape
    FF = wup.shape[0]
    steps = n // W
    T = W * L
    A = average_counts(L)
    cnt = np.zeros((5 * L, 256), np.float32)
    cnt[:, :L] = A.reshape(5 * L, L)
    cnt[:, L:2 * L] = A.reshape(5 * L, L)
    cntt = np.zeros((L, 512), np.float32)
    cntt[:, :5 * L] = A.transpose(2, 0, 1).reshape(L, 5 * L)
    cnt, cntt = (np.asarray(x, BF) for x in (cnt, cntt))
    whole = lambda *s: pl.BlockSpec(s, lambda i: (0,) * len(s), pipeline_mode=pl.Buffered(1))
    anywhere = pl.BlockSpec(memory_space=pl.ANY)
    piece = lambda *s: pl.BlockSpec(s, lambda i: (i,) + (0,) * (len(s) - 1))
    return pl.pallas_call(
        functools.partial(middle_kernel, W, L, D, FF, steps),
        grid=(steps,),
        out_shape=(
            jax.ShapeDtypeStruct((n, L, D), BF),
            jax.ShapeDtypeStruct((n, L, D), F32),
            jax.ShapeDtypeStruct((n, L, D), BF),
            jax.ShapeDtypeStruct((D, D), F32),
            jax.ShapeDtypeStruct((FF, D), F32),
            jax.ShapeDtypeStruct((FF, D), F32),
            jax.ShapeDtypeStruct((168, D), F32),
        ),
        in_specs=[
            pl.BlockSpec(memory_space=pltpu.SMEM),
            piece(W, L, D), piece(W, L, D), piece(W, L, D),
            whole(2 * D, D), whole(FF, D), whole(FF, D), whole(bias.shape[0]), whole(L, L), whole(5 * L, 256), whole(L, 512),
        ],
        out_specs=(
            piece(W, L, D), piece(W, L, D), piece(W, L, D), whole(D, D), anywhere, anywhere, whole(168, D),
        ),
        scratch_shapes=[
            pltpu.VMEM((2, 256, D), BF),
            pltpu.VMEM((T, D), F32),
            pltpu.VMEM((W * 5 * L, D), F32),
            pltpu.VMEM((W * 5 * L, D), F32),
            pltpu.VMEM((T, D), F32),
            pltpu.VMEM((n * L, FF), BF),
            pltpu.VMEM((T, FF), BF),
            pltpu.VMEM((T, D), F32),
            pltpu.VMEM((n * L, D), BF),
            pltpu.VMEM((n * L, D), BF),
            pltpu.VMEM((n * L, FF), BF),
            pltpu.VMEM((T, D), BF),
            pltpu.VMEM((2, 5 * L, D), F32),
            pltpu.VMEM((2, 512, D), BF),
            pltpu.VMEM((20, 8, 128), F32),
            pltpu.VMEM((8, D), F32),
            pltpu.VMEM((2, T, 512), F32),
            pltpu.VMEM((4, 512, D), F32),
            pltpu.SemaphoreType.DMA((4,)),
        ],
        compiler_params=pltpu.CompilerParams(vmem_limit_bytes=60 * 1024 * 1024),
        name="middle",
    )(mix, acts, sig, og, wqo, wup, wdn, bias, invt, cnt, cntt)


def sign_lanes(rows, left, right):
    lane = lax.broadcasted_iota(jnp.int32, (rows, 128), 1)
    return jnp.where(lane < 64, left, right).astype(F32)


def interleave(real, imag, v):
    re, im = real[:, v * 128:(v + 1) * 128], imag[:, v * 128:(v + 1) * 128]
    low = lax.broadcasted_iota(jnp.int32, re.shape, 1) < 64
    return jnp.where(low, re, pltpu.roll(im, 64, 1)), jnp.where(low, pltpu.roll(re, 64, 1), im)


def gather_rows(tiles, w, slots, n):
    reals, imags = [], []
    for v in range(4):
        first = tiles[2 * v, pl.ds(w, slots, stride=n), :]
        second = tiles[2 * v + 1, pl.ds(w, slots, stride=n), :]
        low = lax.broadcasted_iota(jnp.int32, first.shape, 1) < 64
        reals.append(jnp.where(low, first, pltpu.roll(second, 64, 1)).astype(BF))
        imags.append(jnp.where(low, pltpu.roll(first, 64, 1), second).astype(BF))
    return jnp.concatenate([jnp.concatenate(reals, 1), jnp.concatenate(imags, 1)], 0)


def spread_rows(tiles, w, slots, n, spectrum):
    for v in range(4):
        one, two = interleave(spectrum[:slots], spectrum[slots:], v)
        tiles[2 * v, pl.ds(w, slots, stride=n), :] = one
        tiles[2 * v + 1, pl.ds(w, slots, stride=n), :] = two


def swap_halves(x):
    return pltpu.roll(x, 64, 1)


def head_weights(weights, h, pieces, mode, rows):
    return jnp.concatenate([weights[h * pieces + q, mode, rows, :] for q in range(pieces)], 0)


MESH = pl.DeviceIdType.MESH


def move(sizes, at, axis, d):
    return {**at, axis: lax.rem(at[axis] + d, sizes[axis])}


def greet():
    ndp, nmode = lax.axis_size("dp"), lax.axis_size("mode")
    dp, mode = lax.axis_index("dp"), lax.axis_index("mode")
    barrier = pltpu.get_barrier_semaphore()
    for d in range(1, nmode):
        pl.semaphore_signal(barrier, 1, device_id={"dp": dp, "mode": lax.rem(mode + d, nmode)}, device_id_type=MESH)
    for d in range(1, ndp):
        pl.semaphore_signal(barrier, 1, device_id={"dp": lax.rem(dp + d, ndp), "mode": mode}, device_id_type=MESH)
    pl.semaphore_wait(barrier, ndp + nmode - 2)


def staggered(count, *stages):
    k = len(stages)
    if count < k:
        for stage in stages:
            for t in range(count):
                stage(t)
        return
    for t in range(k - 1):
        for s in range(t + 1):
            stages[s](t - s)

    def body(t, _):
        for s in range(k):
            stages[s](t - s)
        return 0
    lax.fori_loop(k - 1, count, body, 0)
    for t in range(count, count + k - 1):
        for s in range(t - count + 1, k):
            stages[s](t - s)


JOIN = 12


def waves(length):
    angle = (np.arange(length)[:, None] * np.arange(length)[None, :] % length) * (2.0 * np.pi / length)
    table = np.zeros((2 * length, 128), np.float32)
    table[:length, :length] = np.cos(angle)
    table[length:, :length] = -np.sin(angle)
    return table


def pick_waves(mode_list, waves_ref, rows):
    slots = mode_list.shape[0]
    for j in range(slots):
        for part in range(2):
            at = mode_list[j] + part * (waves_ref.shape[0] // 2)
            rows[part * slots + j:part * slots + j + 1, :] = waves_ref[pl.ds(at, 1), :]


def row_of(ref, start, size):
    return jnp.concatenate([ref[pl.ds(start + i * 128, 128)].reshape(1, 128) for i in range(size // 128)], 1)


def roles():
    ndp, nmode = lax.axis_size("dp"), lax.axis_size("mode")
    half = nmode // 2
    dp, mode = lax.axis_index("dp"), lax.axis_index("mode")
    b, y, c = lax.rem(dp, half), mode // 2, lax.rem(mode, 2)
    here = {"a": dp // half, "u": jnp.where(c == 0, b, y), "v": jnp.where(c == 0, y, b), "c": c}
    return {"a": ndp // half, "u": half, "v": half, "c": 2}, here


def place_of(sizes, at):
    b = jnp.where(at["c"] == 0, at["u"], at["v"])
    y = jnp.where(at["c"] == 0, at["v"], at["u"])
    return at["a"] * sizes["u"] + b, y * 2 + at["c"]


def device_of(sizes, at):
    dp, mode = place_of(sizes, at)
    return {"dp": dp, "mode": mode}


def partner_of(at):
    return {"a": at["a"], "u": at["v"], "v": at["u"], "c": 1 - at["c"]}


def reducer(sizes, here, own, from_c, from_v, from_u, from_a, out, send, recv_c, recv_v, recv_u, recv_a):
    na, nu, nv = sizes["a"], sizes["u"], sizes["v"]
    rows = from_c.shape[1]
    step = next(s for s in (96, 32, rows) if rows % s == 0)

    def owner(t, e, d):
        return move(sizes, move(sizes, move(sizes, here, "a", t + 1), "u", e), "v", d)

    def spot(at):
        dp, mode = place_of(sizes, at)
        return dp * sizes["v"] + mode // 2

    def to_partner(at):
        n = spot(at)
        return pltpu.make_async_remote_copy(
            src_ref=own(at), dst_ref=from_c.at[n], send_sem=send.at[0], recv_sem=recv_c.at[n],
            device_id=device_of(sizes, partner_of(here)), device_id_type=MESH)

    def chunks(at, terms, store):
        mine = own(at)

        def chunk(i, _):
            part = pl.ds(pl.multiple_of(i * step, step), step) if step != rows else slice(None)
            total = mine[part, :].astype(F32)
            for ref, k in terms:
                total = total + ref[k, part, :].astype(F32)
            store(mine, part, total)
            return 0
        lax.fori_loop(0, rows // step, chunk, 0)

    def keep(mine, part, total):
        mine[part, :] = total.astype(BF)

    def finish(mine, part, total):
        out[part, :] = total

    def slot_v(t, e, d):
        return (t * nu + e) * (nv - 1) + d - 1

    def copy(at, buffer, s, stage, sems, to):
        return pltpu.make_async_remote_copy(
            src_ref=own(at), dst_ref=buffer.at[s], send_sem=send.at[stage], recv_sem=sems.at[s],
            device_id=device_of(sizes, to), device_id_type=MESH)

    def copy_v(t, e, d):
        s = slot_v(t, e, d)
        return copy(owner(t, e, d), from_v, s, 1, recv_v, move(sizes, here, "v", d))

    def copy_u(t, e):
        return copy(owner(t, e, 0), from_u, t * (nu - 1) + e - 1, 2, recv_u, move(sizes, here, "u", e))

    def copy_a(t):
        return copy(owner(t, 0, 0), from_a, t, 3, recv_a, owner(t, 0, 0))

    def heard(at):
        n = spot(at)
        pltpu.make_async_remote_copy(
            src_ref=own(at), dst_ref=from_c.at[n], send_sem=send.at[0], recv_sem=recv_c.at[n],
            device_id=device_of(sizes, partner_of(here)), device_id_type=MESH).wait_recv()
        return [(from_c, n)]

    def first(t):
        for d in range(1, nv):
            for e in range(nu):
                at = owner(t, e, d)
                chunks(at, heard(at), keep)
                copy_v(t, e, d).start()

    def after_v(t, e):
        terms = heard(owner(t, e, 0))
        for d in range(1, nv):
            copy_v(t, e, d).wait_recv()
            terms.append((from_v, slot_v(t, e, d)))
        return terms

    def second(t):
        for e in range(1, nu):
            chunks(owner(t, e, 0), after_v(t, e), keep)
            copy_u(t, e).start()

    def after_u(t):
        terms = after_v(t, 0)
        for e in range(1, nu):
            copy_u(t, e).wait_recv()
            terms.append((from_u, t * (nu - 1) + e - 1))
        return terms

    def third(t):
        chunks(owner(t, 0, 0), after_u(t), keep)
        copy_a(t).start()

    def last():
        terms = after_u(na - 1)
        for t in range(na - 1):
            copy_a(t).wait_recv()
            terms.append((from_a, t))
        chunks(here, terms, finish)

    def drain():
        for stage, count in ((0, from_c.shape[0]), (1, na * nu * (nv - 1)), (2, na * (nu - 1)), (3, na - 1)):
            ref = from_c.at[pl.ds(0, count)]
            pltpu.make_async_copy(ref, ref, send.at[stage]).wait()

    return to_partner, first, second, third, last, drain


def each(start, stop, *steps):
    def body(t, _):
        for s in steps:
            s(t)
        return 0
    lax.fori_loop(start, stop, body, 0)


def tail_kernel(n, L, D, slots, blocks, owner, mode_list, gmix_h, z_h, acts_h, gsum_h, weights_h, gout_h, gup_h, gdn_h,
                obs_ref, wqo_h, waves_ref, eye_ref, sums_ref,
                dense_out, mixer_out, small_out, gin_h,
                gmix, z, acts, gsum, mix, src, tiles, glow, gbias, tmp, con, basis_rows, basist, wq_ref,
                fc0, fc1, fv0, fv1, fu0, fu1, fa0, fa1, small_one, small_two,
                loads, send, recv_c, recv_v, recv_u, recv_a, small_send, small_recv):
    sizes, here = roles()
    ndp, nmode = lax.axis_size("dp"), lax.axis_size("mode")
    dp, mode = lax.axis_index("dp"), lax.axis_index("mode")
    na = sizes["a"]
    per = slots // nmode
    heads = 8
    pieces = ndp // heads
    depth = 64 // pieces
    rows = con.shape[1]
    size = con.shape[0] * rows // blocks

    def load(i, a, b):
        return pltpu.make_async_copy(a, b, loads.at[i])
    firsts = [load(0, gmix_h, gmix), load(1, z_h, z), load(2, weights_h, mix)]
    later = [load(3, acts_h, acts), load(4, gsum_h, gsum), load(18, wqo_h.at[pl.ds(0, D)], wq_ref)]
    grads = []
    start = D
    for i, ref in enumerate((gout_h, gup_h, gdn_h)):
        for c in range(D // 128):
            grads.append(load(5 + i * 4 + c, ref.at[:, pl.ds(c * 128, 128)], src.at[c, pl.ds(start, ref.shape[0]), :]))
        start += ref.shape[0]
    for c in firsts + later + grads:
        c.start()
    greet()

    send_m, first_m, second_m, third_m, last_m, drain_m = reducer(
        sizes, here, lambda at: mix.at[place_of(sizes, at)], fc1, fv1, fu1, fa1, mixer_out,
        send.at[1], recv_c.at[1], recv_v.at[1], recv_u.at[1], recv_a.at[1])

    def con_at(at):
        p, m = place_of(sizes, at)
        return con.at[p * nmode + m]
    send_d, first_d, second_d, third_d, last_d, drain_d = reducer(
        sizes, here, con_at, fc0, fv0, fu0, fa0, dense_out,
        send.at[0], recv_c.at[0], recv_v.at[0], recv_u.at[0], recv_a.at[0])

    pick_waves(mode_list, waves_ref, basis_rows)
    basist[...] = basis_rows[:, 0:L].T.astype(BF)
    firsts[0].wait()

    def spectra(w):
        part = pl.ds(pl.multiple_of(w * L, 32), L)
        spread_rows(tiles, w, slots, n, gmix[part, :].astype(F32))
    each(0, n, spectra)
    firsts[1].wait()
    firsts[2].wait()

    def mix_slots(places):
        taken = []
        for m, jl, h in places:
            y = tiles[h, pl.ds(pl.multiple_of((m * per + jl) * n, n), n), :]
            both = jnp.concatenate([y, swap_halves(y) * sign_lanes(n, 1.0, -1.0)], 0).astype(BF)
            part = pl.ds(pl.multiple_of(jl * depth, depth), depth)
            x = z[h, pl.ds(pl.multiple_of((m * per + jl) * 2 * n, 2 * n), 2 * n), :]
            taken.append((both, head_weights(mix, h, pieces, m, part), x))
        products = [(dot(both, w, NT), dot(x, both, TN).astype(BF)) for both, w, x in taken]
        for (m, jl, h), (x, g) in zip(places, products):
            part = pl.ds(pl.multiple_of(jl * depth, depth), depth)
            tiles[h, pl.ds(pl.multiple_of((m * per + jl) * n, n), n), :] = jnp.concatenate([x[:n], x[n:]], 1)
            for q in range(pieces):
                mix[h * pieces + q, m, part, :] = g[q * depth:(q + 1) * depth]

    if pieces == 1:
        def mix_shard(at):
            p, m = place_of(sizes, at)
            y_at = tiles.at[p, pl.ds(pl.multiple_of(m * per * n, per * n), per * n)]
            z_at = z.at[p, pl.ds(pl.multiple_of(m * per * 2 * n, per * 2 * n), per * 2 * n)]
            w_at = mix.at[p, m]
            for start in range(0, per, JOIN):
                group = range(start, min(start + JOIN, per))
                ys = [y_at[j * n:(j + 1) * n, :] for j in group]
                boths = [jnp.concatenate([y, swap_halves(y) * sign_lanes(n, 1.0, -1.0)], 0).astype(BF) for y in ys]
                xs = [dot(both, w_at[j * 64:(j + 1) * 64, :], NT) for both, j in zip(boths, group)]
                gs = [dot(z_at[j * 2 * n:(j + 1) * 2 * n, :], both, TN).astype(BF) for both, j in zip(boths, group)]
                for x, g, j in zip(xs, gs, group):
                    y_at[j * n:(j + 1) * n, :] = jnp.concatenate([x[:n], x[n:]], 1)
                    w_at[j * 64:(j + 1) * 64, :] = g

        def feed(t, d):
            def pair(e):
                other = move(sizes, move(sizes, move(sizes, partner_of(here), "a", t + 1), "u", e), "v", d)
                mix_shard(other)
                send_m(other).start()
                mix_shard(move(sizes, move(sizes, move(sizes, here, "a", t + 1), "u", e), "v", d))
            each(0, sizes["u"], pair)
        for d in range(1, sizes["v"]):
            each(0, na, lambda t: feed(t, d))
        each(0, na, first_m)
        each(0, na, lambda t: feed(t, 0))
    else:
        def mix_mode(m):
            def slot(jl, _):
                mix_slots([(m, jl, h) for h in range(heads)])
                return 0
            lax.fori_loop(0, per, slot, 0, unroll=2)

        def mode_at(i, core):
            return lax.rem(mode // 2 + 1 + i, nmode // 2) * 2 + core

        def other_modes(i):
            m = mode_at(i, 1 - here["c"])
            mix_mode(m)

            def hand(p):
                half = sizes["u"]
                b, y = lax.rem(p, half), m // 2
                core = 1 - here["c"]
                send_m({"a": p // half, "u": jnp.where(core == 0, b, y), "v": jnp.where(core == 0, y, b), "c": core}).start()
            each(0, ndp, hand)
        each(0, nmode // 2, other_modes)
        each(0, nmode // 2, lambda i: mix_mode(mode_at(i, here["c"])))
        each(0, na, first_m)

    gbias[...] = jnp.zeros_like(gbias)

    def query(w):
        part = pl.ds(pl.multiple_of(w * L, 32), L)
        g = dot(basist[...], gather_rows(tiles, w, slots, n))
        glow[part, :] = g.astype(BF)
        gbias[...] += functools.reduce(lambda p, q: p + q, [g[i * 8:(i + 1) * 8] for i in range(L // 8)])
    each(0, n, query)

    for k, sums in ((0, gbias[...]), (4, sums_ref[0:8, :])):
        total = jnp.sum(sums, axis=0, keepdims=True)
        for c in range(D // 128):
            small_one[mode, k + c:k + c + 1, :] = total[:, c * 128:(c + 1) * 128]
    for k in range(20):
        small_one[mode, 8 + k:9 + k, :] = jnp.sum(sums_ref[8 + 8 * k:16 + 8 * k, 0:128], axis=0, keepdims=True)
    small_one[mode, 28:32, :] = jnp.zeros((4, 128), F32)

    def small_copy(buffer, axis, index, count, d, base):
        return pltpu.make_async_remote_copy(
            src_ref=buffer.at[index], dst_ref=buffer.at[index], send_sem=small_send.at[base + d - 1], recv_sem=small_recv.at[base + d - 1],
            device_id={**{"dp": dp, "mode": mode}, axis: lax.rem(index + d, count)}, device_id_type=MESH)
    ones = [small_copy(small_one, "mode", mode, nmode, d, 0) for d in range(1, nmode)]
    twos = [small_copy(small_two, "dp", dp, ndp, d, nmode - 1) for d in range(1, ndp)]
    for c in ones:
        c.start()

    for c in later:
        c.wait()
    g = dot(acts[...], glow[...], TN)
    for c in range(D // 128):
        src[c, 0:D, :] = g[:, c * 128:(c + 1) * 128]
    each(0, na // 2, second_m)
    for c in grads:
        c.wait()

    per_shard = rows // size
    join = 4 if per_shard % 4 == 0 else 1
    units = per_shard // join

    def pick(s):
        for k in range(units):
            for c in range(D // 128):
                for i in range(join):
                    row = owner[(s * units + k) * join + i] * size
                    tmp[c, i * size:(i + 1) * size, :] = src[c, pl.ds(row, size), :]
                part = slice(k * join * size, (k + 1) * join * size)
                con[s, part, c * 128:(c + 1) * 128] = tmp[c, 0:join * size, :].astype(BF)
    shards = con.shape[0]
    each(0, shards // 2, pick)
    each(na // 2, na, second_m)
    each(0, na // 2, third_m)
    each(shards // 2, shards, pick)

    def hand_line(t):
        other = partner_of(here)
        for d in list(range(1, sizes["v"])) + [0]:
            for e in range(sizes["u"]):
                send_d(move(sizes, move(sizes, move(sizes, other, "a", t + 1), "u", e), "v", d)).start()
    each(0, na, hand_line)
    each(na // 2, na - 1, third_m)

    def input_grad(w):
        part = pl.ds(pl.multiple_of(w * L, 32), L)
        row = obs_ref[pl.ds(w, 1), :].astype(F32)
        mask = dot((eye_ref[...] * row).astype(BF), jnp.ones((L, 128), BF))
        g = gsum[part, :] + dot(glow[part, :], wq_ref[...], NT)
        for c in range(D // 128):
            gsum[part, c * 128:(c + 1) * 128] = g[:, c * 128:(c + 1) * 128] * mask
    for c in ones:
        c.wait()
    small_two[dp] = functools.reduce(lambda p, q: p + q, [small_one[i] for i in range(nmode)])
    for c in twos:
        c.start()
    each(0, na, first_d)
    each(0, n, input_grad)
    result = load(17, gsum, gin_h)
    result.start()
    each(0, 1, second_d)
    each(1, na - 1, second_d, lambda t: third_d(t - 1))
    last_m()
    second_d(na - 1)
    third_d(na - 2)
    last_d()
    for c in twos:
        c.wait()
    total = functools.reduce(lambda p, q: p + q, [small_two[i] for i in range(ndp)])
    small_out[0:8, :] = total[0:8]
    small_out[8:16, :] = jnp.zeros((8, 128), F32)
    small_out[8:16, 0:24] = lax.dot_general(
        jnp.ones((8, 128), F32), total[8:32], NT, precision=lax.Precision.HIGHEST, preferred_element_type=F32)
    drain_m()
    drain_d()
    result.wait()


def tail(gmix, z, acts, gsum, observed, wqo, mode_index, weights, gout, gup, gdn, sums, owner_list, shard_rows):
    n, L = observed.shape
    D = acts.shape[1]
    slots = mode_index.shape[0]
    ndp, nmode, mixer_rows = weights.shape[:3]
    nd = ndp * nmode
    total = nd * shard_rows
    half = nmode // 2
    na = ndp // half
    group = nd // 2
    anywhere = pl.BlockSpec(memory_space=pl.ANY)
    vmem = pl.BlockSpec(memory_space=pltpu.VMEM)
    shapes = ((shard_rows, D), (mixer_rows, 128))
    counts = (group, na * half * (half - 1), na * (half - 1), na - 1)
    sem = lambda *s: pltpu.SemaphoreType.DMA(s)
    return pl.pallas_call(
        functools.partial(tail_kernel, n, L, D, slots, owner_list.shape[0]),
        out_shape=(
            jax.ShapeDtypeStruct(shapes[0], F32), jax.ShapeDtypeStruct(shapes[1], F32), jax.ShapeDtypeStruct((16, 128), F32),
            jax.ShapeDtypeStruct((n * L, D), F32),
        ),
        in_specs=[pl.BlockSpec(memory_space=pltpu.SMEM)] * 2 + [anywhere] * 8 + [
            vmem, anywhere, vmem, vmem, vmem],
        out_specs=(vmem, vmem, vmem, anywhere),
        scratch_shapes=[
            pltpu.VMEM((n * L, D), BF),
            pltpu.VMEM(z.shape, BF),
            pltpu.VMEM((n * L, D), BF),
            pltpu.VMEM((n * L, D), F32),
            pltpu.VMEM(weights.shape, BF),
            pltpu.VMEM((D // 128, total + 8, 128), F32),
            pltpu.VMEM((8, slots * n, 128), F32),
            pltpu.VMEM((n * L, D), BF),
            pltpu.VMEM((8, D), F32),
            pltpu.VMEM((D // 128, 80, 128), F32),
            pltpu.VMEM((nd, shard_rows, D), BF),
            pltpu.VMEM((2 * slots, 128), F32),
            pltpu.VMEM((L, 2 * slots), BF),
            pltpu.VMEM((D, D), BF),
        ] + [pltpu.VMEM((count,) + s, BF) for count in counts for s in shapes] + [
            pltpu.VMEM((nmode, 32, 128), F32), pltpu.VMEM((ndp, 32, 128), F32),
            sem(19), sem(2, 4), sem(2, counts[0]), sem(2, counts[1]), sem(2, counts[2]), sem(2, counts[3]),
            sem(ndp + nmode - 2), sem(ndp + nmode - 2),
        ],
        compiler_params=pltpu.CompilerParams(collective_id=1, has_side_effects=True, vmem_limit_bytes=62 * 1024 * 1024),
        name="tail",
    )(owner_list, mode_index, gmix, z, acts, gsum, weights, gout, gup, gdn, observed, wqo, waves(L), np.eye(L, dtype=np.float32), sums)


def gatherer(sizes, here, slot_of, whole_of, send, send_a, recv):
    na, nu, nv = sizes["a"], sizes["u"], sizes["v"]

    def spot(at):
        dp, mode = place_of(sizes, at)
        return dp * sizes["v"] * 2 + mode

    def copy(at, to, sem):
        ref = slot_of(at)
        return pltpu.make_async_remote_copy(
            src_ref=ref, dst_ref=ref, send_sem=sem, recv_sem=recv.at[spot(at)],
            device_id=device_of(sizes, to), device_id_type=MESH)

    def onward(at, axes):
        for axis, stage in axes:
            for d in range(1, sizes[axis]):
                copy(at, move(sizes, here, axis, d), send.at[stage]).start()
        copy(at, partner_of(here), send.at[2]).start()

    def hop(k, side):
        first, to = here["a"] - side * k, here["a"] + side
        there = (first >= 0) & (first < na) & (to >= 0) & (to < na)
        way = 0 if side == 1 else 1
        inside = lambda x: jnp.clip(x, 0, na - 1)
        return there, lambda: copy({**here, "a": inside(first)}, {**here, "a": inside(to)}, send_a.at[way, k])

    def hops(k, side):
        there, make = hop(k, side)
        pl.when(there)(lambda: make().start())

    def arrived(at):
        copy(at, here, send.at[0]).wait_recv()
        return at

    def lines(k, act):
        for side in ((1, -1) if k else (1,)):
            to = here["a"] - side * k
            pl.when((to >= 0) & (to < na))(lambda side=side, to=to: act({**here, "a": to}, side))

    def start():
        for side in (1, -1):
            hops(0, side)
        onward(here, (("u", 0), ("v", 1)))

    def line(k, then=lambda at: None):
        def act(at, side):
            arrived(at)
            hops(k, side)
            onward(at, (("u", 0), ("v", 1)))
            then(at)
        lines(k, act)

    def second(k, then=lambda at: None):
        def act(at, side):
            for d in range(1, nu):
                to = arrived(move(sizes, at, "u", d))
                onward(to, (("v", 1),))
                then(to)
        lines(k, act)

    def third(k, then=lambda at: None):
        def act(at, side):
            for e in range(nu):
                for d in range(1, nv):
                    to = arrived(move(sizes, move(sizes, at, "u", e), "v", d))
                    onward(to, ())
                    then(to)
        lines(k, act)

    def partner(t, then=lambda at: None):
        other = partner_of(here)
        for e in range(nu):
            for d in range(nv):
                then(arrived(move(sizes, move(sizes, move(sizes, other, "a", t), "u", e), "v", d)))

    def drain():
        for stage, count in ((0, na * (nu - 1)), (1, na * nu * (nv - 1)), (2, na * nu * nv)):
            ref = whole_of(count)
            pltpu.make_async_copy(ref, ref, send.at[stage]).wait()
        for k in range(na):
            for side in (1, -1):
                there, make = hop(k, side)
                pl.when(there)(lambda make=make: make().wait_send())

    return start, line, second, third, partner, drain


def head_kernel(n, L, D, slots, blocks, restore, mode_list, in_h, dense_ref, mixer_ref, obs_ref, bias_ref, waves_ref, inv_ref, eye_ref,
                acts_h, z_h, sig_h, wqo_h, wup_h, wdn_h, weights_h,
                inputs, acts, query, tiles, z, sig, buf, src, table, mix, tmp, basis_rows, basis_ref,
                loads, send, send_a, recv):
    sizes, here = roles()
    ndp, nmode = lax.axis_size("dp"), lax.axis_size("mode")
    dp, mode = lax.axis_index("dp"), lax.axis_index("mode")
    na = sizes["a"]
    per = slots // nmode
    heads = 8
    pieces = ndp // heads
    depth = 64 // pieces
    rows = buf.shape[1]
    total = buf.shape[0] * rows
    size = total // blocks
    join = 4
    units = blocks // join

    def load(i, a, b):
        return pltpu.make_async_copy(a, b, loads.at[i])
    load_in = load(0, in_h, inputs)
    load_in.start()
    pick_waves(mode_list, waves_ref, basis_rows)
    basis_ref[...] = basis_rows[:, 0:L].astype(BF)
    bias = row_of(bias_ref, 0, D)
    buf[dp * nmode + mode] = dense_ref[...].astype(BF)
    mix[dp, mode] = mixer_ref[...].astype(BF)
    greet()

    def buf_at(at):
        p, m = place_of(sizes, at)
        return buf.at[p * nmode + m]

    start_d, line_d, second_d, third_d, partner_d, drain_d = gatherer(
        sizes, here, buf_at, lambda count: buf.at[pl.ds(0, count)], send.at[0], send_a.at[0], recv.at[0])
    mix_at = lambda at: mix.at[place_of(sizes, at)]

    def mix_many(count):
        if count % nmode == 0:
            return mix.at[pl.ds(0, count // nmode)]
        return mix.at[pl.ds(0, count), 0] if count <= ndp else mix.at[pl.ds(0, count // 2), pl.ds(0, 2)]
    start_m, line_m, second_m, third_m, partner_m, drain_m = gatherer(
        sizes, here, mix_at, mix_many, send.at[1], send_a.at[1], recv.at[1])
    start_d()

    def widen(at):
        p, m = place_of(sizes, at)
        k = p * nmode + m
        for c in range(D // 128):
            src[c, pl.ds(k * rows, rows), :] = buf[k, :, c * 128:(c + 1) * 128].astype(F32)
    widen(here)
    load_in.wait()

    def mask(w):
        row = obs_ref[pl.ds(w, 1), :].astype(F32)
        part = pl.ds(pl.multiple_of(w * L, 32), L)
        acts[part, :] = dot((eye_ref[...] * row).astype(BF), inputs[part, :]).astype(BF)
    each(0, n, mask)
    outs = [load(1, acts, acts_h)]
    outs[0].start()
    rest = []
    for k in range(na + 1):
        if k < na - 1:
            line_d(k + 1, widen)
        if k < na:
            second_d(k, widen)
        if k >= 1:
            third_d(k - 1, widen)
        if k == 0:
            start_m()
        if 1 <= k + 1 - 2 < na:
            line_m(k + 1 - 2)
        if 0 <= k - 2 < na:
            second_m(k - 2)
        if 0 <= k - 2 - 1 < 0:
            third_m(k - 2 - 1)
    done_line, done_second, done_third = min(na - 1, na + 1 - 2), min(na - 1, na - 2), min(0 - 1, na - 2 - 1)
    for k in range(na):
        if k > done_line:
            rest.append(lambda k=k: line_m(k))
        if k > done_second:
            rest.append(lambda k=k: second_m(k))
    for k in range(na):
        if k > done_third:
            rest.append(lambda k=k: third_m(k))
    each(0, na, lambda t: partner_d(t, widen))

    def pick(p):
        for c in range(D // 128):
            for i in range(join):
                tmp[c, i * size:(i + 1) * size, :] = src[c, pl.ds(restore[p * join + i] * size, size), :]
            part = pl.ds(pl.multiple_of(p * join * size, 16), join * size)
            table[part, c * 128:(c + 1) * 128] = tmp[c].astype(BF)
    early = -(-D // (join * size))
    each(0, early, pick)
    T = 384

    def project(i):
        part = pl.ds(pl.multiple_of(i * T, T), T)
        query[part, :] = (dot(acts[part, :], table[0:D, :]) + bias).astype(BF)

    def spectra(w):
        part = pl.ds(pl.multiple_of(w * L, 32), L)
        spread_rows(tiles, w, slots, n, dot(basis_ref[...], query[part, :]))

    parts = n * L // T
    for i in range(parts):
        project(i)
    for i in range(4):
        if rest:
            rest.pop(0)()
        each(i * n // 4, (i + 1) * n // 4, spectra)
    while rest:
        rest.pop(0)()

    def table_out():
        at = 0
        for i, ref in enumerate((wqo_h, wup_h, wdn_h)):
            outs.append(load(2 + i, table.at[pl.ds(at, ref.shape[0])], ref))
            outs[-1].start()
            at += ref.shape[0]

    def mix_slots(places):
        taken = []
        for j, jl, m, h in places:
            x = tiles[h, pl.ds(pl.multiple_of(j * n, n), n), :]
            both = jnp.concatenate([x, swap_halves(x)], 0)[:, :64].astype(BF)
            taken.append((both, head_weights(mix, h, pieces, m, pl.ds(pl.multiple_of(jl * depth, depth), depth))))
        products = [dot(both, w) for both, w in taken]
        for (j, jl, m, h), (both, w), y in zip(places, taken, products):
            z[h, pl.ds(pl.multiple_of(j * 2 * n, 2 * n), 2 * n), :] = both
            tiles[h, pl.ds(pl.multiple_of(j * n, n), n), :] = y[:n] + swap_halves(y[n:]) * sign_lanes(n, -1.0, 1.0)

    if pieces == 1:
        def mix_core(core):
            def some(i):
                def slot(jl, _):
                    m = i * 2 + core
                    mix_slots([(m * per + jl, jl, m, p) for p in range(heads)])
                    return 0
                lax.fori_loop(0, per, slot, 0, unroll=4)
            each(0, nmode // 2, some)
        mix_core(here["c"])
        each(early, units, pick)
        table_out()
        each(0, na, partner_m)
        mix_core(1 - here["c"])
    else:
        each(early, units, pick)
        table_out()
        each(0, na, partner_m)

        def slot(j, _):
            mix_slots([(j, lax.rem(j, per), j // per, h) for h in range(heads)])
            return 0
        lax.fori_loop(0, slots, slot, 0, unroll=4)
    outs.append(load(5, mix, weights_h))
    outs[-1].start()
    outs.append(load(6, z, z_h))
    outs[-1].start()

    def signal(w):
        part = pl.ds(pl.multiple_of(w * L, 32), L)
        sig[part, :] = dot(inv_ref[...], gather_rows(tiles, w, slots, n)).astype(BF)
    each(0, n, signal)
    outs.append(load(7, sig, sig_h))
    outs[-1].start()
    drain_d()
    drain_m()
    for o in outs:
        o.wait()


def head(inputs, observed, dense, mixer, restore, bias, mode_index, inv, ff):
    n, L, D = inputs.shape
    slots = mode_index.shape[0]
    ndp, nmode = lax.axis_size("dp"), lax.axis_size("mode")
    nd = ndp * nmode
    rows, mixer_rows = dense.shape[0], mixer.shape[0]
    anywhere = pl.BlockSpec(memory_space=pl.ANY)
    vmem = pl.BlockSpec(memory_space=pltpu.VMEM)
    sem = lambda *s: pltpu.SemaphoreType.DMA(s)
    tokens = n * L
    return pl.pallas_call(
        functools.partial(head_kernel, n, L, D, slots, restore.shape[0]),
        out_shape=(
            jax.ShapeDtypeStruct((tokens, D), BF),
            jax.ShapeDtypeStruct((8, 2 * slots * n, 64), BF),
            jax.ShapeDtypeStruct((tokens, D), BF),
            jax.ShapeDtypeStruct((2 * D, D), BF),
            jax.ShapeDtypeStruct((ff, D), BF),
            jax.ShapeDtypeStruct((ff, D), BF),
            jax.ShapeDtypeStruct((ndp, nmode, mixer_rows, 128), BF),
        ),
        in_specs=[pl.BlockSpec(memory_space=pltpu.SMEM)] * 2 + [anywhere] + [vmem] * 7,
        out_specs=(anywhere,) * 7,
        scratch_shapes=[
            pltpu.VMEM((tokens, D), BF),
            pltpu.VMEM((tokens, D), BF),
            pltpu.VMEM((tokens, D), BF),
            pltpu.VMEM((8, slots * n, 128), F32),
            pltpu.VMEM((8, 2 * slots * n, 64), BF),
            pltpu.VMEM((tokens, D), BF),
            pltpu.VMEM((nd, rows, D), BF),
            pltpu.VMEM((D // 128, nd * rows + 8, 128), F32),
            pltpu.VMEM((nd * rows, D), BF),
            pltpu.VMEM((ndp, nmode, mixer_rows, 128), BF),
            pltpu.VMEM((D // 128, 4 * (nd * rows // restore.shape[0]), 128), F32),
            pltpu.VMEM((2 * slots, 128), F32),
            pltpu.VMEM((2 * slots, L), BF),
            sem(8), sem(2, 3), sem(2, 2, ndp // (nmode // 2)), sem(2, nd),
        ],
        compiler_params=pltpu.CompilerParams(collective_id=0, has_side_effects=True, vmem_limit_bytes=62 * 1024 * 1024),
        name="head",
    )(restore, mode_index, inputs.reshape(tokens, D), dense, mixer, observed, bias, waves(L), inv, np.eye(L, dtype=np.float32))


def adam_terms(weight, gradient, moment, second, step_rate):
    moment_new = BETA_ONE * moment + (1.0 - BETA_ONE) * gradient
    second_new = BETA_TWO * second + (1.0 - BETA_TWO) * gradient * gradient
    scaled_m = moment_new * (1.0 / (1.0 - BETA_ONE**STEP))
    scaled_v = second_new * (1.0 / (1.0 - BETA_TWO**STEP))
    weight_new = weight - step_rate * (scaled_m / (jnp.sqrt(scaled_v) + ADAM_EPS) + DECAY_RATE * weight)
    return moment_new, second_new, weight_new


def update_kernel(chunks, *refs):
    dense, mixer, small, passed = refs[:4], refs[4:8], refs[8:12], refs[12]
    dense_out, mixer_out, small_out, bias_out, passed_out = refs[13:16], refs[16:19], refs[19:22], refs[22], refs[23]
    held, got, put = refs[24:]
    step = held.shape[0] // chunks
    parts = [pl.ds(i * step, step) for i in range(chunks)]
    gets = [pltpu.make_async_copy(passed.at[p], held.at[p], got.at[i]) for i, p in enumerate(parts)]
    puts = [pltpu.make_async_copy(held.at[p], passed_out.at[p], put.at[i]) for i, p in enumerate(parts)]
    for c in gets:
        c.start()
    for ins, outs, rate in ((dense, dense_out, RATE_DENSE), (mixer, mixer_out, RATE_MIXER)):
        for ref, value in zip(outs, adam_terms(*(x[...] for x in ins), rate)):
            ref[...] = value
    for g, p in zip(gets, puts):
        g.wait()
        p.start()
    size = small[0].shape[0]
    for r in range(-(-size // 128)):
        n = min(128, size - r * 128)
        at = pl.ds(r * 128, n)
        grad = small[1][r:r + 1, :][:, :n]
        row = lambda x: x[at].reshape(1, n)
        terms = adam_terms(row(small[0]), grad, row(small[2]), row(small[3]), RATE_SMALL)
        for ref, value in zip(small_out, terms):
            ref[at] = value.reshape(n)
    for r in range(bias_out.shape[0] // 128):
        bias_out[pl.ds(r * 128, 128)] = small[1][4 + r:5 + r, :].reshape(128)
    for p in puts:
        p.wait()


def update(dense, mixer, small, passed):
    vmem = pl.BlockSpec(memory_space=pltpu.VMEM)
    anywhere = pl.BlockSpec(memory_space=pl.ANY)
    like = lambda x: jax.ShapeDtypeStruct(x.shape, x.dtype)
    chunks = 4
    return pl.pallas_call(
        functools.partial(update_kernel, chunks),
        out_shape=(like(dense[0]),) * 3 + (like(mixer[0]),) * 3 + (like(small[0]),) * 3 + (
            jax.ShapeDtypeStruct((dense[0].shape[1],), F32), like(passed)),
        in_specs=[vmem] * 12 + [anywhere],
        out_specs=(vmem,) * 10 + (anywhere,),
        scratch_shapes=[pltpu.VMEM(passed.shape, F32), pltpu.SemaphoreType.DMA((chunks,)), pltpu.SemaphoreType.DMA((chunks,))],
        compiler_params=pltpu.CompilerParams(vmem_limit_bytes=62 * 1024 * 1024),
        name="update",
    )(*dense, *mixer, *small, passed)


def inverse_table(slots, length):
    turn = np.arange(length)[:, None] * np.arange(slots)[None, :] % length
    angle = turn * (2.0 * np.pi / length)
    scale = np.where(np.arange(slots) == 0, 1.0, 2.0) / length
    return np.concatenate([np.cos(angle) * scale, -np.sin(angle) * scale], 1).astype(np.float32).astype(BF)


def shards(
    inputs,
    observed,
    out_grad,
    mode_index,
    owner_list,
    dense_master,
    dense_first,
    dense_second,
    mixer_master,
    mixer_first,
    mixer_second,
    small_master,
    small_first,
    small_second,
):
    ndp, nmode = lax.axis_size("dp"), lax.axis_size("mode")
    length, width = inputs.shape[1:]
    slots = mode_index.shape[0]
    hidden = (dense_master.shape[0] * ndp * nmode - 2 * width) // 2
    inv = inverse_table(slots, length)
    places = jnp.arange(owner_list.shape[0], dtype=jnp.int32)
    restore = jnp.sum(jnp.where(owner_list[None, :] == places[:, None], places[None, :], 0), axis=1)
    acts, spectra, sig, wqo, wup, wdn, weights = head(
        inputs, observed, dense_master, mixer_master.reshape(-1, mixer_master.shape[2]), restore, small_master,
        mode_index, inv, hidden,
    )
    output, grad_summed, grad_mixed, g_out, g_up, g_down, sums = middle(
        small_master, acts.reshape(inputs.shape), sig.reshape(inputs.shape), out_grad, wqo, wup, wdn,
        small_master, np.ascontiguousarray(inv.T),
    )
    dense_mine, mixer_mine, small_all, input_grad = tail(
        grad_mixed.reshape(-1, width), spectra, acts, grad_summed.reshape(-1, width), observed, wqo, mode_index, weights,
        g_out, g_up, g_down, sums, owner_list, dense_master.shape[0],
    )
    flat = lambda x: x.reshape(-1, x.shape[-1])
    dense_first_new, dense_second_new, dense_new, mixer_first_new, mixer_second_new, mixer_new, *small, input_grad = update(
        (dense_master, dense_mine, dense_first, dense_second),
        (flat(mixer_master), mixer_mine, flat(mixer_first), flat(mixer_second)),
        (small_master, small_all, small_first, small_second),
        input_grad,
    )
    mixer_first_new, mixer_second_new, mixer_new = (
        x.reshape(mixer_master.shape) for x in (mixer_first_new, mixer_second_new, mixer_new)
    )
    return (
        output,
        input_grad.reshape(inputs.shape),
        dense_first_new,
        dense_second_new,
        dense_new,
        mixer_first_new,
        mixer_second_new,
        mixer_new,
        *small,
    )


def solution(mesh):
    placed = (
        P(("dp", "mode"), None, None),
        P(("dp", "mode"), None),
        P(("dp", "mode"), None, None),
        P(),
        P(),
        P(("dp", "mode"), None),
        P(("dp", "mode"), None),
        P(("dp", "mode"), None),
        P("mode", "dp", None),
        P("mode", "dp", None),
        P("mode", "dp", None),
        P(),
        P(),
        P(),
    )
    return jax.shard_map(
        shards,
        mesh=mesh,
        in_specs=placed,
        out_specs=(
            P(("dp", "mode"), None, None),
            P(("dp", "mode"), None, None),
            P(("dp", "mode"), None),
            P(("dp", "mode"), None),
            P(("dp", "mode"), None),
            P("mode", "dp", None),
            P("mode", "dp", None),
            P("mode", "dp", None),
            P(),
            P(),
            P(),
            P(),
        ),
        check_vma=False,
    )
```

```python
import functools
import math

import jax
import jax.numpy as jnp
import numpy as np
from jax import lax
from jax.experimental import pallas as pl
from jax.experimental.pallas import tpu as pltpu
from jax.sharding import PartitionSpec as P

STEP = 10
BETA_ONE = 0.9
BETA_TWO = 0.95
ADAM_EPS = 1e-08
DECAY_RATE = 0.1
RATE_DENSE = 0.03
RATE_MIXER = 0.03
RATE_SMALL = 0.5

KERNEL_SIZES = (7, 12, 14, 24, 48)
ODD = (7, 3, 7, 3, 3)
LOG2E = 1.4426950408889634
BF = jnp.bfloat16
F32 = jnp.float32
NT = (((1,), (1,)), ((), ()))
NN = (((1,), (0,)), ((), ()))
TN = (((0,), (0,)), ((), ()))


def dot(a, b, dims=NN):
    return lax.dot_general(a, b, dims, preferred_element_type=F32)


def average_counts(length):
    tables = []
    t = np.arange(length)
    for size in KERNEL_SIZES:
        u = np.clip(t[:, None] - (size - 1) // 2 + np.arange(size)[None, :], 0, length - 1)
        tables.append((u[:, :, None] == t[None, None, :]).sum(1) * (ODD[len(tables)] / size))
    return np.stack(tables).astype(np.float32)


def gelu_parts(h):
    z = jnp.abs(h)
    e = jnp.exp2(h * h * (-0.5 * LOG2E))
    t = 1.0 / (1.0 + (0.3275911 * math.sqrt(0.5)) * z)
    poly = t * (0.5 * 0.254829592 + t * (-0.5 * 0.284496736 + t * (0.5 * 1.421413741 + t * (-0.5 * 1.453152027 + t * (0.5 * 1.061405429)))))
    tail = poly * e
    big = jnp.where(h < 0, tail, 1.0 - tail)
    return big, e * (1.0 / math.sqrt(2 * math.pi))


def middle_kernel(W, L, D, FF, steps,
                  mix_ref, acts_ref, sig_ref, og_ref, wq_ref, wup_h, wdn_h, bias_ref, invt_ref, cnt_ref, cntt_ref,
                  out_ref, gsum_ref, gmix_ref, gw_ref, gup_ref, gdn_ref, small_ref,
                  vs, base, avg1, c1, v1, active, dgelu, first, flow, gb, ghid, glow, avg2, stk, accs, accb, hs, wg, wsem, wup_ref, wdn_ref, lsem):
    step = pl.program_id(0)
    T = W * L
    CH = 16
    CC = 512
    nc = D // CC
    nr = L // CH
    FT = 512

    fetch = [pltpu.make_async_copy(a, b, lsem.at[i]) for i, (a, b) in enumerate(((wup_h, wup_ref), (wdn_h, wdn_ref)))]

    @pl.when(step == 0)
    def _():
        for f in fetch:
            f.start()
        vs[...] = jnp.zeros_like(vs)
        stk[...] = jnp.zeros_like(stk)
        accs[...] = jnp.zeros_like(accs)
        accb[...] = jnp.zeros_like(accb)
        gw_ref[...] = jnp.zeros_like(gw_ref)

    def fold(x):
        y = x[:, 0:128]
        for i in range(1, CC // 128):
            y = y + x[:, i * 128:(i + 1) * 128]
        return y[0:8] + y[8:16]

    def scaled_shares(v, base_at):
        p = [mix_ref[2 * D + base_at + k] for k in range(10)]
        logits = [((p[k] - p[4]) * LOG2E) * v + (p[5 + k] - p[9]) * LOG2E for k in range(4)]
        top = jnp.maximum(functools.reduce(jnp.maximum, logits), 0.0)
        es = [jnp.exp2(l - top) for l in logits] + [jnp.exp2(-top)]
        r = 1.0 / functools.reduce(lambda a, b: a + b, es)
        scale = {7: r * (1.0 / 7.0), 3: r * (1.0 / 3.0)}
        return [e * scale[o] for e, o in zip(es, ODD)]

    def backward(v, g, cs, avs, mean, base_at, store):
        means = {7: 7.0 * mean, 3: 3.0 * mean}
        total = None
        for k in range(5):
            cg = cs[k] * g
            store(k, cg)
            if k < 4:
                t = cg * (means[ODD[k]] - avs[k])
                term = (mix_ref[2 * D + base_at + k] - mix_ref[2 * D + base_at + 4]) * t
                total = term if total is None else total + term
                accs[base_at + k] += fold(t * v)
                accs[base_at + 5 + k] += fold(t)
        return total

    bias = row_of(bias_ref, D, D)
    sig = sig_ref[...].reshape(T, D)
    base[...] = dot(sig, wq_ref[D:2 * D, :])

    def cut(w, source):
        for i in range(nr):
            for c in range(nc):
                cols = slice(c * CC, (c + 1) * CC)
                v = source(w, i, cols)
                hi = v.astype(BF)
                vs[w % 2, i * CH:(i + 1) * CH, cols] = hi
                vs[w % 2, L + i * CH:L + (i + 1) * CH, cols] = (v - hi.astype(F32)).astype(BF)

    def summed(w, i, cols):
        rows = slice(w * L + i * CH, w * L + (i + 1) * CH)
        v = base[rows, cols] + acts_ref[w, i * CH:(i + 1) * CH, cols].astype(F32) + bias[:, cols]
        v1[rows, cols] = v
        return v

    def averages_one(w):
        cut(w, summed)
        avg1[w * 5 * L:(w + 1) * 5 * L, :] = dot(cnt_ref[...], vs[w % 2])

    def decompose_one(w):
        for i in range(nr):
            for c in range(nc):
                cols = slice(c * CC, (c + 1) * CC)
                rows = slice(w * L + i * CH, w * L + (i + 1) * CH)
                v = v1[rows, cols]
                cs = scaled_shares(v, 0)
                mean = None
                for k in range(5):
                    at = slice((w * 5 + k) * L + i * CH, (w * 5 + k) * L + (i + 1) * CH)
                    u = cs[k] * avg1[at, cols]
                    c1[at, cols] = cs[k]
                    mean = u if mean is None else mean + u
                f = v - mean
                first[rows, cols] = f
                flow[pl.ds(pl.multiple_of(step * T + w * L + i * CH, CH), CH), cols] = f.astype(BF)

    averages_one(0)
    for w in range(W):
        if w + 1 < W:
            averages_one(w + 1)
        decompose_one(w)

    here_t = pl.ds(pl.multiple_of(step * T, CH), T)
    base[...] = first[...]

    def up(n):
        return dot(flow[here_t, :], wup_ref[n * FT:(n + 1) * FT, :], NT)

    tiles = FF // FT
    @pl.when(step == 0)
    def _():
        for f in fetch:
            f.wait()
    hs[0] = up(0)
    for n in range(tiles + 1):
        if n + 1 < tiles:
            hs[(n + 1) % 2] = up(n + 1)
        if n < tiles:
            h = hs[n % 2]
            big, small = gelu_parts(h)
            active[here_t, n * FT:(n + 1) * FT] = (h * big).astype(BF)
            dgelu[:, n * FT:(n + 1) * FT] = (big + h * small).astype(BF)
        if n:
            base[...] += dot(active[here_t, (n - 1) * FT:n * FT], wdn_ref[(n - 1) * FT:n * FT, :])

    def branch(w, i, cols):
        return base[w * L + i * CH:w * L + (i + 1) * CH, cols]

    def averages_two(w):
        cut(w, branch)
        avg2[w % 2] = dot(cnt_ref[...], vs[w % 2])

    def keep_at(w, i, cols):
        def keep(k, cg):
            stk[w % 2, k * L + i * CH:k * L + (i + 1) * CH, cols] = cg.astype(BF)
        return keep

    def decompose_two(w):
        for i in range(nr):
            for c in range(nc):
                cols = slice(c * CC, (c + 1) * CC)
                rows = slice(w * L + i * CH, w * L + (i + 1) * CH)
                here = slice(i * CH, (i + 1) * CH)
                v = base[rows, cols]
                cs = scaled_shares(v, 10)
                avs = [avg2[w % 2, k * L + i * CH:k * L + (i + 1) * CH, cols] for k in range(5)]
                mean = functools.reduce(lambda a, b: a + b, [c_ * a_ for c_, a_ in zip(cs, avs)])
                out_ref[w, here, cols] = (v - mean).astype(BF)
                g = og_ref[w, here, cols].astype(F32)
                base[rows, cols] = g + backward(v, g, cs, avs, mean, 10, keep_at(w, i, cols))

    def back_two(w):
        rows = slice(w * L, (w + 1) * L)
        gs = base[rows, :] - dot(cntt_ref[...], stk[w % 2])
        base[rows, :] = gs
        gb[pl.ds(pl.multiple_of(step * T + w * L, 32), L), :] = gs.astype(BF)

    averages_two(0)
    for w in range(W):
        if w + 1 < W:
            averages_two(w + 1)
        decompose_two(w)
        if w:
            back_two(w - 1)
    back_two(W - 1)

    def down(n):
        return dot(gb[here_t, :], wdn_ref[n * FT:(n + 1) * FT, :], NT)

    hs[0] = down(0)
    for n in range(tiles + 1):
        if n + 1 < tiles:
            hs[(n + 1) % 2] = down(n + 1)
        if n < tiles:
            ghid[here_t, n * FT:(n + 1) * FT] = (hs[n % 2] * dgelu[:, n * FT:(n + 1) * FT].astype(F32)).astype(BF)
        if n:
            base[...] += dot(ghid[here_t, (n - 1) * FT:n * FT], wup_ref[(n - 1) * FT:n * FT, :])

    def decompose_three(w):
        for i in range(nr):
            for c in range(nc):
                cols = slice(c * CC, (c + 1) * CC)
                rows = slice(w * L + i * CH, w * L + (i + 1) * CH)
                v = v1[rows, cols]
                g = base[rows, cols]
                ats = [slice((w * 5 + k) * L + i * CH, (w * 5 + k) * L + (i + 1) * CH) for k in range(5)]
                cs = [c1[at, cols] for at in ats]
                avs = [avg1[at, cols] for at in ats]
                mean = v - first[rows, cols]
                extra = backward(v, g, cs, avs, mean, 0, keep_at(w, i, cols))
                base[rows, cols] = g + extra
                accb[:, cols] += extra[0:8] + extra[8:16]

    def back_three(w):
        rows = slice(w * L, (w + 1) * L)
        gs = base[rows, :] - dot(cntt_ref[...], stk[w % 2])
        gsum_ref[w] = gs
        glow[rows, :] = gs.astype(BF)

    for w in range(W):
        decompose_three(w)
        if w:
            back_three(w - 1)
    back_three(W - 1)

    back = dot(glow[...], wq_ref[D:2 * D, :], NT).astype(BF)
    for w in range(W):
        gmix_ref[w] = dot(invt_ref[...], back[w * L:(w + 1) * L, :]).astype(BF)
    gw_ref[...] += dot(sig, glow[...], TN)

    @pl.when(step == steps - 1)
    def _():
        small_ref[0:8, :] = accb[...]
        for at in (4, 9, 14, 19):
            accs[at] = -(accs[at - 4] + accs[at - 3] + accs[at - 2] + accs[at - 1])
        for k in range(20):
            small_ref[8 + 8 * k:16 + 8 * k, 0:128] = accs[k]
            small_ref[8 + 8 * k:16 + 8 * k, 128:512] = jnp.zeros((8, 384), F32)

        copies = {}
        for n in range(tiles):
            part = slice(n * FT, (n + 1) * FT)
            for i, (left, right, ref) in enumerate(((ghid, flow, gup_ref), (active, gb, gdn_ref))):
                k = (n % 2) * 2 + i
                if n >= 2:
                    copies[n - 2, i].wait()
                wg[k] = dot(left[:, part], right[...], TN)
                copies[n, i] = pltpu.make_async_copy(wg.at[k], ref.at[pl.ds(n * FT, FT)], wsem.at[k])
                copies[n, i].start()
        for n in range(max(tiles - 2, 0), tiles):
            for i in range(2):
                copies[n, i].wait()


def middle(mix, acts, sig, og, wqo, wup, wdn, bias, invt, W=4):
    n, L, D = acts.shape
    FF = wup.shape[0]
    steps = n // W
    T = W * L
    A = average_counts(L)
    cnt = np.zeros((5 * L, 256), np.float32)
    cnt[:, :L] = A.reshape(5 * L, L)
    cnt[:, L:2 * L] = A.reshape(5 * L, L)
    cntt = np.zeros((L, 512), np.float32)
    cntt[:, :5 * L] = A.transpose(2, 0, 1).reshape(L, 5 * L)
    cnt, cntt = (np.asarray(x, BF) for x in (cnt, cntt))
    whole = lambda *s: pl.BlockSpec(s, lambda i: (0,) * len(s), pipeline_mode=pl.Buffered(1))
    anywhere = pl.BlockSpec(memory_space=pl.ANY)
    piece = lambda *s: pl.BlockSpec(s, lambda i: (i,) + (0,) * (len(s) - 1))
    return pl.pallas_call(
        functools.partial(middle_kernel, W, L, D, FF, steps),
        grid=(steps,),
        out_shape=(
            jax.ShapeDtypeStruct((n, L, D), BF),
            jax.ShapeDtypeStruct((n, L, D), F32),
            jax.ShapeDtypeStruct((n, L, D), BF),
            jax.ShapeDtypeStruct((D, D), F32),
            jax.ShapeDtypeStruct((FF, D), F32),
            jax.ShapeDtypeStruct((FF, D), F32),
            jax.ShapeDtypeStruct((168, D), F32),
        ),
        in_specs=[
            pl.BlockSpec(memory_space=pltpu.SMEM),
            piece(W, L, D), piece(W, L, D), piece(W, L, D),
            whole(2 * D, D), anywhere, anywhere, whole(bias.shape[0]), whole(L, L), whole(5 * L, 256), whole(L, 512),
        ],
        out_specs=(
            piece(W, L, D), piece(W, L, D), piece(W, L, D), whole(D, D), anywhere, anywhere, whole(168, D),
        ),
        scratch_shapes=[
            pltpu.VMEM((2, 256, D), BF),
            pltpu.VMEM((T, D), F32),
            pltpu.VMEM((W * 5 * L, D), F32),
            pltpu.VMEM((W * 5 * L, D), F32),
            pltpu.VMEM((T, D), F32),
            pltpu.VMEM((n * L, FF), BF),
            pltpu.VMEM((T, FF), BF),
            pltpu.VMEM((T, D), F32),
            pltpu.VMEM((n * L, D), BF),
            pltpu.VMEM((n * L, D), BF),
            pltpu.VMEM((n * L, FF), BF),
            pltpu.VMEM((T, D), BF),
            pltpu.VMEM((2, 5 * L, D), F32),
            pltpu.VMEM((2, 512, D), BF),
            pltpu.VMEM((20, 8, 128), F32),
            pltpu.VMEM((8, D), F32),
            pltpu.VMEM((2, T, 512), F32),
            pltpu.VMEM((4, 512, D), F32),
            pltpu.SemaphoreType.DMA((4,)),
            pltpu.VMEM((FF, D), BF),
            pltpu.VMEM((FF, D), BF),
            pltpu.SemaphoreType.DMA((2,)),
        ],
        compiler_params=pltpu.CompilerParams(vmem_limit_bytes=60 * 1024 * 1024),
        name="middle",
    )(mix, acts, sig, og, wqo, wup, wdn, bias, invt, cnt, cntt)


def sign_lanes(rows, left, right):
    lane = lax.broadcasted_iota(jnp.int32, (rows, 128), 1)
    return jnp.where(lane < 64, left, right).astype(F32)


def interleave(real, imag, v):
    re, im = real[:, v * 128:(v + 1) * 128], imag[:, v * 128:(v + 1) * 128]
    low = lax.broadcasted_iota(jnp.int32, re.shape, 1) < 64
    return jnp.where(low, re, pltpu.roll(im, 64, 1)), jnp.where(low, pltpu.roll(re, 64, 1), im)


def gather_rows(tiles, w, slots, n):
    reals, imags = [], []
    for v in range(4):
        first = tiles[2 * v, pl.ds(w, slots, stride=n), :]
        second = tiles[2 * v + 1, pl.ds(w, slots, stride=n), :]
        low = lax.broadcasted_iota(jnp.int32, first.shape, 1) < 64
        reals.append(jnp.where(low, first, pltpu.roll(second, 64, 1)).astype(BF))
        imags.append(jnp.where(low, pltpu.roll(first, 64, 1), second).astype(BF))
    return jnp.concatenate([jnp.concatenate(reals, 1), jnp.concatenate(imags, 1)], 0)


def spread_rows(tiles, w, slots, n, spectrum):
    for v in range(4):
        one, two = interleave(spectrum[:slots], spectrum[slots:], v)
        tiles[2 * v, pl.ds(w, slots, stride=n), :] = one
        tiles[2 * v + 1, pl.ds(w, slots, stride=n), :] = two


def swap_halves(x):
    return pltpu.roll(x, 64, 1)


def head_weights(weights, h, pieces, mode, rows):
    return jnp.concatenate([weights[h * pieces + q, mode, rows, :] for q in range(pieces)], 0)


MESH = pl.DeviceIdType.MESH


def move(sizes, at, axis, d):
    return {**at, axis: lax.rem(at[axis] + d, sizes[axis])}


def greet():
    ndp, nmode = lax.axis_size("dp"), lax.axis_size("mode")
    dp, mode = lax.axis_index("dp"), lax.axis_index("mode")
    barrier = pltpu.get_barrier_semaphore()
    for d in range(1, nmode):
        pl.semaphore_signal(barrier, 1, device_id={"dp": dp, "mode": lax.rem(mode + d, nmode)}, device_id_type=MESH)
    for d in range(1, ndp):
        pl.semaphore_signal(barrier, 1, device_id={"dp": lax.rem(dp + d, ndp), "mode": mode}, device_id_type=MESH)
    pl.semaphore_wait(barrier, ndp + nmode - 2)


def staggered(count, *stages):
    k = len(stages)
    if count < k:
        for stage in stages:
            for t in range(count):
                stage(t)
        return
    for t in range(k - 1):
        for s in range(t + 1):
            stages[s](t - s)

    def body(t, _):
        for s in range(k):
            stages[s](t - s)
        return 0
    lax.fori_loop(k - 1, count, body, 0)
    for t in range(count, count + k - 1):
        for s in range(t - count + 1, k):
            stages[s](t - s)


JOIN = 12


def waves(length):
    angle = (np.arange(length)[:, None] * np.arange(length)[None, :] % length) * (2.0 * np.pi / length)
    table = np.zeros((2 * length, 128), np.float32)
    table[:length, :length] = np.cos(angle)
    table[length:, :length] = -np.sin(angle)
    return table


def pick_waves(mode_list, waves_ref, rows):
    slots = mode_list.shape[0]
    for j in range(slots):
        for part in range(2):
            at = mode_list[j] + part * (waves_ref.shape[0] // 2)
            rows[part * slots + j:part * slots + j + 1, :] = waves_ref[pl.ds(at, 1), :]


def row_of(ref, start, size):
    return jnp.concatenate([ref[pl.ds(start + i * 128, 128)].reshape(1, 128) for i in range(size // 128)], 1)


def roles():
    ndp, nmode = lax.axis_size("dp"), lax.axis_size("mode")
    half = nmode // 2
    dp, mode = lax.axis_index("dp"), lax.axis_index("mode")
    b, y, c = lax.rem(dp, half), mode // 2, lax.rem(mode, 2)
    here = {"a": dp // half, "u": jnp.where(c == 0, b, y), "v": jnp.where(c == 0, y, b), "c": c}
    return {"a": ndp // half, "u": half, "v": half, "c": 2}, here


def place_of(sizes, at):
    b = jnp.where(at["c"] == 0, at["u"], at["v"])
    y = jnp.where(at["c"] == 0, at["v"], at["u"])
    return at["a"] * sizes["u"] + b, y * 2 + at["c"]


def device_of(sizes, at):
    dp, mode = place_of(sizes, at)
    return {"dp": dp, "mode": mode}


def partner_of(at):
    return {"a": at["a"], "u": at["v"], "v": at["u"], "c": 1 - at["c"]}


def reducer(sizes, here, own, from_c, from_v, from_u, from_a, out, send, recv_c, recv_v, recv_u, recv_a):
    na, nu, nv = sizes["a"], sizes["u"], sizes["v"]
    rows = from_c.shape[1]
    step = next(s for s in (96, 32, rows) if rows % s == 0)

    def owner(t, e, d):
        return move(sizes, move(sizes, move(sizes, here, "a", t + 1), "u", e), "v", d)

    def spot(at):
        dp, mode = place_of(sizes, at)
        return dp * sizes["v"] + mode // 2

    def to_partner(at):
        n = spot(at)
        return pltpu.make_async_remote_copy(
            src_ref=own(at), dst_ref=from_c.at[n], send_sem=send.at[0], recv_sem=recv_c.at[n],
            device_id=device_of(sizes, partner_of(here)), device_id_type=MESH)

    def chunks(at, terms, store):
        mine = own(at)

        def chunk(i, _):
            part = pl.ds(pl.multiple_of(i * step, step), step) if step != rows else slice(None)
            total = mine[part, :].astype(F32)
            for ref, k in terms:
                total = total + ref[k, part, :].astype(F32)
            store(mine, part, total)
            return 0
        lax.fori_loop(0, rows // step, chunk, 0)

    def keep(mine, part, total):
        mine[part, :] = total.astype(BF)

    def finish(mine, part, total):
        out[part, :] = total

    def slot_v(t, e, d):
        return (t * nu + e) * (nv - 1) + d - 1

    def copy(at, buffer, s, stage, sems, to):
        return pltpu.make_async_remote_copy(
            src_ref=own(at), dst_ref=buffer.at[s], send_sem=send.at[stage], recv_sem=sems.at[s],
            device_id=device_of(sizes, to), device_id_type=MESH)

    def copy_v(t, e, d):
        s = slot_v(t, e, d)
        return copy(owner(t, e, d), from_v, s, 1, recv_v, move(sizes, here, "v", d))

    def copy_u(t, e):
        return copy(owner(t, e, 0), from_u, t * (nu - 1) + e - 1, 2, recv_u, move(sizes, here, "u", e))

    def copy_a(t):
        return copy(owner(t, 0, 0), from_a, t, 3, recv_a, owner(t, 0, 0))

    def heard(at):
        n = spot(at)
        pltpu.make_async_remote_copy(
            src_ref=own(at), dst_ref=from_c.at[n], send_sem=send.at[0], recv_sem=recv_c.at[n],
            device_id=device_of(sizes, partner_of(here)), device_id_type=MESH).wait_recv()
        return [(from_c, n)]

    def first(t):
        for d in range(1, nv):
            for e in range(nu):
                at = owner(t, e, d)
                chunks(at, heard(at), keep)
                copy_v(t, e, d).start()

    def after_v(t, e):
        terms = heard(owner(t, e, 0))
        for d in range(1, nv):
            copy_v(t, e, d).wait_recv()
            terms.append((from_v, slot_v(t, e, d)))
        return terms

    def second(t):
        for e in range(1, nu):
            chunks(owner(t, e, 0), after_v(t, e), keep)
            copy_u(t, e).start()

    def after_u(t):
        terms = after_v(t, 0)
        for e in range(1, nu):
            copy_u(t, e).wait_recv()
            terms.append((from_u, t * (nu - 1) + e - 1))
        return terms

    def third(t):
        chunks(owner(t, 0, 0), after_u(t), keep)
        copy_a(t).start()

    def last():
        terms = after_u(na - 1)
        for t in range(na - 1):
            copy_a(t).wait_recv()
            terms.append((from_a, t))
        chunks(here, terms, finish)

    def drain():
        for stage, count in ((0, from_c.shape[0]), (1, na * nu * (nv - 1)), (2, na * (nu - 1)), (3, na - 1)):
            ref = from_c.at[pl.ds(0, count)]
            pltpu.make_async_copy(ref, ref, send.at[stage]).wait()

    return to_partner, first, second, third, last, drain


def each(start, stop, *steps):
    def body(t, _):
        for s in steps:
            s(t)
        return 0
    lax.fori_loop(start, stop, body, 0)


def tail_kernel(n, L, D, slots, blocks, owner, mode_list, gmix_h, z_h, acts_h, gsum_h, weights_h, gout_h, gup_h, gdn_h,
                obs_ref, wqo_h, waves_ref, eye_ref, sums_ref,
                dense_out, mixer_out, small_out, gin_h,
                gmix, z, acts, gsum, mix, src, tiles, glow, gbias, tmp, con, basis_rows, basist, wq_ref,
                fc0, fc1, fv0, fv1, fu0, fu1, fa0, fa1, small_one, small_two,
                loads, send, recv_c, recv_v, recv_u, recv_a, small_send, small_recv):
    sizes, here = roles()
    ndp, nmode = lax.axis_size("dp"), lax.axis_size("mode")
    dp, mode = lax.axis_index("dp"), lax.axis_index("mode")
    na = sizes["a"]
    per = slots // nmode
    heads = 8
    pieces = ndp // heads
    depth = 64 // pieces
    rows = con.shape[1]
    size = con.shape[0] * rows // blocks

    def load(i, a, b):
        return pltpu.make_async_copy(a, b, loads.at[i])
    firsts = [load(0, gmix_h, gmix), load(1, z_h, z), load(2, weights_h, mix)]
    later = [load(3, acts_h, acts), load(4, gsum_h, gsum), load(18, wqo_h.at[pl.ds(0, D)], wq_ref)]
    grads = []
    start = D
    for i, ref in enumerate((gout_h, gup_h, gdn_h)):
        for c in range(D // 128):
            grads.append(load(5 + i * 4 + c, ref.at[:, pl.ds(c * 128, 128)], src.at[c, pl.ds(start, ref.shape[0]), :]))
        start += ref.shape[0]
    for c in firsts + later + grads:
        c.start()
    greet()

    send_m, first_m, second_m, third_m, last_m, drain_m = reducer(
        sizes, here, lambda at: mix.at[place_of(sizes, at)], fc1, fv1, fu1, fa1, mixer_out,
        send.at[1], recv_c.at[1], recv_v.at[1], recv_u.at[1], recv_a.at[1])

    def con_at(at):
        p, m = place_of(sizes, at)
        return con.at[p * nmode + m]
    send_d, first_d, second_d, third_d, last_d, drain_d = reducer(
        sizes, here, con_at, fc0, fv0, fu0, fa0, dense_out,
        send.at[0], recv_c.at[0], recv_v.at[0], recv_u.at[0], recv_a.at[0])

    pick_waves(mode_list, waves_ref, basis_rows)
    basist[...] = basis_rows[:, 0:L].T.astype(BF)
    firsts[0].wait()

    def spectra(w):
        part = pl.ds(pl.multiple_of(w * L, 32), L)
        spread_rows(tiles, w, slots, n, gmix[part, :].astype(F32))
    each(0, n, spectra)
    firsts[1].wait()
    firsts[2].wait()

    def mix_slots(places):
        taken = []
        for m, jl, h in places:
            y = tiles[h, pl.ds(pl.multiple_of((m * per + jl) * n, n), n), :]
            both = jnp.concatenate([y, swap_halves(y) * sign_lanes(n, 1.0, -1.0)], 0).astype(BF)
            part = pl.ds(pl.multiple_of(jl * depth, depth), depth)
            x = z[h, pl.ds(pl.multiple_of((m * per + jl) * 2 * n, 2 * n), 2 * n), :]
            taken.append((both, head_weights(mix, h, pieces, m, part), x))
        products = [(dot(both, w, NT), dot(x, both, TN).astype(BF)) for both, w, x in taken]
        for (m, jl, h), (x, g) in zip(places, products):
            part = pl.ds(pl.multiple_of(jl * depth, depth), depth)
            tiles[h, pl.ds(pl.multiple_of((m * per + jl) * n, n), n), :] = jnp.concatenate([x[:n], x[n:]], 1)
            for q in range(pieces):
                mix[h * pieces + q, m, part, :] = g[q * depth:(q + 1) * depth]

    if pieces == 1:
        def mix_shard(at):
            p, m = place_of(sizes, at)
            y_at = tiles.at[p, pl.ds(pl.multiple_of(m * per * n, per * n), per * n)]
            z_at = z.at[p, pl.ds(pl.multiple_of(m * per * 2 * n, per * 2 * n), per * 2 * n)]
            w_at = mix.at[p, m]
            for start in range(0, per, JOIN):
                group = range(start, min(start + JOIN, per))
                ys = [y_at[j * n:(j + 1) * n, :] for j in group]
                boths = [jnp.concatenate([y, swap_halves(y) * sign_lanes(n, 1.0, -1.0)], 0).astype(BF) for y in ys]
                xs = [dot(both, w_at[j * 64:(j + 1) * 64, :], NT) for both, j in zip(boths, group)]
                gs = [dot(z_at[j * 2 * n:(j + 1) * 2 * n, :], both, TN).astype(BF) for both, j in zip(boths, group)]
                for x, g, j in zip(xs, gs, group):
                    y_at[j * n:(j + 1) * n, :] = jnp.concatenate([x[:n], x[n:]], 1)
                    w_at[j * 64:(j + 1) * 64, :] = g

        def feed(t, d):
            def pair(e):
                other = move(sizes, move(sizes, move(sizes, partner_of(here), "a", t + 1), "u", e), "v", d)
                mix_shard(other)
                send_m(other).start()
                mix_shard(move(sizes, move(sizes, move(sizes, here, "a", t + 1), "u", e), "v", d))
            each(0, sizes["u"], pair)
        for d in range(1, sizes["v"]):
            each(0, na, lambda t: feed(t, d))
        each(0, na, first_m)
        each(0, na, lambda t: feed(t, 0))
    else:
        def mix_mode(m):
            def slot(jl, _):
                mix_slots([(m, jl, h) for h in range(heads)])
                return 0
            lax.fori_loop(0, per, slot, 0, unroll=2)

        def mode_at(i, core):
            return lax.rem(mode // 2 + 1 + i, nmode // 2) * 2 + core

        def other_modes(i):
            m = mode_at(i, 1 - here["c"])
            mix_mode(m)

            def hand(p):
                half = sizes["u"]
                b, y = lax.rem(p, half), m // 2
                core = 1 - here["c"]
                send_m({"a": p // half, "u": jnp.where(core == 0, b, y), "v": jnp.where(core == 0, y, b), "c": core}).start()
            each(0, ndp, hand)
        each(0, nmode // 2, other_modes)
        each(0, nmode // 2, lambda i: mix_mode(mode_at(i, here["c"])))
        each(0, na, first_m)

    gbias[...] = jnp.zeros_like(gbias)

    def query(w):
        part = pl.ds(pl.multiple_of(w * L, 32), L)
        g = dot(basist[...], gather_rows(tiles, w, slots, n))
        glow[part, :] = g.astype(BF)
        gbias[...] += functools.reduce(lambda p, q: p + q, [g[i * 8:(i + 1) * 8] for i in range(L // 8)])
    each(0, n, query)

    for k, sums in ((0, gbias[...]), (4, sums_ref[0:8, :])):
        total = jnp.sum(sums, axis=0, keepdims=True)
        for c in range(D // 128):
            small_one[mode, k + c:k + c + 1, :] = total[:, c * 128:(c + 1) * 128]
    for k in range(20):
        small_one[mode, 8 + k:9 + k, :] = jnp.sum(sums_ref[8 + 8 * k:16 + 8 * k, 0:128], axis=0, keepdims=True)
    small_one[mode, 28:32, :] = jnp.zeros((4, 128), F32)

    def small_copy(buffer, axis, index, count, d, base):
        return pltpu.make_async_remote_copy(
            src_ref=buffer.at[index], dst_ref=buffer.at[index], send_sem=small_send.at[base + d - 1], recv_sem=small_recv.at[base + d - 1],
            device_id={**{"dp": dp, "mode": mode}, axis: lax.rem(index + d, count)}, device_id_type=MESH)
    ones = [small_copy(small_one, "mode", mode, nmode, d, 0) for d in range(1, nmode)]
    twos = [small_copy(small_two, "dp", dp, ndp, d, nmode - 1) for d in range(1, ndp)]
    for c in ones:
        c.start()

    for c in later:
        c.wait()
    g = dot(acts[...], glow[...], TN)
    for c in range(D // 128):
        src[c, 0:D, :] = g[:, c * 128:(c + 1) * 128]
    each(0, na // 2, second_m)
    for c in grads:
        c.wait()

    per_shard = rows // size
    join = 4 if per_shard % 4 == 0 else 1
    units = per_shard // join

    def pick(s):
        for k in range(units):
            for c in range(D // 128):
                for i in range(join):
                    row = owner[(s * units + k) * join + i] * size
                    tmp[c, i * size:(i + 1) * size, :] = src[c, pl.ds(row, size), :]
                part = slice(k * join * size, (k + 1) * join * size)
                con[s, part, c * 128:(c + 1) * 128] = tmp[c, 0:join * size, :].astype(BF)
    shards = con.shape[0]
    each(0, shards // 2, pick)
    each(na // 2, na, second_m)
    each(0, na // 2, third_m)
    each(shards // 2, shards, pick)

    def hand_line(t):
        other = partner_of(here)
        for d in list(range(1, sizes["v"])) + [0]:
            for e in range(sizes["u"]):
                send_d(move(sizes, move(sizes, move(sizes, other, "a", t + 1), "u", e), "v", d)).start()
    each(0, na, hand_line)
    each(na // 2, na - 1, third_m)

    def input_grad(w):
        part = pl.ds(pl.multiple_of(w * L, 32), L)
        row = obs_ref[pl.ds(w, 1), :].astype(F32)
        mask = dot((eye_ref[...] * row).astype(BF), jnp.ones((L, 128), BF))
        g = gsum[part, :] + dot(glow[part, :], wq_ref[...], NT)
        for c in range(D // 128):
            gsum[part, c * 128:(c + 1) * 128] = g[:, c * 128:(c + 1) * 128] * mask
    for c in ones:
        c.wait()
    small_two[dp] = functools.reduce(lambda p, q: p + q, [small_one[i] for i in range(nmode)])
    for c in twos:
        c.start()
    each(0, na, first_d)
    each(0, n, input_grad)
    result = load(17, gsum, gin_h)
    result.start()
    each(0, 1, second_d)
    each(1, na - 1, second_d, lambda t: third_d(t - 1))
    last_m()
    second_d(na - 1)
    third_d(na - 2)
    last_d()
    for c in twos:
        c.wait()
    total = functools.reduce(lambda p, q: p + q, [small_two[i] for i in range(ndp)])
    small_out[0:8, :] = total[0:8]
    small_out[8:16, :] = jnp.zeros((8, 128), F32)
    small_out[8:16, 0:24] = lax.dot_general(
        jnp.ones((8, 128), F32), total[8:32], NT, precision=lax.Precision.HIGHEST, preferred_element_type=F32)
    drain_m()
    drain_d()
    result.wait()


def tail(gmix, z, acts, gsum, observed, wqo, mode_index, weights, gout, gup, gdn, sums, owner_list, shard_rows):
    n, L = observed.shape
    D = acts.shape[1]
    slots = mode_index.shape[0]
    ndp, nmode, mixer_rows = weights.shape[:3]
    nd = ndp * nmode
    total = nd * shard_rows
    half = nmode // 2
    na = ndp // half
    group = nd // 2
    anywhere = pl.BlockSpec(memory_space=pl.ANY)
    vmem = pl.BlockSpec(memory_space=pltpu.VMEM)
    shapes = ((shard_rows, D), (mixer_rows, 128))
    counts = (group, na * half * (half - 1), na * (half - 1), na - 1)
    sem = lambda *s: pltpu.SemaphoreType.DMA(s)
    return pl.pallas_call(
        functools.partial(tail_kernel, n, L, D, slots, owner_list.shape[0]),
        out_shape=(
            jax.ShapeDtypeStruct(shapes[0], F32), jax.ShapeDtypeStruct(shapes[1], F32), jax.ShapeDtypeStruct((16, 128), F32),
            jax.ShapeDtypeStruct((n * L, D), F32),
        ),
        in_specs=[pl.BlockSpec(memory_space=pltpu.SMEM)] * 2 + [anywhere] * 8 + [
            vmem, anywhere, vmem, vmem, vmem],
        out_specs=(vmem, vmem, vmem, anywhere),
        scratch_shapes=[
            pltpu.VMEM((n * L, D), BF),
            pltpu.VMEM(z.shape, BF),
            pltpu.VMEM((n * L, D), BF),
            pltpu.VMEM((n * L, D), F32),
            pltpu.VMEM(weights.shape, BF),
            pltpu.VMEM((D // 128, total + 8, 128), F32),
            pltpu.VMEM((8, slots * n, 128), F32),
            pltpu.VMEM((n * L, D), BF),
            pltpu.VMEM((8, D), F32),
            pltpu.VMEM((D // 128, 80, 128), F32),
            pltpu.VMEM((nd, shard_rows, D), BF),
            pltpu.VMEM((2 * slots, 128), F32),
            pltpu.VMEM((L, 2 * slots), BF),
            pltpu.VMEM((D, D), BF),
        ] + [pltpu.VMEM((count,) + s, BF) for count in counts for s in shapes] + [
            pltpu.VMEM((nmode, 32, 128), F32), pltpu.VMEM((ndp, 32, 128), F32),
            sem(19), sem(2, 4), sem(2, counts[0]), sem(2, counts[1]), sem(2, counts[2]), sem(2, counts[3]),
            sem(ndp + nmode - 2), sem(ndp + nmode - 2),
        ],
        compiler_params=pltpu.CompilerParams(collective_id=1, has_side_effects=True, vmem_limit_bytes=62 * 1024 * 1024),
        name="tail",
    )(owner_list, mode_index, gmix, z, acts, gsum, weights, gout, gup, gdn, observed, wqo, waves(L), np.eye(L, dtype=np.float32), sums)


def gatherer(sizes, here, slot_of, whole_of, send, send_a, recv):
    na, nu, nv = sizes["a"], sizes["u"], sizes["v"]

    def spot(at):
        dp, mode = place_of(sizes, at)
        return dp * sizes["v"] * 2 + mode

    def copy(at, to, sem):
        ref = slot_of(at)
        return pltpu.make_async_remote_copy(
            src_ref=ref, dst_ref=ref, send_sem=sem, recv_sem=recv.at[spot(at)],
            device_id=device_of(sizes, to), device_id_type=MESH)

    def onward(at, axes):
        for axis, stage in axes:
            for d in range(1, sizes[axis]):
                copy(at, move(sizes, here, axis, d), send.at[stage]).start()
        copy(at, partner_of(here), send.at[2]).start()

    def hop(k, side):
        first, to = here["a"] - side * k, here["a"] + side
        there = (first >= 0) & (first < na) & (to >= 0) & (to < na)
        way = 0 if side == 1 else 1
        inside = lambda x: jnp.clip(x, 0, na - 1)
        return there, lambda: copy({**here, "a": inside(first)}, {**here, "a": inside(to)}, send_a.at[way, k])

    def hops(k, side):
        there, make = hop(k, side)
        pl.when(there)(lambda: make().start())

    def arrived(at):
        copy(at, here, send.at[0]).wait_recv()
        return at

    def lines(k, act):
        for side in ((1, -1) if k else (1,)):
            to = here["a"] - side * k
            pl.when((to >= 0) & (to < na))(lambda side=side, to=to: act({**here, "a": to}, side))

    def start():
        for side in (1, -1):
            hops(0, side)
        onward(here, (("u", 0), ("v", 1)))

    def line(k, then=lambda at: None):
        def act(at, side):
            arrived(at)
            hops(k, side)
            onward(at, (("u", 0), ("v", 1)))
            then(at)
        lines(k, act)

    def second(k, then=lambda at: None):
        def act(at, side):
            for d in range(1, nu):
                to = arrived(move(sizes, at, "u", d))
                onward(to, (("v", 1),))
                then(to)
        lines(k, act)

    def third(k, then=lambda at: None):
        def act(at, side):
            for e in range(nu):
                for d in range(1, nv):
                    to = arrived(move(sizes, move(sizes, at, "u", e), "v", d))
                    onward(to, ())
                    then(to)
        lines(k, act)

    def partner(t, then=lambda at: None):
        other = partner_of(here)
        for e in range(nu):
            for d in range(nv):
                then(arrived(move(sizes, move(sizes, move(sizes, other, "a", t), "u", e), "v", d)))

    def drain():
        for stage, count in ((0, na * (nu - 1)), (1, na * nu * (nv - 1)), (2, na * nu * nv)):
            ref = whole_of(count)
            pltpu.make_async_copy(ref, ref, send.at[stage]).wait()
        for k in range(na):
            for side in (1, -1):
                there, make = hop(k, side)
                pl.when(there)(lambda make=make: make().wait_send())

    return start, line, second, third, partner, drain


def head_kernel(n, L, D, slots, blocks, restore, mode_list, in_h, dense_ref, mixer_ref, obs_ref, bias_ref, waves_ref, inv_ref, eye_ref,
                acts_h, z_h, sig_h, wqo_h, wup_h, wdn_h, weights_h,
                inputs, acts, query, tiles, z, sig, buf, src, table, mix, tmp, basis_rows, basis_ref,
                loads, send, send_a, recv):
    sizes, here = roles()
    ndp, nmode = lax.axis_size("dp"), lax.axis_size("mode")
    dp, mode = lax.axis_index("dp"), lax.axis_index("mode")
    na = sizes["a"]
    per = slots // nmode
    heads = 8
    pieces = ndp // heads
    depth = 64 // pieces
    rows = buf.shape[1]
    total = buf.shape[0] * rows
    size = total // blocks
    join = 4
    units = blocks // join

    def load(i, a, b):
        return pltpu.make_async_copy(a, b, loads.at[i])
    load_in = load(0, in_h, inputs)
    load_in.start()
    pick_waves(mode_list, waves_ref, basis_rows)
    basis_ref[...] = basis_rows[:, 0:L].astype(BF)
    bias = row_of(bias_ref, 0, D)
    buf[dp * nmode + mode] = dense_ref[...].astype(BF)
    mix[dp, mode] = mixer_ref[...].astype(BF)
    greet()

    def buf_at(at):
        p, m = place_of(sizes, at)
        return buf.at[p * nmode + m]

    start_d, line_d, second_d, third_d, partner_d, drain_d = gatherer(
        sizes, here, buf_at, lambda count: buf.at[pl.ds(0, count)], send.at[0], send_a.at[0], recv.at[0])
    mix_at = lambda at: mix.at[place_of(sizes, at)]

    def mix_many(count):
        if count % nmode == 0:
            return mix.at[pl.ds(0, count // nmode)]
        return mix.at[pl.ds(0, count), 0] if count <= ndp else mix.at[pl.ds(0, count // 2), pl.ds(0, 2)]
    start_m, line_m, second_m, third_m, partner_m, drain_m = gatherer(
        sizes, here, mix_at, mix_many, send.at[1], send_a.at[1], recv.at[1])
    start_d()

    def widen(at):
        p, m = place_of(sizes, at)
        k = p * nmode + m
        for c in range(D // 128):
            src[c, pl.ds(k * rows, rows), :] = buf[k, :, c * 128:(c + 1) * 128].astype(F32)
    widen(here)
    load_in.wait()

    def mask(w):
        row = obs_ref[pl.ds(w, 1), :].astype(F32)
        part = pl.ds(pl.multiple_of(w * L, 32), L)
        acts[part, :] = dot((eye_ref[...] * row).astype(BF), inputs[part, :]).astype(BF)
    each(0, n, mask)
    outs = [load(1, acts, acts_h)]
    outs[0].start()
    rest = []
    for k in range(na + 1):
        if k < na - 1:
            line_d(k + 1, widen)
        if k < na:
            second_d(k, widen)
        if k >= 1:
            third_d(k - 1, widen)
        if k == 1:
            start_m()
        if 1 <= k + 1 - 2 < na:
            line_m(k + 1 - 2)
        if 0 <= k - 2 < na:
            second_m(k - 2)
        if 0 <= k - 2 - 1 < 0:
            third_m(k - 2 - 1)
    done_line, done_second, done_third = min(na - 1, na + 1 - 2), min(na - 1, na - 2), min(0 - 1, na - 2 - 1)
    for k in range(na):
        if k > done_line:
            rest.append(lambda k=k: line_m(k))
        if k > done_second:
            rest.append(lambda k=k: second_m(k))
    for k in range(na):
        if k > done_third:
            rest.append(lambda k=k: third_m(k))
    each(0, na, lambda t: partner_d(t, widen))

    def pick(p):
        for c in range(D // 128):
            for i in range(join):
                tmp[c, i * size:(i + 1) * size, :] = src[c, pl.ds(restore[p * join + i] * size, size), :]
            part = pl.ds(pl.multiple_of(p * join * size, 16), join * size)
            table[part, c * 128:(c + 1) * 128] = tmp[c].astype(BF)
    early = -(-D // (join * size))
    each(0, early, pick)
    T = 384

    def project(i):
        part = pl.ds(pl.multiple_of(i * T, T), T)
        query[part, :] = (dot(acts[part, :], table[0:D, :]) + bias).astype(BF)

    def spectra(w):
        part = pl.ds(pl.multiple_of(w * L, 32), L)
        spread_rows(tiles, w, slots, n, dot(basis_ref[...], query[part, :]))

    parts = n * L // T
    for i in range(parts):
        project(i)
    for i in range(4):
        if rest:
            rest.pop(0)()
        each(i * n // 4, (i + 1) * n // 4, spectra)
    while rest:
        rest.pop(0)()

    def table_out():
        at = 0
        for i, ref in enumerate((wqo_h, wup_h, wdn_h)):
            outs.append(load(2 + i, table.at[pl.ds(at, ref.shape[0])], ref))
            outs[-1].start()
            at += ref.shape[0]

    def mix_slots(places):
        taken = []
        for j, jl, m, h in places:
            x = tiles[h, pl.ds(pl.multiple_of(j * n, n), n), :]
            both = jnp.concatenate([x, swap_halves(x)], 0)[:, :64].astype(BF)
            taken.append((both, head_weights(mix, h, pieces, m, pl.ds(pl.multiple_of(jl * depth, depth), depth))))
        products = [dot(both, w) for both, w in taken]
        for (j, jl, m, h), (both, w), y in zip(places, taken, products):
            z[h, pl.ds(pl.multiple_of(j * 2 * n, 2 * n), 2 * n), :] = both
            tiles[h, pl.ds(pl.multiple_of(j * n, n), n), :] = y[:n] + swap_halves(y[n:]) * sign_lanes(n, -1.0, 1.0)

    if pieces == 1:
        def mix_core(core):
            def some(i):
                def slot(jl, _):
                    m = i * 2 + core
                    mix_slots([(m * per + jl, jl, m, p) for p in range(heads)])
                    return 0
                lax.fori_loop(0, per, slot, 0, unroll=4)
            each(0, nmode // 2, some)
        mix_core(here["c"])
        each(early, units, pick)
        table_out()
        each(0, na, partner_m)
        mix_core(1 - here["c"])
    else:
        each(early, units, pick)
        table_out()
        each(0, na, partner_m)

        def slot(j, _):
            mix_slots([(j, lax.rem(j, per), j // per, h) for h in range(heads)])
            return 0
        lax.fori_loop(0, slots, slot, 0, unroll=4)
    outs.append(load(5, mix, weights_h))
    outs[-1].start()
    outs.append(load(6, z, z_h))
    outs[-1].start()

    def signal(w):
        part = pl.ds(pl.multiple_of(w * L, 32), L)
        sig[part, :] = dot(inv_ref[...], gather_rows(tiles, w, slots, n)).astype(BF)
    each(0, n, signal)
    outs.append(load(7, sig, sig_h))
    outs[-1].start()
    drain_d()
    drain_m()
    for o in outs:
        o.wait()


def head(inputs, observed, dense, mixer, restore, bias, mode_index, inv, ff):
    n, L, D = inputs.shape
    slots = mode_index.shape[0]
    ndp, nmode = lax.axis_size("dp"), lax.axis_size("mode")
    nd = ndp * nmode
    rows, mixer_rows = dense.shape[0], mixer.shape[0]
    anywhere = pl.BlockSpec(memory_space=pl.ANY)
    vmem = pl.BlockSpec(memory_space=pltpu.VMEM)
    sem = lambda *s: pltpu.SemaphoreType.DMA(s)
    tokens = n * L
    return pl.pallas_call(
        functools.partial(head_kernel, n, L, D, slots, restore.shape[0]),
        out_shape=(
            jax.ShapeDtypeStruct((tokens, D), BF),
            jax.ShapeDtypeStruct((8, 2 * slots * n, 64), BF),
            jax.ShapeDtypeStruct((tokens, D), BF),
            jax.ShapeDtypeStruct((2 * D, D), BF),
            jax.ShapeDtypeStruct((ff, D), BF),
            jax.ShapeDtypeStruct((ff, D), BF),
            jax.ShapeDtypeStruct((ndp, nmode, mixer_rows, 128), BF),
        ),
        in_specs=[pl.BlockSpec(memory_space=pltpu.SMEM)] * 2 + [anywhere] + [vmem] * 7,
        out_specs=(anywhere,) * 7,
        scratch_shapes=[
            pltpu.VMEM((tokens, D), BF),
            pltpu.VMEM((tokens, D), BF),
            pltpu.VMEM((tokens, D), BF),
            pltpu.VMEM((8, slots * n, 128), F32),
            pltpu.VMEM((8, 2 * slots * n, 64), BF),
            pltpu.VMEM((tokens, D), BF),
            pltpu.VMEM((nd, rows, D), BF),
            pltpu.VMEM((D // 128, nd * rows + 8, 128), F32),
            pltpu.VMEM((nd * rows, D), BF),
            pltpu.VMEM((ndp, nmode, mixer_rows, 128), BF),
            pltpu.VMEM((D // 128, 4 * (nd * rows // restore.shape[0]), 128), F32),
            pltpu.VMEM((2 * slots, 128), F32),
            pltpu.VMEM((2 * slots, L), BF),
            sem(8), sem(2, 3), sem(2, 2, ndp // (nmode // 2)), sem(2, nd),
        ],
        compiler_params=pltpu.CompilerParams(collective_id=0, has_side_effects=True, vmem_limit_bytes=62 * 1024 * 1024),
        name="head",
    )(restore, mode_index, inputs.reshape(tokens, D), dense, mixer, observed, bias, waves(L), inv, np.eye(L, dtype=np.float32))


def adam_terms(weight, gradient, moment, second, step_rate):
    moment_new = BETA_ONE * moment + (1.0 - BETA_ONE) * gradient
    second_new = BETA_TWO * second + (1.0 - BETA_TWO) * gradient * gradient
    scaled_m = moment_new * (1.0 / (1.0 - BETA_ONE**STEP))
    scaled_v = second_new * (1.0 / (1.0 - BETA_TWO**STEP))
    weight_new = weight - step_rate * (scaled_m / (jnp.sqrt(scaled_v) + ADAM_EPS) + DECAY_RATE * weight)
    return moment_new, second_new, weight_new


def update_kernel(chunks, *refs):
    dense, mixer, small, passed = refs[:4], refs[4:8], refs[8:12], refs[12]
    dense_out, mixer_out, small_out, bias_out, passed_out = refs[13:16], refs[16:19], refs[19:22], refs[22], refs[23]
    held, got, put = refs[24:]
    step = held.shape[0] // chunks
    parts = [pl.ds(i * step, step) for i in range(chunks)]
    gets = [pltpu.make_async_copy(passed.at[p], held.at[p], got.at[i]) for i, p in enumerate(parts)]
    puts = [pltpu.make_async_copy(held.at[p], passed_out.at[p], put.at[i]) for i, p in enumerate(parts)]
    for c in gets:
        c.start()
    for i, (ins, outs, rate) in enumerate(((dense, dense_out, RATE_DENSE), (mixer, mixer_out, RATE_MIXER))):
        for ref, value in zip(outs, adam_terms(*(x[...] for x in ins), rate)):
            ref[...] = value
        if i == 0:
            for g, p in zip(gets, puts):
                g.wait()
                p.start()
    size = small[0].shape[0]
    for r in range(-(-size // 128)):
        n = min(128, size - r * 128)
        at = pl.ds(r * 128, n)
        grad = small[1][r:r + 1, :][:, :n]
        row = lambda x: x[at].reshape(1, n)
        terms = adam_terms(row(small[0]), grad, row(small[2]), row(small[3]), RATE_SMALL)
        for ref, value in zip(small_out, terms):
            ref[at] = value.reshape(n)
    for r in range(bias_out.shape[0] // 128):
        bias_out[pl.ds(r * 128, 128)] = small[1][4 + r:5 + r, :].reshape(128)
    for p in puts:
        p.wait()


def update(dense, mixer, small, passed):
    vmem = pl.BlockSpec(memory_space=pltpu.VMEM)
    anywhere = pl.BlockSpec(memory_space=pl.ANY)
    like = lambda x: jax.ShapeDtypeStruct(x.shape, x.dtype)
    chunks = 4
    return pl.pallas_call(
        functools.partial(update_kernel, chunks),
        out_shape=(like(dense[0]),) * 3 + (like(mixer[0]),) * 3 + (like(small[0]),) * 3 + (
            jax.ShapeDtypeStruct((dense[0].shape[1],), F32), like(passed)),
        in_specs=[vmem] * 12 + [anywhere],
        out_specs=(vmem,) * 10 + (anywhere,),
        scratch_shapes=[pltpu.VMEM(passed.shape, F32), pltpu.SemaphoreType.DMA((chunks,)), pltpu.SemaphoreType.DMA((chunks,))],
        compiler_params=pltpu.CompilerParams(vmem_limit_bytes=62 * 1024 * 1024),
        name="update",
    )(*dense, *mixer, *small, passed)


def inverse_table(slots, length):
    turn = np.arange(length)[:, None] * np.arange(slots)[None, :] % length
    angle = turn * (2.0 * np.pi / length)
    scale = np.where(np.arange(slots) == 0, 1.0, 2.0) / length
    return np.concatenate([np.cos(angle) * scale, -np.sin(angle) * scale], 1).astype(np.float32).astype(BF)


def shards(
    inputs,
    observed,
    out_grad,
    mode_index,
    owner_list,
    dense_master,
    dense_first,
    dense_second,
    mixer_master,
    mixer_first,
    mixer_second,
    small_master,
    small_first,
    small_second,
):
    ndp, nmode = lax.axis_size("dp"), lax.axis_size("mode")
    length, width = inputs.shape[1:]
    slots = mode_index.shape[0]
    hidden = (dense_master.shape[0] * ndp * nmode - 2 * width) // 2
    inv = inverse_table(slots, length)
    places = jnp.arange(owner_list.shape[0], dtype=jnp.int32)
    restore = jnp.sum(jnp.where(owner_list[None, :] == places[:, None], places[None, :], 0), axis=1)
    acts, spectra, sig, wqo, wup, wdn, weights = head(
        inputs, observed, dense_master, mixer_master.reshape(-1, mixer_master.shape[2]), restore, small_master,
        mode_index, inv, hidden,
    )
    output, grad_summed, grad_mixed, g_out, g_up, g_down, sums = middle(
        small_master, acts.reshape(inputs.shape), sig.reshape(inputs.shape), out_grad, wqo, wup, wdn,
        small_master, np.ascontiguousarray(inv.T),
    )
    dense_mine, mixer_mine, small_all, input_grad = tail(
        grad_mixed.reshape(-1, width), spectra, acts, grad_summed.reshape(-1, width), observed, wqo, mode_index, weights,
        g_out, g_up, g_down, sums, owner_list, dense_master.shape[0],
    )
    flat = lambda x: x.reshape(-1, x.shape[-1])
    dense_first_new, dense_second_new, dense_new, mixer_first_new, mixer_second_new, mixer_new, *small, input_grad = update(
        (dense_master, dense_mine, dense_first, dense_second),
        (flat(mixer_master), mixer_mine, flat(mixer_first), flat(mixer_second)),
        (small_master, small_all, small_first, small_second),
        input_grad,
    )
    mixer_first_new, mixer_second_new, mixer_new = (
        x.reshape(mixer_master.shape) for x in (mixer_first_new, mixer_second_new, mixer_new)
    )
    return (
        output,
        input_grad.reshape(inputs.shape),
        dense_first_new,
        dense_second_new,
        dense_new,
        mixer_first_new,
        mixer_second_new,
        mixer_new,
        *small,
    )


def solution(mesh):
    placed = (
        P(("dp", "mode"), None, None),
        P(("dp", "mode"), None),
        P(("dp", "mode"), None, None),
        P(),
        P(),
        P(("dp", "mode"), None),
        P(("dp", "mode"), None),
        P(("dp", "mode"), None),
        P("mode", "dp", None),
        P("mode", "dp", None),
        P("mode", "dp", None),
        P(),
        P(),
        P(),
    )
    return jax.shard_map(
        shards,
        mesh=mesh,
        in_specs=placed,
        out_specs=(
            P(("dp", "mode"), None, None),
            P(("dp", "mode"), None, None),
            P(("dp", "mode"), None),
            P(("dp", "mode"), None),
            P(("dp", "mode"), None),
            P("mode", "dp", None),
            P("mode", "dp", None),
            P("mode", "dp", None),
            P(),
            P(),
            P(),
            P(),
        ),
        check_vma=False,
    )
```

```python
import functools
import math

import jax
import jax.numpy as jnp
import numpy as np
from jax import lax
from jax.experimental import pallas as pl
from jax.experimental.pallas import tpu as pltpu
from jax.sharding import PartitionSpec as P

STEP = 10
BETA_ONE = 0.9
BETA_TWO = 0.95
ADAM_EPS = 1e-08
DECAY_RATE = 0.1
RATE_DENSE = 0.03
RATE_MIXER = 0.03
RATE_SMALL = 0.5

KERNEL_SIZES = (7, 12, 14, 24, 48)
ODD = (7, 3, 7, 3, 3)
LOG2E = 1.4426950408889634
BF = jnp.bfloat16
F32 = jnp.float32
NT = (((1,), (1,)), ((), ()))
NN = (((1,), (0,)), ((), ()))
TN = (((0,), (0,)), ((), ()))


def dot(a, b, dims=NN):
    return lax.dot_general(a, b, dims, preferred_element_type=F32)


def average_counts(length):
    tables = []
    t = np.arange(length)
    for size in KERNEL_SIZES:
        u = np.clip(t[:, None] - (size - 1) // 2 + np.arange(size)[None, :], 0, length - 1)
        tables.append((u[:, :, None] == t[None, None, :]).sum(1) * (ODD[len(tables)] / size))
    return np.stack(tables).astype(np.float32)


def gelu_parts(h):
    z = jnp.abs(h)
    e = jnp.exp2(h * h * (-0.5 * LOG2E))
    t = 1.0 / (1.0 + (0.3275911 * math.sqrt(0.5)) * z)
    poly = t * (0.5 * 0.254829592 + t * (-0.5 * 0.284496736 + t * (0.5 * 1.421413741 + t * (-0.5 * 1.453152027 + t * (0.5 * 1.061405429)))))
    tail = poly * e
    big = jnp.where(h < 0, tail, 1.0 - tail)
    return big, e * (1.0 / math.sqrt(2 * math.pi))


def middle_kernel(W, L, D, FF, steps,
                  mix_ref, acts_ref, sig_ref, og_ref, wq_ref, wup_h, wdn_h, bias_ref, invt_ref, cnt_ref, cntt_ref,
                  out_ref, gsum_ref, gmix_ref, gw_ref, gup_ref, gdn_ref, small_ref,
                  vs, base, avg1, c1, v1, active, dgelu, first, flow, gb, ghid, glow, avg2, stk, accs, accb, hs, wg, wsem, wup_ref, wdn_ref, lsem):
    step = pl.program_id(0)
    T = W * L
    CH = 16
    CC = 512
    nc = D // CC
    nr = L // CH
    FT = 512

    fetch = [pltpu.make_async_copy(a, b, lsem.at[i]) for i, (a, b) in enumerate(((wup_h, wup_ref), (wdn_h, wdn_ref)))]

    @pl.when(step == 0)
    def _():
        for f in fetch:
            f.start()
        vs[...] = jnp.zeros_like(vs)
        stk[...] = jnp.zeros_like(stk)
        accs[...] = jnp.zeros_like(accs)
        accb[...] = jnp.zeros_like(accb)
        gw_ref[...] = jnp.zeros_like(gw_ref)

    def fold(x):
        y = x[:, 0:128]
        for i in range(1, CC // 128):
            y = y + x[:, i * 128:(i + 1) * 128]
        return y[0:8] + y[8:16]

    def scaled_shares(v, base_at):
        p = [mix_ref[2 * D + base_at + k] for k in range(10)]
        logits = [((p[k] - p[4]) * LOG2E) * v + (p[5 + k] - p[9]) * LOG2E for k in range(4)]
        top = jnp.maximum(functools.reduce(jnp.maximum, logits), 0.0)
        es = [jnp.exp2(l - top) for l in logits] + [jnp.exp2(-top)]
        r = 1.0 / functools.reduce(lambda a, b: a + b, es)
        scale = {7: r * (1.0 / 7.0), 3: r * (1.0 / 3.0)}
        return [e * scale[o] for e, o in zip(es, ODD)]

    def backward(v, g, cs, avs, mean, base_at, store):
        means = {7: 7.0 * mean, 3: 3.0 * mean}
        total = None
        for k in range(5):
            cg = cs[k] * g
            store(k, cg)
            if k < 4:
                t = cg * (means[ODD[k]] - avs[k])
                term = (mix_ref[2 * D + base_at + k] - mix_ref[2 * D + base_at + 4]) * t
                total = term if total is None else total + term
                accs[base_at + k] += fold(t * v)
                accs[base_at + 5 + k] += fold(t)
        return total

    bias = row_of(bias_ref, D, D)
    sig = sig_ref[...].reshape(T, D)
    base[...] = dot(sig, wq_ref[D:2 * D, :])

    def cut(w, source):
        for i in range(nr):
            for c in range(nc):
                cols = slice(c * CC, (c + 1) * CC)
                v = source(w, i, cols)
                hi = v.astype(BF)
                vs[w % 2, i * CH:(i + 1) * CH, cols] = hi
                vs[w % 2, L + i * CH:L + (i + 1) * CH, cols] = (v - hi.astype(F32)).astype(BF)

    def summed(w, i, cols):
        rows = slice(w * L + i * CH, w * L + (i + 1) * CH)
        v = base[rows, cols] + acts_ref[w, i * CH:(i + 1) * CH, cols].astype(F32) + bias[:, cols]
        v1[rows, cols] = v
        return v

    def averages_one(w):
        cut(w, summed)
        avg1[w * 5 * L:(w + 1) * 5 * L, :] = dot(cnt_ref[...], vs[w % 2])

    def decompose_one(w):
        for i in range(nr):
            for c in range(nc):
                cols = slice(c * CC, (c + 1) * CC)
                rows = slice(w * L + i * CH, w * L + (i + 1) * CH)
                v = v1[rows, cols]
                cs = scaled_shares(v, 0)
                mean = None
                for k in range(5):
                    at = slice((w * 5 + k) * L + i * CH, (w * 5 + k) * L + (i + 1) * CH)
                    u = cs[k] * avg1[at, cols]
                    c1[at, cols] = cs[k]
                    mean = u if mean is None else mean + u
                f = v - mean
                first[rows, cols] = f
                flow[pl.ds(pl.multiple_of(step * T + w * L + i * CH, CH), CH), cols] = f.astype(BF)

    averages_one(0)
    for w in range(W):
        if w + 1 < W:
            averages_one(w + 1)
        decompose_one(w)

    here_t = pl.ds(pl.multiple_of(step * T, CH), T)
    base[...] = first[...]

    def up(n):
        return dot(flow[here_t, :], wup_ref[n * FT:(n + 1) * FT, :], NT)

    tiles = FF // FT
    @pl.when(step == 0)
    def _():
        for f in fetch:
            f.wait()
    hs[0] = up(0)
    for n in range(tiles + 1):
        if n + 1 < tiles:
            hs[(n + 1) % 2] = up(n + 1)
        if n < tiles:
            h = hs[n % 2]
            big, small = gelu_parts(h)
            active[here_t, n * FT:(n + 1) * FT] = (h * big).astype(BF)
            dgelu[:, n * FT:(n + 1) * FT] = (big + h * small).astype(BF)
        if n:
            base[...] += dot(active[here_t, (n - 1) * FT:n * FT], wdn_ref[(n - 1) * FT:n * FT, :])

    def branch(w, i, cols):
        return base[w * L + i * CH:w * L + (i + 1) * CH, cols]

    def averages_two(w):
        cut(w, branch)
        avg2[w % 2] = dot(cnt_ref[...], vs[w % 2])

    def keep_at(w, i, cols):
        def keep(k, cg):
            stk[w % 2, k * L + i * CH:k * L + (i + 1) * CH, cols] = cg.astype(BF)
        return keep

    def decompose_two(w):
        for i in range(nr):
            for c in range(nc):
                cols = slice(c * CC, (c + 1) * CC)
                rows = slice(w * L + i * CH, w * L + (i + 1) * CH)
                here = slice(i * CH, (i + 1) * CH)
                v = base[rows, cols]
                cs = scaled_shares(v, 10)
                avs = [avg2[w % 2, k * L + i * CH:k * L + (i + 1) * CH, cols] for k in range(5)]
                mean = functools.reduce(lambda a, b: a + b, [c_ * a_ for c_, a_ in zip(cs, avs)])
                out_ref[w, here, cols] = (v - mean).astype(BF)
                g = og_ref[w, here, cols].astype(F32)
                base[rows, cols] = g + backward(v, g, cs, avs, mean, 10, keep_at(w, i, cols))

    def back_two(w):
        rows = slice(w * L, (w + 1) * L)
        gs = base[rows, :] - dot(cntt_ref[...], stk[w % 2])
        base[rows, :] = gs
        gb[pl.ds(pl.multiple_of(step * T + w * L, 32), L), :] = gs.astype(BF)

    averages_two(0)
    for w in range(W):
        if w + 1 < W:
            averages_two(w + 1)
        decompose_two(w)
        if w:
            back_two(w - 1)
    back_two(W - 1)

    def down(n):
        return dot(gb[here_t, :], wdn_ref[n * FT:(n + 1) * FT, :], NT)

    hs[0] = down(0)
    for n in range(tiles + 1):
        if n + 1 < tiles:
            hs[(n + 1) % 2] = down(n + 1)
        if n < tiles:
            ghid[here_t, n * FT:(n + 1) * FT] = (hs[n % 2] * dgelu[:, n * FT:(n + 1) * FT].astype(F32)).astype(BF)
        if n:
            base[...] += dot(ghid[here_t, (n - 1) * FT:n * FT], wup_ref[(n - 1) * FT:n * FT, :])

    def decompose_three(w):
        for i in range(nr):
            for c in range(nc):
                cols = slice(c * CC, (c + 1) * CC)
                rows = slice(w * L + i * CH, w * L + (i + 1) * CH)
                v = v1[rows, cols]
                g = base[rows, cols]
                ats = [slice((w * 5 + k) * L + i * CH, (w * 5 + k) * L + (i + 1) * CH) for k in range(5)]
                cs = [c1[at, cols] for at in ats]
                avs = [avg1[at, cols] for at in ats]
                mean = v - first[rows, cols]
                extra = backward(v, g, cs, avs, mean, 0, keep_at(w, i, cols))
                base[rows, cols] = g + extra
                accb[:, cols] += extra[0:8] + extra[8:16]

    def back_three(w):
        rows = slice(w * L, (w + 1) * L)
        gs = base[rows, :] - dot(cntt_ref[...], stk[w % 2])
        gsum_ref[w] = gs
        glow[rows, :] = gs.astype(BF)

    for w in range(W):
        decompose_three(w)
        if w:
            back_three(w - 1)
    back_three(W - 1)

    back = dot(glow[...], wq_ref[D:2 * D, :], NT).astype(BF)
    for w in range(W):
        gmix_ref[w] = dot(invt_ref[...], back[w * L:(w + 1) * L, :]).astype(BF)
    gw_ref[...] += dot(sig, glow[...], TN)

    @pl.when(step == steps - 1)
    def _():
        small_ref[0:8, :] = accb[...]
        for at in (4, 9, 14, 19):
            accs[at] = -(accs[at - 4] + accs[at - 3] + accs[at - 2] + accs[at - 1])
        for k in range(20):
            small_ref[8 + 8 * k:16 + 8 * k, 0:128] = accs[k]
            small_ref[8 + 8 * k:16 + 8 * k, 128:512] = jnp.zeros((8, 384), F32)

        copies = {}
        for n in range(tiles):
            part = slice(n * FT, (n + 1) * FT)
            for i, (left, right, ref) in enumerate(((ghid, flow, gup_ref), (active, gb, gdn_ref))):
                k = (n % 2) * 2 + i
                if n >= 2:
                    copies[n - 2, i].wait()
                wg[k] = dot(left[:, part], right[...], TN)
                copies[n, i] = pltpu.make_async_copy(wg.at[k], ref.at[pl.ds(n * FT, FT)], wsem.at[k])
                copies[n, i].start()
        for n in range(max(tiles - 2, 0), tiles):
            for i in range(2):
                copies[n, i].wait()


def middle(mix, acts, sig, og, wqo, wup, wdn, bias, invt, W=4):
    n, L, D = acts.shape
    FF = wup.shape[0]
    steps = n // W
    T = W * L
    A = average_counts(L)
    cnt = np.zeros((5 * L, 256), np.float32)
    cnt[:, :L] = A.reshape(5 * L, L)
    cnt[:, L:2 * L] = A.reshape(5 * L, L)
    cntt = np.zeros((L, 512), np.float32)
    cntt[:, :5 * L] = A.transpose(2, 0, 1).reshape(L, 5 * L)
    cnt, cntt = (np.asarray(x, BF) for x in (cnt, cntt))
    whole = lambda *s: pl.BlockSpec(s, lambda i: (0,) * len(s), pipeline_mode=pl.Buffered(1))
    anywhere = pl.BlockSpec(memory_space=pl.ANY)
    piece = lambda *s: pl.BlockSpec(s, lambda i: (i,) + (0,) * (len(s) - 1))
    return pl.pallas_call(
        functools.partial(middle_kernel, W, L, D, FF, steps),
        grid=(steps,),
        out_shape=(
            jax.ShapeDtypeStruct((n, L, D), BF),
            jax.ShapeDtypeStruct((n, L, D), F32),
            jax.ShapeDtypeStruct((n, L, D), BF),
            jax.ShapeDtypeStruct((D, D), F32),
            jax.ShapeDtypeStruct((FF, D), F32),
            jax.ShapeDtypeStruct((FF, D), F32),
            jax.ShapeDtypeStruct((168, D), F32),
        ),
        in_specs=[
            pl.BlockSpec(memory_space=pltpu.SMEM),
            piece(W, L, D), piece(W, L, D), piece(W, L, D),
            whole(2 * D, D), anywhere, anywhere, whole(bias.shape[0]), whole(L, L), whole(5 * L, 256), whole(L, 512),
        ],
        out_specs=(
            piece(W, L, D), piece(W, L, D), piece(W, L, D), whole(D, D), anywhere, anywhere, whole(168, D),
        ),
        scratch_shapes=[
            pltpu.VMEM((2, 256, D), BF),
            pltpu.VMEM((T, D), F32),
            pltpu.VMEM((W * 5 * L, D), F32),
            pltpu.VMEM((W * 5 * L, D), F32),
            pltpu.VMEM((T, D), F32),
            pltpu.VMEM((n * L, FF), BF),
            pltpu.VMEM((T, FF), BF),
            pltpu.VMEM((T, D), F32),
            pltpu.VMEM((n * L, D), BF),
            pltpu.VMEM((n * L, D), BF),
            pltpu.VMEM((n * L, FF), BF),
            pltpu.VMEM((T, D), BF),
            pltpu.VMEM((2, 5 * L, D), F32),
            pltpu.VMEM((2, 512, D), BF),
            pltpu.VMEM((20, 8, 128), F32),
            pltpu.VMEM((8, D), F32),
            pltpu.VMEM((2, T, 512), F32),
            pltpu.VMEM((4, 512, D), F32),
            pltpu.SemaphoreType.DMA((4,)),
            pltpu.VMEM((FF, D), BF),
            pltpu.VMEM((FF, D), BF),
            pltpu.SemaphoreType.DMA((2,)),
        ],
        compiler_params=pltpu.CompilerParams(vmem_limit_bytes=60 * 1024 * 1024),
        name="middle",
    )(mix, acts, sig, og, wqo, wup, wdn, bias, invt, cnt, cntt)


def sign_lanes(rows, left, right):
    lane = lax.broadcasted_iota(jnp.int32, (rows, 128), 1)
    return jnp.where(lane < 64, left, right).astype(F32)


def interleave(real, imag, v):
    re, im = real[:, v * 128:(v + 1) * 128], imag[:, v * 128:(v + 1) * 128]
    low = lax.broadcasted_iota(jnp.int32, re.shape, 1) < 64
    return jnp.where(low, re, pltpu.roll(im, 64, 1)), jnp.where(low, pltpu.roll(re, 64, 1), im)


def gather_rows(tiles, w, slots, n):
    reals, imags = [], []
    for v in range(4):
        first = tiles[2 * v, pl.ds(w, slots, stride=n), :]
        second = tiles[2 * v + 1, pl.ds(w, slots, stride=n), :]
        low = lax.broadcasted_iota(jnp.int32, first.shape, 1) < 64
        reals.append(jnp.where(low, first, pltpu.roll(second, 64, 1)).astype(BF))
        imags.append(jnp.where(low, pltpu.roll(first, 64, 1), second).astype(BF))
    return jnp.concatenate([jnp.concatenate(reals, 1), jnp.concatenate(imags, 1)], 0)


def spread_rows(tiles, w, slots, n, spectrum):
    for v in range(4):
        one, two = interleave(spectrum[:slots], spectrum[slots:], v)
        tiles[2 * v, pl.ds(w, slots, stride=n), :] = one
        tiles[2 * v + 1, pl.ds(w, slots, stride=n), :] = two


def swap_halves(x):
    return pltpu.roll(x, 64, 1)


def head_weights(weights, h, pieces, mode, rows):
    return jnp.concatenate([weights[h * pieces + q, mode, rows, :] for q in range(pieces)], 0)


MESH = pl.DeviceIdType.MESH


def move(sizes, at, axis, d):
    return {**at, axis: lax.rem(at[axis] + d, sizes[axis])}


def greet():
    ndp, nmode = lax.axis_size("dp"), lax.axis_size("mode")
    dp, mode = lax.axis_index("dp"), lax.axis_index("mode")
    barrier = pltpu.get_barrier_semaphore()
    for d in range(1, nmode):
        pl.semaphore_signal(barrier, 1, device_id={"dp": dp, "mode": lax.rem(mode + d, nmode)}, device_id_type=MESH)
    for d in range(1, ndp):
        pl.semaphore_signal(barrier, 1, device_id={"dp": lax.rem(dp + d, ndp), "mode": mode}, device_id_type=MESH)
    pl.semaphore_wait(barrier, ndp + nmode - 2)


def staggered(count, *stages):
    k = len(stages)
    if count < k:
        for stage in stages:
            for t in range(count):
                stage(t)
        return
    for t in range(k - 1):
        for s in range(t + 1):
            stages[s](t - s)

    def body(t, _):
        for s in range(k):
            stages[s](t - s)
        return 0
    lax.fori_loop(k - 1, count, body, 0)
    for t in range(count, count + k - 1):
        for s in range(t - count + 1, k):
            stages[s](t - s)


JOIN = 12


def waves(length):
    angle = (np.arange(length)[:, None] * np.arange(length)[None, :] % length) * (2.0 * np.pi / length)
    table = np.zeros((2 * length, 128), np.float32)
    table[:length, :length] = np.cos(angle)
    table[length:, :length] = -np.sin(angle)
    return table


def pick_waves(mode_list, waves_ref, rows):
    slots = mode_list.shape[0]
    for j in range(slots):
        for part in range(2):
            at = mode_list[j] + part * (waves_ref.shape[0] // 2)
            rows[part * slots + j:part * slots + j + 1, :] = waves_ref[pl.ds(at, 1), :]


def row_of(ref, start, size):
    return jnp.concatenate([ref[pl.ds(start + i * 128, 128)].reshape(1, 128) for i in range(size // 128)], 1)


def roles():
    ndp, nmode = lax.axis_size("dp"), lax.axis_size("mode")
    half = nmode // 2
    dp, mode = lax.axis_index("dp"), lax.axis_index("mode")
    b, y, c = lax.rem(dp, half), mode // 2, lax.rem(mode, 2)
    here = {"a": dp // half, "u": jnp.where(c == 0, b, y), "v": jnp.where(c == 0, y, b), "c": c}
    return {"a": ndp // half, "u": half, "v": half, "c": 2}, here


def place_of(sizes, at):
    b = jnp.where(at["c"] == 0, at["u"], at["v"])
    y = jnp.where(at["c"] == 0, at["v"], at["u"])
    return at["a"] * sizes["u"] + b, y * 2 + at["c"]


def device_of(sizes, at):
    dp, mode = place_of(sizes, at)
    return {"dp": dp, "mode": mode}


def partner_of(at):
    return {"a": at["a"], "u": at["v"], "v": at["u"], "c": 1 - at["c"]}


def reducer(sizes, here, own, from_c, from_v, from_u, from_a, out, send, recv_c, recv_v, recv_u, recv_a):
    na, nu, nv = sizes["a"], sizes["u"], sizes["v"]
    rows = from_c.shape[1]
    step = next(s for s in (96, 32, rows) if rows % s == 0)

    def owner(t, e, d):
        return move(sizes, move(sizes, move(sizes, here, "a", t + 1), "u", e), "v", d)

    def spot(at):
        dp, mode = place_of(sizes, at)
        return dp * sizes["v"] + mode // 2

    def to_partner(at):
        n = spot(at)
        return pltpu.make_async_remote_copy(
            src_ref=own(at), dst_ref=from_c.at[n], send_sem=send.at[0], recv_sem=recv_c.at[n],
            device_id=device_of(sizes, partner_of(here)), device_id_type=MESH)

    def chunks(at, terms, store):
        mine = own(at)

        def chunk(i, _):
            part = pl.ds(pl.multiple_of(i * step, step), step) if step != rows else slice(None)
            total = mine[part, :].astype(F32)
            for ref, k in terms:
                total = total + ref[k, part, :].astype(F32)
            store(mine, part, total)
            return 0
        lax.fori_loop(0, rows // step, chunk, 0)

    def keep(mine, part, total):
        mine[part, :] = total.astype(BF)

    def finish(mine, part, total):
        out[part, :] = total

    def slot_v(t, e, d):
        return (t * nu + e) * (nv - 1) + d - 1

    def copy(at, buffer, s, stage, sems, to):
        return pltpu.make_async_remote_copy(
            src_ref=own(at), dst_ref=buffer.at[s], send_sem=send.at[stage], recv_sem=sems.at[s],
            device_id=device_of(sizes, to), device_id_type=MESH)

    def copy_v(t, e, d):
        s = slot_v(t, e, d)
        return copy(owner(t, e, d), from_v, s, 1, recv_v, move(sizes, here, "v", d))

    def copy_u(t, e):
        return copy(owner(t, e, 0), from_u, t * (nu - 1) + e - 1, 2, recv_u, move(sizes, here, "u", e))

    def copy_a(t):
        return copy(owner(t, 0, 0), from_a, t, 3, recv_a, owner(t, 0, 0))

    def heard(at):
        n = spot(at)
        pltpu.make_async_remote_copy(
            src_ref=own(at), dst_ref=from_c.at[n], send_sem=send.at[0], recv_sem=recv_c.at[n],
            device_id=device_of(sizes, partner_of(here)), device_id_type=MESH).wait_recv()
        return [(from_c, n)]

    def first(t):
        for d in range(1, nv):
            for e in range(nu):
                at = owner(t, e, d)
                chunks(at, heard(at), keep)
                copy_v(t, e, d).start()

    def after_v(t, e):
        terms = heard(owner(t, e, 0))
        for d in range(1, nv):
            copy_v(t, e, d).wait_recv()
            terms.append((from_v, slot_v(t, e, d)))
        return terms

    def second(t):
        for e in range(1, nu):
            chunks(owner(t, e, 0), after_v(t, e), keep)
            copy_u(t, e).start()

    def after_u(t):
        terms = after_v(t, 0)
        for e in range(1, nu):
            copy_u(t, e).wait_recv()
            terms.append((from_u, t * (nu - 1) + e - 1))
        return terms

    def third(t):
        chunks(owner(t, 0, 0), after_u(t), keep)
        copy_a(t).start()

    def last():
        terms = after_u(na - 1)
        for t in range(na - 1):
            copy_a(t).wait_recv()
            terms.append((from_a, t))
        chunks(here, terms, finish)

    def drain():
        for stage, count in ((0, from_c.shape[0]), (1, na * nu * (nv - 1)), (2, na * (nu - 1)), (3, na - 1)):
            ref = from_c.at[pl.ds(0, count)]
            pltpu.make_async_copy(ref, ref, send.at[stage]).wait()

    return to_partner, first, second, third, last, drain


def each(start, stop, *steps):
    def body(t, _):
        for s in steps:
            s(t)
        return 0
    lax.fori_loop(start, stop, body, 0)


def tail_kernel(n, L, D, slots, blocks, owner, mode_list, gmix_h, z_h, acts_h, gsum_h, weights_h, gout_h, gup_h, gdn_h,
                obs_ref, wqo_h, waves_ref, eye_ref, sums_ref,
                dense_out, mixer_out, small_out, gin_h,
                gmix, z, acts, gsum, mix, src, tiles, glow, gbias, tmp, con, basis_rows, basist, wq_ref,
                fc0, fc1, fv0, fv1, fu0, fu1, fa0, fa1, small_one, small_two,
                loads, send, recv_c, recv_v, recv_u, recv_a, small_send, small_recv):
    sizes, here = roles()
    ndp, nmode = lax.axis_size("dp"), lax.axis_size("mode")
    dp, mode = lax.axis_index("dp"), lax.axis_index("mode")
    na = sizes["a"]
    per = slots // nmode
    heads = 8
    pieces = ndp // heads
    depth = 64 // pieces
    rows = con.shape[1]
    size = con.shape[0] * rows // blocks

    def load(i, a, b):
        return pltpu.make_async_copy(a, b, loads.at[i])
    firsts = [load(0, gmix_h, gmix), load(1, z_h, z), load(2, weights_h, mix)]
    later = [load(3, acts_h, acts), load(4, gsum_h, gsum), load(18, wqo_h.at[pl.ds(0, D)], wq_ref)]
    grads = []
    start = D
    for i, ref in enumerate((gout_h, gup_h, gdn_h)):
        for c in range(D // 128):
            grads.append(load(5 + i * 4 + c, ref.at[:, pl.ds(c * 128, 128)], src.at[c, pl.ds(start, ref.shape[0]), :]))
        start += ref.shape[0]
    for c in firsts + later + grads:
        c.start()
    greet()

    send_m, first_m, second_m, third_m, last_m, drain_m = reducer(
        sizes, here, lambda at: mix.at[place_of(sizes, at)], fc1, fv1, fu1, fa1, mixer_out,
        send.at[1], recv_c.at[1], recv_v.at[1], recv_u.at[1], recv_a.at[1])

    def con_at(at):
        p, m = place_of(sizes, at)
        return con.at[p * nmode + m]
    send_d, first_d, second_d, third_d, last_d, drain_d = reducer(
        sizes, here, con_at, fc0, fv0, fu0, fa0, dense_out,
        send.at[0], recv_c.at[0], recv_v.at[0], recv_u.at[0], recv_a.at[0])

    pick_waves(mode_list, waves_ref, basis_rows)
    basist[...] = basis_rows[:, 0:L].T.astype(BF)
    firsts[0].wait()

    def spectra(w):
        part = pl.ds(pl.multiple_of(w * L, 32), L)
        spread_rows(tiles, w, slots, n, gmix[part, :].astype(F32))
    each(0, n, spectra)
    firsts[1].wait()
    firsts[2].wait()

    def mix_slots(places):
        taken = []
        for m, jl, h in places:
            y = tiles[h, pl.ds(pl.multiple_of((m * per + jl) * n, n), n), :]
            both = jnp.concatenate([y, swap_halves(y) * sign_lanes(n, 1.0, -1.0)], 0).astype(BF)
            part = pl.ds(pl.multiple_of(jl * depth, depth), depth)
            x = z[h, pl.ds(pl.multiple_of((m * per + jl) * 2 * n, 2 * n), 2 * n), :]
            taken.append((both, head_weights(mix, h, pieces, m, part), x))
        products = [(dot(both, w, NT), dot(x, both, TN).astype(BF)) for both, w, x in taken]
        for (m, jl, h), (x, g) in zip(places, products):
            part = pl.ds(pl.multiple_of(jl * depth, depth), depth)
            tiles[h, pl.ds(pl.multiple_of((m * per + jl) * n, n), n), :] = jnp.concatenate([x[:n], x[n:]], 1)
            for q in range(pieces):
                mix[h * pieces + q, m, part, :] = g[q * depth:(q + 1) * depth]

    if pieces == 1:
        def mix_shard(at):
            p, m = place_of(sizes, at)
            y_at = tiles.at[p, pl.ds(pl.multiple_of(m * per * n, per * n), per * n)]
            z_at = z.at[p, pl.ds(pl.multiple_of(m * per * 2 * n, per * 2 * n), per * 2 * n)]
            w_at = mix.at[p, m]
            for start in range(0, per, JOIN):
                group = range(start, min(start + JOIN, per))
                ys = [y_at[j * n:(j + 1) * n, :] for j in group]
                boths = [jnp.concatenate([y, swap_halves(y) * sign_lanes(n, 1.0, -1.0)], 0).astype(BF) for y in ys]
                xs = [dot(both, w_at[j * 64:(j + 1) * 64, :], NT) for both, j in zip(boths, group)]
                gs = [dot(z_at[j * 2 * n:(j + 1) * 2 * n, :], both, TN).astype(BF) for both, j in zip(boths, group)]
                for x, g, j in zip(xs, gs, group):
                    y_at[j * n:(j + 1) * n, :] = jnp.concatenate([x[:n], x[n:]], 1)
                    w_at[j * 64:(j + 1) * 64, :] = g

        def feed(t, d):
            def pair(e):
                other = move(sizes, move(sizes, move(sizes, partner_of(here), "a", t + 1), "u", e), "v", d)
                mix_shard(other)
                send_m(other).start()
                mix_shard(move(sizes, move(sizes, move(sizes, here, "a", t + 1), "u", e), "v", d))
            each(0, sizes["u"], pair)
        def far(t):
            for d in range(1, sizes["v"]):
                feed(t, d)
        staggered(na, far, first_m)
        each(0, na, lambda t: feed(t, 0))
    else:
        def mix_mode(m):
            def slot(jl, _):
                mix_slots([(m, jl, h) for h in range(heads)])
                return 0
            lax.fori_loop(0, per, slot, 0, unroll=2)

        def mode_at(i, core):
            return lax.rem(mode // 2 + 1 + i, nmode // 2) * 2 + core

        def other_modes(i):
            m = mode_at(i, 1 - here["c"])
            mix_mode(m)

            def hand(p):
                half = sizes["u"]
                b, y = lax.rem(p, half), m // 2
                core = 1 - here["c"]
                send_m({"a": p // half, "u": jnp.where(core == 0, b, y), "v": jnp.where(core == 0, y, b), "c": core}).start()
            each(0, ndp, hand)
        each(0, nmode // 2, other_modes)
        each(0, nmode // 2, lambda i: mix_mode(mode_at(i, here["c"])))
        each(0, na, first_m)

    gbias[...] = jnp.zeros_like(gbias)

    def query(w):
        part = pl.ds(pl.multiple_of(w * L, 32), L)
        g = dot(basist[...], gather_rows(tiles, w, slots, n))
        glow[part, :] = g.astype(BF)
        gbias[...] += functools.reduce(lambda p, q: p + q, [g[i * 8:(i + 1) * 8] for i in range(L // 8)])
    each(0, n // 2, query)
    each(0, 1, second_m)
    each(n // 2, n, query)

    for k, sums in ((0, gbias[...]), (4, sums_ref[0:8, :])):
        total = jnp.sum(sums, axis=0, keepdims=True)
        for c in range(D // 128):
            small_one[mode, k + c:k + c + 1, :] = total[:, c * 128:(c + 1) * 128]
    for k in range(20):
        small_one[mode, 8 + k:9 + k, :] = jnp.sum(sums_ref[8 + 8 * k:16 + 8 * k, 0:128], axis=0, keepdims=True)
    small_one[mode, 28:32, :] = jnp.zeros((4, 128), F32)

    def small_copy(buffer, axis, index, count, d, base):
        return pltpu.make_async_remote_copy(
            src_ref=buffer.at[index], dst_ref=buffer.at[index], send_sem=small_send.at[base + d - 1], recv_sem=small_recv.at[base + d - 1],
            device_id={**{"dp": dp, "mode": mode}, axis: lax.rem(index + d, count)}, device_id_type=MESH)
    ones = [small_copy(small_one, "mode", mode, nmode, d, 0) for d in range(1, nmode)]
    twos = [small_copy(small_two, "dp", dp, ndp, d, nmode - 1) for d in range(1, ndp)]
    for c in ones:
        c.start()

    for c in later:
        c.wait()
    g = dot(acts[...], glow[...], TN)
    for c in range(D // 128):
        src[c, 0:D, :] = g[:, c * 128:(c + 1) * 128]
    each(1, na // 2, second_m)
    for c in grads:
        c.wait()

    per_shard = rows // size
    join = 4 if per_shard % 4 == 0 else 1
    units = per_shard // join

    def pick(s):
        for k in range(units):
            for c in range(D // 128):
                for i in range(join):
                    row = owner[(s * units + k) * join + i] * size
                    tmp[c, i * size:(i + 1) * size, :] = src[c, pl.ds(row, size), :]
                part = slice(k * join * size, (k + 1) * join * size)
                con[s, part, c * 128:(c + 1) * 128] = tmp[c, 0:join * size, :].astype(BF)
    shards = con.shape[0]
    each(0, shards // 2, pick)
    each(na // 2, na, second_m)
    each(0, na // 2, third_m)
    each(shards // 2, shards, pick)

    def hand_line(t):
        other = partner_of(here)
        for d in list(range(1, sizes["v"])) + [0]:
            for e in range(sizes["u"]):
                send_d(move(sizes, move(sizes, move(sizes, other, "a", t + 1), "u", e), "v", d)).start()
    each(0, na, hand_line)
    each(na // 2, na - 1, third_m)

    def input_grad(w):
        part = pl.ds(pl.multiple_of(w * L, 32), L)
        row = obs_ref[pl.ds(w, 1), :].astype(F32)
        mask = dot((eye_ref[...] * row).astype(BF), jnp.ones((L, 128), BF))
        g = gsum[part, :] + dot(glow[part, :], wq_ref[...], NT)
        for c in range(D // 128):
            gsum[part, c * 128:(c + 1) * 128] = g[:, c * 128:(c + 1) * 128] * mask
    for c in ones:
        c.wait()
    small_two[dp] = functools.reduce(lambda p, q: p + q, [small_one[i] for i in range(nmode)])
    for c in twos:
        c.start()
    each(0, na, first_d)
    each(0, n, input_grad)
    result = load(17, gsum, gin_h)
    result.start()
    each(0, 1, second_d)
    each(1, na - 1, second_d, lambda t: third_d(t - 1))
    last_m()
    second_d(na - 1)
    third_d(na - 2)
    last_d()
    for c in twos:
        c.wait()
    total = functools.reduce(lambda p, q: p + q, [small_two[i] for i in range(ndp)])
    small_out[0:8, :] = total[0:8]
    small_out[8:16, :] = jnp.zeros((8, 128), F32)
    small_out[8:16, 0:24] = lax.dot_general(
        jnp.ones((8, 128), F32), total[8:32], NT, precision=lax.Precision.HIGHEST, preferred_element_type=F32)
    drain_m()
    drain_d()
    result.wait()


def tail(gmix, z, acts, gsum, observed, wqo, mode_index, weights, gout, gup, gdn, sums, owner_list, shard_rows):
    n, L = observed.shape
    D = acts.shape[1]
    slots = mode_index.shape[0]
    ndp, nmode, mixer_rows = weights.shape[:3]
    nd = ndp * nmode
    total = nd * shard_rows
    half = nmode // 2
    na = ndp // half
    group = nd // 2
    anywhere = pl.BlockSpec(memory_space=pl.ANY)
    vmem = pl.BlockSpec(memory_space=pltpu.VMEM)
    shapes = ((shard_rows, D), (mixer_rows, 128))
    counts = (group, na * half * (half - 1), na * (half - 1), na - 1)
    sem = lambda *s: pltpu.SemaphoreType.DMA(s)
    return pl.pallas_call(
        functools.partial(tail_kernel, n, L, D, slots, owner_list.shape[0]),
        out_shape=(
            jax.ShapeDtypeStruct(shapes[0], F32), jax.ShapeDtypeStruct(shapes[1], F32), jax.ShapeDtypeStruct((16, 128), F32),
            jax.ShapeDtypeStruct((n * L, D), F32),
        ),
        in_specs=[pl.BlockSpec(memory_space=pltpu.SMEM)] * 2 + [anywhere] * 8 + [
            vmem, anywhere, vmem, vmem, vmem],
        out_specs=(vmem, vmem, vmem, anywhere),
        scratch_shapes=[
            pltpu.VMEM((n * L, D), BF),
            pltpu.VMEM(z.shape, BF),
            pltpu.VMEM((n * L, D), BF),
            pltpu.VMEM((n * L, D), F32),
            pltpu.VMEM(weights.shape, BF),
            pltpu.VMEM((D // 128, total + 8, 128), F32),
            pltpu.VMEM((8, slots * n, 128), F32),
            pltpu.VMEM((n * L, D), BF),
            pltpu.VMEM((8, D), F32),
            pltpu.VMEM((D // 128, 80, 128), F32),
            pltpu.VMEM((nd, shard_rows, D), BF),
            pltpu.VMEM((2 * slots, 128), F32),
            pltpu.VMEM((L, 2 * slots), BF),
            pltpu.VMEM((D, D), BF),
        ] + [pltpu.VMEM((count,) + s, BF) for count in counts for s in shapes] + [
            pltpu.VMEM((nmode, 32, 128), F32), pltpu.VMEM((ndp, 32, 128), F32),
            sem(19), sem(2, 4), sem(2, counts[0]), sem(2, counts[1]), sem(2, counts[2]), sem(2, counts[3]),
            sem(ndp + nmode - 2), sem(ndp + nmode - 2),
        ],
        compiler_params=pltpu.CompilerParams(collective_id=1, has_side_effects=True, vmem_limit_bytes=62 * 1024 * 1024),
        name="tail",
    )(owner_list, mode_index, gmix, z, acts, gsum, weights, gout, gup, gdn, observed, wqo, waves(L), np.eye(L, dtype=np.float32), sums)


def gatherer(sizes, here, slot_of, whole_of, send, send_a, recv):
    na, nu, nv = sizes["a"], sizes["u"], sizes["v"]

    def spot(at):
        dp, mode = place_of(sizes, at)
        return dp * sizes["v"] * 2 + mode

    def copy(at, to, sem):
        ref = slot_of(at)
        return pltpu.make_async_remote_copy(
            src_ref=ref, dst_ref=ref, send_sem=sem, recv_sem=recv.at[spot(at)],
            device_id=device_of(sizes, to), device_id_type=MESH)

    def onward(at, axes):
        for axis, stage in axes:
            for d in range(1, sizes[axis]):
                copy(at, move(sizes, here, axis, d), send.at[stage]).start()
        copy(at, partner_of(here), send.at[2]).start()

    def hop(k, side):
        first, to = here["a"] - side * k, here["a"] + side
        there = (first >= 0) & (first < na) & (to >= 0) & (to < na)
        way = 0 if side == 1 else 1
        inside = lambda x: jnp.clip(x, 0, na - 1)
        return there, lambda: copy({**here, "a": inside(first)}, {**here, "a": inside(to)}, send_a.at[way, k])

    def hops(k, side):
        there, make = hop(k, side)
        pl.when(there)(lambda: make().start())

    def arrived(at):
        copy(at, here, send.at[0]).wait_recv()
        return at

    def lines(k, act):
        for side in ((1, -1) if k else (1,)):
            to = here["a"] - side * k
            pl.when((to >= 0) & (to < na))(lambda side=side, to=to: act({**here, "a": to}, side))

    def start():
        for side in (1, -1):
            hops(0, side)
        onward(here, (("u", 0), ("v", 1)))

    def line(k, then=lambda at: None):
        def act(at, side):
            arrived(at)
            hops(k, side)
            onward(at, (("u", 0), ("v", 1)))
            then(at)
        lines(k, act)

    def second(k, then=lambda at: None):
        def act(at, side):
            for d in range(1, nu):
                to = arrived(move(sizes, at, "u", d))
                onward(to, (("v", 1),))
                then(to)
        lines(k, act)

    def third(k, then=lambda at: None):
        def act(at, side):
            for e in range(nu):
                for d in range(1, nv):
                    to = arrived(move(sizes, move(sizes, at, "u", e), "v", d))
                    onward(to, ())
                    then(to)
        lines(k, act)

    def partner(t, then=lambda at: None):
        other = partner_of(here)
        for e in range(nu):
            for d in range(nv):
                then(arrived(move(sizes, move(sizes, move(sizes, other, "a", t), "u", e), "v", d)))

    def drain():
        for stage, count in ((0, na * (nu - 1)), (1, na * nu * (nv - 1)), (2, na * nu * nv)):
            ref = whole_of(count)
            pltpu.make_async_copy(ref, ref, send.at[stage]).wait()
        for k in range(na):
            for side in (1, -1):
                there, make = hop(k, side)
                pl.when(there)(lambda make=make: make().wait_send())

    return start, line, second, third, partner, drain


def head_kernel(n, L, D, slots, blocks, restore, mode_list, in_h, dense_ref, mixer_ref, obs_ref, bias_ref, waves_ref, inv_ref, eye_ref,
                acts_h, z_h, sig_h, wqo_h, wup_h, wdn_h, weights_h,
                inputs, acts, query, tiles, z, sig, buf, src, table, mix, tmp, basis_rows, basis_ref,
                loads, send, send_a, recv):
    sizes, here = roles()
    ndp, nmode = lax.axis_size("dp"), lax.axis_size("mode")
    dp, mode = lax.axis_index("dp"), lax.axis_index("mode")
    na = sizes["a"]
    per = slots // nmode
    heads = 8
    pieces = ndp // heads
    depth = 64 // pieces
    rows = buf.shape[1]
    total = buf.shape[0] * rows
    size = total // blocks
    join = 4
    units = blocks // join

    def load(i, a, b):
        return pltpu.make_async_copy(a, b, loads.at[i])
    load_in = load(0, in_h, inputs)
    load_in.start()
    pick_waves(mode_list, waves_ref, basis_rows)
    basis_ref[...] = basis_rows[:, 0:L].astype(BF)
    bias = row_of(bias_ref, 0, D)
    buf[dp * nmode + mode] = dense_ref[...].astype(BF)
    mix[dp, mode] = mixer_ref[...].astype(BF)
    greet()

    def buf_at(at):
        p, m = place_of(sizes, at)
        return buf.at[p * nmode + m]

    start_d, line_d, second_d, third_d, partner_d, drain_d = gatherer(
        sizes, here, buf_at, lambda count: buf.at[pl.ds(0, count)], send.at[0], send_a.at[0], recv.at[0])
    mix_at = lambda at: mix.at[place_of(sizes, at)]

    def mix_many(count):
        if count % nmode == 0:
            return mix.at[pl.ds(0, count // nmode)]
        return mix.at[pl.ds(0, count), 0] if count <= ndp else mix.at[pl.ds(0, count // 2), pl.ds(0, 2)]
    start_m, line_m, second_m, third_m, partner_m, drain_m = gatherer(
        sizes, here, mix_at, mix_many, send.at[1], send_a.at[1], recv.at[1])
    start_d()

    def widen(at):
        p, m = place_of(sizes, at)
        k = p * nmode + m
        for c in range(D // 128):
            src[c, pl.ds(k * rows, rows), :] = buf[k, :, c * 128:(c + 1) * 128].astype(F32)
    widen(here)
    load_in.wait()

    def mask(w):
        row = obs_ref[pl.ds(w, 1), :].astype(F32)
        part = pl.ds(pl.multiple_of(w * L, 32), L)
        acts[part, :] = dot((eye_ref[...] * row).astype(BF), inputs[part, :]).astype(BF)
    each(0, n, mask)
    outs = [load(1, acts, acts_h)]
    outs[0].start()
    rest = []
    for k in range(na + 1):
        if k < na - 1:
            line_d(k + 1, widen)
        if k < na:
            second_d(k, widen)
        if k >= 1:
            third_d(k - 1, widen)
        if k == 1:
            start_m()
        if 1 <= k + 1 - 2 < na:
            line_m(k + 1 - 2)
        if 0 <= k - 2 < na:
            second_m(k - 2)
        if 0 <= k - 2 - 1 < 0:
            third_m(k - 2 - 1)
    done_line, done_second, done_third = min(na - 1, na + 1 - 2), min(na - 1, na - 2), min(0 - 1, na - 2 - 1)
    for k in range(na):
        if k > done_line:
            rest.append(lambda k=k: line_m(k))
        if k > done_second:
            rest.append(lambda k=k: second_m(k))
    for k in range(na):
        if k > done_third:
            rest.append(lambda k=k: third_m(k))
    each(0, na, lambda t: partner_d(t, widen))

    def pick(p):
        for c in range(D // 128):
            for i in range(join):
                tmp[c, i * size:(i + 1) * size, :] = src[c, pl.ds(restore[p * join + i] * size, size), :]
            part = pl.ds(pl.multiple_of(p * join * size, 16), join * size)
            table[part, c * 128:(c + 1) * 128] = tmp[c].astype(BF)
    early = -(-D // (join * size))
    each(0, early, pick)
    T = 384

    def project(i):
        part = pl.ds(pl.multiple_of(i * T, T), T)
        query[part, :] = (dot(acts[part, :], table[0:D, :]) + bias).astype(BF)

    def spectra(w):
        part = pl.ds(pl.multiple_of(w * L, 32), L)
        spread_rows(tiles, w, slots, n, dot(basis_ref[...], query[part, :]))

    parts = n * L // T
    for i in range(parts):
        project(i)
    for i in range(4):
        if rest:
            rest.pop(0)()
        each(i * n // 4, (i + 1) * n // 4, spectra)
    while rest:
        rest.pop(0)()

    def table_out():
        at = 0
        for i, ref in enumerate((wqo_h, wup_h, wdn_h)):
            outs.append(load(2 + i, table.at[pl.ds(at, ref.shape[0])], ref))
            outs[-1].start()
            at += ref.shape[0]

    def mix_slots(places):
        taken = []
        for j, jl, m, h in places:
            x = tiles[h, pl.ds(pl.multiple_of(j * n, n), n), :]
            both = jnp.concatenate([x, swap_halves(x)], 0)[:, :64].astype(BF)
            taken.append((both, head_weights(mix, h, pieces, m, pl.ds(pl.multiple_of(jl * depth, depth), depth))))
        products = [dot(both, w) for both, w in taken]
        for (j, jl, m, h), (both, w), y in zip(places, taken, products):
            z[h, pl.ds(pl.multiple_of(j * 2 * n, 2 * n), 2 * n), :] = both
            tiles[h, pl.ds(pl.multiple_of(j * n, n), n), :] = y[:n] + swap_halves(y[n:]) * sign_lanes(n, -1.0, 1.0)

    if pieces == 1:
        def mix_core(core):
            def some(i):
                def slot(jl, _):
                    m = i * 2 + core
                    mix_slots([(m * per + jl, jl, m, p) for p in range(heads)])
                    return 0
                lax.fori_loop(0, per, slot, 0, unroll=4)
            each(0, nmode // 2, some)
        mix_core(here["c"])
        each(early, units, pick)
        table_out()
        each(0, na, partner_m)
        mix_core(1 - here["c"])
    else:
        each(early, units, pick)
        table_out()
        each(0, na, partner_m)

        def slot(j, _):
            mix_slots([(j, lax.rem(j, per), j // per, h) for h in range(heads)])
            return 0
        lax.fori_loop(0, slots, slot, 0, unroll=4)
    outs.append(load(5, mix, weights_h))
    outs[-1].start()
    outs.append(load(6, z, z_h))
    outs[-1].start()

    def signal(w):
        part = pl.ds(pl.multiple_of(w * L, 32), L)
        sig[part, :] = dot(inv_ref[...], gather_rows(tiles, w, slots, n)).astype(BF)
    each(0, n, signal)
    outs.append(load(7, sig, sig_h))
    outs[-1].start()
    drain_d()
    drain_m()
    for o in outs:
        o.wait()


def head(inputs, observed, dense, mixer, restore, bias, mode_index, inv, ff):
    n, L, D = inputs.shape
    slots = mode_index.shape[0]
    ndp, nmode = lax.axis_size("dp"), lax.axis_size("mode")
    nd = ndp * nmode
    rows, mixer_rows = dense.shape[0], mixer.shape[0]
    anywhere = pl.BlockSpec(memory_space=pl.ANY)
    vmem = pl.BlockSpec(memory_space=pltpu.VMEM)
    sem = lambda *s: pltpu.SemaphoreType.DMA(s)
    tokens = n * L
    return pl.pallas_call(
        functools.partial(head_kernel, n, L, D, slots, restore.shape[0]),
        out_shape=(
            jax.ShapeDtypeStruct((tokens, D), BF),
            jax.ShapeDtypeStruct((8, 2 * slots * n, 64), BF),
            jax.ShapeDtypeStruct((tokens, D), BF),
            jax.ShapeDtypeStruct((2 * D, D), BF),
            jax.ShapeDtypeStruct((ff, D), BF),
            jax.ShapeDtypeStruct((ff, D), BF),
            jax.ShapeDtypeStruct((ndp, nmode, mixer_rows, 128), BF),
        ),
        in_specs=[pl.BlockSpec(memory_space=pltpu.SMEM)] * 2 + [anywhere] + [vmem] * 7,
        out_specs=(anywhere,) * 7,
        scratch_shapes=[
            pltpu.VMEM((tokens, D), BF),
            pltpu.VMEM((tokens, D), BF),
            pltpu.VMEM((tokens, D), BF),
            pltpu.VMEM((8, slots * n, 128), F32),
            pltpu.VMEM((8, 2 * slots * n, 64), BF),
            pltpu.VMEM((tokens, D), BF),
            pltpu.VMEM((nd, rows, D), BF),
            pltpu.VMEM((D // 128, nd * rows + 8, 128), F32),
            pltpu.VMEM((nd * rows, D), BF),
            pltpu.VMEM((ndp, nmode, mixer_rows, 128), BF),
            pltpu.VMEM((D // 128, 4 * (nd * rows // restore.shape[0]), 128), F32),
            pltpu.VMEM((2 * slots, 128), F32),
            pltpu.VMEM((2 * slots, L), BF),
            sem(8), sem(2, 3), sem(2, 2, ndp // (nmode // 2)), sem(2, nd),
        ],
        compiler_params=pltpu.CompilerParams(collective_id=0, has_side_effects=True, vmem_limit_bytes=62 * 1024 * 1024),
        name="head",
    )(restore, mode_index, inputs.reshape(tokens, D), dense, mixer, observed, bias, waves(L), inv, np.eye(L, dtype=np.float32))


def adam_terms(weight, gradient, moment, second, step_rate):
    moment_new = BETA_ONE * moment + (1.0 - BETA_ONE) * gradient
    second_new = BETA_TWO * second + (1.0 - BETA_TWO) * gradient * gradient
    scaled_m = moment_new * (1.0 / (1.0 - BETA_ONE**STEP))
    scaled_v = second_new * (1.0 / (1.0 - BETA_TWO**STEP))
    weight_new = weight - step_rate * (scaled_m / (jnp.sqrt(scaled_v) + ADAM_EPS) + DECAY_RATE * weight)
    return moment_new, second_new, weight_new


def update_kernel(chunks, *refs):
    dense, mixer, small, passed = refs[:4], refs[4:8], refs[8:12], refs[12]
    dense_out, mixer_out, small_out, bias_out, passed_out = refs[13:16], refs[16:19], refs[19:22], refs[22], refs[23]
    held, got, put = refs[24:]
    step = held.shape[0] // chunks
    parts = [pl.ds(i * step, step) for i in range(chunks)]
    gets = [pltpu.make_async_copy(passed.at[p], held.at[p], got.at[i]) for i, p in enumerate(parts)]
    puts = [pltpu.make_async_copy(held.at[p], passed_out.at[p], put.at[i]) for i, p in enumerate(parts)]
    for c in gets:
        c.start()
    for i, (ins, outs, rate) in enumerate(((dense, dense_out, RATE_DENSE), (mixer, mixer_out, RATE_MIXER))):
        for ref, value in zip(outs, adam_terms(*(x[...] for x in ins), rate)):
            ref[...] = value
        if i == 0:
            for g, p in zip(gets, puts):
                g.wait()
                p.start()
    size = small[0].shape[0]
    for r in range(-(-size // 128)):
        n = min(128, size - r * 128)
        at = pl.ds(r * 128, n)
        grad = small[1][r:r + 1, :][:, :n]
        row = lambda x: x[at].reshape(1, n)
        terms = adam_terms(row(small[0]), grad, row(small[2]), row(small[3]), RATE_SMALL)
        for ref, value in zip(small_out, terms):
            ref[at] = value.reshape(n)
    for r in range(bias_out.shape[0] // 128):
        bias_out[pl.ds(r * 128, 128)] = small[1][4 + r:5 + r, :].reshape(128)
    for p in puts:
        p.wait()


def update(dense, mixer, small, passed):
    vmem = pl.BlockSpec(memory_space=pltpu.VMEM)
    anywhere = pl.BlockSpec(memory_space=pl.ANY)
    like = lambda x: jax.ShapeDtypeStruct(x.shape, x.dtype)
    chunks = 4
    return pl.pallas_call(
        functools.partial(update_kernel, chunks),
        out_shape=(like(dense[0]),) * 3 + (like(mixer[0]),) * 3 + (like(small[0]),) * 3 + (
            jax.ShapeDtypeStruct((dense[0].shape[1],), F32), like(passed)),
        in_specs=[vmem] * 12 + [anywhere],
        out_specs=(vmem,) * 10 + (anywhere,),
        scratch_shapes=[pltpu.VMEM(passed.shape, F32), pltpu.SemaphoreType.DMA((chunks,)), pltpu.SemaphoreType.DMA((chunks,))],
        compiler_params=pltpu.CompilerParams(vmem_limit_bytes=62 * 1024 * 1024),
        name="update",
    )(*dense, *mixer, *small, passed)


def inverse_table(slots, length):
    turn = np.arange(length)[:, None] * np.arange(slots)[None, :] % length
    angle = turn * (2.0 * np.pi / length)
    scale = np.where(np.arange(slots) == 0, 1.0, 2.0) / length
    return np.concatenate([np.cos(angle) * scale, -np.sin(angle) * scale], 1).astype(np.float32).astype(BF)


def shards(
    inputs,
    observed,
    out_grad,
    mode_index,
    owner_list,
    dense_master,
    dense_first,
    dense_second,
    mixer_master,
    mixer_first,
    mixer_second,
    small_master,
    small_first,
    small_second,
):
    ndp, nmode = lax.axis_size("dp"), lax.axis_size("mode")
    length, width = inputs.shape[1:]
    slots = mode_index.shape[0]
    hidden = (dense_master.shape[0] * ndp * nmode - 2 * width) // 2
    inv = inverse_table(slots, length)
    places = jnp.arange(owner_list.shape[0], dtype=jnp.int32)
    restore = jnp.sum(jnp.where(owner_list[None, :] == places[:, None], places[None, :], 0), axis=1)
    acts, spectra, sig, wqo, wup, wdn, weights = head(
        inputs, observed, dense_master, mixer_master.reshape(-1, mixer_master.shape[2]), restore, small_master,
        mode_index, inv, hidden,
    )
    output, grad_summed, grad_mixed, g_out, g_up, g_down, sums = middle(
        small_master, acts.reshape(inputs.shape), sig.reshape(inputs.shape), out_grad, wqo, wup, wdn,
        small_master, np.ascontiguousarray(inv.T),
    )
    dense_mine, mixer_mine, small_all, input_grad = tail(
        grad_mixed.reshape(-1, width), spectra, acts, grad_summed.reshape(-1, width), observed, wqo, mode_index, weights,
        g_out, g_up, g_down, sums, owner_list, dense_master.shape[0],
    )
    flat = lambda x: x.reshape(-1, x.shape[-1])
    dense_first_new, dense_second_new, dense_new, mixer_first_new, mixer_second_new, mixer_new, *small, input_grad = update(
        (dense_master, dense_mine, dense_first, dense_second),
        (flat(mixer_master), mixer_mine, flat(mixer_first), flat(mixer_second)),
        (small_master, small_all, small_first, small_second),
        input_grad,
    )
    mixer_first_new, mixer_second_new, mixer_new = (
        x.reshape(mixer_master.shape) for x in (mixer_first_new, mixer_second_new, mixer_new)
    )
    return (
        output,
        input_grad.reshape(inputs.shape),
        dense_first_new,
        dense_second_new,
        dense_new,
        mixer_first_new,
        mixer_second_new,
        mixer_new,
        *small,
    )


def solution(mesh):
    placed = (
        P(("dp", "mode"), None, None),
        P(("dp", "mode"), None),
        P(("dp", "mode"), None, None),
        P(),
        P(),
        P(("dp", "mode"), None),
        P(("dp", "mode"), None),
        P(("dp", "mode"), None),
        P("mode", "dp", None),
        P("mode", "dp", None),
        P("mode", "dp", None),
        P(),
        P(),
        P(),
    )
    return jax.shard_map(
        shards,
        mesh=mesh,
        in_specs=placed,
        out_specs=(
            P(("dp", "mode"), None, None),
            P(("dp", "mode"), None, None),
            P(("dp", "mode"), None),
            P(("dp", "mode"), None),
            P(("dp", "mode"), None),
            P("mode", "dp", None),
            P("mode", "dp", None),
            P("mode", "dp", None),
            P(),
            P(),
            P(),
            P(),
        ),
        check_vma=False,
    )
```
